128 devices in a mesh: lon: 16 (over y, z_hi, core), lat: 8 (over z_lo, x).
Axes of the slice: x: 4, y: 4, z: 4 (z_hi: 2, z_lo: 2; z = z_hi * 2 + z_lo), core: 2. Of those that a mesh axis runs over, the one named last changes fastest.
Arguments:
- tracers: float32 [2, 4, 512, 4096], P(None, None, 'lat', 'lon'), may hold values from -6 to 6
- velocity: float32 [3, 4, 512, 4096], P(None, None, 'lat', 'lon'), may hold values from -0.15 to 0.15
- slopes: float32 [2, 4, 512, 4096], P(None, None, 'lat', 'lon'), may hold values from -1 to 1
- diffusivity: float32 [4, 512, 4096], P(None, 'lat', 'lon'), may hold values from 0.02 to 0.1
- sea_mask: int32 [4, 512, 4096], P(None, 'lat', 'lon'), may hold values from 0 to 1, as said below
Outputs:
- tracers_next: float32 [2, 4, 512, 4096], P(None, None, 'lat', 'lon')
The draws below stay inside these ranges and needn't reach their ends.
Inputs may be any that keep to these rules, and one draw needn't show every extreme that they name: `sea_mask`: 1 marks sea and 0 land; the sea cells of each column are its top levels.
All inputs are finite; a program needn't handle non-finite values.
Results may differ from the reference program's by a relative error of at most 0.0003.
Values sent between devices are 32-bit elements; how exact they have to be, the bound alone decides.
No kernel may reach another device: no remote copies, remote signals or barrier semaphores. Data moves between devices by JAX's collectives and lax.ppermute only.
A program may use at most 64 MiB of HBM per device.

```python
import math
import jax
import jax.numpy as jnp
from jax import lax

K = 4
CY = 64
CX = 256
NY = 512
NX = 4096


def border_band(width):
    rows = jnp.arange(NY, dtype=jnp.int32) % CY
    cols = jnp.arange(NX, dtype=jnp.int32) % CX
    near_row = jnp.minimum(rows, CY - 1 - rows) < width
    near_col = jnp.minimum(cols, CX - 1 - cols) < width
    return jnp.logical_or(near_row[:, None], near_col[None, :])


def banded_field(key, shape, edge_lo, edge_hi, inner_half):
    sign_key, size_key, inner_key = jax.random.split(key, 3)
    coin = jax.random.uniform(sign_key, shape, jnp.float32, 0.0, 1.0)
    signs = jnp.where(coin < 0.5, 1.0, -1.0)
    edge = signs * jax.random.uniform(size_key, shape, jnp.float32, edge_lo, edge_hi)
    inner = jax.random.uniform(inner_key, shape, jnp.float32, -inner_half, inner_half)
    band = border_band(3)
    return jnp.where(band, edge, inner).astype(jnp.float32)


def draw_tracers(key, part):
    shape = (2, K, NY, NX)
    return banded_field(jax.random.fold_in(key, 12), shape, 3.0, 6.0, 0.6)


def draw_velocity(key, part):
    shape = (3, K, NY, NX)
    return banded_field(jax.random.fold_in(key, 22), shape, 0.1, 0.15, 0.05)


def draw_slopes(key, part):
    shape = (2, K, NY, NX)
    return banded_field(jax.random.fold_in(key, 32), shape, 0.6, 1.0, 0.3)


def draw_sea_mask(key, part):
    first_key, second_key = jax.random.split(key)
    depth = jnp.maximum(jax.random.randint(first_key, (NY, NX), 0, K + 1), jax.random.randint(second_key, (NY, NX), 0, K + 1))
    levels = jnp.arange(K, dtype=jnp.int32)
    return (levels[:, None, None] < depth[None, :, :]).astype(jnp.int32)


def steps_of(own_key, shape, pieces, least, top_value):
    def one(position, shards_of):
        steps = jax.random.uniform(jax.random.fold_in(jax.random.fold_in(own_key, 6), position), (shards_of,), jnp.float32, least / len(pieces), top_value / len(pieces))
        return jnp.repeat(jnp.exp(steps), shape[position] // shards_of).reshape((-1,) + (1,) * (len(shape) - position - 1))

    gain = one(*pieces[0])
    for cut in pieces[1:]:
        gain = gain * one(*cut)
    return gain


def setup_inputs(seed: int = 0) -> dict:
    seeds = jax.random.split(jax.random.key(seed), 6)
    tracers = draw_tracers(jax.random.fold_in(seeds[5], 71), 0)
    velocity = draw_velocity(jax.random.fold_in(seeds[5], 71), 0)
    slopes = draw_slopes(jax.random.fold_in(seeds[5], 71), 0)
    diffusivity = jnp.clip(jnp.exp(math.log(0.1) - 1.609438 * jax.random.uniform(seeds[3], (K, NY, NX), jnp.float32) ** steps_of(seeds[3], (K, NY, NX), ((1, 8), (2, 16)), -0.2, 0.2)), 0.02, 0.1)
    sea_mask = draw_sea_mask(jax.random.fold_in(seeds[5], 71), 0)
    return {"tracers": tracers, "velocity": velocity, "slopes": slopes, "diffusivity": diffusivity, "sea_mask": sea_mask}


def minmod(first, second):
    smaller = jnp.minimum(jnp.abs(first), jnp.abs(second))
    agreeing = first * second > 0.0
    return jnp.where(agreeing, jnp.where(first > 0.0, smaller, -smaller), 0.0)


def take(array, start, count, direction):
    return lax.slice_in_dim(array, start, start + count, axis=direction)


def face_flux(tracer, marker, speed_cells, direction):
    length = tracer.shape[direction]
    open_face = take(marker, 0, length - 1, direction) * take(marker, 1, length - 1, direction)
    steps = (take(tracer, 1, length - 1, direction) - take(tracer, 0, length - 1, direction)) * open_face
    speeds = 0.5 * (take(speed_cells, 0, length - 1, direction) + take(speed_cells, 1, length - 1, direction)) * open_face
    speed = take(speeds, 1, length - 3, direction)
    centre = take(steps, 1, length - 3, direction)
    upwind = jnp.where(speed >= 0.0, take(steps, 0, length - 3, direction), take(steps, 2, length - 3, direction))
    flux = (jnp.maximum(speed, 0.0) * take(tracer, 1, length - 3, direction)
            + jnp.minimum(speed, 0.0) * take(tracer, 2, length - 3, direction)
            + 0.5 * jnp.abs(speed) * (1.0 - jnp.abs(speed)) * minmod(upwind, centre))
    return take(flux, 1, length - 4, direction) - take(flux, 0, length - 4, direction)


def trimmed(array, margin):
    return array[:, margin:array.shape[1] - margin, margin:array.shape[2] - margin]


def advect(tracer, marker, eastward, northward, downward):
    across_x = face_flux(tracer, marker, eastward, 2)[:, 2:-2, :]
    across_y = face_flux(tracer, marker, northward, 1)[:, :, 2:-2]
    levels = ((2, 2), (0, 0), (0, 0))
    across_z = face_flux(jnp.pad(trimmed(tracer, 2), levels), jnp.pad(trimmed(marker, 2), levels),
                         jnp.pad(downward, levels), 0)
    return (trimmed(tracer, 2) - across_x - across_y - across_z) * trimmed(marker, 2)


def diffuse(tracer, slope_east, slope_north, diffusivity, marker):
    levels = ((1, 1), (0, 0), (0, 0))
    padded = jnp.pad(tracer, levels)
    padded_marker = jnp.pad(marker, levels)
    step_z = (padded[1:] - padded[:-1]) * padded_marker[1:] * padded_marker[:-1]
    centre_z = 0.5 * (step_z[:-1] + step_z[1:])
    open_x = marker[:, :, 1:] * marker[:, :, :-1]
    step_x = (tracer[:, :, 1:] - tracer[:, :, :-1]) * open_x
    centre_x = 0.5 * (step_x[:, :, :-1] + step_x[:, :, 1:])
    open_y = marker[:, 1:, :] * marker[:, :-1, :]
    step_y = (tracer[:, 1:, :] - tracer[:, :-1, :]) * open_y
    centre_y = 0.5 * (step_y[:, :-1, :] + step_y[:, 1:, :])
    flux_x = -0.5 * (diffusivity[:, :, 1:] + diffusivity[:, :, :-1]) * (
        step_x + 0.5 * (slope_east[:, :, 1:] + slope_east[:, :, :-1]) * 0.5 * (centre_z[:, :, 1:] + centre_z[:, :, :-1])) * open_x
    flux_y = -0.5 * (diffusivity[:, 1:, :] + diffusivity[:, :-1, :]) * (
        step_y + 0.5 * (slope_north[:, 1:, :] + slope_north[:, :-1, :]) * 0.5 * (centre_z[:, 1:, :] + centre_z[:, :-1, :])) * open_y
    across_x = flux_x[:, 1:-1, 1:] - flux_x[:, 1:-1, :-1]
    across_y = flux_y[:, 1:, 1:-1] - flux_y[:, :-1, 1:-1]
    inner_x = centre_x[:, 1:-1, :]
    inner_y = centre_y[:, :, 1:-1]
    east_in = trimmed(slope_east, 1)
    north_in = trimmed(slope_north, 1)
    kappa_in = trimmed(diffusivity, 1)
    marker_in = trimmed(marker, 1)
    east_face = 0.5 * (east_in[1:] + east_in[:-1])
    north_face = 0.5 * (north_in[1:] + north_in[:-1])
    flux_z = -0.5 * (kappa_in[1:] + kappa_in[:-1]) * (
        east_face * 0.5 * (inner_x[1:] + inner_x[:-1])
        + north_face * 0.5 * (inner_y[1:] + inner_y[:-1])
        + (east_face * east_face + north_face * north_face) * step_z[1:-1, 1:-1, 1:-1]) * marker_in[1:] * marker_in[:-1]
    flux_z = jnp.pad(flux_z, levels)
    across_z = flux_z[1:] - flux_z[:-1]
    return (trimmed(tracer, 1) - across_x - across_y - across_z) * marker_in


def extend_global(field, margin, sign):
    beside_all = jnp.concatenate([field[:, :, -margin:], field, field[:, :, :margin]], axis=2)
    folded = sign * jnp.flip(beside_all[:, -margin:, :], (1, 2))
    below = jnp.zeros((field.shape[0], margin, beside_all.shape[2]), jnp.float32)
    return jnp.concatenate([below, beside_all, folded], axis=1)


def reference(tracers, velocity, slopes, diffusivity, sea_mask):
    marker = sea_mask.astype(jnp.float32)
    marker_two = extend_global(marker, 2, 1.0)
    east_two = extend_global(velocity[0], 2, -1.0)
    north_two = extend_global(velocity[1], 2, -1.0)
    advected = [advect(extend_global(tracers[member], 2, 1.0), marker_two, east_two, north_two, velocity[2])
                for member in range(2)]
    marker_one = extend_global(marker, 1, 1.0)
    east_one = extend_global(slopes[0], 1, -1.0)
    north_one = extend_global(slopes[1], 1, -1.0)
    kappa_one = extend_global(diffusivity, 1, 1.0)
    result = [diffuse(extend_global(advected[member], 1, 1.0), east_one, north_one, kappa_one, marker_one)
              for member in range(2)]
    return jnp.stack(result)
```

```python
import jax
import jax.numpy as jnp
from jax import lax
from jax.experimental import pallas as pl
from jax.experimental.pallas import tpu as pltpu
from jax.sharding import PartitionSpec as P


ROWS = 64
LANES = 128
F32 = jnp.float32
VMEM = pl.BlockSpec(memory_space=pltpu.VMEM)
LIMIT = 48 * 1024 * 1024
FIELDS = ("c", "m", "u", "v", "w", "sx", "k", "sy")
SIDE = FIELDS[:7]


def lane_of():
    return lax.broadcasted_iota(jnp.int32, (8, LANES), 1)


def low_of():
    return lax.broadcasted_iota(jnp.int32, (8, LANES), 0) < 4


def twice_low(x):
    return jnp.where(low_of(), x, pltpu.roll(x, 4, 0))


def twice_high(x):
    return jnp.where(low_of(), pltpu.roll(x, 4, 0), x)


def load_rows(halves, row):
    out = []
    for tracer, velocity, slope, kappa, mask in halves:
        eight = lambda ref, start: ref.reshape(ref.shape[0] * ROWS, LANES)[pl.ds(start + row, 8, stride=ROWS), :]
        four = lambda ref: ref.reshape(ref.shape[0] * ROWS, LANES)[pl.ds(row, 4, stride=ROWS), :]
        out.append(
            {
                "c": eight(tracer, 0),
                "uv": eight(velocity, 0),
                "vw": eight(velocity, 4 * ROWS),
                "s": eight(slope, 0),
                "k": four(kappa),
                "m": four(mask).astype(F32),
            }
        )
    return out


def halves_of(refs):
    return [refs[0::2], refs[1::2]]


def pack_kernel(*refs):
    halves, packed = halves_of(refs[:10]), refs[10]
    lane, low = lane_of(), low_of()
    second = jnp.logical_or(lane == 1, lane == 126)

    def group(g, carry):
        total = jnp.zeros((8, LANES), F32)
        for part in range(8):
            left, right = load_rows(halves, part * 8 + g)
            rim = {n: jnp.where(lane[: left[n].shape[0]] < 64, left[n], right[n]) for n in left}
            mk = jnp.concatenate([rim["m"], rim["k"]], axis=0)
            mku = jnp.where(jnp.logical_and(second, jnp.logical_not(low)), pltpu.roll(rim["uv"], 4, 0), mk)
            sw = jnp.where(low, rim["s"], rim["vw"])
            slots = jnp.where(lane < 14, pltpu.roll(rim["uv"], 13, 1), pltpu.roll(sw, 15, 1))
            slots = jnp.where(lane < 12, pltpu.roll(mku, 9, 1), slots)
            slots = jnp.where(lane < 6, pltpu.roll(rim["c"], 3, 1), slots)
            if part:
                slots = pltpu.roll(slots, 16 * part, 1)
                total = jnp.where(lane < 16 * part, total, slots)
            else:
                total = slots
        packed[g] = total
        return carry

    lax.fori_loop(0, 8, group, 0)


def rows_kernel(*refs):
    halves, outs = halves_of(refs[:10]), dict(zip(FIELDS, refs[10:]))

    def row_group(block, carry):
        for inner in range(4):
            row = block * 4 + inner
            for half, values in enumerate(load_rows(halves, row)):
                full = {
                    "c": values["c"],
                    "m": jnp.concatenate([values["m"]] * 2, axis=0),
                    "u": twice_low(values["uv"]),
                    "v": twice_low(values["vw"]),
                    "w": twice_high(values["vw"]),
                    "sx": twice_low(values["s"]),
                    "sy": twice_high(values["s"]),
                    "k": jnp.concatenate([values["k"]] * 2, axis=0),
                }
                for name in FIELDS:
                    outs[name][row, :, half * LANES : (half + 1) * LANES] = full[name]
        return carry

    lax.fori_loop(0, ROWS // 4, row_group, 0)


def edge_kernel(*refs):
    from_far, from_near = refs[0], refs[1]
    fields = dict(zip(FIELDS, refs[2:10]))
    rim, send_a, send_b = refs[10:]
    lane, low = lane_of(), low_of()
    lon, lat = lax.axis_index("lon"), lax.axis_index("lat")
    slot = lane % 16
    west = (slot < 3) | ((slot >= 6) & (slot < 9)) | (slot == 12) | (slot == 14)
    far_is_west = jnp.broadcast_to(lon % 2, (8, LANES)) == 0
    take_far = west == far_is_west
    for g in range(8):
        rim[g] = jnp.where(take_far, from_far[g], from_near[g])

    def message(top):
        row = lambda q: jnp.where(top, ROWS - 1 - q, q)
        part = lambda name, q, h: fields[name][row(q), :, h * LANES : (h + 1) * LANES]
        pair = lambda n1, q1, n2, q2: [jnp.where(low, part(n1, q1, h), part(n2, q2, h)) for h in range(2)]
        tiles = [[part("c", q, h) for h in range(2)] for q in range(3)]
        tiles += [pair("m", 0, "v", 0), pair("m", 1, "v", 1), pair("m", 2, "u", 0), pair("w", 0, "sy", 0)]
        corners = [pltpu.roll(rim[jnp.where(top, 7 - q, q)], jnp.where(top, 16, 0), 1) for q in range(3)]
        return tiles, [part("k", 0, h) for h in range(2)], corners

    def store(ref, tiles, kappa, corners):
        for i, tile in enumerate(tiles):
            for h in range(2):
                ref[i, :, h * LANES : (h + 1) * LANES] = tile[h]
        packed = corners[0]
        for q in (1, 2):
            packed = jnp.where(lane < 16 * q, packed, pltpu.roll(corners[q], 16 * q, 1))
        ref[7, :, :LANES] = jnp.where(low, kappa[0], pltpu.roll(packed, 4, 0))
        ref[7, :, LANES:] = jnp.where(low, kappa[1], packed)

    even = lat % 2 == 0
    store(send_a, *message(even))
    folds = lat == lax.axis_size("lat") - 1

    @pl.when(jnp.logical_not(folds))
    def _():
        store(send_b, *message(jnp.logical_not(even)))

    @pl.when(folds)
    def _():
        tiles, kappa, corners = message(True)
        backward = LANES - 1 - lane
        flip = lambda x, index: jnp.take_along_axis(x, index, axis=1, mode="promise_in_bounds")
        flip_tile = lambda tile: [flip(tile[1], backward), flip(tile[0], backward)]
        sign = jnp.where(low, 1.0, -1.0)
        turned = [flip_tile(tile) for tile in tiles]
        turned = turned[:3] + [[sign * x for x in tile] for tile in turned[3:]]
        index = jnp.where(lane < 6, 5 - lane, jnp.where(lane < 12, 17 - lane, jnp.where(lane < 14, 25 - lane, 29 - lane)))
        index = jnp.where(lane < 16, index, lane)
        uv = (lane == 12) | (lane == 13) | (((lane == 7) | (lane == 10)) & jnp.logical_not(low))
        corner_sign = jnp.where(uv, -1.0, 1.0)
        store(send_b, turned, flip_tile(kappa), [corner_sign * flip(x, index) for x in corners])


def decode_rim(vector, part):
    lane = lane_of()
    at = lambda first: pltpu.roll(vector, lax.rem(2 * LANES - 16 * part - first, LANES), 1)
    mku, uv, sw = at(9), at(13), at(15)
    second = jnp.logical_or(lane == 1, lane == 126)
    high = twice_high(mku)
    return {
        "c": at(3),
        "m": twice_low(mku),
        "u": jnp.where(second, high, twice_low(uv)),
        "v": twice_high(uv),
        "w": twice_high(sw),
        "sx": twice_low(sw),
        "k": high,
    }


def plus(tiles):
    last = lane_of() == LANES - 1
    turned = [pltpu.roll(t, LANES - 1, 1) for t in tiles]
    return [jnp.where(last, turned[(i + 1) % 3], turned[i]) for i in range(3)]


def minus(tiles, count=3):
    first = lane_of() == 0
    turned = [pltpu.roll(t, 1, 1) for t in tiles]
    return [jnp.where(first, turned[(i + 2) % 3], turned[i]) for i in range(count)]


def each(function, *lists):
    return [function(*values) for values in zip(*lists)]


def below(x):
    return pltpu.roll(x, 7, 0)


def above(x):
    return pltpu.roll(x, 1, 0)


def face_flux(here, there, speed, back, step, ahead):
    positive = speed >= 0.0
    upwind = jnp.where(positive, back, ahead)
    size = jnp.abs(speed)
    limited = jnp.maximum(jnp.minimum(upwind, step), 0.0) + jnp.minimum(jnp.maximum(upwind, step), 0.0)
    return speed * jnp.where(positive, here, there) + 0.5 * (size - size * size) * limited


def not_bottom():
    return lax.broadcasted_iota(jnp.int32, (8, LANES), 0) % 4 != 3


def open_below(marker):
    return jnp.where(not_bottom(), marker * below(marker), 0.0)


def face_speed(one, two, opened):
    return 0.5 * (one + two) * opened


def advect_rows(get, first, count):
    c = {j: get("c", first + j) for j in range(-2, count + 2)}
    m = {j: get("m", first + j) for j in range(-2, count + 2)}
    v = {j: get("v", first + j) for j in range(-1, count + 1)}
    opened = {j: each(jnp.multiply, m[j], m[j + 1]) for j in range(-2, count + 1)}
    step = {j: each(lambda a, b, o: (b - a) * o, c[j], c[j + 1], opened[j]) for j in range(-2, count + 1)}
    flux = {}
    for j in range(-1, count):
        speed = each(face_speed, v[j], v[j + 1], opened[j])
        flux[j] = each(face_flux, c[j], c[j + 1], speed, step[j - 1], step[j], step[j + 1])
    result = []
    for j in range(count):
        east = plus(c[j])
        opened_x = each(jnp.multiply, m[j], plus(m[j]))
        u = get("u", first + j)
        speed = each(face_speed, u, plus(u), opened_x)
        step_x = each(lambda a, b, o: (b - a) * o, c[j], east, opened_x)
        flux_x = each(face_flux, c[j], east, speed, minus(step_x), step_x, plus(step_x))
        total = each(lambda f, g, a, b: (f - g) + (a - b), flux_x, minus(flux_x), flux[j], flux[j - 1])
        w = get("w", first + j)

        def finish(value, marker, down, across):
            opened_z = open_below(marker)
            under = below(value)
            step_z = (under - value) * opened_z
            speed_z = face_speed(down, below(down), opened_z)
            flux_z = face_flux(value, under, speed_z, above(step_z), step_z, below(step_z))
            return (value - across - (flux_z - above(flux_z))) * marker

        result.append(each(finish, c[j], m[j], w, total))
    return result


def diffuse_rows(get, first, count):
    a = {j: get("a", first + j) for j in range(-1, count + 1)}
    m = {j: get("m", first + j) for j in range(-1, count + 1)}
    k = {j: get("k", first + j) for j in range(-1, count + 1)}
    sy = {j: get("sy", first + j) for j in range(-1, count + 1)}
    step_z, twice_z = {}, {}
    for j in range(-1, count + 1):
        wide = 3 if 0 <= j < count else 2
        step_z[j] = each(lambda x, o: (below(x) - x) * open_below(o), a[j][:wide], m[j])
        twice_z[j] = each(lambda x: above(x) + x, step_z[j])
    step_y, flux_y = {}, {}
    for j in range(-1, count):
        opened = each(jnp.multiply, m[j][:2], m[j + 1][:2])
        step_y[j] = each(lambda x, y, o: (y - x) * o, a[j][:2], a[j + 1][:2], opened)
        flux_y[j] = each(
            lambda k1, k2, o, s, s1, s2, z1, z2: 0.5 * (k1 + k2) * o * (s + 0.125 * (s1 + s2) * (z1 + z2)),
            k[j], k[j + 1], opened, step_y[j], sy[j], sy[j + 1], twice_z[j], twice_z[j + 1],
        )
    result = []
    for j in range(count):
        sx = get("sx", first + j)
        opened = each(jnp.multiply, m[j], plus(m[j]))
        step_x = each(lambda x, y, o: (y - x) * o, a[j], plus(a[j]), opened)
        flux_x = each(
            lambda k1, k2, o, s, s1, s2, z1, z2: 0.5 * (k1 + k2) * o * (s + 0.125 * (s1 + s2) * (z1 + z2)),
            k[j], plus(k[j]), opened, step_x, sx, plus(sx), twice_z[j], plus(twice_z[j]),
        )
        twice_x = each(jnp.add, step_x, minus(step_x, 2))
        twice_y = each(jnp.add, step_y[j - 1], step_y[j])
        total = each(lambda f, g, p, q: (f - g) + (p - q), flux_x, minus(flux_x, 2), flux_y[j], flux_y[j - 1])

        def finish(value, marker, kappa, east, north, tx, ty, sz, across):
            face_east, face_north = 0.5 * (east + below(east)), 0.5 * (north + below(north))
            flux_z = (
                0.5 * (kappa + below(kappa)) * open_below(marker)
                * (0.25 * (face_east * (tx + below(tx)) + face_north * (ty + below(ty)))
                   + (face_east * face_east + face_north * face_north) * sz)
            )
            return (value + across + (flux_z - above(flux_z))) * marker

        result.append(each(finish, a[j][:2], m[j], k[j], sx, sy[j], twice_x, twice_y, step_z[j], total))
    return result


def tiles_of(ref, row, count):
    return [ref[row, :, t * LANES : (t + 1) * LANES] for t in range(count)]


def interior_kernel(*refs):
    fields, rim = dict(zip(FIELDS, refs[:8])), refs[8]
    sides = dict(zip(SIDE, refs[9:16]))
    advected, out = refs[16:]

    def spread(g, carry):
        for part in range(8):
            row = part * 8 + g
            for name, value in decode_rim(rim[g], part).items():
                sides[name][row] = value
        return carry

    lax.fori_loop(0, 8, spread, 0)

    def get(name, row):
        if name == "a":
            return tiles_of(advected, row, 3)
        if name == "sy":
            return tiles_of(fields[name], row, 2)
        return tiles_of(fields[name], row, 2) + [sides[name][row]]

    def advect_block(block, carry):
        first = 2 + 4 * block
        for j, tiles in enumerate(advect_rows(get, first, 4)):
            for t in range(3):
                advected[first + j, :, t * LANES : (t + 1) * LANES] = tiles[t]
        return carry

    lax.fori_loop(0, 15, advect_block, 0)

    def diffuse_block(block, carry):
        first = 3 + 2 * block
        for j, tiles in enumerate(diffuse_rows(get, first, 2)):
            for t in range(2):
                out[first + j, :, t * LANES : (t + 1) * LANES] = tiles[t]
        return carry

    lax.fori_loop(0, 29, diffuse_block, 0)


def rim_kernel(*refs):
    got_a, got_b = refs[0], refs[1]
    fields = dict(zip(FIELDS, refs[2:10]))
    sides = dict(zip(SIDE, refs[10:17]))
    advected, inner, out, edges, sems = refs[17:]
    middle = pltpu.make_async_copy
    copies = [middle(inner.at[8:56, i], out.at[i, 8:56], sems.at[i]) for i in range(8)]
    for copy in copies:
        copy.start()
    low = low_of()
    lat = lax.axis_index("lat")
    even = jnp.broadcast_to(lat % 2, (8, LANES)) == 0
    floor = jnp.broadcast_to(lat, (8, LANES)) == 0

    def halo(is_north):
        def tile(i, h):
            a = got_a[i, :, h * LANES : (h + 1) * LANES]
            b = got_b[i, :, h * LANES : (h + 1) * LANES]
            if is_north:
                return jnp.where(even, a, b)
            return jnp.where(floor, 0.0, jnp.where(even, b, a))

        tiles = [[tile(i, h) for h in range(2)] for i in range(8)]
        high = lambda i: [twice_high(x) for x in tiles[i]]
        below_four = lambda i: [twice_low(x) for x in tiles[i]]
        corner = jnp.where(low, pltpu.roll(tiles[7][0], 4, 0), tiles[7][1])
        rows = []
        for q in range(3):
            side = decode_rim(corner, q)
            main = {"c": tiles[q], "m": below_four(3 + q)}
            if q < 2:
                main["v"] = high(3 + q)
            if q == 0:
                main.update(u=high(5), w=below_four(6), sy=high(6), k=below_four(7))
                main["sx"] = main["k"]
            rows.append({n: x + [side[n]] if n in side else x for n, x in main.items()})
        return rows

    for is_north in (False, True):
        rows = halo(is_north)
        start = ROWS - 2 if is_north else -1
        made = {}

        def get(name, row):
            if name == "a":
                return made[row] if row in made else tiles_of(advected, row, 3)
            if row < 0:
                return rows[-row - 1][name]
            if row >= ROWS:
                return rows[row - ROWS][name]
            if name == "sy":
                return tiles_of(fields[name], row, 2)
            return tiles_of(fields[name], row, 2) + [sides[name][row]]

        for j, tiles in enumerate(advect_rows(get, start, 3)):
            made[start + j] = tiles
        final = ROWS - 3 if is_north else 0
        base = ROWS - 8 if is_north else 0
        done = {final + j: x for j, x in enumerate(diffuse_rows(get, final, 3))}
        for h in range(2):
            stack = [done[j][h] if j in done else inner[j, :, h * LANES : (h + 1) * LANES] for j in range(base, base + 8)]
            edges[int(is_north), :, :, h * LANES : (h + 1) * LANES] = jnp.transpose(jnp.stack(stack), (1, 0, 2))
        copy = middle(edges.at[int(is_north)], out.at[:, base : base + 8], sems.at[8 + int(is_north)])
        copy.start()
        copies.append(copy)
    for copy in copies:
        copy.wait()


def call(kernel, shapes, *operands, **options):
    return pl.pallas_call(
        kernel,
        out_shape=[jax.ShapeDtypeStruct(s, F32) for s in shapes],
        in_specs=[VMEM] * len(operands),
        out_specs=[VMEM] * len(shapes),
        compiler_params=pltpu.CompilerParams(vmem_limit_bytes=LIMIT),
        **options,
    )(*operands)


def from_fields(kernel, shapes, arrays, **options):
    specs, operands = [], []
    for x in arrays:
        for h in range(2):
            specs.append(pl.BlockSpec((x.shape[0], ROWS, LANES), lambda i, h=h: (0, 0, h)))
            operands.append(x)
    return pl.pallas_call(
        kernel,
        grid=(1,),
        out_shape=[jax.ShapeDtypeStruct(s, F32) for s in shapes],
        in_specs=specs,
        out_specs=[VMEM] * len(shapes),
        compiler_params=pltpu.CompilerParams(vmem_limit_bytes=LIMIT),
        **options,
    )(*operands)


def make(lons, lats):
    def spot(lon, lat):
        return (lon % lons) * lats + lat

    near = [(spot(i, j), spot(i ^ 1, j)) for i in range(lons) for j in range(lats)]
    far = [(spot(i, j), spot(i + 1 if i % 2 else i - 1, j)) for i in range(lons) for j in range(lats)]
    pair_a = [(spot(i, j), spot(i, j ^ 1)) for i in range(lons) for j in range(lats)]
    pair_b = []
    for i in range(lons):
        for j in range(lats):
            if j == 0:
                pair_b.append((spot(i, j), spot(i ^ 1, j)))
            elif j == lats - 1:
                pair_b.append((spot(i, j), spot(lons - 1 - i, j)))
            else:
                pair_b.append((spot(i, j), spot(i, j + 1 if j % 2 else j - 1)))

    def move(x, route):
        return lax.ppermute(x, ("lon", "lat"), route)

    def shards(tracers, velocity, slopes, diffusivity, sea_mask):
        plane = lambda x: x.reshape(-1, ROWS, 2 * LANES)
        arrays = [plane(tracers), plane(velocity), plane(slopes), diffusivity, sea_mask]
        full, side = (ROWS, 8, 2 * LANES), (ROWS, 8, LANES)
        (packed,) = from_fields(pack_kernel, [(8, 8, LANES)], arrays)
        far_got, near_got = move(packed, far), move(packed, near)
        fields = from_fields(
            rows_kernel, [full] * 8, arrays,
            cost_estimate=pl.CostEstimate(flops=10**7, bytes_accessed=6 * 10**6, transcendentals=0),
        )
        rim, send_a, send_b = call(edge_kernel, [(8, 8, LANES), (8, 8, 2 * LANES), (8, 8, 2 * LANES)], far_got, near_got, *fields)
        got_b, got_a = move(send_b, pair_b), move(send_a, pair_a)
        *rest, advected, inner = call(
            interior_kernel, [side] * 7 + [(ROWS, 8, 3 * LANES), full], *fields, rim,
            cost_estimate=pl.CostEstimate(flops=2 * 10**7, bytes_accessed=10**7, transcendentals=0),
        )
        out = pl.pallas_call(
            rim_kernel,
            out_shape=jax.ShapeDtypeStruct((8, ROWS, 2 * LANES), F32),
            in_specs=[VMEM] * 19,
            out_specs=pl.BlockSpec(memory_space=pl.ANY),
            scratch_shapes=[pltpu.VMEM((2, 8, 8, 2 * LANES), F32), pltpu.SemaphoreType.DMA((10,))],
            compiler_params=pltpu.CompilerParams(vmem_limit_bytes=LIMIT),
        )(got_a, got_b, *fields, *rest, advected, inner)
        return out.reshape(tracers.shape)

    return shards


def solution(mesh):
    return jax.shard_map(
        make(mesh.shape["lon"], mesh.shape["lat"]),
        mesh=mesh,
        in_specs=(
            P(None, None, "lat", "lon"),
            P(None, None, "lat", "lon"),
            P(None, None, "lat", "lon"),
            P(None, "lat", "lon"),
            P(None, "lat", "lon"),
        ),
        out_specs=P(None, None, "lat", "lon"),
        check_vma=False,
    )
```

```python
import jax
import jax.numpy as jnp
from jax import lax
from jax.experimental import pallas as pl
from jax.experimental.pallas import tpu as pltpu
from jax.sharding import PartitionSpec as P


ROWS = 64
LANES = 128
F32 = jnp.float32
VMEM = pl.BlockSpec(memory_space=pltpu.VMEM)
LIMIT = 16 * 1024 * 1024
FIELDS = ("c", "m", "u", "v", "w", "sx", "k", "sy")
GROUPS = ("c", "mu", "vw", "sk")


def lane_of():
    return lax.broadcasted_iota(jnp.int32, (8, LANES), 1)


def low_of():
    return lax.broadcasted_iota(jnp.int32, (8, LANES), 0) < 4


def twice_low(x):
    return jnp.where(low_of(), x, pltpu.roll(x, 4, 0))


def twice_high(x):
    return jnp.where(low_of(), pltpu.roll(x, 4, 0), x)


def load_rows(halves, row):
    out = []
    for tracer, velocity, slope, kappa, mask in halves:
        eight = lambda ref, start: ref.reshape(ref.shape[0] * ROWS, LANES)[pl.ds(start + row, 8, stride=ROWS), :]
        four = lambda ref: ref.reshape(ref.shape[0] * ROWS, LANES)[pl.ds(row, 4, stride=ROWS), :]
        out.append(
            {
                "c": eight(tracer, 0),
                "uv": eight(velocity, 0),
                "vw": eight(velocity, 4 * ROWS),
                "s": eight(slope, 0),
                "k": four(kappa),
                "m": four(mask).astype(F32),
            }
        )
    return out


def pack_kernel(*refs):
    arrays, parts, message, spare, sems = refs[:5], refs[5:15], refs[15], refs[16], refs[17]
    copies = []
    for i, array in enumerate(arrays):
        for h in range(2):
            part = pltpu.make_async_copy(
                array.at[:, :, h * LANES : (h + 1) * LANES], parts[2 * i + h], sems.at[2 * i + h]
            )
            part.start()
            copies.append(part)
    for part in copies:
        part.wait()
    halves = [parts[0::2], parts[1::2]]
    lane, low = lane_of(), low_of()

    def group(g, carry):
        first = second = jnp.zeros((8, LANES), F32)
        for part in range(8):
            left, right = load_rows(halves, part * 8 + g)
            rim = {n: jnp.where(lane[: left[n].shape[0]] < 64, left[n], right[n]) for n in left}
            mk = jnp.concatenate([rim["m"], rim["k"]], axis=0)
            mu = jnp.where(low, mk, pltpu.roll(rim["uv"], 4, 0))
            sk = jnp.where(low, rim["s"], mk)
            base = 16 * part
            before, half = lane < base, lane < base + 8
            one = jnp.where(half, pltpu.roll(rim["c"], (base + 4) % LANES, 1), pltpu.roll(mu, (base + 12) % LANES, 1))
            two = jnp.where(half, pltpu.roll(rim["vw"], (base + 4) % LANES, 1), pltpu.roll(sk, (base + 12) % LANES, 1))
            first = jnp.where(before, first, one)
            second = jnp.where(before, second, two)
        message[g] = first
        spare[g] = second
        return carry

    lax.fori_loop(0, 8, group, 0)
    slot = lane % 8
    for pair in range(2):
        total = pltpu.roll(spare[4 * pair], LANES - 2, 1)
        for i in range(1, 4):
            moved = spare[4 * pair + i] if i == 1 else pltpu.roll(spare[4 * pair + i], 2 * i - 2, 1)
            total = jnp.where((slot == (2 * i + 1) % 8) | (slot == (2 * i + 2) % 8), moved, total)
        message[8 + pair] = total


def rows_kernel(*refs):
    parts, outs, advected = refs[:10], dict(zip(FIELDS, refs[10:18])), refs[18]
    halves = [parts[0::2], parts[1::2]]

    def row_group(block, carry):
        for inner in range(8):
            row = block * 8 + inner
            for half, values in enumerate(load_rows(halves, row)):
                full = {
                    "c": values["c"],
                    "m": jnp.concatenate([values["m"]] * 2, axis=0),
                    "u": twice_low(values["uv"]),
                    "v": twice_low(values["vw"]),
                    "w": twice_high(values["vw"]),
                    "sx": twice_low(values["s"]),
                    "sy": twice_high(values["s"]),
                    "k": jnp.concatenate([values["k"]] * 2, axis=0),
                }
                for name in FIELDS:
                    outs[name][row, :, half * LANES : (half + 1) * LANES] = full[name]
        return carry

    lax.fori_loop(0, ROWS // 8, row_group, 0)
    get = lambda name, row: tiles_of(outs[name], row, 2)

    def advect_block(block, carry):
        first = 2 + 10 * block
        for j, tiles in enumerate(advect_rows(get, first, 10)):
            for t in range(2):
                advected[first + j, :, t * LANES : (t + 1) * LANES] = tiles[t]
        return carry

    lax.fori_loop(0, 6, advect_block, 0)


def edge_kernel(*refs):
    from_far, from_near, own, spare = refs[:4]
    fields = dict(zip(FIELDS, refs[4:12]))
    strips, send_a, send_b = refs[12:]
    lane, low = lane_of(), low_of()
    lon, lat = lax.axis_index("lon"), lax.axis_index("lat")
    slot = lane % 16
    far_is_west = jnp.broadcast_to(lon % 2, (8, LANES)) == 0

    def strip(mine, east, west, late):
        shift = lambda x, by: pltpu.roll(x, (by - 8 * late) % LANES, 1) if by != 8 * late else x
        inner = jnp.where(slot < 4, shift(mine, 0), shift(east, 0))
        outer = jnp.where(slot < 10, shift(west, 6), shift(mine, 6))
        return jnp.where(slot < 7, inner, outer)

    for g in range(8):
        for which in range(2):
            if which == 0:
                far, near, mine = from_far[g], from_near[g], own[g]
            else:
                back = (2 - 2 * (g % 4)) % LANES
                turn = lambda x: pltpu.roll(x, back, 1) if back else x
                far, near, mine = turn(from_far[8 + g // 4]), turn(from_near[8 + g // 4]), spare[g]
            east, west = jnp.where(far_is_west, near, far), jnp.where(far_is_west, far, near)
            for late in range(2):
                strips[2 * which + late, g] = strip(mine, east, west, late)

    def message(top):
        row = lambda q: jnp.where(top, ROWS - 1 - q, q)
        part = lambda name, q, h: fields[name][row(q), :, h * LANES : (h + 1) * LANES]
        pair = lambda n1, q1, n2, q2: [jnp.where(low, part(n1, q1, h), part(n2, q2, h)) for h in range(2)]
        tiles = [[part("c", q, h) for h in range(2)] for q in range(3)]
        tiles += [pair("m", 0, "v", 0), pair("m", 1, "v", 1), pair("m", 2, "u", 0), pair("w", 0, "sy", 0)]
        corners = [
            pltpu.roll(strips[i, jnp.where(top, 7 - q, q)], jnp.where(top, 16, 0), 1) for q in range(2) for i in range(3)
        ]
        return tiles, [part("k", 0, h) for h in range(2)], corners

    def store(ref, tiles, kappa, corners):
        for i, tile in enumerate(tiles):
            for h in range(2):
                ref[i, :, h * LANES : (h + 1) * LANES] = tile[h]
        packed = corners[0]
        for i in range(1, 6):
            packed = jnp.where(lane < 16 * i, packed, pltpu.roll(corners[i], 16 * i, 1))
        ref[7, :, :LANES] = jnp.where(low, kappa[0], pltpu.roll(packed, 4, 0))
        ref[7, :, LANES:] = jnp.where(low, kappa[1], packed)

    even = lat % 2 == 0
    store(send_a, *message(even))
    folds = lat == lax.axis_size("lat") - 1

    @pl.when(jnp.logical_not(folds))
    def _():
        store(send_b, *message(jnp.logical_not(even)))

    @pl.when(folds)
    def _():
        tiles, kappa, corners = message(True)
        backward = LANES - 1 - lane
        flip = lambda x, index: jnp.take_along_axis(x, index, axis=1, mode="promise_in_bounds")
        flip_tile = lambda tile: [flip(tile[1], backward), flip(tile[0], backward)]
        sign = jnp.where(low, 1.0, -1.0)
        turned = [flip_tile(tile) for tile in tiles]
        turned = turned[:3] + [[sign * x for x in tile] for tile in turned[3:]]
        index = jnp.where(lane < 14, 13 - lane, lane)
        corner_signs = [1.0, sign, -sign]
        store(send_b, turned, flip_tile(kappa), [corner_signs[i % 3] * flip(x, index) for i, x in enumerate(corners)])


def split_groups(groups):
    return {
        "c": groups["c"],
        "m": twice_low(groups["mu"]),
        "u": twice_high(groups["mu"]),
        "v": twice_low(groups["vw"]),
        "w": twice_high(groups["vw"]),
        "sx": twice_low(groups["sk"]),
        "k": twice_high(groups["sk"]),
    }


def third_tile(groups, bases):
    east = lane_of() < 64
    tile = lambda x, base: jnp.where(
        east, pltpu.roll(x, (2 * LANES - 4 - base) % LANES, 1), pltpu.roll(x, (2 * LANES - 10 - base) % LANES, 1)
    )
    return split_groups({n: tile(groups[n], bases[n]) for n in GROUPS})


def plus(tiles):
    last = lane_of() == LANES - 1
    turned = [pltpu.roll(t, LANES - 1, 1) for t in tiles]
    if len(tiles) == 1:
        return turned
    return [jnp.where(last, turned[(i + 1) % len(tiles)], turned[i]) for i in range(len(tiles))]


def minus(tiles, count=3, west=None):
    first = lane_of() == 0
    turned = [pltpu.roll(t, 1, 1) for t in tiles]
    if len(tiles) == 1:
        return turned
    before = [turned[-1] if west is None else west] + turned[:-1]
    return [jnp.where(first, before[i], turned[i]) for i in range(min(count, len(tiles)))]


def each(function, *lists):
    return [function(*values) for values in zip(*lists)]


def below(x):
    return pltpu.roll(x, 7, 0)


def above(x):
    return pltpu.roll(x, 1, 0)


def face_flux(here, there, speed, back, step, ahead):
    positive = speed >= 0.0
    upwind = jnp.where(positive, back, ahead)
    size = jnp.abs(speed)
    limited = jnp.maximum(jnp.minimum(upwind, step), 0.0) + jnp.minimum(jnp.maximum(upwind, step), 0.0)
    return speed * jnp.where(positive, here, there) + 0.5 * (size - size * size) * limited


def not_bottom():
    return lax.broadcasted_iota(jnp.int32, (8, LANES), 0) % 4 != 3


def open_below(marker):
    return jnp.where(not_bottom(), marker * below(marker), 0.0)


def face_speed(one, two, opened):
    return 0.5 * (one + two) * opened


def advect_rows(get, first, count):
    c = {j: get("c", first + j) for j in range(-2, count + 2)}
    m = {j: get("m", first + j) for j in range(-2, count + 2)}
    v = {j: get("v", first + j) for j in range(-1, count + 1)}
    opened = {j: each(jnp.multiply, m[j], m[j + 1]) for j in range(-2, count + 1)}
    step = {j: each(lambda a, b, o: (b - a) * o, c[j], c[j + 1], opened[j]) for j in range(-2, count + 1)}
    flux = {}
    for j in range(-1, count):
        speed = each(face_speed, v[j], v[j + 1], opened[j])
        flux[j] = each(face_flux, c[j], c[j + 1], speed, step[j - 1], step[j], step[j + 1])
    result = []
    for j in range(count):
        east = plus(c[j])
        opened_x = each(jnp.multiply, m[j], plus(m[j]))
        u = get("u", first + j)
        speed = each(face_speed, u, plus(u), opened_x)
        step_x = each(lambda a, b, o: (b - a) * o, c[j], east, opened_x)
        flux_x = each(face_flux, c[j], east, speed, minus(step_x), step_x, plus(step_x))
        total = each(lambda f, g, a, b: (f - g) + (a - b), flux_x, minus(flux_x), flux[j], flux[j - 1])
        w = get("w", first + j)

        def finish(value, marker, down, across):
            opened_z = open_below(marker)
            under = below(value)
            step_z = (under - value) * opened_z
            speed_z = face_speed(down, below(down), opened_z)
            flux_z = face_flux(value, under, speed_z, above(step_z), step_z, below(step_z))
            return (value - across - (flux_z - above(flux_z))) * marker

        result.append(each(finish, c[j], m[j], w, total))
    return result


def slope_flux(k1, k2, opened, step, s1, s2, z1, z2):
    return 0.5 * (k1 + k2) * opened * (step + 0.125 * (s1 + s2) * (z1 + z2))


def eastward(a, m, k, sx, twice_z):
    opened = each(jnp.multiply, m, plus(m))
    step = each(lambda x, y, o: (y - x) * o, a, plus(a), opened)
    return step, each(slope_flux, k, plus(k), opened, step, sx, plus(sx), twice_z, plus(twice_z))


def diffuse_rows(get, first, count, beside=None):
    a = {j: get("a", first + j) for j in range(-1, count + 1)}
    m = {j: get("m", first + j) for j in range(-1, count + 1)}
    k = {j: get("k", first + j) for j in range(-1, count + 1)}
    sy = {j: get("sy", first + j) for j in range(-1, count + 1)}
    step_z, twice_z = {}, {}
    for j in range(-1, count + 1):
        wide = 3 if 0 <= j < count else 2
        step_z[j] = each(lambda x, o: (below(x) - x) * open_below(o), a[j][:wide], m[j])
        twice_z[j] = each(lambda x: above(x) + x, step_z[j])
    step_y, flux_y = {}, {}
    for j in range(-1, count):
        opened = each(jnp.multiply, m[j][:2], m[j + 1][:2])
        step_y[j] = each(lambda x, y, o: (y - x) * o, a[j][:2], a[j + 1][:2], opened)
        flux_y[j] = each(
            slope_flux, k[j], k[j + 1], opened, step_y[j], sy[j], sy[j + 1], twice_z[j], twice_z[j + 1]
        )
    result = []
    last = lane_of() == LANES - 1
    for j in range(count):
        sx = get("sx", first + j)
        step_x, flux_x = eastward(a[j], m[j], k[j], sx, twice_z[j])
        west = [None, None]
        if beside:
            east, west = beside(first + j)
            step_x = [step_x[0], jnp.where(last, east[0], step_x[1])]
            flux_x = [flux_x[0], jnp.where(last, east[1], flux_x[1])]
        twice_x = each(jnp.add, step_x, minus(step_x, 2, west[0]))
        twice_y = each(jnp.add, step_y[j - 1], step_y[j])
        total = each(lambda f, g, p, q: (f - g) + (p - q), flux_x, minus(flux_x, 2, west[1]), flux_y[j], flux_y[j - 1])

        def finish(value, marker, kappa, east, north, tx, ty, sz, across):
            face_east, face_north = 0.5 * (east + below(east)), 0.5 * (north + below(north))
            flux_z = (
                0.5 * (kappa + below(kappa)) * open_below(marker)
                * (0.25 * (face_east * (tx + below(tx)) + face_north * (ty + below(ty)))
                   + (face_east * face_east + face_north * face_north) * sz)
            )
            return (value + across + (flux_z - above(flux_z))) * marker

        result.append(each(finish, a[j][:2], m[j], k[j], sx, sy[j], twice_x, twice_y, step_z[j], total))
    return result


def tiles_of(ref, row, count):
    return [ref[row, :, t * LANES : (t + 1) * LANES] for t in range(count)]


def interior_kernel(*refs):
    fields, advected, strips = dict(zip(FIELDS, refs[:8])), refs[8], refs[9]
    out, kept, narrow = refs[10:]
    lane = lane_of()
    near_east, near_west = lane >= LANES - 2, lane < 2

    full = [split_groups({n: strips[i, g] for i, n in enumerate(GROUPS)}) for g in range(8)]

    def get_strip(name, g):
        x = full[g % 8][name]
        return [x if 0 <= g < 8 else pltpu.roll(x, 16 if g < 0 else LANES - 16, 1)]

    for g, (a,) in enumerate(advect_rows(get_strip, 0, 8)):
        part = full[g]
        step_z = (below(a) - a) * open_below(part["m"])
        step, flux = eastward([a], [part["m"]], [part["k"]], [part["sx"]], [above(step_z) + step_z])
        narrow[0, g], narrow[1, g], narrow[2, g] = a, step[0], flux[0]

    def lanes_to(which, row, lane_from, lane_to):
        part = row // 8
        return pltpu.roll(narrow[which, row - 8 * part], lax.rem(2 * LANES + lane_to - lane_from - 16 * part, LANES), 1)

    def get(name, row):
        if name != "a":
            return tiles_of(fields[name], row, 2)
        left, right = tiles_of(advected, row, 2)
        return [
            jnp.where(near_west, lanes_to(0, row, 10, 0), left),
            jnp.where(near_east, lanes_to(0, row, 3, LANES - 1), right),
        ]

    def beside(row):
        return [lanes_to(i, row, 3, LANES - 1) for i in (1, 2)], [lanes_to(i, row, 9, 0) for i in (1, 2)]

    for i, row in enumerate((3, ROWS - 4)):
        for t, tile in enumerate(get("a", row)):
            kept[i, :, t * LANES : (t + 1) * LANES] = tile

    def diffuse_block(block, carry):
        first = jnp.minimum(3 + 6 * block, ROWS - 3 - 6)
        for j, tiles in enumerate(diffuse_rows(get, first, 6, beside)):
            for t in range(2):
                out[first + j, :, t * LANES : (t + 1) * LANES] = tiles[t]
        return carry

    lax.fori_loop(0, 10, diffuse_block, 0)


def rim_kernel(*refs):
    got_a, got_b = refs[0], refs[1]
    fields = dict(zip(FIELDS, refs[2:10]))
    strips, inner, kept, out, edges, sems = refs[10:]
    middle = pltpu.make_async_copy
    copies = [middle(inner.at[8:56, i], out.at[i, 8:56], sems.at[i]) for i in range(8)]
    for copy in copies:
        copy.start()
    low = low_of()
    lat = lax.axis_index("lat")
    even = jnp.broadcast_to(lat % 2, (8, LANES)) == 0
    floor = jnp.broadcast_to(lat, (8, LANES)) == 0

    def halo(is_north):
        def tile(i, h):
            a = got_a[i, :, h * LANES : (h + 1) * LANES]
            b = got_b[i, :, h * LANES : (h + 1) * LANES]
            if is_north:
                return jnp.where(even, a, b)
            return jnp.where(floor, 0.0, jnp.where(even, b, a))

        tiles = [[tile(i, h) for h in range(2)] for i in range(8)]
        high = lambda i: [twice_high(x) for x in tiles[i]]
        below_four = lambda i: [twice_low(x) for x in tiles[i]]
        corner = jnp.where(low, pltpu.roll(tiles[7][0], 4, 0), tiles[7][1])
        rows = []
        for q in range(3):
            bases = {n: 16 * (3 * min(q, 1) + min(i, 2)) for i, n in enumerate(GROUPS)}
            side = third_tile({n: corner for n in GROUPS}, bases)
            main = {"c": tiles[q], "m": below_four(3 + q)}
            if q < 2:
                main["v"] = high(3 + q)
            if q == 0:
                main.update(u=high(5), w=below_four(6), sy=high(6), k=below_four(7))
                main["sx"] = main["k"]
            rows.append({n: x + [side[n]] if n in side else x for n, x in main.items()})
        return rows

    for is_north in (False, True):
        rows = halo(is_north)
        start = ROWS - 3 if is_north else -1
        made, sides = {}, {}
        for row in range(*((ROWS - 5, ROWS) if is_north else (0, 5))):
            base = 16 * (row // 8)
            sides[row] = third_tile({n: strips[i, row % 8] for i, n in enumerate(GROUPS)}, dict.fromkeys(GROUPS, base))

        def get(name, row):
            if name == "a":
                return made[row] if row in made else tiles_of(kept, int(is_north), 2)
            if row < 0:
                return rows[-row - 1][name]
            if row >= ROWS:
                return rows[row - ROWS][name]
            if name == "sy":
                return tiles_of(fields[name], row, 2)
            return tiles_of(fields[name], row, 2) + [sides[row][name]]

        for j, tiles in enumerate(advect_rows(get, start, 4)):
            made[start + j] = tiles
        final = ROWS - 3 if is_north else 0
        base = ROWS - 8 if is_north else 0
        done = {final + j: x for j, x in enumerate(diffuse_rows(get, final, 3))}
        for h in range(2):
            stack = [done[j][h] if j in done else inner[j, :, h * LANES : (h + 1) * LANES] for j in range(base, base + 8)]
            edges[int(is_north), :, :, h * LANES : (h + 1) * LANES] = jnp.transpose(jnp.stack(stack), (1, 0, 2))
        copy = middle(edges.at[int(is_north)], out.at[:, base : base + 8], sems.at[8 + int(is_north)])
        copy.start()
        copies.append(copy)
    for copy in copies:
        copy.wait()


def call(kernel, shapes, *operands, **options):
    return pl.pallas_call(
        kernel,
        out_shape=[jax.ShapeDtypeStruct(s, F32) for s in shapes],
        in_specs=[VMEM] * len(operands),
        out_specs=[VMEM] * len(shapes),
        compiler_params=pltpu.CompilerParams(vmem_limit_bytes=LIMIT),
        **options,
    )(*operands)


def make(lons, lats):
    def spot(lon, lat):
        return (lon % lons) * lats + lat

    near = [(spot(i, j), spot(i ^ 1, j)) for i in range(lons) for j in range(lats)]
    far = [(spot(i, j), spot(i + 1 if i % 2 else i - 1, j)) for i in range(lons) for j in range(lats)]
    pair_a = [(spot(i, j), spot(i, j ^ 1)) for i in range(lons) for j in range(lats)]
    pair_b = []
    for i in range(lons):
        for j in range(lats):
            if j == 0:
                pair_b.append((spot(i, j), spot(i ^ 1, j)))
            elif j == lats - 1:
                pair_b.append((spot(i, j), spot(lons - 1 - i, j)))
            else:
                pair_b.append((spot(i, j), spot(i, j + 1 if j % 2 else j - 1)))

    def move(x, route):
        return lax.ppermute(x, ("lon", "lat"), route)

    def shards(tracers, velocity, slopes, diffusivity, sea_mask):
        plane = lambda x: x.reshape(-1, ROWS, 2 * LANES)
        arrays = [plane(tracers), plane(velocity), plane(slopes), diffusivity, sea_mask]
        full, side = (ROWS, 8, 2 * LANES), (8, 8, LANES)
        *parts, packed, spare = pl.pallas_call(
            pack_kernel,
            out_shape=[jax.ShapeDtypeStruct(x.shape[:2] + (LANES,), x.dtype) for x in arrays for _ in range(2)]
            + [jax.ShapeDtypeStruct((10, 8, LANES), F32), jax.ShapeDtypeStruct(side, F32)],
            in_specs=[pl.BlockSpec(memory_space=pl.ANY)] * 5,
            out_specs=[VMEM] * 12,
            scratch_shapes=[pltpu.SemaphoreType.DMA((10,))],
            compiler_params=pltpu.CompilerParams(vmem_limit_bytes=LIMIT),
        )(*arrays)
        far_got, near_got = move(packed, far), move(packed, near)
        *fields, advected = call(
            rows_kernel, [full] * 9, *parts,
            cost_estimate=pl.CostEstimate(flops=10**7, bytes_accessed=6 * 10**6, transcendentals=0),
        )
        strips, send_a, send_b = call(
            edge_kernel, [(4,) + side, (8, 8, 2 * LANES), (8, 8, 2 * LANES)], far_got, near_got, packed, spare, *fields
        )
        got_b, got_a = move(send_b, pair_b), move(send_a, pair_a)
        inner, kept = call(
            interior_kernel, [full, (2, 8, 2 * LANES)], *fields, advected, strips,
            scratch_shapes=[pltpu.VMEM((3,) + side, F32)],
            cost_estimate=pl.CostEstimate(flops=2 * 10**7, bytes_accessed=10**7, transcendentals=0),
        )
        out = pl.pallas_call(
            rim_kernel,
            out_shape=jax.ShapeDtypeStruct((8, ROWS, 2 * LANES), F32),
            in_specs=[VMEM] * 13,
            out_specs=pl.BlockSpec(memory_space=pl.ANY),
            scratch_shapes=[pltpu.VMEM((2, 8, 8, 2 * LANES), F32), pltpu.SemaphoreType.DMA((10,))],
            compiler_params=pltpu.CompilerParams(vmem_limit_bytes=LIMIT),
        )(got_a, got_b, *fields, strips, inner, kept)
        return out.reshape(tracers.shape)

    return shards


def solution(mesh):
    return jax.shard_map(
        make(mesh.shape["lon"], mesh.shape["lat"]),
        mesh=mesh,
        in_specs=(
            P(None, None, "lat", "lon"),
            P(None, None, "lat", "lon"),
            P(None, None, "lat", "lon"),
            P(None, "lat", "lon"),
            P(None, "lat", "lon"),
        ),
        out_specs=P(None, None, "lat", "lon"),
        check_vma=False,
    )
```

```python
import jax
import jax.numpy as jnp
from jax import lax
from jax.experimental import pallas as pl
from jax.experimental.pallas import tpu as pltpu
from jax.sharding import PartitionSpec as P


ROWS = 64
LANES = 128
F32 = jnp.float32
VMEM = pl.BlockSpec(memory_space=pltpu.VMEM)
LIMIT = 16 * 1024 * 1024
GROUPS = ("c", "mu", "vw", "sk")


def lane_of():
    return lax.broadcasted_iota(jnp.int32, (8, LANES), 1)


def low_of():
    return lax.broadcasted_iota(jnp.int32, (8, LANES), 0) < 4


def twice_low(x):
    return jnp.where(low_of(), x, pltpu.roll(x, 4, 0))


def twice_high(x):
    return jnp.where(low_of(), pltpu.roll(x, 4, 0), x)


def eight(ref, start, row):
    return ref.reshape(ref.shape[0] * ROWS, LANES)[pl.ds(start * ROWS + row, 8, stride=ROWS), :]


def four(ref, row):
    return ref.reshape(ref.shape[0] * ROWS, LANES)[pl.ds(row, 4, stride=ROWS), :].astype(F32)


def field_half(parts, name, row, h):
    tracer, velocity, slope, kappa, mask = parts[h::2]
    if name == "c":
        return eight(tracer, 0, row)
    if name == "u":
        return twice_low(eight(velocity, 0, row))
    if name == "v":
        return twice_low(eight(velocity, 4, row))
    if name == "w":
        return twice_high(eight(velocity, 4, row))
    if name == "sx":
        return twice_low(eight(slope, 0, row))
    if name == "sy":
        return twice_high(eight(slope, 0, row))
    return jnp.concatenate([four(kappa if name == "k" else mask, row)] * 2, axis=0)


def field_tiles(parts, name, row):
    return [field_half(parts, name, row, h) for h in range(2)]


def pack_kernel(*refs):
    arrays, parts, message, spare, sems = refs[:5], refs[5:15], refs[15], refs[16], refs[17]
    copies = []
    for i, array in enumerate(arrays):
        for h in range(2):
            part = pltpu.make_async_copy(
                array.at[:, :, h * LANES : (h + 1) * LANES], parts[2 * i + h], sems.at[2 * i + h]
            )
            part.start()
            copies.append(part)
    for part in copies:
        part.wait()
    lane, low = lane_of(), low_of()
    rim_of = lambda load: jnp.where(lane < 64, load(0), load(1))

    def group(g, carry):
        first = second = jnp.zeros((8, LANES), F32)
        for part in range(8):
            row = part * 8 + g
            c, uv, vw, s = [
                rim_of(lambda h: eight(parts[2 * i + h], start, row)) for i, start in ((0, 0), (1, 0), (1, 4), (2, 0))
            ]
            mk = rim_of(lambda h: jnp.concatenate([four(parts[8 + h], row), four(parts[6 + h], row)], axis=0))
            mu = jnp.where(low, mk, pltpu.roll(uv, 4, 0))
            sk = jnp.where(low, s, mk)
            base = 16 * part
            before, half = lane < base, lane < base + 8
            one = jnp.where(half, pltpu.roll(c, (base + 4) % LANES, 1), pltpu.roll(mu, (base + 12) % LANES, 1))
            two = jnp.where(half, pltpu.roll(vw, (base + 4) % LANES, 1), pltpu.roll(sk, (base + 12) % LANES, 1))
            first = jnp.where(before, first, one)
            second = jnp.where(before, second, two)
        message[g] = first
        spare[g] = second
        return carry

    lax.fori_loop(0, 8, group, 0)
    slot = lane % 8
    for pair in range(2):
        total = pltpu.roll(spare[4 * pair], LANES - 2, 1)
        for i in range(1, 4):
            moved = spare[4 * pair + i] if i == 1 else pltpu.roll(spare[4 * pair + i], 2 * i - 2, 1)
            total = jnp.where((slot == (2 * i + 1) % 8) | (slot == (2 * i + 2) % 8), moved, total)
        message[8 + pair] = total


def advect_kernel(*refs):
    parts, advected = refs[:10], refs[10]
    get = lambda name, row: field_tiles(parts, name, row)

    def advect_block(block, carry):
        first = 2 + 15 * block
        for j, tiles in enumerate(advect_rows(get, first, 15)):
            for t in range(2):
                advected[first + j, :, t * LANES : (t + 1) * LANES] = tiles[t]
        return carry

    lax.fori_loop(0, 4, advect_block, 0)


def edge_kernel(*refs):
    from_far, from_near, own, spare = refs[:4]
    parts = refs[4:14]
    strips, send_a, send_b = refs[15:]
    lane, low = lane_of(), low_of()
    lon, lat = lax.axis_index("lon"), lax.axis_index("lat")
    slot = lane % 16
    far_is_west = jnp.broadcast_to(lon % 2, (8, LANES)) == 0

    def strip(mine, east, west, late):
        shift = lambda x, by: pltpu.roll(x, (by - 8 * late) % LANES, 1) if by != 8 * late else x
        inner = jnp.where(slot < 4, shift(mine, 0), shift(east, 0))
        outer = jnp.where(slot < 10, shift(west, 6), shift(mine, 6))
        return jnp.where(slot < 7, inner, outer)

    for g in range(8):
        for which in range(2):
            if which == 0:
                far, near, mine = from_far[g], from_near[g], own[g]
            else:
                back = (2 - 2 * (g % 4)) % LANES
                turn = lambda x: pltpu.roll(x, back, 1) if back else x
                far, near, mine = turn(from_far[8 + g // 4]), turn(from_near[8 + g // 4]), spare[g]
            east, west = jnp.where(far_is_west, near, far), jnp.where(far_is_west, far, near)
            for late in range(2):
                strips[2 * which + late, g] = strip(mine, east, west, late)

    def message(top):
        row = lambda q: jnp.where(top, ROWS - 1 - q, q)
        part = lambda name, q, h: field_half(parts, name, row(q), h)
        pair = lambda n1, q1, n2, q2: [jnp.where(low, part(n1, q1, h), part(n2, q2, h)) for h in range(2)]
        tiles = [[part("c", q, h) for h in range(2)] for q in range(3)]
        tiles += [pair("m", 0, "v", 0), pair("m", 1, "v", 1), pair("m", 2, "u", 0), pair("w", 0, "sy", 0)]
        corners = [
            pltpu.roll(strips[i, jnp.where(top, 7 - q, q)], jnp.where(top, 16, 0), 1) for q in range(2) for i in range(3)
        ]
        return tiles, [part("k", 0, h) for h in range(2)], corners

    def store(ref, tiles, kappa, corners):
        for i, tile in enumerate(tiles):
            for h in range(2):
                ref[i, :, h * LANES : (h + 1) * LANES] = tile[h]
        packed = corners[0]
        for i in range(1, 6):
            packed = jnp.where(lane < 16 * i, packed, pltpu.roll(corners[i], 16 * i, 1))
        ref[7, :, :LANES] = jnp.where(low, kappa[0], pltpu.roll(packed, 4, 0))
        ref[7, :, LANES:] = jnp.where(low, kappa[1], packed)

    even = lat % 2 == 0
    store(send_a, *message(even))
    folds = lat == lax.axis_size("lat") - 1

    @pl.when(jnp.logical_not(folds))
    def _():
        store(send_b, *message(jnp.logical_not(even)))

    @pl.when(folds)
    def _():
        tiles, kappa, corners = message(True)
        backward = LANES - 1 - lane
        flip = lambda x, index: jnp.take_along_axis(x, index, axis=1, mode="promise_in_bounds")
        flip_tile = lambda tile: [flip(tile[1], backward), flip(tile[0], backward)]
        sign = jnp.where(low, 1.0, -1.0)
        turned = [flip_tile(tile) for tile in tiles]
        turned = turned[:3] + [[sign * x for x in tile] for tile in turned[3:]]
        index = jnp.where(lane < 14, 13 - lane, lane)
        corner_signs = [1.0, sign, -sign]
        store(send_b, turned, flip_tile(kappa), [corner_signs[i % 3] * flip(x, index) for i, x in enumerate(corners)])


def split_groups(groups):
    return {
        "c": groups["c"],
        "m": twice_low(groups["mu"]),
        "u": twice_high(groups["mu"]),
        "v": twice_low(groups["vw"]),
        "w": twice_high(groups["vw"]),
        "sx": twice_low(groups["sk"]),
        "k": twice_high(groups["sk"]),
    }


def third_tile(groups, bases):
    east = lane_of() < 64
    tile = lambda x, base: jnp.where(
        east, pltpu.roll(x, (2 * LANES - 4 - base) % LANES, 1), pltpu.roll(x, (2 * LANES - 10 - base) % LANES, 1)
    )
    return split_groups({n: tile(groups[n], bases[n]) for n in GROUPS})


def plus(tiles):
    last = lane_of() == LANES - 1
    turned = [pltpu.roll(t, LANES - 1, 1) for t in tiles]
    if len(tiles) == 1:
        return turned
    return [jnp.where(last, turned[(i + 1) % len(tiles)], turned[i]) for i in range(len(tiles))]


def minus(tiles, count=3, west=None):
    first = lane_of() == 0
    turned = [pltpu.roll(t, 1, 1) for t in tiles]
    if len(tiles) == 1:
        return turned
    before = [turned[-1] if west is None else west] + turned[:-1]
    return [jnp.where(first, before[i], turned[i]) for i in range(min(count, len(tiles)))]


def each(function, *lists):
    return [function(*values) for values in zip(*lists)]


def below(x):
    return pltpu.roll(x, 7, 0)


def above(x):
    return pltpu.roll(x, 1, 0)


def face_flux(here, there, speed, back, step, ahead):
    positive = speed >= 0.0
    upwind = jnp.where(positive, back, ahead)
    size = jnp.abs(speed)
    limited = jnp.maximum(jnp.minimum(upwind, step), 0.0) + jnp.minimum(jnp.maximum(upwind, step), 0.0)
    return speed * jnp.where(positive, here, there) + 0.5 * (size - size * size) * limited


def not_bottom():
    return lax.broadcasted_iota(jnp.int32, (8, LANES), 0) % 4 != 3


def open_below(marker):
    return jnp.where(not_bottom(), marker * below(marker), 0.0)


def face_speed(one, two, opened):
    return 0.5 * (one + two) * opened


def advect_rows(get, first, count):
    c = {j: get("c", first + j) for j in range(-2, count + 2)}
    m = {j: get("m", first + j) for j in range(-2, count + 2)}
    v = {j: get("v", first + j) for j in range(-1, count + 1)}
    opened = {j: each(jnp.multiply, m[j], m[j + 1]) for j in range(-2, count + 1)}
    step = {j: each(lambda a, b, o: (b - a) * o, c[j], c[j + 1], opened[j]) for j in range(-2, count + 1)}
    flux = {}
    for j in range(-1, count):
        speed = each(face_speed, v[j], v[j + 1], opened[j])
        flux[j] = each(face_flux, c[j], c[j + 1], speed, step[j - 1], step[j], step[j + 1])
    result = []
    for j in range(count):
        east = plus(c[j])
        opened_x = each(jnp.multiply, m[j], plus(m[j]))
        u = get("u", first + j)
        speed = each(face_speed, u, plus(u), opened_x)
        step_x = each(lambda a, b, o: (b - a) * o, c[j], east, opened_x)
        flux_x = each(face_flux, c[j], east, speed, minus(step_x), step_x, plus(step_x))
        total = each(lambda f, g, a, b: (f - g) + (a - b), flux_x, minus(flux_x), flux[j], flux[j - 1])
        w = get("w", first + j)

        def finish(value, marker, down, across):
            opened_z = open_below(marker)
            under = below(value)
            step_z = (under - value) * opened_z
            speed_z = face_speed(down, below(down), opened_z)
            flux_z = face_flux(value, under, speed_z, above(step_z), step_z, below(step_z))
            return (value - across - (flux_z - above(flux_z))) * marker

        result.append(each(finish, c[j], m[j], w, total))
    return result


def slope_flux(k1, k2, opened, step, s1, s2, z1, z2):
    return 0.5 * (k1 + k2) * opened * (step + 0.125 * (s1 + s2) * (z1 + z2))


def eastward(a, m, k, sx, twice_z):
    opened = each(jnp.multiply, m, plus(m))
    step = each(lambda x, y, o: (y - x) * o, a, plus(a), opened)
    return step, each(slope_flux, k, plus(k), opened, step, sx, plus(sx), twice_z, plus(twice_z))


def diffuse_rows(get, first, count, beside=None):
    a = {j: get("a", first + j) for j in range(-1, count + 1)}
    m = {j: get("m", first + j) for j in range(-1, count + 1)}
    k = {j: get("k", first + j) for j in range(-1, count + 1)}
    sy = {j: get("sy", first + j) for j in range(-1, count + 1)}
    step_z, twice_z = {}, {}
    for j in range(-1, count + 1):
        wide = 3 if 0 <= j < count else 2
        step_z[j] = each(lambda x, o: (below(x) - x) * open_below(o), a[j][:wide], m[j])
        twice_z[j] = each(lambda x: above(x) + x, step_z[j])
    step_y, flux_y = {}, {}
    for j in range(-1, count):
        opened = each(jnp.multiply, m[j][:2], m[j + 1][:2])
        step_y[j] = each(lambda x, y, o: (y - x) * o, a[j][:2], a[j + 1][:2], opened)
        flux_y[j] = each(
            slope_flux, k[j], k[j + 1], opened, step_y[j], sy[j], sy[j + 1], twice_z[j], twice_z[j + 1]
        )
    result = []
    last = lane_of() == LANES - 1
    for j in range(count):
        sx = get("sx", first + j)
        step_x, flux_x = eastward(a[j], m[j], k[j], sx, twice_z[j])
        west = [None, None]
        if beside:
            east, west = beside(first + j)
            step_x = [step_x[0], jnp.where(last, east[0], step_x[1])]
            flux_x = [flux_x[0], jnp.where(last, east[1], flux_x[1])]
        twice_x = each(jnp.add, step_x, minus(step_x, 2, west[0]))
        twice_y = each(jnp.add, step_y[j - 1], step_y[j])
        total = each(lambda f, g, p, q: (f - g) + (p - q), flux_x, minus(flux_x, 2, west[1]), flux_y[j], flux_y[j - 1])

        def finish(value, marker, kappa, east, north, tx, ty, sz, across):
            face_east, face_north = 0.5 * (east + below(east)), 0.5 * (north + below(north))
            flux_z = (
                0.5 * (kappa + below(kappa)) * open_below(marker)
                * (0.25 * (face_east * (tx + below(tx)) + face_north * (ty + below(ty)))
                   + (face_east * face_east + face_north * face_north) * sz)
            )
            return (value + across + (flux_z - above(flux_z))) * marker

        result.append(each(finish, a[j][:2], m[j], k[j], sx, sy[j], twice_x, twice_y, step_z[j], total))
    return result


def tiles_of(ref, row, count):
    return [ref[row, :, t * LANES : (t + 1) * LANES] for t in range(count)]


def interior_kernel(*refs):
    parts, advected, strips = refs[:10], refs[10], refs[11]
    out, kept, narrow = refs[12:]
    lane = lane_of()
    near_east, near_west = lane >= LANES - 2, lane < 2

    full = [split_groups({n: strips[i, g] for i, n in enumerate(GROUPS)}) for g in range(8)]

    def get_strip(name, g):
        x = full[g % 8][name]
        return [x if 0 <= g < 8 else pltpu.roll(x, 16 if g < 0 else LANES - 16, 1)]

    for g, (a,) in enumerate(advect_rows(get_strip, 0, 8)):
        part = full[g]
        step_z = (below(a) - a) * open_below(part["m"])
        step, flux = eastward([a], [part["m"]], [part["k"]], [part["sx"]], [above(step_z) + step_z])
        narrow[0, g], narrow[1, g], narrow[2, g] = a, step[0], flux[0]

    def lanes_to(which, row, lane_from, lane_to):
        part = row // 8
        return pltpu.roll(narrow[which, row - 8 * part], lax.rem(2 * LANES + lane_to - lane_from - 16 * part, LANES), 1)

    def get(name, row):
        if name != "a":
            return field_tiles(parts, name, row)
        left, right = tiles_of(advected, row, 2)
        return [
            jnp.where(near_west, lanes_to(0, row, 10, 0), left),
            jnp.where(near_east, lanes_to(0, row, 3, LANES - 1), right),
        ]

    def beside(row):
        return [lanes_to(i, row, 3, LANES - 1) for i in (1, 2)], [lanes_to(i, row, 9, 0) for i in (1, 2)]

    for i, row in enumerate((3, ROWS - 4)):
        for t, tile in enumerate(get("a", row)):
            kept[i, :, t * LANES : (t + 1) * LANES] = tile

    def diffuse_block(block, carry):
        first = jnp.minimum(3 + 6 * block, ROWS - 3 - 6)
        for j, tiles in enumerate(diffuse_rows(get, first, 6, beside)):
            for t in range(2):
                out[first + j, :, t * LANES : (t + 1) * LANES] = tiles[t]
        return carry

    lax.fori_loop(0, 10, diffuse_block, 0)


def rim_kernel(*refs):
    got_a, got_b = refs[0], refs[1]
    parts = refs[2:12]
    strips, inner, kept, out, edges, sems = refs[12:]
    middle = pltpu.make_async_copy
    copies = [middle(inner.at[8:56, i], out.at[i, 8:56], sems.at[i]) for i in range(8)]
    for copy in copies:
        copy.start()
    low = low_of()
    lat = lax.axis_index("lat")
    even = jnp.broadcast_to(lat % 2, (8, LANES)) == 0
    floor = jnp.broadcast_to(lat, (8, LANES)) == 0

    def halo(is_north):
        def tile(i, h):
            a = got_a[i, :, h * LANES : (h + 1) * LANES]
            b = got_b[i, :, h * LANES : (h + 1) * LANES]
            if is_north:
                return jnp.where(even, a, b)
            return jnp.where(floor, 0.0, jnp.where(even, b, a))

        tiles = [[tile(i, h) for h in range(2)] for i in range(8)]
        high = lambda i: [twice_high(x) for x in tiles[i]]
        below_four = lambda i: [twice_low(x) for x in tiles[i]]
        corner = jnp.where(low, pltpu.roll(tiles[7][0], 4, 0), tiles[7][1])
        rows = []
        for q in range(3):
            bases = {n: 16 * (3 * min(q, 1) + min(i, 2)) for i, n in enumerate(GROUPS)}
            side = third_tile({n: corner for n in GROUPS}, bases)
            main = {"c": tiles[q], "m": below_four(3 + q)}
            if q < 2:
                main["v"] = high(3 + q)
            if q == 0:
                main.update(u=high(5), w=below_four(6), sy=high(6), k=below_four(7))
                main["sx"] = main["k"]
            rows.append({n: x + [side[n]] if n in side else x for n, x in main.items()})
        return rows

    for is_north in (False, True):
        rows = halo(is_north)
        start = ROWS - 3 if is_north else -1
        made, sides = {}, {}
        for row in range(*((ROWS - 5, ROWS) if is_north else (0, 5))):
            base = 16 * (row // 8)
            sides[row] = third_tile({n: strips[i, row % 8] for i, n in enumerate(GROUPS)}, dict.fromkeys(GROUPS, base))

        def get(name, row):
            if name == "a":
                return made[row] if row in made else tiles_of(kept, int(is_north), 2)
            if row < 0:
                return rows[-row - 1][name]
            if row >= ROWS:
                return rows[row - ROWS][name]
            tiles = field_tiles(parts, name, row)
            return tiles if name == "sy" else tiles + [sides[row][name]]

        for j, tiles in enumerate(advect_rows(get, start, 4)):
            made[start + j] = tiles
        final = ROWS - 3 if is_north else 0
        base = ROWS - 8 if is_north else 0
        done = {final + j: x for j, x in enumerate(diffuse_rows(get, final, 3))}
        for h in range(2):
            stack = [done[j][h] if j in done else inner[j, :, h * LANES : (h + 1) * LANES] for j in range(base, base + 8)]
            edges[int(is_north), :, :, h * LANES : (h + 1) * LANES] = jnp.transpose(jnp.stack(stack), (1, 0, 2))
        copy = middle(edges.at[int(is_north)], out.at[:, base : base + 8], sems.at[8 + int(is_north)])
        copy.start()
        copies.append(copy)
    for copy in copies:
        copy.wait()


def call(kernel, shapes, *operands, **options):
    return pl.pallas_call(
        kernel,
        out_shape=[jax.ShapeDtypeStruct(s, F32) for s in shapes],
        in_specs=[VMEM] * len(operands),
        out_specs=[VMEM] * len(shapes),
        compiler_params=pltpu.CompilerParams(vmem_limit_bytes=LIMIT),
        **options,
    )(*operands)


def make(lons, lats):
    def spot(lon, lat):
        return (lon % lons) * lats + lat

    near = [(spot(i, j), spot(i ^ 1, j)) for i in range(lons) for j in range(lats)]
    far = [(spot(i, j), spot(i + 1 if i % 2 else i - 1, j)) for i in range(lons) for j in range(lats)]
    pair_a = [(spot(i, j), spot(i, j ^ 1)) for i in range(lons) for j in range(lats)]
    pair_b = []
    for i in range(lons):
        for j in range(lats):
            if j == 0:
                pair_b.append((spot(i, j), spot(i ^ 1, j)))
            elif j == lats - 1:
                pair_b.append((spot(i, j), spot(lons - 1 - i, j)))
            else:
                pair_b.append((spot(i, j), spot(i, j + 1 if j % 2 else j - 1)))

    def move(x, route):
        return lax.ppermute(x, ("lon", "lat"), route)

    def shards(tracers, velocity, slopes, diffusivity, sea_mask):
        plane = lambda x: x.reshape(-1, ROWS, 2 * LANES)
        arrays = [plane(tracers), plane(velocity), plane(slopes), diffusivity, sea_mask]
        arrays = [pltpu.with_memory_space_constraint(x, pltpu.HBM) for x in arrays]
        full, side = (ROWS, 8, 2 * LANES), (8, 8, LANES)
        *parts, packed, spare = pl.pallas_call(
            pack_kernel,
            out_shape=[jax.ShapeDtypeStruct(x.shape[:2] + (LANES,), x.dtype) for x in arrays for _ in range(2)]
            + [jax.ShapeDtypeStruct((10, 8, LANES), F32), jax.ShapeDtypeStruct(side, F32)],
            in_specs=[pl.BlockSpec(memory_space=pltpu.HBM)] * 5,
            out_specs=[VMEM] * 12,
            scratch_shapes=[pltpu.SemaphoreType.DMA((10,))],
            compiler_params=pltpu.CompilerParams(vmem_limit_bytes=LIMIT),
        )(*arrays)
        far_got, near_got = move(packed, far), move(packed, near)
        (advected,) = call(
            advect_kernel, [full], *parts,
            cost_estimate=pl.CostEstimate(flops=10**7, bytes_accessed=6 * 10**6, transcendentals=0),
        )
        strips, send_a, send_b = call(
            edge_kernel, [(4,) + side, (8, 8, 2 * LANES), (8, 8, 2 * LANES)], far_got, near_got, packed, spare, *parts, advected
        )
        got_b, got_a = move(send_b, pair_b), move(send_a, pair_a)
        inner, kept = call(
            interior_kernel, [full, (2, 8, 2 * LANES)], *parts, advected, strips,
            scratch_shapes=[pltpu.VMEM((3,) + side, F32)],
            cost_estimate=pl.CostEstimate(flops=2 * 10**7, bytes_accessed=10**7, transcendentals=0),
        )
        out = pl.pallas_call(
            rim_kernel,
            out_shape=jax.ShapeDtypeStruct((8, ROWS, 2 * LANES), F32),
            in_specs=[VMEM] * 15,
            out_specs=pl.BlockSpec(memory_space=pl.ANY),
            scratch_shapes=[pltpu.VMEM((2, 8, 8, 2 * LANES), F32), pltpu.SemaphoreType.DMA((10,))],
            compiler_params=pltpu.CompilerParams(vmem_limit_bytes=LIMIT),
        )(got_a, got_b, *parts, strips, inner, kept)
        return out.reshape(tracers.shape)

    return shards


def solution(mesh):
    return jax.shard_map(
        make(mesh.shape["lon"], mesh.shape["lat"]),
        mesh=mesh,
        in_specs=(
            P(None, None, "lat", "lon"),
            P(None, None, "lat", "lon"),
            P(None, None, "lat", "lon"),
            P(None, "lat", "lon"),
            P(None, "lat", "lon"),
        ),
        out_specs=P(None, None, "lat", "lon"),
        check_vma=False,
    )
```

```python
import jax
import jax.numpy as jnp
from jax import lax
from jax.experimental import pallas as pl
from jax.experimental.pallas import tpu as pltpu
from jax.sharding import PartitionSpec as P


ROWS = 64
LANES = 128
F32 = jnp.float32
VMEM = pl.BlockSpec(memory_space=pltpu.VMEM)
LIMIT = 16 * 1024 * 1024
GROUPS = ("c", "mu", "vw", "sk")


def lane_of():
    return lax.broadcasted_iota(jnp.int32, (8, LANES), 1)


def low_of():
    return lax.broadcasted_iota(jnp.int32, (8, LANES), 0) < 4


def twice_low(x):
    return jnp.where(low_of(), x, pltpu.roll(x, 4, 0))


def twice_high(x):
    return jnp.where(low_of(), pltpu.roll(x, 4, 0), x)


def eight(ref, start, row):
    return ref.reshape(ref.shape[0] * ROWS, LANES)[pl.ds(start * ROWS + row, 8, stride=ROWS), :]


def four(ref, row):
    return ref.reshape(ref.shape[0] * ROWS, LANES)[pl.ds(row, 4, stride=ROWS), :].astype(F32)


def field_half(parts, name, row, h):
    tracer, velocity, slope, kappa, mask = parts[h::2]
    if name == "c":
        return eight(tracer, 0, row)
    if name == "u":
        return twice_low(eight(velocity, 0, row))
    if name == "v":
        return twice_low(eight(velocity, 4, row))
    if name == "w":
        return twice_high(eight(velocity, 4, row))
    if name == "sx":
        return twice_low(eight(slope, 0, row))
    if name == "sy":
        return twice_high(eight(slope, 0, row))
    return jnp.concatenate([four(kappa if name == "k" else mask, row)] * 2, axis=0)


def field_tiles(parts, name, row):
    return [field_half(parts, name, row, h) for h in range(2)]


def pack_kernel(*refs):
    arrays, parts, message, spare, sems = refs[:5], refs[5:15], refs[15], refs[16], refs[17]
    copies = []
    for i, array in enumerate(arrays):
        for h in range(2):
            part = pltpu.make_async_copy(
                array.at[:, :, h * LANES : (h + 1) * LANES], parts[2 * i + h], sems.at[2 * i + h]
            )
            part.start()
            copies.append(part)
    for part in copies:
        part.wait()
    lane, low = lane_of(), low_of()
    rim_of = lambda load: jnp.where(lane < 64, load(0), load(1))

    def group(g):
        first = second = jnp.zeros((8, LANES), F32)
        for part in range(8):
            row = part * 8 + g
            c, uv, vw, s = [
                rim_of(lambda h: eight(parts[2 * i + h], start, row)) for i, start in ((0, 0), (1, 0), (1, 4), (2, 0))
            ]
            mk = rim_of(lambda h: jnp.concatenate([four(parts[8 + h], row), four(parts[6 + h], row)], axis=0))
            mu = jnp.where(low, mk, pltpu.roll(uv, 4, 0))
            sk = jnp.where(low, s, mk)
            base = 16 * part
            before, half = lane < base, lane < base + 8
            one = jnp.where(half, pltpu.roll(c, (base + 4) % LANES, 1), pltpu.roll(mu, (base + 12) % LANES, 1))
            two = jnp.where(half, pltpu.roll(vw, (base + 4) % LANES, 1), pltpu.roll(sk, (base + 12) % LANES, 1))
            first = jnp.where(before, first, one)
            second = jnp.where(before, second, two)
        message[g] = first
        spare[g] = second

    for g in range(8):
        group(g)
    slot = lane % 8
    for pair in range(2):
        total = pltpu.roll(spare[4 * pair], LANES - 2, 1)
        for i in range(1, 4):
            moved = spare[4 * pair + i] if i == 1 else pltpu.roll(spare[4 * pair + i], 2 * i - 2, 1)
            total = jnp.where((slot == (2 * i + 1) % 8) | (slot == (2 * i + 2) % 8), moved, total)
        message[8 + pair] = total


def advect_kernel(*refs):
    parts, advected = refs[:10], refs[10]
    get = lambda name, row: field_tiles(parts, name, row)

    def advect_block(block, carry):
        first = 2 + 15 * block
        for j, tiles in enumerate(advect_rows(get, first, 15)):
            for t in range(2):
                advected[first + j, :, t * LANES : (t + 1) * LANES] = tiles[t]
        return carry

    lax.fori_loop(0, 4, advect_block, 0)


def edge_kernel(*refs):
    from_near, from_far, own, spare = refs[:4]
    parts = refs[4:14]
    strips, send_a, send_b = refs[15:]
    lane, low = lane_of(), low_of()
    lon, lat = lax.axis_index("lon"), lax.axis_index("lat")
    slot = lane % 16
    far_is_west = jnp.broadcast_to(lon % 2, (8, LANES)) == 0

    def strip(mine, east, west, late):
        shift = lambda x, by: pltpu.roll(x, (by - 8 * late) % LANES, 1) if by != 8 * late else x
        inner = jnp.where(slot < 4, shift(mine, 0), shift(east, 0))
        outer = jnp.where(slot < 10, shift(west, 6), shift(mine, 6))
        return jnp.where(slot < 7, inner, outer)

    for g in range(8):
        for which in range(2):
            if which == 0:
                far, near, mine = from_far[g], from_near[g], own[g]
            else:
                back = (2 - 2 * (g % 4)) % LANES
                turn = lambda x: pltpu.roll(x, back, 1) if back else x
                far, near, mine = turn(from_far[8 + g // 4]), turn(from_near[8 + g // 4]), spare[g]
            east, west = jnp.where(far_is_west, near, far), jnp.where(far_is_west, far, near)
            for late in range(2):
                strips[2 * which + late, g] = strip(mine, east, west, late)

    def message(top):
        row = lambda q: jnp.where(top, ROWS - 1 - q, q)
        part = lambda name, q, h: field_half(parts, name, row(q), h)
        pair = lambda n1, q1, n2, q2: [jnp.where(low, part(n1, q1, h), part(n2, q2, h)) for h in range(2)]
        tiles = [[part("c", q, h) for h in range(2)] for q in range(3)]
        tiles += [pair("m", 0, "v", 0), pair("m", 1, "v", 1), pair("m", 2, "u", 0), pair("w", 0, "sy", 0)]
        corners = [
            pltpu.roll(strips[i, jnp.where(top, 7 - q, q)], jnp.where(top, 16, 0), 1) for q in range(2) for i in range(3)
        ]
        return tiles, [part("k", 0, h) for h in range(2)], corners

    def store(ref, tiles, kappa, corners):
        for i, tile in enumerate(tiles):
            for h in range(2):
                ref[i, :, h * LANES : (h + 1) * LANES] = tile[h]
        packed = corners[0]
        for i in range(1, 6):
            packed = jnp.where(lane < 16 * i, packed, pltpu.roll(corners[i], 16 * i, 1))
        ref[7, :, :LANES] = jnp.where(low, kappa[0], pltpu.roll(packed, 4, 0))
        ref[7, :, LANES:] = jnp.where(low, kappa[1], packed)

    even = lat % 2 == 0
    store(send_a, *message(even))
    folds = lat == lax.axis_size("lat") - 1

    @pl.when(jnp.logical_not(folds))
    def _():
        store(send_b, *message(jnp.logical_not(even)))

    @pl.when(folds)
    def _():
        tiles, kappa, corners = message(True)
        backward = LANES - 1 - lane
        flip = lambda x, index: jnp.take_along_axis(x, index, axis=1, mode="promise_in_bounds")
        flip_tile = lambda tile: [flip(tile[1], backward), flip(tile[0], backward)]
        sign = jnp.where(low, 1.0, -1.0)
        turned = [flip_tile(tile) for tile in tiles]
        turned = turned[:3] + [[sign * x for x in tile] for tile in turned[3:]]
        index = jnp.where(lane < 14, 13 - lane, lane)
        corner_signs = [1.0, sign, -sign]
        store(send_b, turned, flip_tile(kappa), [corner_signs[i % 3] * flip(x, index) for i, x in enumerate(corners)])


def split_groups(groups):
    return {
        "c": groups["c"],
        "m": twice_low(groups["mu"]),
        "u": twice_high(groups["mu"]),
        "v": twice_low(groups["vw"]),
        "w": twice_high(groups["vw"]),
        "sx": twice_low(groups["sk"]),
        "k": twice_high(groups["sk"]),
    }


def third_tile(groups, bases):
    east = lane_of() < 64
    tile = lambda x, base: jnp.where(
        east, pltpu.roll(x, (2 * LANES - 4 - base) % LANES, 1), pltpu.roll(x, (2 * LANES - 10 - base) % LANES, 1)
    )
    return split_groups({n: tile(groups[n], bases[n]) for n in GROUPS})


def plus(tiles):
    last = lane_of() == LANES - 1
    turned = [pltpu.roll(t, LANES - 1, 1) for t in tiles]
    if len(tiles) == 1:
        return turned
    return [jnp.where(last, turned[(i + 1) % len(tiles)], turned[i]) for i in range(len(tiles))]


def minus(tiles, count=3, west=None):
    first = lane_of() == 0
    turned = [pltpu.roll(t, 1, 1) for t in tiles]
    if len(tiles) == 1:
        return turned
    before = [turned[-1] if west is None else west] + turned[:-1]
    return [jnp.where(first, before[i], turned[i]) for i in range(min(count, len(tiles)))]


def each(function, *lists):
    return [function(*values) for values in zip(*lists)]


def below(x):
    return pltpu.roll(x, 7, 0)


def above(x):
    return pltpu.roll(x, 1, 0)


def face_flux(here, there, speed, back, step, ahead):
    positive = speed >= 0.0
    upwind = jnp.where(positive, back, ahead)
    size = jnp.abs(speed)
    limited = jnp.maximum(jnp.minimum(upwind, step), 0.0) + jnp.minimum(jnp.maximum(upwind, step), 0.0)
    return speed * jnp.where(positive, here, there) + 0.5 * (size - size * size) * limited


def not_bottom():
    return lax.broadcasted_iota(jnp.int32, (8, LANES), 0) % 4 != 3


def open_below(marker):
    return jnp.where(not_bottom(), marker * below(marker), 0.0)


def face_speed(one, two, opened):
    return 0.5 * (one + two) * opened


def advect_rows(get, first, count):
    c = {j: get("c", first + j) for j in range(-2, count + 2)}
    m = {j: get("m", first + j) for j in range(-2, count + 2)}
    v = {j: get("v", first + j) for j in range(-1, count + 1)}
    opened = {j: each(jnp.multiply, m[j], m[j + 1]) for j in range(-2, count + 1)}
    step = {j: each(lambda a, b, o: (b - a) * o, c[j], c[j + 1], opened[j]) for j in range(-2, count + 1)}
    flux = {}
    for j in range(-1, count):
        speed = each(face_speed, v[j], v[j + 1], opened[j])
        flux[j] = each(face_flux, c[j], c[j + 1], speed, step[j - 1], step[j], step[j + 1])
    result = []
    for j in range(count):
        east = plus(c[j])
        opened_x = each(jnp.multiply, m[j], plus(m[j]))
        u = get("u", first + j)
        speed = each(face_speed, u, plus(u), opened_x)
        step_x = each(lambda a, b, o: (b - a) * o, c[j], east, opened_x)
        flux_x = each(face_flux, c[j], east, speed, minus(step_x), step_x, plus(step_x))
        total = each(lambda f, g, a, b: (f - g) + (a - b), flux_x, minus(flux_x), flux[j], flux[j - 1])
        w = get("w", first + j)

        def finish(value, marker, down, across):
            opened_z = open_below(marker)
            under = below(value)
            step_z = (under - value) * opened_z
            speed_z = face_speed(down, below(down), opened_z)
            flux_z = face_flux(value, under, speed_z, above(step_z), step_z, below(step_z))
            return (value - across - (flux_z - above(flux_z))) * marker

        result.append(each(finish, c[j], m[j], w, total))
    return result


def slope_flux(k1, k2, opened, step, s1, s2, z1, z2):
    return 0.5 * (k1 + k2) * opened * (step + 0.125 * (s1 + s2) * (z1 + z2))


def eastward(a, m, k, sx, twice_z):
    opened = each(jnp.multiply, m, plus(m))
    step = each(lambda x, y, o: (y - x) * o, a, plus(a), opened)
    return step, each(slope_flux, k, plus(k), opened, step, sx, plus(sx), twice_z, plus(twice_z))


def diffuse_rows(get, first, count, beside=None):
    a = {j: get("a", first + j) for j in range(-1, count + 1)}
    m = {j: get("m", first + j) for j in range(-1, count + 1)}
    k = {j: get("k", first + j) for j in range(-1, count + 1)}
    sy = {j: get("sy", first + j) for j in range(-1, count + 1)}
    step_z, twice_z = {}, {}
    for j in range(-1, count + 1):
        wide = 3 if 0 <= j < count else 2
        step_z[j] = each(lambda x, o: (below(x) - x) * open_below(o), a[j][:wide], m[j])
        twice_z[j] = each(lambda x: above(x) + x, step_z[j])
    step_y, flux_y = {}, {}
    for j in range(-1, count):
        opened = each(jnp.multiply, m[j][:2], m[j + 1][:2])
        step_y[j] = each(lambda x, y, o: (y - x) * o, a[j][:2], a[j + 1][:2], opened)
        flux_y[j] = each(
            slope_flux, k[j], k[j + 1], opened, step_y[j], sy[j], sy[j + 1], twice_z[j], twice_z[j + 1]
        )
    result = []
    last = lane_of() == LANES - 1
    for j in range(count):
        sx = get("sx", first + j)
        step_x, flux_x = eastward(a[j], m[j], k[j], sx, twice_z[j])
        west = [None, None]
        if beside:
            east, west = beside(first + j)
            step_x = [step_x[0], jnp.where(last, east[0], step_x[1])]
            flux_x = [flux_x[0], jnp.where(last, east[1], flux_x[1])]
        twice_x = each(jnp.add, step_x, minus(step_x, 2, west[0]))
        twice_y = each(jnp.add, step_y[j - 1], step_y[j])
        total = each(lambda f, g, p, q: (f - g) + (p - q), flux_x, minus(flux_x, 2, west[1]), flux_y[j], flux_y[j - 1])

        def finish(value, marker, kappa, east, north, tx, ty, sz, across):
            face_east, face_north = 0.5 * (east + below(east)), 0.5 * (north + below(north))
            flux_z = (
                0.5 * (kappa + below(kappa)) * open_below(marker)
                * (0.25 * (face_east * (tx + below(tx)) + face_north * (ty + below(ty)))
                   + (face_east * face_east + face_north * face_north) * sz)
            )
            return (value + across + (flux_z - above(flux_z))) * marker

        result.append(each(finish, a[j][:2], m[j], k[j], sx, sy[j], twice_x, twice_y, step_z[j], total))
    return result


def tiles_of(ref, row, count):
    return [ref[row, :, t * LANES : (t + 1) * LANES] for t in range(count)]


def interior_kernel(*refs):
    parts, advected, strips = refs[:10], refs[10], refs[11]
    out, kept, narrow = refs[12:]
    lane = lane_of()
    near_east, near_west = lane >= LANES - 2, lane < 2

    full = [split_groups({n: strips[i, g] for i, n in enumerate(GROUPS)}) for g in range(8)]

    def get_strip(name, g):
        x = full[g % 8][name]
        return [x if 0 <= g < 8 else pltpu.roll(x, 16 if g < 0 else LANES - 16, 1)]

    for g, (a,) in enumerate(advect_rows(get_strip, 0, 8)):
        part = full[g]
        step_z = (below(a) - a) * open_below(part["m"])
        step, flux = eastward([a], [part["m"]], [part["k"]], [part["sx"]], [above(step_z) + step_z])
        narrow[0, g], narrow[1, g], narrow[2, g] = a, step[0], flux[0]

    def lanes_to(which, row, lane_from, lane_to):
        part = row // 8
        return pltpu.roll(narrow[which, row - 8 * part], lax.rem(2 * LANES + lane_to - lane_from - 16 * part, LANES), 1)

    def get(name, row):
        if name != "a":
            return field_tiles(parts, name, row)
        left, right = tiles_of(advected, row, 2)
        return [
            jnp.where(near_west, lanes_to(0, row, 10, 0), left),
            jnp.where(near_east, lanes_to(0, row, 3, LANES - 1), right),
        ]

    def beside(row):
        return [lanes_to(i, row, 3, LANES - 1) for i in (1, 2)], [lanes_to(i, row, 9, 0) for i in (1, 2)]

    for i, row in enumerate((3, ROWS - 4)):
        for t, tile in enumerate(get("a", row)):
            kept[i, :, t * LANES : (t + 1) * LANES] = tile

    def diffuse_block(block, carry):
        first = jnp.minimum(3 + 10 * block, ROWS - 3 - 10)
        for j, tiles in enumerate(diffuse_rows(get, first, 10, beside)):
            for t in range(2):
                out[first + j, :, t * LANES : (t + 1) * LANES] = tiles[t]
        return carry

    lax.fori_loop(0, 6, diffuse_block, 0)


def rim_kernel(*refs):
    got_b, got_a = refs[0], refs[1]
    parts = refs[2:12]
    strips, inner, kept, out, edges, sems = refs[12:]
    middle = pltpu.make_async_copy
    copies = [middle(inner.at[8:56, i], out.at[i, 8:56], sems.at[i]) for i in range(8)]
    for copy in copies:
        copy.start()
    low = low_of()
    lat = lax.axis_index("lat")
    even = jnp.broadcast_to(lat % 2, (8, LANES)) == 0
    floor = jnp.broadcast_to(lat, (8, LANES)) == 0

    def halo(is_north):
        def tile(i, h):
            a = got_a[i, :, h * LANES : (h + 1) * LANES]
            b = got_b[i, :, h * LANES : (h + 1) * LANES]
            if is_north:
                return jnp.where(even, a, b)
            return jnp.where(floor, 0.0, jnp.where(even, b, a))

        tiles = [[tile(i, h) for h in range(2)] for i in range(8)]
        high = lambda i: [twice_high(x) for x in tiles[i]]
        below_four = lambda i: [twice_low(x) for x in tiles[i]]
        corner = jnp.where(low, pltpu.roll(tiles[7][0], 4, 0), tiles[7][1])
        rows = []
        for q in range(3):
            bases = {n: 16 * (3 * min(q, 1) + min(i, 2)) for i, n in enumerate(GROUPS)}
            side = third_tile({n: corner for n in GROUPS}, bases)
            main = {"c": tiles[q], "m": below_four(3 + q)}
            if q < 2:
                main["v"] = high(3 + q)
            if q == 0:
                main.update(u=high(5), w=below_four(6), sy=high(6), k=below_four(7))
                main["sx"] = main["k"]
            rows.append({n: x + [side[n]] if n in side else x for n, x in main.items()})
        return rows

    for is_north in (False, True):
        rows = halo(is_north)
        start = ROWS - 3 if is_north else -1
        made, sides = {}, {}
        for row in range(*((ROWS - 5, ROWS) if is_north else (0, 5))):
            base = 16 * (row // 8)
            sides[row] = third_tile({n: strips[i, row % 8] for i, n in enumerate(GROUPS)}, dict.fromkeys(GROUPS, base))

        def get(name, row):
            if name == "a":
                return made[row] if row in made else tiles_of(kept, int(is_north), 2)
            if row < 0:
                return rows[-row - 1][name]
            if row >= ROWS:
                return rows[row - ROWS][name]
            tiles = field_tiles(parts, name, row)
            return tiles if name == "sy" else tiles + [sides[row][name]]

        for j, tiles in enumerate(advect_rows(get, start, 4)):
            made[start + j] = tiles
        final = ROWS - 3 if is_north else 0
        base = ROWS - 8 if is_north else 0
        done = {final + j: x for j, x in enumerate(diffuse_rows(get, final, 3))}
        for h in range(2):
            stack = [done[j][h] if j in done else inner[j, :, h * LANES : (h + 1) * LANES] for j in range(base, base + 8)]
            edges[int(is_north), :, :, h * LANES : (h + 1) * LANES] = jnp.transpose(jnp.stack(stack), (1, 0, 2))
        copy = middle(edges.at[int(is_north)], out.at[:, base : base + 8], sems.at[8 + int(is_north)])
        copy.start()
        copies.append(copy)
    for copy in copies:
        copy.wait()


def call(kernel, shapes, *operands, **options):
    return pl.pallas_call(
        kernel,
        out_shape=[jax.ShapeDtypeStruct(s, F32) for s in shapes],
        in_specs=[VMEM] * len(operands),
        out_specs=[VMEM] * len(shapes),
        compiler_params=pltpu.CompilerParams(vmem_limit_bytes=LIMIT),
        **options,
    )(*operands)


def make(lons, lats):
    def spot(lon, lat):
        return (lon % lons) * lats + lat

    near = [(spot(i, j), spot(i ^ 1, j)) for i in range(lons) for j in range(lats)]
    far = [(spot(i, j), spot(i + 1 if i % 2 else i - 1, j)) for i in range(lons) for j in range(lats)]
    pair_a = [(spot(i, j), spot(i, j ^ 1)) for i in range(lons) for j in range(lats)]
    pair_b = []
    for i in range(lons):
        for j in range(lats):
            if j == 0:
                pair_b.append((spot(i, j), spot(i ^ 1, j)))
            elif j == lats - 1:
                pair_b.append((spot(i, j), spot(lons - 1 - i, j)))
            else:
                pair_b.append((spot(i, j), spot(i, j + 1 if j % 2 else j - 1)))

    def move(x, route):
        return lax.ppermute(x, ("lon", "lat"), route)

    def shards(tracers, velocity, slopes, diffusivity, sea_mask):
        plane = lambda x: x.reshape(-1, ROWS, 2 * LANES)
        arrays = [plane(tracers), plane(velocity), plane(slopes), diffusivity, sea_mask]
        arrays = [pltpu.with_memory_space_constraint(x, pltpu.HBM) for x in arrays]
        full, side = (ROWS, 8, 2 * LANES), (8, 8, LANES)
        *parts, packed, spare = pl.pallas_call(
            pack_kernel,
            out_shape=[jax.ShapeDtypeStruct(x.shape[:2] + (LANES,), x.dtype) for x in arrays for _ in range(2)]
            + [jax.ShapeDtypeStruct((10, 8, LANES), F32), jax.ShapeDtypeStruct(side, F32)],
            in_specs=[pl.BlockSpec(memory_space=pltpu.HBM)] * 5,
            out_specs=[VMEM] * 12,
            scratch_shapes=[pltpu.SemaphoreType.DMA((10,))],
            compiler_params=pltpu.CompilerParams(vmem_limit_bytes=LIMIT),
        )(*arrays)
        far_got, near_got = move(packed, far), move(packed, near)
        (advected,) = call(
            advect_kernel, [full], *parts,
            cost_estimate=pl.CostEstimate(flops=10**7, bytes_accessed=6 * 10**6, transcendentals=0),
        )
        strips, send_a, send_b = call(
            edge_kernel, [(4,) + side, (8, 8, 2 * LANES), (8, 8, 2 * LANES)], near_got, far_got, packed, spare, *parts, advected
        )
        got_b, got_a = move(send_b, pair_b), move(send_a, pair_a)
        inner, kept = call(
            interior_kernel, [full, (2, 8, 2 * LANES)], *parts, advected, strips,
            scratch_shapes=[pltpu.VMEM((3,) + side, F32)],
            cost_estimate=pl.CostEstimate(flops=2 * 10**7, bytes_accessed=10**7, transcendentals=0),
        )
        out = pl.pallas_call(
            rim_kernel,
            out_shape=jax.ShapeDtypeStruct((8, ROWS, 2 * LANES), F32),
            in_specs=[VMEM] * 15,
            out_specs=pl.BlockSpec(memory_space=pl.ANY),
            scratch_shapes=[pltpu.VMEM((2, 8, 8, 2 * LANES), F32), pltpu.SemaphoreType.DMA((10,))],
            compiler_params=pltpu.CompilerParams(vmem_limit_bytes=LIMIT),
        )(got_b, got_a, *parts, strips, inner, kept)
        return out.reshape(tracers.shape)

    return shards


def solution(mesh):
    return jax.shard_map(
        make(mesh.shape["lon"], mesh.shape["lat"]),
        mesh=mesh,
        in_specs=(
            P(None, None, "lat", "lon"),
            P(None, None, "lat", "lon"),
            P(None, None, "lat", "lon"),
            P(None, "lat", "lon"),
            P(None, "lat", "lon"),
        ),
        out_specs=P(None, None, "lat", "lon"),
        check_vma=False,
    )
```

```python
import jax
import jax.numpy as jnp
from jax import lax
from jax.experimental import pallas as pl
from jax.experimental.pallas import tpu as pltpu
from jax.sharding import PartitionSpec as P


ROWS = 64
LANES = 128
F32 = jnp.float32
VMEM = pl.BlockSpec(memory_space=pltpu.VMEM)
LIMIT = 16 * 1024 * 1024
GROUPS = ("c", "mu", "vw", "sk")
KEPT = (2, 3, ROWS - 4, ROWS - 3)


def lane_of():
    return lax.broadcasted_iota(jnp.int32, (8, LANES), 1)


def low_of():
    return lax.broadcasted_iota(jnp.int32, (8, LANES), 0) < 4


def twice_low(x):
    return jnp.where(low_of(), x, pltpu.roll(x, 4, 0))


def twice_high(x):
    return jnp.where(low_of(), pltpu.roll(x, 4, 0), x)


def eight(ref, start, row):
    return ref.reshape(ref.shape[0] * ROWS, LANES)[pl.ds(start * ROWS + row, 8, stride=ROWS), :]


def four(ref, row):
    return ref.reshape(ref.shape[0] * ROWS, LANES)[pl.ds(row, 4, stride=ROWS), :].astype(F32)


def field_half(rows, name, row, h):
    which, turn = {
        "u": (1, twice_low), "v": (1, twice_high), "w": (2, twice_high),
        "sx": (3, twice_low), "sy": (3, twice_high), "m": (4, twice_low), "k": (4, twice_high),
    }.get(name, (0, None))
    value = rows[which][row, :, h * LANES : (h + 1) * LANES]
    return turn(value) if turn else value


def field_tiles(rows, name, row):
    return [field_half(rows, name, row, h) for h in range(2)]


def pack_kernel(*refs):
    arrays, rows, message, spare, parts, sems = refs[:5], refs[5:10], refs[10], refs[11], refs[12:22], refs[22]
    copies = []
    for i, array in enumerate(arrays):
        for h in range(2):
            part = pltpu.make_async_copy(
                array.at[:, :, h * LANES : (h + 1) * LANES], parts[2 * i + h], sems.at[2 * i + h]
            )
            part.start()
            copies.append(part)
    for part in copies:
        part.wait()
    lane, low = lane_of(), low_of()
    scale = jnp.where(low, 1.0, 0.5)

    def group(g):
        first = second = jnp.zeros((8, LANES), F32)
        for part in range(8):
            row = part * 8 + g
            rims = []
            for h in range(2):
                tracer, velocity, slope, kappa, mask = parts[h::2]
                mk = jnp.concatenate([four(mask, row), four(kappa, row)], axis=0) * scale
                loaded = (
                    eight(tracer, 0, row), eight(velocity, 0, row), eight(velocity, 4, row),
                    eight(slope, 0, row) * 0.125, mk,
                )
                for ref, value in zip(rows, loaded):
                    ref[row, :, h * LANES : (h + 1) * LANES] = value
                rims.append(loaded)
            c, uv, vw, s, mk = [jnp.where(lane < 64, a, b) for a, b in zip(*rims)]
            mu = jnp.where(low, mk, pltpu.roll(uv, 4, 0))
            sk = jnp.where(low, s, mk)
            base = 16 * part
            before, half = lane < base, lane < base + 8
            one = jnp.where(half, pltpu.roll(c, (base + 4) % LANES, 1), pltpu.roll(mu, (base + 12) % LANES, 1))
            two = jnp.where(half, pltpu.roll(vw, (base + 4) % LANES, 1), pltpu.roll(sk, (base + 12) % LANES, 1))
            first = jnp.where(before, first, one)
            second = jnp.where(before, second, two)
        message[g] = first
        spare[g] = second

    for g in range(8):
        group(g)
    slot = lane % 8
    for pair in range(2):
        total = pltpu.roll(spare[4 * pair], LANES - 2, 1)
        for i in range(1, 4):
            moved = spare[4 * pair + i] if i == 1 else pltpu.roll(spare[4 * pair + i], 2 * i - 2, 1)
            total = jnp.where((slot == (2 * i + 1) % 8) | (slot == (2 * i + 2) % 8), moved, total)
        message[8 + pair] = total


def advect_kernel(*refs):
    rows, advected = refs[:5], refs[5]
    get = lambda name, row: field_tiles(rows, name, row)

    def advect_block(block, carry):
        first = 2 + 15 * block
        for j, tiles in enumerate(advect_rows(get, first, 15)):
            for t in range(2):
                advected[first + j, :, t * LANES : (t + 1) * LANES] = tiles[t]
        return carry

    lax.fori_loop(0, 4, advect_block, 0)


def edge_kernel(*refs):
    from_near, from_far, own, spare = refs[:4]
    rows = refs[4:9]
    strips, send_a, send_b = refs[10:]
    lane, low = lane_of(), low_of()
    lon, lat = lax.axis_index("lon"), lax.axis_index("lat")
    slot = lane % 16
    far_is_west = jnp.broadcast_to(lon % 2, (8, LANES)) == 0

    def strip(mine, east, west, late):
        shift = lambda x, by: pltpu.roll(x, (by - 8 * late) % LANES, 1) if by != 8 * late else x
        inner = jnp.where(slot < 4, shift(mine, 0), shift(east, 0))
        outer = jnp.where(slot < 10, shift(west, 6), shift(mine, 6))
        return jnp.where(slot < 7, inner, outer)

    for g in range(8):
        for which in range(2):
            if which == 0:
                far, near, mine = from_far[g], from_near[g], own[g]
            else:
                back = (2 - 2 * (g % 4)) % LANES
                turn = lambda x: pltpu.roll(x, back, 1) if back else x
                far, near, mine = turn(from_far[8 + g // 4]), turn(from_near[8 + g // 4]), spare[g]
            east, west = jnp.where(far_is_west, near, far), jnp.where(far_is_west, far, near)
            for late in range(2):
                strips[2 * which + late, g] = strip(mine, east, west, late)

    def message(top):
        row = lambda q: jnp.where(top, ROWS - 1 - q, q)
        part = lambda name, q, h: field_half(rows, name, row(q), h)
        pair = lambda n1, q1, n2, q2: [jnp.where(low, part(n1, q1, h), part(n2, q2, h)) for h in range(2)]
        tiles = [[part("c", q, h) for h in range(2)] for q in range(3)]
        tiles += [pair("m", 0, "v", 0), pair("m", 1, "v", 1), pair("m", 2, "u", 0), pair("w", 0, "sy", 0)]
        corners = [
            pltpu.roll(strips[i, jnp.where(top, 7 - q, q)], jnp.where(top, 16, 0), 1) for q in range(2) for i in range(3)
        ]
        return tiles, [part("k", 0, h) for h in range(2)], corners

    def store(ref, tiles, kappa, corners):
        for i, tile in enumerate(tiles):
            for h in range(2):
                ref[i, :, h * LANES : (h + 1) * LANES] = tile[h]
        packed = corners[0]
        for i in range(1, 6):
            packed = jnp.where(lane < 16 * i, packed, pltpu.roll(corners[i], 16 * i, 1))
        ref[7, :, :LANES] = jnp.where(low, kappa[0], pltpu.roll(packed, 4, 0))
        ref[7, :, LANES:] = jnp.where(low, kappa[1], packed)

    even = lat % 2 == 0
    store(send_a, *message(even))
    folds = lat == lax.axis_size("lat") - 1

    @pl.when(jnp.logical_not(folds))
    def _():
        store(send_b, *message(jnp.logical_not(even)))

    @pl.when(folds)
    def _():
        tiles, kappa, corners = message(True)
        backward = LANES - 1 - lane
        flip = lambda x, index: jnp.take_along_axis(x, index, axis=1, mode="promise_in_bounds")
        flip_tile = lambda tile: [flip(tile[1], backward), flip(tile[0], backward)]
        sign = jnp.where(low, 1.0, -1.0)
        turned = [flip_tile(tile) for tile in tiles]
        turned = turned[:3] + [[sign * x for x in tile] for tile in turned[3:]]
        index = jnp.where(lane < 14, 13 - lane, lane)
        corner_signs = [1.0, sign, -sign]
        store(send_b, turned, flip_tile(kappa), [corner_signs[i % 3] * flip(x, index) for i, x in enumerate(corners)])


def split_groups(groups):
    return {
        "c": groups["c"],
        "m": twice_low(groups["mu"]),
        "u": twice_high(groups["mu"]),
        "v": twice_low(groups["vw"]),
        "w": twice_high(groups["vw"]),
        "sx": twice_low(groups["sk"]),
        "k": twice_high(groups["sk"]),
    }


def third_tile(groups, bases):
    east = lane_of() < 64
    tile = lambda x, base: jnp.where(
        east, pltpu.roll(x, (2 * LANES - 4 - base) % LANES, 1), pltpu.roll(x, (2 * LANES - 10 - base) % LANES, 1)
    )
    return split_groups({n: tile(groups[n], bases[n]) for n in GROUPS})


def plus(tiles):
    last = lane_of() == LANES - 1
    turned = [pltpu.roll(t, LANES - 1, 1) for t in tiles]
    if len(tiles) == 1:
        return turned
    return [jnp.where(last, turned[(i + 1) % len(tiles)], turned[i]) for i in range(len(tiles))]


def minus(tiles, count=3, west=None):
    first = lane_of() == 0
    turned = [pltpu.roll(t, 1, 1) for t in tiles]
    if len(tiles) == 1:
        return turned
    before = [turned[-1] if west is None else west] + turned[:-1]
    return [jnp.where(first, before[i], turned[i]) for i in range(min(count, len(tiles)))]


def each(function, *lists):
    return [function(*values) for values in zip(*lists)]


def below(x):
    return pltpu.roll(x, 7, 0)


def above(x):
    return pltpu.roll(x, 1, 0)


def face_flux(here, there, speed, back, step, ahead):
    positive = speed >= 0.0
    upwind = jnp.where(positive, back, ahead)
    size = jnp.abs(speed)
    limited = jnp.minimum(jnp.maximum(upwind, jnp.minimum(step, 0.0)), jnp.maximum(step, 0.0))
    return speed * jnp.where(positive, here, there) + (size - size * size) * limited


def not_bottom():
    return lax.broadcasted_iota(jnp.int32, (8, LANES), 0) % 4 != 3


def open_below(marker):
    return jnp.where(not_bottom(), below(marker), 0.0)


def face_speed(one, two, half_open):
    return (one + two) * half_open


def advect_rows(get, first, count):
    c = {j: get("c", first + j) for j in range(-2, count + 2)}
    m = {j: get("m", first + j) for j in range(-2, count + 2)}
    v = {j: get("v", first + j) for j in range(-1, count + 1)}
    half = {j: each(lambda x: 0.5 * x, m[j]) for j in range(-2, count + 2)}
    opened = {j: each(jnp.multiply, half[j], m[j + 1]) for j in range(-2, count + 1)}
    step = {j: each(lambda a, b, o: (b - a) * o, c[j], c[j + 1], opened[j]) for j in range(-2, count + 1)}
    flux = {}
    for j in range(-1, count):
        speed = each(face_speed, v[j], v[j + 1], opened[j])
        flux[j] = each(face_flux, c[j], c[j + 1], speed, step[j - 1], step[j], step[j + 1])
    result = []
    for j in range(count):
        east = plus(c[j])
        opened_x = each(jnp.multiply, half[j], plus(m[j]))
        u = get("u", first + j)
        speed = each(face_speed, u, plus(u), opened_x)
        step_x = each(lambda a, b, o: (b - a) * o, c[j], east, opened_x)
        flux_x = each(face_flux, c[j], east, speed, minus(step_x), step_x, plus(step_x))
        total = each(lambda f, g, a, b: (f - g) + (a - b), flux_x, minus(flux_x), flux[j], flux[j - 1])
        w = get("w", first + j)

        def finish(value, marker, halved, down, across):
            opened_z = open_below(halved)
            under = below(value)
            step_z = (under - value) * opened_z
            speed_z = face_speed(down, below(down), opened_z)
            flux_z = face_flux(value, under, speed_z, above(step_z), step_z, below(step_z))
            return (value - across - (flux_z - above(flux_z))) * marker

        result.append(each(finish, c[j], m[j], half[j], w, total))
    return result


def slope_flux(k1, k2, opened, step, s1, s2, z1, z2):
    return (k1 + k2) * opened * (step + (s1 + s2) * (z1 + z2))


def eastward(a, m, k, sx, twice_z):
    opened = each(jnp.multiply, m, plus(m))
    step = each(lambda x, y, o: (y - x) * o, a, plus(a), opened)
    return step, each(slope_flux, k, plus(k), opened, step, sx, plus(sx), twice_z, plus(twice_z))


def diffuse_rows(get, first, count, beside=None):
    a = {j: get("a", first + j) for j in range(-1, count + 1)}
    m = {j: get("m", first + j) for j in range(-1, count + 1)}
    k = {j: get("k", first + j) for j in range(-1, count + 1)}
    sy = {j: get("sy", first + j) for j in range(-1, count + 1)}
    step_z, twice_z = {}, {}
    for j in range(-1, count + 1):
        wide = 3 if 0 <= j < count else 2
        step_z[j] = each(lambda x, o: (below(x) - x) * open_below(o), a[j][:wide], m[j])
        twice_z[j] = each(lambda x: above(x) + x, step_z[j])
    step_y, flux_y = {}, {}
    for j in range(-1, count):
        opened = each(jnp.multiply, m[j][:2], m[j + 1][:2])
        step_y[j] = each(lambda x, y, o: (y - x) * o, a[j][:2], a[j + 1][:2], opened)
        flux_y[j] = each(
            slope_flux, k[j], k[j + 1], opened, step_y[j], sy[j], sy[j + 1], twice_z[j], twice_z[j + 1]
        )
    result = []
    last = lane_of() == LANES - 1
    for j in range(count):
        sx = get("sx", first + j)
        step_x, flux_x = eastward(a[j], m[j], k[j], sx, twice_z[j])
        west = [None, None]
        if beside:
            east, west = beside(first + j)
            step_x = [step_x[0], jnp.where(last, east[0], step_x[1])]
            flux_x = [flux_x[0], jnp.where(last, east[1], flux_x[1])]
        twice_x = each(jnp.add, step_x, minus(step_x, 2, west[0]))
        twice_y = each(jnp.add, step_y[j - 1], step_y[j])
        total = each(lambda f, g, p, q: (f - g) + (p - q), flux_x, minus(flux_x, 2, west[1]), flux_y[j], flux_y[j - 1])

        def finish(value, marker, kappa, east, north, tx, ty, sz, across):
            face_east, face_north = east + below(east), north + below(north)
            flux_z = (kappa + below(kappa)) * open_below(marker) * (
                face_east * (tx + below(tx)) + face_north * (ty + below(ty))
                + (face_east * face_east + face_north * face_north) * (16.0 * sz)
            )
            return (value + across + (flux_z - above(flux_z))) * marker

        result.append(each(finish, a[j][:2], m[j], k[j], sx, sy[j], twice_x, twice_y, step_z[j], total))
    return result


def tiles_of(ref, row, count):
    return [ref[row, :, t * LANES : (t + 1) * LANES] for t in range(count)]


def interior_kernel(*refs):
    rows, advected, strips = refs[:5], refs[5], refs[6]
    out, kept, narrow = refs[7:]
    lane = lane_of()
    near_east, near_west = lane >= LANES - 2, lane < 2

    full = [split_groups({n: strips[i, g] for i, n in enumerate(GROUPS)}) for g in range(8)]

    def get_strip(name, g):
        x = full[g % 8][name]
        return [x if 0 <= g < 8 else pltpu.roll(x, 16 if g < 0 else LANES - 16, 1)]

    for g, (a,) in enumerate(advect_rows(get_strip, 0, 8)):
        part = full[g]
        step_z = (below(a) - a) * open_below(part["m"])
        step, flux = eastward([a], [part["m"]], [part["k"]], [part["sx"]], [above(step_z) + step_z])
        narrow[0, g], narrow[1, g], narrow[2, g] = a, step[0], flux[0]

    def lanes_to(which, row, lane_from, lane_to):
        part = row // 8
        return pltpu.roll(narrow[which, row - 8 * part], lax.rem(2 * LANES + lane_to - lane_from - 16 * part, LANES), 1)

    def get(name, row):
        if name != "a":
            return field_tiles(rows, name, row)
        left, right = tiles_of(advected, row, 2)
        return [
            jnp.where(near_west, lanes_to(0, row, 10, 0), left),
            jnp.where(near_east, lanes_to(0, row, 3, LANES - 1), right),
        ]

    def beside(row):
        return [lanes_to(i, row, 3, LANES - 1) for i in (1, 2)], [lanes_to(i, row, 9, 0) for i in (1, 2)]

    for i, row in enumerate(KEPT):
        third = jnp.where(lane < 64, lanes_to(0, row, 4, 0), lanes_to(0, row, 9, LANES - 1))
        for t, tile in enumerate(get("a", row) + [third]):
            kept[i, :, t * LANES : (t + 1) * LANES] = tile

    def diffuse_block(block, carry):
        first = jnp.minimum(3 + 10 * block, ROWS - 3 - 10)
        for j, tiles in enumerate(diffuse_rows(get, first, 10, beside)):
            for t in range(2):
                out[first + j, :, t * LANES : (t + 1) * LANES] = tiles[t]
        return carry

    lax.fori_loop(0, 6, diffuse_block, 0)


def rim_kernel(*refs):
    got_b, got_a = refs[0], refs[1]
    fields = refs[2:7]
    strips, inner, kept, out, edges, sems = refs[7:]
    middle = pltpu.make_async_copy
    copies = [middle(inner.at[8:56, i], out.at[i, 8:56], sems.at[i]) for i in range(8)]
    for copy in copies:
        copy.start()
    low = low_of()
    lat = lax.axis_index("lat")
    even = jnp.broadcast_to(lat % 2, (8, LANES)) == 0
    floor = jnp.broadcast_to(lat, (8, LANES)) == 0

    def halo(is_north):
        def tile(i, h):
            a = got_a[i, :, h * LANES : (h + 1) * LANES]
            b = got_b[i, :, h * LANES : (h + 1) * LANES]
            if is_north:
                return jnp.where(even, a, b)
            return jnp.where(floor, 0.0, jnp.where(even, b, a))

        tiles = [[tile(i, h) for h in range(2)] for i in range(8)]
        high = lambda i: [twice_high(x) for x in tiles[i]]
        below_four = lambda i: [twice_low(x) for x in tiles[i]]
        corner = jnp.where(low, pltpu.roll(tiles[7][0], 4, 0), tiles[7][1])
        rows = []
        for q in range(3):
            bases = {n: 16 * (3 * min(q, 1) + min(i, 2)) for i, n in enumerate(GROUPS)}
            side = third_tile({n: corner for n in GROUPS}, bases)
            main = {"c": tiles[q], "m": below_four(3 + q)}
            if q < 2:
                main["v"] = high(3 + q)
            if q == 0:
                main.update(u=high(5), w=below_four(6), sy=high(6), k=below_four(7))
                main["sx"] = main["k"]
            rows.append({n: x + [side[n]] if n in side else x for n, x in main.items()})
        return rows

    for is_north in (False, True):
        rows = halo(is_north)
        start = ROWS - 2 if is_north else -1
        made, sides = {}, {}
        for row in range(*((ROWS - 4, ROWS) if is_north else (0, 4))):
            base = 16 * (row // 8)
            sides[row] = third_tile({n: strips[i, row % 8] for i, n in enumerate(GROUPS)}, dict.fromkeys(GROUPS, base))

        def get(name, row):
            if name == "a":
                return made[row] if row in made else tiles_of(kept, KEPT.index(row), 3)
            if row < 0:
                return rows[-row - 1][name]
            if row >= ROWS:
                return rows[row - ROWS][name]
            tiles = field_tiles(fields, name, row)
            return tiles if name == "sy" else tiles + [sides[row][name]]

        for j, tiles in enumerate(advect_rows(get, start, 3)):
            made[start + j] = tiles
        final = ROWS - 3 if is_north else 0
        base = ROWS - 8 if is_north else 0
        done = {final + j: x for j, x in enumerate(diffuse_rows(get, final, 3))}
        for h in range(2):
            stack = [done[j][h] if j in done else inner[j, :, h * LANES : (h + 1) * LANES] for j in range(base, base + 8)]
            edges[int(is_north), :, :, h * LANES : (h + 1) * LANES] = jnp.transpose(jnp.stack(stack), (1, 0, 2))
        copy = middle(edges.at[int(is_north)], out.at[:, base : base + 8], sems.at[8 + int(is_north)])
        copy.start()
        copies.append(copy)
    for copy in copies:
        copy.wait()


def call(kernel, shapes, *operands, **options):
    return pl.pallas_call(
        kernel,
        out_shape=[jax.ShapeDtypeStruct(s, F32) for s in shapes],
        in_specs=[VMEM] * len(operands),
        out_specs=[VMEM] * len(shapes),
        compiler_params=pltpu.CompilerParams(vmem_limit_bytes=LIMIT),
        **options,
    )(*operands)


def make(lons, lats):
    def spot(lon, lat):
        return (lon % lons) * lats + lat

    near = [(spot(i, j), spot(i ^ 1, j)) for i in range(lons) for j in range(lats)]
    far = [(spot(i, j), spot(i + 1 if i % 2 else i - 1, j)) for i in range(lons) for j in range(lats)]
    pair_a = [(spot(i, j), spot(i, j ^ 1)) for i in range(lons) for j in range(lats)]
    pair_b = []
    for i in range(lons):
        for j in range(lats):
            if j == 0:
                pair_b.append((spot(i, j), spot(i ^ 1, j)))
            elif j == lats - 1:
                pair_b.append((spot(i, j), spot(lons - 1 - i, j)))
            else:
                pair_b.append((spot(i, j), spot(i, j + 1 if j % 2 else j - 1)))

    def move(x, route):
        return lax.ppermute(x, ("lon", "lat"), route)

    def shards(tracers, velocity, slopes, diffusivity, sea_mask):
        plane = lambda x: x.reshape(-1, ROWS, 2 * LANES)
        arrays = [plane(tracers), plane(velocity), plane(slopes), diffusivity, sea_mask]
        arrays = [pltpu.with_memory_space_constraint(x, pltpu.HBM) for x in arrays]
        full, side = (ROWS, 8, 2 * LANES), (8, 8, LANES)
        *rows, packed, spare = pl.pallas_call(
            pack_kernel,
            out_shape=[jax.ShapeDtypeStruct(shape, F32) for shape in [full] * 5 + [(10, 8, LANES), side]],
            in_specs=[pl.BlockSpec(memory_space=pltpu.HBM)] * 5,
            out_specs=[VMEM] * 7,
            scratch_shapes=[pltpu.VMEM(x.shape[:2] + (LANES,), x.dtype) for x in arrays for _ in range(2)]
            + [pltpu.SemaphoreType.DMA((10,))],
            compiler_params=pltpu.CompilerParams(vmem_limit_bytes=LIMIT),
        )(*arrays)
        far_got, near_got = move(packed, far), move(packed, near)
        (advected,) = call(
            advect_kernel, [full], *rows,
            cost_estimate=pl.CostEstimate(flops=10**7, bytes_accessed=6 * 10**6, transcendentals=0),
        )
        strips, send_a, send_b = call(
            edge_kernel, [(4,) + side, (8, 8, 2 * LANES), (8, 8, 2 * LANES)], near_got, far_got, packed, spare, *rows, advected
        )
        got_b, got_a = move(send_b, pair_b), move(send_a, pair_a)
        inner, kept = call(
            interior_kernel, [full, (4, 8, 3 * LANES)], *rows, advected, strips,
            scratch_shapes=[pltpu.VMEM((3,) + side, F32)],
            cost_estimate=pl.CostEstimate(flops=2 * 10**7, bytes_accessed=10**7, transcendentals=0),
        )
        out = pl.pallas_call(
            rim_kernel,
            out_shape=jax.ShapeDtypeStruct((8, ROWS, 2 * LANES), F32),
            in_specs=[VMEM] * 10,
            out_specs=pl.BlockSpec(memory_space=pl.ANY),
            scratch_shapes=[pltpu.VMEM((2, 8, 8, 2 * LANES), F32), pltpu.SemaphoreType.DMA((10,))],
            compiler_params=pltpu.CompilerParams(vmem_limit_bytes=LIMIT),
        )(got_b, got_a, *rows, strips, inner, kept)
        return out.reshape(tracers.shape)

    return shards


def solution(mesh):
    return jax.shard_map(
        make(mesh.shape["lon"], mesh.shape["lat"]),
        mesh=mesh,
        in_specs=(
            P(None, None, "lat", "lon"),
            P(None, None, "lat", "lon"),
            P(None, None, "lat", "lon"),
            P(None, "lat", "lon"),
            P(None, "lat", "lon"),
        ),
        out_specs=P(None, None, "lat", "lon"),
        check_vma=False,
    )
```

```python
import jax
import jax.numpy as jnp
from jax import lax
from jax.experimental import pallas as pl
from jax.experimental.pallas import tpu as pltpu
from jax.sharding import PartitionSpec as P


ROWS = 64
LANES = 128
F32 = jnp.float32
VMEM = pl.BlockSpec(memory_space=pltpu.VMEM)
LIMIT = 16 * 1024 * 1024
CHUNKS = 2
GROUPS = ("c", "mu", "vw", "sk")
KEPT = (2, 3, ROWS - 4, ROWS - 3)


def lane_of():
    return lax.broadcasted_iota(jnp.int32, (8, LANES), 1)


def low_of():
    return lax.broadcasted_iota(jnp.int32, (8, LANES), 0) < 4


def twice_low(x):
    return jnp.where(low_of(), x, pltpu.roll(x, 4, 0))


def twice_high(x):
    return jnp.where(low_of(), pltpu.roll(x, 4, 0), x)


def field_half(rows, name, row, h):
    which, turn = {
        "u": (1, twice_low), "v": (1, twice_high), "w": (2, twice_high),
        "sx": (3, twice_low), "sy": (3, twice_high), "m": (4, twice_low), "k": (4, twice_high),
    }.get(name, (0, None))
    value = rows[which][row, :, h * LANES : (h + 1) * LANES]
    return turn(value) if turn else value


def field_tiles(rows, name, row):
    return [field_half(rows, name, row, h) for h in range(2)]


def pack_kernel(*refs):
    arrays, rows, message, spare, held, sems = refs[:5], refs[5:10], refs[10], refs[11], refs[12:17], refs[17]
    copies = []
    for chunk in range(CHUNKS):
        span = slice(chunk * ROWS // CHUNKS, (chunk + 1) * ROWS // CHUNKS)
        copies.append(
            [
                pltpu.make_async_copy(array.at[:, span], hold.at[:, span], sems.at[chunk, i])
                for i, (array, hold) in enumerate(zip(arrays, held))
            ]
        )
        for copy in copies[-1]:
            copy.start()
    lane, low = lane_of(), low_of()
    scale = jnp.where(low, 1.0, 0.5)
    tracer, velocity, slope, kappa, mask = held
    first, second = [None] * 8, [None] * 8
    for part in range(8):
        if part * CHUNKS % 8 == 0:
            for copy in copies[part * CHUNKS // 8]:
                copy.wait()
        span = slice(8 * part, 8 * part + 8)
        halves = []
        for h in range(2):
            wide = slice(h * LANES, (h + 1) * LANES)
            planes = [
                tracer[:, span, wide], velocity[0:8, span, wide], velocity[4:12, span, wide], slope[:, span, wide],
                jnp.concatenate([mask[:, span, wide].astype(F32), kappa[:, span, wide]], axis=0),
            ]
            halves.append([jnp.transpose(x, (1, 0, 2)) for x in planes])
        base = 16 * part
        before, half = lane < base, lane < base + 8
        for g in range(8):
            rims = []
            for h in range(2):
                c, uv, vw, s, mk = [x[g] for x in halves[h]]
                loaded = (c, uv, vw, s * 0.125, mk * scale)
                for ref, value in zip(rows, loaded):
                    ref[8 * part + g, :, h * LANES : (h + 1) * LANES] = value
                rims.append(loaded)
            c, uv, vw, s, mk = [jnp.where(lane < 64, a, b) for a, b in zip(*rims)]
            mu = jnp.where(low, mk, pltpu.roll(uv, 4, 0))
            sk = jnp.where(low, s, mk)
            one = jnp.where(half, pltpu.roll(c, (base + 4) % LANES, 1), pltpu.roll(mu, (base + 12) % LANES, 1))
            two = jnp.where(half, pltpu.roll(vw, (base + 4) % LANES, 1), pltpu.roll(sk, (base + 12) % LANES, 1))
            first[g] = jnp.where(before, first[g], one) if part else one
            second[g] = jnp.where(before, second[g], two) if part else two
    for g in range(8):
        message[g] = first[g]
        spare[g] = second[g]
    slot = lane % 8
    for pair in range(2):
        total = pltpu.roll(second[4 * pair], LANES - 2, 1)
        for i in range(1, 4):
            moved = second[4 * pair + i] if i == 1 else pltpu.roll(second[4 * pair + i], 2 * i - 2, 1)
            total = jnp.where((slot == (2 * i + 1) % 8) | (slot == (2 * i + 2) % 8), moved, total)
        message[8 + pair] = total


def advect_kernel(*refs):
    rows, advected = refs[:5], refs[5]
    get = lambda name, row: field_tiles(rows, name, row)

    def advect_block(block, carry):
        first = 2 + 15 * block
        for j, tiles in enumerate(advect_rows(get, first, 15)):
            for t in range(2):
                advected[first + j, :, t * LANES : (t + 1) * LANES] = tiles[t]
        return carry

    lax.fori_loop(0, 4, advect_block, 0)


def strip_at(g, which, late, from_near, from_far, own, spare):
    slot = lane_of() % 16
    far_is_west = jnp.broadcast_to(lax.axis_index("lon") % 2, (8, LANES)) == 0
    if which == 0:
        far, near, mine = from_far[g], from_near[g], own[g]
    else:
        back = (2 - 2 * (g % 4)) % LANES
        turn = lambda x: pltpu.roll(x, back, 1) if back else x
        far, near, mine = turn(from_far[8 + g // 4]), turn(from_near[8 + g // 4]), spare[g]
    east, west = jnp.where(far_is_west, near, far), jnp.where(far_is_west, far, near)
    shift = lambda x, by: pltpu.roll(x, (by - 8 * late) % LANES, 1) if by != 8 * late else x
    inner = jnp.where(slot < 4, shift(mine, 0), shift(east, 0))
    outer = jnp.where(slot < 10, shift(west, 6), shift(mine, 6))
    return jnp.where(slot < 7, inner, outer)


def edge_kernel(*refs):
    sources, rows = refs[:4], refs[4:9]
    send_a, send_b = refs[10:]
    lane, low = lane_of(), low_of()
    lat = lax.axis_index("lat")
    strips = {(i, g): strip_at(g, i // 2, i % 2, *sources) for i in range(3) for g in (0, 1, 6, 7)}

    def message(top):
        row = lambda q: jnp.where(top, ROWS - 1 - q, q)
        part = lambda name, q, h: field_half(rows, name, row(q), h)
        pair = lambda n1, q1, n2, q2: [jnp.where(low, part(n1, q1, h), part(n2, q2, h)) for h in range(2)]
        tiles = [[part("c", q, h) for h in range(2)] for q in range(3)]
        tiles += [pair("m", 0, "v", 0), pair("m", 1, "v", 1), pair("m", 2, "u", 0), pair("w", 0, "sy", 0)]
        corners = [
            jnp.where(top, pltpu.roll(strips[i, 7 - q], 16, 1), strips[i, q]) for q in range(2) for i in range(3)
        ]
        return tiles, [part("k", 0, h) for h in range(2)], corners

    def store(ref, tiles, kappa, corners):
        for i, tile in enumerate(tiles):
            for h in range(2):
                ref[i, :, h * LANES : (h + 1) * LANES] = tile[h]
        packed = corners[0]
        for i in range(1, 6):
            packed = jnp.where(lane < 16 * i, packed, pltpu.roll(corners[i], 16 * i, 1))
        ref[7, :, :LANES] = jnp.where(low, kappa[0], pltpu.roll(packed, 4, 0))
        ref[7, :, LANES:] = jnp.where(low, kappa[1], packed)

    even = lat % 2 == 0
    store(send_a, *message(even))
    folds = lat == lax.axis_size("lat") - 1

    @pl.when(jnp.logical_not(folds))
    def _():
        store(send_b, *message(jnp.logical_not(even)))

    @pl.when(folds)
    def _():
        tiles, kappa, corners = message(True)
        backward = LANES - 1 - lane
        flip = lambda x, index: jnp.take_along_axis(x, index, axis=1, mode="promise_in_bounds")
        flip_tile = lambda tile: [flip(tile[1], backward), flip(tile[0], backward)]
        sign = jnp.where(low, 1.0, -1.0)
        turned = [flip_tile(tile) for tile in tiles]
        turned = turned[:3] + [[sign * x for x in tile] for tile in turned[3:]]
        index = jnp.where(lane < 14, 13 - lane, lane)
        corner_signs = [1.0, sign, -sign]
        store(send_b, turned, flip_tile(kappa), [corner_signs[i % 3] * flip(x, index) for i, x in enumerate(corners)])


def split_groups(groups):
    return {
        "c": groups["c"],
        "m": twice_low(groups["mu"]),
        "u": twice_high(groups["mu"]),
        "v": twice_low(groups["vw"]),
        "w": twice_high(groups["vw"]),
        "sx": twice_low(groups["sk"]),
        "k": twice_high(groups["sk"]),
    }


def third_tile(groups, bases):
    east = lane_of() < 64
    tile = lambda x, base: jnp.where(
        east, pltpu.roll(x, (2 * LANES - 4 - base) % LANES, 1), pltpu.roll(x, (2 * LANES - 10 - base) % LANES, 1)
    )
    return split_groups({n: tile(groups[n], bases[n]) for n in GROUPS})


def plus(tiles):
    last = lane_of() == LANES - 1
    turned = [pltpu.roll(t, LANES - 1, 1) for t in tiles]
    if len(tiles) == 1:
        return turned
    return [jnp.where(last, turned[(i + 1) % len(tiles)], turned[i]) for i in range(len(tiles))]


def minus(tiles, count=3, west=None):
    first = lane_of() == 0
    turned = [pltpu.roll(t, 1, 1) for t in tiles]
    if len(tiles) == 1:
        return turned
    before = [turned[-1] if west is None else west] + turned[:-1]
    return [jnp.where(first, before[i], turned[i]) for i in range(min(count, len(tiles)))]


def each(function, *lists):
    return [function(*values) for values in zip(*lists)]


def below(x):
    return pltpu.roll(x, 7, 0)


def above(x):
    return pltpu.roll(x, 1, 0)


def face_flux(here, there, speed, back, step, ahead):
    positive = speed >= 0.0
    upwind = jnp.where(positive, back, ahead)
    size = jnp.abs(speed)
    limited = jnp.minimum(jnp.maximum(upwind, jnp.minimum(step, 0.0)), jnp.maximum(step, 0.0))
    return speed * jnp.where(positive, here, there) + (size - size * size) * limited


def not_bottom():
    return lax.broadcasted_iota(jnp.int32, (8, LANES), 0) % 4 != 3


def open_below(marker):
    return jnp.where(not_bottom(), below(marker), 0.0)


def face_speed(one, two, half_open):
    return (one + two) * half_open


def advect_rows(get, first, count):
    c = {j: get("c", first + j) for j in range(-2, count + 2)}
    m = {j: get("m", first + j) for j in range(-2, count + 2)}
    v = {j: get("v", first + j) for j in range(-1, count + 1)}
    half = {j: each(lambda x: 0.5 * x, m[j]) for j in range(-2, count + 2)}
    opened = {j: each(jnp.multiply, half[j], m[j + 1]) for j in range(-2, count + 1)}
    step = {j: each(lambda a, b, o: (b - a) * o, c[j], c[j + 1], opened[j]) for j in range(-2, count + 1)}
    flux = {}
    for j in range(-1, count):
        speed = each(face_speed, v[j], v[j + 1], opened[j])
        flux[j] = each(face_flux, c[j], c[j + 1], speed, step[j - 1], step[j], step[j + 1])
    result = []
    for j in range(count):
        east = plus(c[j])
        opened_x = each(jnp.multiply, half[j], plus(m[j]))
        u = get("u", first + j)
        speed = each(face_speed, u, plus(u), opened_x)
        step_x = each(lambda a, b, o: (b - a) * o, c[j], east, opened_x)
        flux_x = each(face_flux, c[j], east, speed, minus(step_x), step_x, plus(step_x))
        total = each(lambda f, g, a, b: (f - g) + (a - b), flux_x, minus(flux_x), flux[j], flux[j - 1])
        w = get("w", first + j)

        def finish(value, marker, halved, down, across):
            opened_z = open_below(halved)
            under = below(value)
            step_z = (under - value) * opened_z
            speed_z = face_speed(down, below(down), opened_z)
            flux_z = face_flux(value, under, speed_z, above(step_z), step_z, below(step_z))
            return (value - across - (flux_z - above(flux_z))) * marker

        result.append(each(finish, c[j], m[j], half[j], w, total))
    return result


def slope_flux(k1, k2, opened, step, s1, s2, z1, z2):
    return (k1 + k2) * opened * (step + (s1 + s2) * (z1 + z2))


def eastward(a, m, k, sx, twice_z):
    opened = each(jnp.multiply, m, plus(m))
    step = each(lambda x, y, o: (y - x) * o, a, plus(a), opened)
    return step, each(slope_flux, k, plus(k), opened, step, sx, plus(sx), twice_z, plus(twice_z))


def diffuse_rows(get, first, count, beside=None):
    a = {j: get("a", first + j) for j in range(-1, count + 1)}
    m = {j: get("m", first + j) for j in range(-1, count + 1)}
    k = {j: get("k", first + j) for j in range(-1, count + 1)}
    sy = {j: get("sy", first + j) for j in range(-1, count + 1)}
    step_z, twice_z = {}, {}
    for j in range(-1, count + 1):
        wide = 3 if 0 <= j < count else 2
        step_z[j] = each(lambda x, o: (below(x) - x) * open_below(o), a[j][:wide], m[j])
        twice_z[j] = each(lambda x: above(x) + x, step_z[j])
    step_y, flux_y = {}, {}
    for j in range(-1, count):
        opened = each(jnp.multiply, m[j][:2], m[j + 1][:2])
        step_y[j] = each(lambda x, y, o: (y - x) * o, a[j][:2], a[j + 1][:2], opened)
        flux_y[j] = each(
            slope_flux, k[j], k[j + 1], opened, step_y[j], sy[j], sy[j + 1], twice_z[j], twice_z[j + 1]
        )
    result = []
    last = lane_of() == LANES - 1
    for j in range(count):
        sx = get("sx", first + j)
        step_x, flux_x = eastward(a[j], m[j], k[j], sx, twice_z[j])
        west = [None, None]
        if beside:
            east, west = beside(first + j)
            step_x = [step_x[0], jnp.where(last, east[0], step_x[1])]
            flux_x = [flux_x[0], jnp.where(last, east[1], flux_x[1])]
        twice_x = each(jnp.add, step_x, minus(step_x, 2, west[0]))
        twice_y = each(jnp.add, step_y[j - 1], step_y[j])
        total = each(lambda f, g, p, q: (f - g) + (p - q), flux_x, minus(flux_x, 2, west[1]), flux_y[j], flux_y[j - 1])

        def finish(value, marker, kappa, east, north, tx, ty, sz, across):
            face_east, face_north = east + below(east), north + below(north)
            flux_z = (kappa + below(kappa)) * open_below(marker) * (
                face_east * (tx + below(tx)) + face_north * (ty + below(ty))
                + (face_east * face_east + face_north * face_north) * (16.0 * sz)
            )
            return (value + across + (flux_z - above(flux_z))) * marker

        result.append(each(finish, a[j][:2], m[j], k[j], sx, sy[j], twice_x, twice_y, step_z[j], total))
    return result


def tiles_of(ref, row, count):
    return [ref[row, :, t * LANES : (t + 1) * LANES] for t in range(count)]


def interior_kernel(*refs):
    rows, advected, sources = refs[:5], refs[5], refs[6:10]
    out, kept, strips, narrow = refs[10:]
    lane = lane_of()
    near_east, near_west = lane >= LANES - 2, lane < 2

    full = []
    for g in range(8):
        groups = {n: strip_at(g, i // 2, i % 2, *sources) for i, n in enumerate(GROUPS)}
        full.append(split_groups(groups))
        for i, n in enumerate(GROUPS):
            strips[i, g] = groups[n]

    def get_strip(name, g):
        x = full[g % 8][name]
        return [x if 0 <= g < 8 else pltpu.roll(x, 16 if g < 0 else LANES - 16, 1)]

    for g, (a,) in enumerate(advect_rows(get_strip, 0, 8)):
        part = full[g]
        step_z = (below(a) - a) * open_below(part["m"])
        step, flux = eastward([a], [part["m"]], [part["k"]], [part["sx"]], [above(step_z) + step_z])
        narrow[0, g], narrow[1, g], narrow[2, g] = a, step[0], flux[0]

    def lanes_to(which, row, lane_from, lane_to):
        part = row // 8
        return pltpu.roll(narrow[which, row - 8 * part], lax.rem(2 * LANES + lane_to - lane_from - 16 * part, LANES), 1)

    def get(name, row):
        if name != "a":
            return field_tiles(rows, name, row)
        left, right = tiles_of(advected, row, 2)
        return [
            jnp.where(near_west, lanes_to(0, row, 10, 0), left),
            jnp.where(near_east, lanes_to(0, row, 3, LANES - 1), right),
        ]

    def beside(row):
        return [lanes_to(i, row, 3, LANES - 1) for i in (1, 2)], [lanes_to(i, row, 9, 0) for i in (1, 2)]

    for i, row in enumerate(KEPT):
        third = jnp.where(lane < 64, lanes_to(0, row, 4, 0), lanes_to(0, row, 9, LANES - 1))
        for t, tile in enumerate(get("a", row) + [third]):
            kept[i, :, t * LANES : (t + 1) * LANES] = tile

    def diffuse_block(block, carry):
        first = jnp.minimum(3 + 10 * block, ROWS - 3 - 10)
        for j, tiles in enumerate(diffuse_rows(get, first, 10, beside)):
            for t in range(2):
                out[first + j, :, t * LANES : (t + 1) * LANES] = tiles[t]
        return carry

    lax.fori_loop(0, 6, diffuse_block, 0)


def rim_kernel(*refs):
    got_a, got_b = refs[0], refs[1]
    fields = refs[2:7]
    strips, inner, kept, out, edges, sems = refs[7:]
    middle = pltpu.make_async_copy
    copies = [middle(inner.at[8:56, i], out.at[i, 8:56], sems.at[i]) for i in range(8)]
    for copy in copies:
        copy.start()
    low = low_of()
    lat = lax.axis_index("lat")
    even = jnp.broadcast_to(lat % 2, (8, LANES)) == 0
    floor = jnp.broadcast_to(lat, (8, LANES)) == 0

    def halo(is_north):
        def tile(i, h):
            a = got_a[i, :, h * LANES : (h + 1) * LANES]
            b = got_b[i, :, h * LANES : (h + 1) * LANES]
            if is_north:
                return jnp.where(even, a, b)
            return jnp.where(floor, 0.0, jnp.where(even, b, a))

        tiles = [[tile(i, h) for h in range(2)] for i in range(8)]
        high = lambda i: [twice_high(x) for x in tiles[i]]
        below_four = lambda i: [twice_low(x) for x in tiles[i]]
        corner = jnp.where(low, pltpu.roll(tiles[7][0], 4, 0), tiles[7][1])
        rows = []
        for q in range(3):
            bases = {n: 16 * (3 * min(q, 1) + min(i, 2)) for i, n in enumerate(GROUPS)}
            side = third_tile({n: corner for n in GROUPS}, bases)
            main = {"c": tiles[q], "m": below_four(3 + q)}
            if q < 2:
                main["v"] = high(3 + q)
            if q == 0:
                main.update(u=high(5), w=below_four(6), sy=high(6), k=below_four(7))
                main["sx"] = main["k"]
            rows.append({n: x + [side[n]] if n in side else x for n, x in main.items()})
        return rows

    for is_north in (False, True):
        rows = halo(is_north)
        start = ROWS - 2 if is_north else -1
        made, sides = {}, {}
        for row in range(*((ROWS - 4, ROWS) if is_north else (0, 4))):
            base = 16 * (row // 8)
            sides[row] = third_tile({n: strips[i, row % 8] for i, n in enumerate(GROUPS)}, dict.fromkeys(GROUPS, base))

        def get(name, row):
            if name == "a":
                return made[row] if row in made else tiles_of(kept, KEPT.index(row), 3)
            if row < 0:
                return rows[-row - 1][name]
            if row >= ROWS:
                return rows[row - ROWS][name]
            tiles = field_tiles(fields, name, row)
            return tiles if name == "sy" else tiles + [sides[row][name]]

        for j, tiles in enumerate(advect_rows(get, start, 3)):
            made[start + j] = tiles
        final = ROWS - 3 if is_north else 0
        base = ROWS - 8 if is_north else 0
        done = {final + j: x for j, x in enumerate(diffuse_rows(get, final, 3))}
        for h in range(2):
            stack = [done[j][h] if j in done else inner[j, :, h * LANES : (h + 1) * LANES] for j in range(base, base + 8)]
            edges[int(is_north), :, :, h * LANES : (h + 1) * LANES] = jnp.transpose(jnp.stack(stack), (1, 0, 2))
        copy = middle(edges.at[int(is_north)], out.at[:, base : base + 8], sems.at[8 + int(is_north)])
        copy.start()
        copies.append(copy)
    for copy in copies:
        copy.wait()


def call(kernel, shapes, *operands, **options):
    return pl.pallas_call(
        kernel,
        out_shape=[jax.ShapeDtypeStruct(s, F32) for s in shapes],
        in_specs=[VMEM] * len(operands),
        out_specs=[VMEM] * len(shapes),
        compiler_params=pltpu.CompilerParams(vmem_limit_bytes=LIMIT),
        **options,
    )(*operands)


def make(lons, lats):
    def spot(lon, lat):
        return (lon % lons) * lats + lat

    near = [(spot(i, j), spot(i ^ 1, j)) for i in range(lons) for j in range(lats)]
    far = [(spot(i, j), spot(i + 1 if i % 2 else i - 1, j)) for i in range(lons) for j in range(lats)]
    pair_a = [(spot(i, j), spot(i, j ^ 1)) for i in range(lons) for j in range(lats)]
    pair_b = []
    for i in range(lons):
        for j in range(lats):
            if j == 0:
                pair_b.append((spot(i, j), spot(i ^ 1, j)))
            elif j == lats - 1:
                pair_b.append((spot(i, j), spot(lons - 1 - i, j)))
            else:
                pair_b.append((spot(i, j), spot(i, j + 1 if j % 2 else j - 1)))

    def move(x, route):
        return lax.ppermute(x, ("lon", "lat"), route)

    def shards(tracers, velocity, slopes, diffusivity, sea_mask):
        plane = lambda x: x.reshape(-1, ROWS, 2 * LANES)
        arrays = [plane(tracers), plane(velocity), plane(slopes), diffusivity, sea_mask]
        arrays = [pltpu.with_memory_space_constraint(x, pltpu.HBM) for x in arrays]
        full, side = (ROWS, 8, 2 * LANES), (8, 8, LANES)
        *rows, packed, spare = pl.pallas_call(
            pack_kernel,
            out_shape=[jax.ShapeDtypeStruct(shape, F32) for shape in [full] * 5 + [(10, 8, LANES), side]],
            in_specs=[pl.BlockSpec(memory_space=pltpu.HBM)] * 5,
            out_specs=[VMEM] * 7,
            scratch_shapes=[pltpu.VMEM(x.shape, x.dtype) for x in arrays] + [pltpu.SemaphoreType.DMA((CHUNKS, 5))],
            compiler_params=pltpu.CompilerParams(vmem_limit_bytes=LIMIT),
        )(*arrays)
        far_got, near_got = move(packed, far), move(packed, near)
        (advected,) = call(
            advect_kernel, [full], *rows,
            cost_estimate=pl.CostEstimate(flops=10**7, bytes_accessed=6 * 10**6, transcendentals=0),
        )
        send_a, send_b = call(
            edge_kernel, [(8, 8, 2 * LANES)] * 2, near_got, far_got, packed, spare, *rows, advected
        )
        got_a, got_b = move(send_a, pair_a), move(send_b, pair_b)
        inner, kept, strips = call(
            interior_kernel, [full, (4, 8, 3 * LANES), (4,) + side], *rows, advected, near_got, far_got, packed, spare,
            scratch_shapes=[pltpu.VMEM((3,) + side, F32)],
            cost_estimate=pl.CostEstimate(flops=2 * 10**7, bytes_accessed=10**7, transcendentals=0),
        )
        out = pl.pallas_call(
            rim_kernel,
            out_shape=jax.ShapeDtypeStruct((8, ROWS, 2 * LANES), F32),
            in_specs=[VMEM] * 10,
            out_specs=pl.BlockSpec(memory_space=pl.ANY),
            scratch_shapes=[pltpu.VMEM((2, 8, 8, 2 * LANES), F32), pltpu.SemaphoreType.DMA((10,))],
            compiler_params=pltpu.CompilerParams(vmem_limit_bytes=LIMIT),
        )(got_a, got_b, *rows, strips, inner, kept)
        return out.reshape(tracers.shape)

    return shards


def solution(mesh):
    return jax.shard_map(
        make(mesh.shape["lon"], mesh.shape["lat"]),
        mesh=mesh,
        in_specs=(
            P(None, None, "lat", "lon"),
            P(None, None, "lat", "lon"),
            P(None, None, "lat", "lon"),
            P(None, "lat", "lon"),
            P(None, "lat", "lon"),
        ),
        out_specs=P(None, None, "lat", "lon"),
        check_vma=False,
    )
```

```python
import jax
import jax.numpy as jnp
from jax import lax
from jax.experimental import pallas as pl
from jax.experimental.pallas import tpu as pltpu
from jax.sharding import PartitionSpec as P


ROWS = 64
LANES = 128
F32 = jnp.float32
VMEM = pl.BlockSpec(memory_space=pltpu.VMEM)
LIMIT = 16 * 1024 * 1024
CHUNKS = 2
GROUPS = ("c", "mu", "vw", "sk")
KEPT = (2, 3, ROWS - 4, ROWS - 3)


def lane_of():
    return lax.broadcasted_iota(jnp.int32, (8, LANES), 1)


def low_of():
    return lax.broadcasted_iota(jnp.int32, (8, LANES), 0) < 4


def twice_low(x):
    return jnp.where(low_of(), x, pltpu.roll(x, 4, 0))


def twice_high(x):
    return jnp.where(low_of(), pltpu.roll(x, 4, 0), x)


def field_half(rows, name, row, h):
    which, turn = {
        "u": (1, twice_low), "v": (1, twice_high), "w": (2, twice_high),
        "sx": (3, twice_low), "sy": (3, twice_high), "m": (4, twice_low), "k": (4, twice_high),
    }.get(name, (0, None))
    value = rows[which][row, :, h * LANES : (h + 1) * LANES]
    return turn(value) if turn else value


def field_tiles(rows, name, row):
    return [field_half(rows, name, row, h) for h in range(2)]


def pack_kernel(*refs):
    arrays, rows, (to_near, to_far, own, spare), held, sems = refs[:5], refs[5:10], refs[10:14], refs[14:19], refs[19]
    copies = []
    for chunk in range(CHUNKS):
        span = slice(chunk * ROWS // CHUNKS, (chunk + 1) * ROWS // CHUNKS)
        copies.append(
            [
                pltpu.make_async_copy(array.at[:, span], hold.at[:, span], sems.at[chunk, i])
                for i, (array, hold) in enumerate(zip(arrays, held))
            ]
        )
        for copy in copies[-1]:
            copy.start()
    lane, low = lane_of(), low_of()
    scale = jnp.where(low, 1.0, 0.5)
    tracer, velocity, slope, kappa, mask = held
    first, second = [None] * 8, [None] * 8
    for part in range(8):
        if part * CHUNKS % 8 == 0:
            for copy in copies[part * CHUNKS // 8]:
                copy.wait()
        span = slice(8 * part, 8 * part + 8)
        halves = []
        for h in range(2):
            wide = slice(h * LANES, (h + 1) * LANES)
            planes = [
                tracer[:, span, wide], velocity[0:8, span, wide], velocity[4:12, span, wide], slope[:, span, wide],
                jnp.concatenate([mask[:, span, wide].astype(F32), kappa[:, span, wide]], axis=0),
            ]
            halves.append([jnp.transpose(x, (1, 0, 2)) for x in planes])
        base = 16 * part
        before, half = lane < base, lane < base + 8
        for g in range(8):
            rims = []
            for h in range(2):
                c, uv, vw, s, mk = [x[g] for x in halves[h]]
                loaded = (c, uv, vw, s * 0.125, mk * scale)
                for ref, value in zip(rows, loaded):
                    ref[8 * part + g, :, h * LANES : (h + 1) * LANES] = value
                rims.append(loaded)
            c, uv, vw, s, mk = [jnp.where(lane < 64, a, b) for a, b in zip(*rims)]
            mu = jnp.where(low, mk, pltpu.roll(uv, 4, 0))
            sk = jnp.where(low, s, mk)
            one = jnp.where(half, pltpu.roll(c, (base + 4) % LANES, 1), pltpu.roll(mu, (base + 12) % LANES, 1))
            two = jnp.where(half, pltpu.roll(vw, (base + 4) % LANES, 1), pltpu.roll(sk, (base + 12) % LANES, 1))
            first[g] = jnp.where(before, first[g], one) if part else one
            second[g] = jnp.where(before, second[g], two) if part else two
    for g in range(8):
        own[g] = first[g]
        spare[g] = second[g]
    slot = lane % 8
    to_east = jnp.broadcast_to(lax.axis_index("lon") % 2, (8, LANES)) == 0
    for pair in range(4):
        east, west = [], []
        for g in (2 * pair, 2 * pair + 1):
            east.append(jnp.where(slot == 0, pltpu.roll(second[g], LANES - 3, 1), first[g]))
            west.append(jnp.where(slot == 7, pltpu.roll(second[g], 3, 1), first[g]))
        eastern = jnp.where(slot < 4, east[0], pltpu.roll(east[1], 4, 1))
        western = jnp.where(slot < 4, pltpu.roll(west[0], LANES - 4, 1), west[1])
        to_near[pair] = jnp.where(to_east, eastern, western)
        to_far[pair] = jnp.where(to_east, western, eastern)


def advect_kernel(*refs):
    rows, advected = refs[:5], refs[5]
    get = lambda name, row: field_tiles(rows, name, row)

    def advect_block(block, carry):
        first = 2 + 15 * block
        for j, tiles in enumerate(advect_rows(get, first, 15)):
            for t in range(2):
                advected[first + j, :, t * LANES : (t + 1) * LANES] = tiles[t]
        return carry

    lax.fori_loop(0, 4, advect_block, 0)


def strip_at(g, which, late, from_far, from_near, own, spare):
    slot = lane_of() % 16
    far_is_west = jnp.broadcast_to(lax.axis_index("lon") % 2, (8, LANES)) == 0
    near, far, mine = from_near[g // 2], from_far[g // 2], (spare if which else own)[g]
    east, west = jnp.where(far_is_west, near, far), jnp.where(far_is_west, far, near)
    shift = lambda x, by: pltpu.roll(x, by % LANES, 1) if by else x
    odd = 4 * (g % 2)
    east = shift(east, (1 if which else 4) - odd - 8 * late)
    west = shift(west, (9 if which else 6) - odd - 8 * late)
    inner = jnp.where(slot < 4, shift(mine, -8 * late), east)
    outer = jnp.where(slot < 10, west, shift(mine, 6 - 8 * late))
    return jnp.where(slot < 7, inner, outer)


def edge_kernel(*refs):
    sources, rows = refs[:4], refs[4:9]
    send_a, send_b = refs[10:]
    lane, low = lane_of(), low_of()
    lat = lax.axis_index("lat")
    strips = {(i, g): strip_at(g, i // 2, i % 2, *sources) for i in range(3) for g in (0, 1, 6, 7)}

    def message(top):
        row = lambda q: jnp.where(top, ROWS - 1 - q, q)
        part = lambda name, q, h: field_half(rows, name, row(q), h)
        pair = lambda n1, q1, n2, q2: [jnp.where(low, part(n1, q1, h), part(n2, q2, h)) for h in range(2)]
        tiles = [[part("c", q, h) for h in range(2)] for q in range(3)]
        tiles += [pair("m", 0, "v", 0), pair("m", 1, "v", 1), pair("m", 2, "u", 0), pair("w", 0, "sy", 0)]
        corners = [
            jnp.where(top, pltpu.roll(strips[i, 7 - q], 16, 1), strips[i, q]) for q in range(2) for i in range(3)
        ]
        return tiles, [part("k", 0, h) for h in range(2)], corners

    def store(ref, tiles, kappa, corners):
        for i, tile in enumerate(tiles):
            for h in range(2):
                ref[i, :, h * LANES : (h + 1) * LANES] = tile[h]
        packed = corners[0]
        for i in range(1, 6):
            packed = jnp.where(lane < 16 * i, packed, pltpu.roll(corners[i], 16 * i, 1))
        ref[7, :, :LANES] = jnp.where(low, kappa[0], pltpu.roll(packed, 4, 0))
        ref[7, :, LANES:] = jnp.where(low, kappa[1], packed)

    even = lat % 2 == 0
    store(send_a, *message(even))
    folds = lat == lax.axis_size("lat") - 1

    @pl.when(jnp.logical_not(folds))
    def _():
        store(send_b, *message(jnp.logical_not(even)))

    @pl.when(folds)
    def _():
        tiles, kappa, corners = message(True)
        backward = LANES - 1 - lane
        flip = lambda x, index: jnp.take_along_axis(x, index, axis=1, mode="promise_in_bounds")
        flip_tile = lambda tile: [flip(tile[1], backward), flip(tile[0], backward)]
        sign = jnp.where(low, 1.0, -1.0)
        turned = [flip_tile(tile) for tile in tiles]
        turned = turned[:3] + [[sign * x for x in tile] for tile in turned[3:]]
        index = jnp.where(lane < 14, 13 - lane, lane)
        corner_signs = [1.0, sign, -sign]
        store(send_b, turned, flip_tile(kappa), [corner_signs[i % 3] * flip(x, index) for i, x in enumerate(corners)])


def split_groups(groups):
    return {
        "c": groups["c"],
        "m": twice_low(groups["mu"]),
        "u": twice_high(groups["mu"]),
        "v": twice_low(groups["vw"]),
        "w": twice_high(groups["vw"]),
        "sx": twice_low(groups["sk"]),
        "k": twice_high(groups["sk"]),
    }


def third_tile(groups, bases):
    east = lane_of() < 64
    tile = lambda x, base: jnp.where(
        east, pltpu.roll(x, (2 * LANES - 4 - base) % LANES, 1), pltpu.roll(x, (2 * LANES - 10 - base) % LANES, 1)
    )
    return split_groups({n: tile(groups[n], bases[n]) for n in GROUPS})


def plus(tiles):
    last = lane_of() == LANES - 1
    turned = [pltpu.roll(t, LANES - 1, 1) for t in tiles]
    if len(tiles) == 1:
        return turned
    return [jnp.where(last, turned[(i + 1) % len(tiles)], turned[i]) for i in range(len(tiles))]


def minus(tiles, count=3, west=None):
    first = lane_of() == 0
    turned = [pltpu.roll(t, 1, 1) for t in tiles]
    if len(tiles) == 1:
        return turned
    before = [turned[-1] if west is None else west] + turned[:-1]
    return [jnp.where(first, before[i], turned[i]) for i in range(min(count, len(tiles)))]


def each(function, *lists):
    return [function(*values) for values in zip(*lists)]


def below(x):
    return pltpu.roll(x, 7, 0)


def above(x):
    return pltpu.roll(x, 1, 0)


def face_flux(here, there, speed, back, step, ahead):
    positive = speed >= 0.0
    upwind = jnp.where(positive, back, ahead)
    size = jnp.abs(speed)
    limited = jnp.minimum(jnp.maximum(upwind, jnp.minimum(step, 0.0)), jnp.maximum(step, 0.0))
    return speed * jnp.where(positive, here, there) + (size - size * size) * limited


def not_bottom():
    return lax.broadcasted_iota(jnp.int32, (8, LANES), 0) % 4 != 3


def open_below(marker):
    return jnp.where(not_bottom(), below(marker), 0.0)


def face_speed(one, two, half_open):
    return (one + two) * half_open


def advect_rows(get, first, count):
    c = {j: get("c", first + j) for j in range(-2, count + 2)}
    m = {j: get("m", first + j) for j in range(-2, count + 2)}
    v = {j: get("v", first + j) for j in range(-1, count + 1)}
    half = {j: each(lambda x: 0.5 * x, m[j]) for j in range(-2, count + 2)}
    opened = {j: each(jnp.multiply, half[j], m[j + 1]) for j in range(-2, count + 1)}
    step = {j: each(lambda a, b, o: (b - a) * o, c[j], c[j + 1], opened[j]) for j in range(-2, count + 1)}
    flux = {}
    for j in range(-1, count):
        speed = each(face_speed, v[j], v[j + 1], opened[j])
        flux[j] = each(face_flux, c[j], c[j + 1], speed, step[j - 1], step[j], step[j + 1])
    result = []
    for j in range(count):
        east = plus(c[j])
        opened_x = each(jnp.multiply, half[j], plus(m[j]))
        u = get("u", first + j)
        speed = each(face_speed, u, plus(u), opened_x)
        step_x = each(lambda a, b, o: (b - a) * o, c[j], east, opened_x)
        flux_x = each(face_flux, c[j], east, speed, minus(step_x), step_x, plus(step_x))
        total = each(lambda f, g, a, b: (f - g) + (a - b), flux_x, minus(flux_x), flux[j], flux[j - 1])
        w = get("w", first + j)

        def finish(value, marker, halved, down, across):
            opened_z = open_below(halved)
            under = below(value)
            step_z = (under - value) * opened_z
            speed_z = face_speed(down, below(down), opened_z)
            flux_z = face_flux(value, under, speed_z, above(step_z), step_z, below(step_z))
            return (value - across - (flux_z - above(flux_z))) * marker

        result.append(each(finish, c[j], m[j], half[j], w, total))
    return result


def slope_flux(k1, k2, opened, step, s1, s2, z1, z2):
    return (k1 + k2) * opened * (step + (s1 + s2) * (z1 + z2))


def eastward(a, m, k, sx, twice_z):
    opened = each(jnp.multiply, m, plus(m))
    step = each(lambda x, y, o: (y - x) * o, a, plus(a), opened)
    return step, each(slope_flux, k, plus(k), opened, step, sx, plus(sx), twice_z, plus(twice_z))


def diffuse_rows(get, first, count, beside=None):
    a = {j: get("a", first + j) for j in range(-1, count + 1)}
    m = {j: get("m", first + j) for j in range(-1, count + 1)}
    k = {j: get("k", first + j) for j in range(-1, count + 1)}
    sy = {j: get("sy", first + j) for j in range(-1, count + 1)}
    step_z, twice_z = {}, {}
    for j in range(-1, count + 1):
        wide = 3 if 0 <= j < count else 2
        step_z[j] = each(lambda x, o: (below(x) - x) * open_below(o), a[j][:wide], m[j])
        twice_z[j] = each(lambda x: above(x) + x, step_z[j])
    step_y, flux_y = {}, {}
    for j in range(-1, count):
        opened = each(jnp.multiply, m[j][:2], m[j + 1][:2])
        step_y[j] = each(lambda x, y, o: (y - x) * o, a[j][:2], a[j + 1][:2], opened)
        flux_y[j] = each(
            slope_flux, k[j], k[j + 1], opened, step_y[j], sy[j], sy[j + 1], twice_z[j], twice_z[j + 1]
        )
    result = []
    last = lane_of() == LANES - 1
    for j in range(count):
        sx = get("sx", first + j)
        step_x, flux_x = eastward(a[j], m[j], k[j], sx, twice_z[j])
        west = [None, None]
        if beside:
            east, west = beside(first + j)
            step_x = [step_x[0], jnp.where(last, east[0], step_x[1])]
            flux_x = [flux_x[0], jnp.where(last, east[1], flux_x[1])]
        twice_x = each(jnp.add, step_x, minus(step_x, 2, west[0]))
        twice_y = each(jnp.add, step_y[j - 1], step_y[j])
        total = each(lambda f, g, p, q: (f - g) + (p - q), flux_x, minus(flux_x, 2, west[1]), flux_y[j], flux_y[j - 1])

        def finish(value, marker, kappa, east, north, tx, ty, sz, across):
            face_east, face_north = east + below(east), north + below(north)
            flux_z = (kappa + below(kappa)) * open_below(marker) * (
                face_east * (tx + below(tx)) + face_north * (ty + below(ty))
                + (face_east * face_east + face_north * face_north) * (16.0 * sz)
            )
            return (value + across + (flux_z - above(flux_z))) * marker

        result.append(each(finish, a[j][:2], m[j], k[j], sx, sy[j], twice_x, twice_y, step_z[j], total))
    return result


def tiles_of(ref, row, count):
    return [ref[row, :, t * LANES : (t + 1) * LANES] for t in range(count)]


def interior_kernel(*refs):
    rows, advected, sources = refs[:5], refs[5], refs[6:10]
    out, kept, strips, narrow = refs[10:]
    lane = lane_of()
    near_east, near_west = lane >= LANES - 2, lane < 2

    full = []
    for g in range(8):
        groups = {n: strip_at(g, i // 2, i % 2, *sources) for i, n in enumerate(GROUPS)}
        full.append(split_groups(groups))
        for i, n in enumerate(GROUPS):
            strips[i, g] = groups[n]

    def get_strip(name, g):
        x = full[g % 8][name]
        return [x if 0 <= g < 8 else pltpu.roll(x, 16 if g < 0 else LANES - 16, 1)]

    for g, (a,) in enumerate(advect_rows(get_strip, 0, 8)):
        part = full[g]
        step_z = (below(a) - a) * open_below(part["m"])
        step, flux = eastward([a], [part["m"]], [part["k"]], [part["sx"]], [above(step_z) + step_z])
        narrow[0, g], narrow[1, g], narrow[2, g] = a, step[0], flux[0]

    def lanes_to(which, row, lane_from, lane_to):
        part = row // 8
        return pltpu.roll(narrow[which, row - 8 * part], lax.rem(2 * LANES + lane_to - lane_from - 16 * part, LANES), 1)

    def get(name, row):
        if name != "a":
            return field_tiles(rows, name, row)
        left, right = tiles_of(advected, row, 2)
        return [
            jnp.where(near_west, lanes_to(0, row, 10, 0), left),
            jnp.where(near_east, lanes_to(0, row, 3, LANES - 1), right),
        ]

    def beside(row):
        return [lanes_to(i, row, 3, LANES - 1) for i in (1, 2)], [lanes_to(i, row, 9, 0) for i in (1, 2)]

    for i, row in enumerate(KEPT):
        third = jnp.where(lane < 64, lanes_to(0, row, 4, 0), lanes_to(0, row, 9, LANES - 1))
        for t, tile in enumerate(get("a", row) + [third]):
            kept[i, :, t * LANES : (t + 1) * LANES] = tile

    def diffuse_block(block, carry):
        first = jnp.minimum(3 + 10 * block, ROWS - 3 - 10)
        for j, tiles in enumerate(diffuse_rows(get, first, 10, beside)):
            for t in range(2):
                out[first + j, :, t * LANES : (t + 1) * LANES] = tiles[t]
        return carry

    lax.fori_loop(0, 6, diffuse_block, 0)


def rim_kernel(*refs):
    got_b, got_a = refs[0], refs[1]
    fields = refs[2:7]
    strips, inner, kept, out, edges, sems = refs[7:]
    middle = pltpu.make_async_copy
    copies = [middle(inner.at[8:56, i], out.at[i, 8:56], sems.at[i]) for i in range(8)]
    for copy in copies:
        copy.start()
    low = low_of()
    lat = lax.axis_index("lat")
    even = jnp.broadcast_to(lat % 2, (8, LANES)) == 0
    floor = jnp.broadcast_to(lat, (8, LANES)) == 0

    def halo(is_north):
        def tile(i, h):
            a = got_a[i, :, h * LANES : (h + 1) * LANES]
            b = got_b[i, :, h * LANES : (h + 1) * LANES]
            if is_north:
                return jnp.where(even, a, b)
            return jnp.where(floor, 0.0, jnp.where(even, b, a))

        tiles = [[tile(i, h) for h in range(2)] for i in range(8)]
        high = lambda i: [twice_high(x) for x in tiles[i]]
        below_four = lambda i: [twice_low(x) for x in tiles[i]]
        corner = jnp.where(low, pltpu.roll(tiles[7][0], 4, 0), tiles[7][1])
        rows = []
        for q in range(3):
            bases = {n: 16 * (3 * min(q, 1) + min(i, 2)) for i, n in enumerate(GROUPS)}
            side = third_tile({n: corner for n in GROUPS}, bases)
            main = {"c": tiles[q], "m": below_four(3 + q)}
            if q < 2:
                main["v"] = high(3 + q)
            if q == 0:
                main.update(u=high(5), w=below_four(6), sy=high(6), k=below_four(7))
                main["sx"] = main["k"]
            rows.append({n: x + [side[n]] if n in side else x for n, x in main.items()})
        return rows

    for is_north in (False, True):
        rows = halo(is_north)
        start = ROWS - 2 if is_north else -1
        made, sides = {}, {}
        for row in range(*((ROWS - 4, ROWS) if is_north else (0, 4))):
            base = 16 * (row // 8)
            sides[row] = third_tile({n: strips[i, row % 8] for i, n in enumerate(GROUPS)}, dict.fromkeys(GROUPS, base))

        def get(name, row):
            if name == "a":
                return made[row] if row in made else tiles_of(kept, KEPT.index(row), 3)
            if row < 0:
                return rows[-row - 1][name]
            if row >= ROWS:
                return rows[row - ROWS][name]
            tiles = field_tiles(fields, name, row)
            return tiles if name == "sy" else tiles + [sides[row][name]]

        for j, tiles in enumerate(advect_rows(get, start, 3)):
            made[start + j] = tiles
        final = ROWS - 3 if is_north else 0
        base = ROWS - 8 if is_north else 0
        done = {final + j: x for j, x in enumerate(diffuse_rows(get, final, 3))}
        for h in range(2):
            stack = [done[j][h] if j in done else inner[j, :, h * LANES : (h + 1) * LANES] for j in range(base, base + 8)]
            edges[int(is_north), :, :, h * LANES : (h + 1) * LANES] = jnp.transpose(jnp.stack(stack), (1, 0, 2))
        copy = middle(edges.at[int(is_north)], out.at[:, base : base + 8], sems.at[8 + int(is_north)])
        copy.start()
        copies.append(copy)
    for copy in copies:
        copy.wait()


def call(kernel, shapes, *operands, **options):
    return pl.pallas_call(
        kernel,
        out_shape=[jax.ShapeDtypeStruct(s, F32) for s in shapes],
        in_specs=[VMEM] * len(operands),
        out_specs=[VMEM] * len(shapes),
        compiler_params=pltpu.CompilerParams(vmem_limit_bytes=LIMIT),
        **options,
    )(*operands)


def make(lons, lats):
    def spot(lon, lat):
        return (lon % lons) * lats + lat

    near = [(spot(i, j), spot(i ^ 1, j)) for i in range(lons) for j in range(lats)]
    far = [(spot(i, j), spot(i + 1 if i % 2 else i - 1, j)) for i in range(lons) for j in range(lats)]
    pair_a = [(spot(i, j), spot(i, j ^ 1)) for i in range(lons) for j in range(lats)]
    pair_b = []
    for i in range(lons):
        for j in range(lats):
            if j == 0:
                pair_b.append((spot(i, j), spot(i ^ 1, j)))
            elif j == lats - 1:
                pair_b.append((spot(i, j), spot(lons - 1 - i, j)))
            else:
                pair_b.append((spot(i, j), spot(i, j + 1 if j % 2 else j - 1)))

    def move(x, route):
        return lax.ppermute(x, ("lon", "lat"), route)

    def shards(tracers, velocity, slopes, diffusivity, sea_mask):
        plane = lambda x: x.reshape(-1, ROWS, 2 * LANES)
        arrays = [plane(tracers), plane(velocity), plane(slopes), diffusivity, sea_mask]
        arrays = [pltpu.with_memory_space_constraint(x, pltpu.HBM) for x in arrays]
        full, side = (ROWS, 8, 2 * LANES), (8, 8, LANES)
        *rows, to_near, to_far, own, spare = pl.pallas_call(
            pack_kernel,
            out_shape=[jax.ShapeDtypeStruct(shape, F32) for shape in [full] * 5 + [(4, 8, LANES)] * 2 + [side] * 2],
            in_specs=[pl.BlockSpec(memory_space=pltpu.HBM)] * 5,
            out_specs=[VMEM] * 9,
            scratch_shapes=[pltpu.VMEM(x.shape, x.dtype) for x in arrays] + [pltpu.SemaphoreType.DMA((CHUNKS, 5))],
            compiler_params=pltpu.CompilerParams(vmem_limit_bytes=LIMIT),
        )(*arrays)
        far_got, near_got = move(to_far, far), move(to_near, near)
        (advected,) = call(
            advect_kernel, [full], *rows,
            cost_estimate=pl.CostEstimate(flops=10**7, bytes_accessed=6 * 10**6, transcendentals=0),
        )
        send_a, send_b = call(
            edge_kernel, [(8, 8, 2 * LANES)] * 2, far_got, near_got, own, spare, *rows, advected
        )
        got_a, got_b = move(send_a, pair_a), move(send_b, pair_b)
        inner, kept, strips = call(
            interior_kernel, [full, (4, 8, 3 * LANES), (4,) + side], *rows, advected, far_got, near_got, own, spare,
            scratch_shapes=[pltpu.VMEM((3,) + side, F32)],
            cost_estimate=pl.CostEstimate(flops=2 * 10**7, bytes_accessed=10**7, transcendentals=0),
        )
        out = pl.pallas_call(
            rim_kernel,
            out_shape=jax.ShapeDtypeStruct((8, ROWS, 2 * LANES), F32),
            in_specs=[VMEM] * 10,
            out_specs=pl.BlockSpec(memory_space=pl.ANY),
            scratch_shapes=[pltpu.VMEM((2, 8, 8, 2 * LANES), F32), pltpu.SemaphoreType.DMA((10,))],
            compiler_params=pltpu.CompilerParams(vmem_limit_bytes=LIMIT),
        )(got_b, got_a, *rows, strips, inner, kept)
        return out.reshape(tracers.shape)

    return shards


def solution(mesh):
    return jax.shard_map(
        make(mesh.shape["lon"], mesh.shape["lat"]),
        mesh=mesh,
        in_specs=(
            P(None, None, "lat", "lon"),
            P(None, None, "lat", "lon"),
            P(None, None, "lat", "lon"),
            P(None, "lat", "lon"),
            P(None, "lat", "lon"),
        ),
        out_specs=P(None, None, "lat", "lon"),
        check_vma=False,
    )
```

```python
import jax
import jax.numpy as jnp
from jax import lax
from jax.experimental import pallas as pl
from jax.experimental.pallas import tpu as pltpu
from jax.sharding import PartitionSpec as P


ROWS = 64
LANES = 128
F32 = jnp.float32
VMEM = pl.BlockSpec(memory_space=pltpu.VMEM)
LIMIT = 16 * 1024 * 1024
CHUNKS = 2
GROUPS = ("c", "mu", "vw", "sk")
KEPT = (2, 3, ROWS - 4, ROWS - 3)


def lane_of():
    return lax.broadcasted_iota(jnp.int32, (8, LANES), 1)


def low_of():
    return lax.broadcasted_iota(jnp.int32, (8, LANES), 0) < 4


def twice_low(x):
    return jnp.where(low_of(), x, pltpu.roll(x, 4, 0))


def twice_high(x):
    return jnp.where(low_of(), pltpu.roll(x, 4, 0), x)


def field_half(rows, name, row, h):
    which, turn = {
        "u": (1, twice_low), "v": (1, twice_high), "w": (2, twice_high),
        "sx": (3, twice_low), "sy": (3, twice_high), "m": (4, twice_low), "k": (4, twice_high),
    }.get(name, (0, None))
    value = rows[which][row, :, h * LANES : (h + 1) * LANES]
    return turn(value) if turn else value


def field_tiles(rows, name, row):
    return [field_half(rows, name, row, h) for h in range(2)]


def row_planes(held, span, h):
    tracer, velocity, slope, kappa, mask = held
    wide = slice(h * LANES, (h + 1) * LANES)
    return [
        tracer[:, span, wide], velocity[0:8, span, wide], velocity[4:12, span, wide], slope[:, span, wide],
        jnp.concatenate([mask[:, span, wide].astype(F32), kappa[:, span, wide]], axis=0),
    ]


def scaled(groups):
    c, uv, vw, s, mk = groups
    return c, uv, vw, s * 0.125, mk * jnp.where(low_of(), 1.0, 0.5)


def pack_kernel(*refs):
    arrays, held, (to_near, to_far, own, spare), sems = refs[:5], refs[5:10], refs[10:14], refs[14]
    copies = []
    for chunk in range(CHUNKS):
        span = slice(chunk * ROWS // CHUNKS, (chunk + 1) * ROWS // CHUNKS)
        copies.append(
            [
                pltpu.make_async_copy(array.at[:, span], hold.at[:, span], sems.at[chunk, i])
                for i, (array, hold) in enumerate(zip(arrays, held))
            ]
        )
        for copy in copies[-1]:
            copy.start()
    lane, low = lane_of(), low_of()
    inside = lax.broadcasted_iota(jnp.int32, (8, 8, LANES), 2) < 64
    first, second = [None] * 8, [None] * 8
    for part in range(8):
        if part * CHUNKS % 8 == 0:
            for copy in copies[part * CHUNKS // 8]:
                copy.wait()
        span = slice(8 * part, 8 * part + 8)
        rims = []
        for left, right in zip(*[row_planes(held, span, h) for h in range(2)]):
            rims.append(jnp.transpose(jnp.where(inside, left, right), (1, 0, 2)))
        base = 16 * part
        before, half = lane < base, lane < base + 8
        for g in range(8):
            c, uv, vw, s, mk = scaled([x[g] for x in rims])
            mu = jnp.where(low, mk, pltpu.roll(uv, 4, 0))
            sk = jnp.where(low, s, mk)
            one = jnp.where(half, pltpu.roll(c, (base + 4) % LANES, 1), pltpu.roll(mu, (base + 12) % LANES, 1))
            two = jnp.where(half, pltpu.roll(vw, (base + 4) % LANES, 1), pltpu.roll(sk, (base + 12) % LANES, 1))
            first[g] = jnp.where(before, first[g], one) if part else one
            second[g] = jnp.where(before, second[g], two) if part else two
    for g in range(8):
        own[g] = first[g]
        spare[g] = second[g]
    slot = lane % 8
    to_east = jnp.broadcast_to(lax.axis_index("lon") % 2, (8, LANES)) == 0
    for pair in range(4):
        east, west = [], []
        for g in (2 * pair, 2 * pair + 1):
            east.append(jnp.where(slot == 0, pltpu.roll(second[g], LANES - 3, 1), first[g]))
            west.append(jnp.where(slot == 7, pltpu.roll(second[g], 3, 1), first[g]))
        eastern = jnp.where(slot < 4, east[0], pltpu.roll(east[1], 4, 1))
        western = jnp.where(slot < 4, pltpu.roll(west[0], LANES - 4, 1), west[1])
        to_near[pair] = jnp.where(to_east, eastern, western)
        to_far[pair] = jnp.where(to_east, western, eastern)


def advect_kernel(*refs):
    held, rows, advected, send_a, send_b = refs[:5], refs[5:10], refs[10], refs[11], refs[12]
    for part in range(8):
        for h in range(2):
            turned = [jnp.transpose(x, (1, 0, 2)) for x in row_planes(held, slice(8 * part, 8 * part + 8), h)]
            for g in range(8):
                for ref, value in zip(rows, scaled([x[g] for x in turned])):
                    ref[8 * part + g, :, h * LANES : (h + 1) * LANES] = value
    get = lambda name, row: field_tiles(rows, name, row)

    def advect_block(block, carry):
        first = 2 + 15 * block
        for j, tiles in enumerate(advect_rows(get, first, 15)):
            for t in range(2):
                advected[first + j, :, t * LANES : (t + 1) * LANES] = tiles[t]
        return carry

    lax.fori_loop(0, 4, advect_block, 0)
    put_messages(rows, send_a, send_b)


def put_messages(rows, send_a, send_b):
    lane, low = lane_of(), low_of()
    lat = lax.axis_index("lat")

    def message(top):
        row = lambda q: jnp.where(top, ROWS - 1 - q, q)
        part = lambda name, q, h: field_half(rows, name, row(q), h)
        pair = lambda n1, q1, n2, q2: [jnp.where(low, part(n1, q1, h), part(n2, q2, h)) for h in range(2)]
        tiles = [[part("c", q, h) for h in range(2)] for q in range(3)]
        tiles += [pair("m", 0, "v", 0), pair("m", 1, "v", 1), pair("m", 2, "u", 0), pair("w", 0, "sy", 0)]
        return tiles + [[part("k", 0, h) for h in range(2)]]

    def store(ref, tiles):
        for i, tile in enumerate(tiles):
            for h in range(2):
                ref[i, :, h * LANES : (h + 1) * LANES] = tile[h]

    even = lat % 2 == 0
    store(send_a, message(even))
    folds = lat == lax.axis_size("lat") - 1

    @pl.when(jnp.logical_not(folds))
    def _():
        store(send_b, message(jnp.logical_not(even)))

    @pl.when(folds)
    def _():
        backward = LANES - 1 - lane
        flip = lambda x: jnp.take_along_axis(x, backward, axis=1, mode="promise_in_bounds")
        turned = [[flip(tile[1]), flip(tile[0])] for tile in message(True)]
        sign = jnp.where(low, 1.0, -1.0)
        store(send_b, turned[:3] + [[sign * x for x in tile] for tile in turned[3:7]] + turned[7:])


def strip_at(g, which, late, from_far, from_near, own, spare):
    slot = lane_of() % 16
    far_is_west = jnp.broadcast_to(lax.axis_index("lon") % 2, (8, LANES)) == 0
    near, far, mine = from_near[g // 2], from_far[g // 2], (spare if which else own)[g]
    east, west = jnp.where(far_is_west, near, far), jnp.where(far_is_west, far, near)
    shift = lambda x, by: pltpu.roll(x, by % LANES, 1) if by else x
    odd = 4 * (g % 2)
    east = shift(east, (1 if which else 4) - odd - 8 * late)
    west = shift(west, (9 if which else 6) - odd - 8 * late)
    inner = jnp.where(slot < 4, shift(mine, -8 * late), east)
    outer = jnp.where(slot < 10, west, shift(mine, 6 - 8 * late))
    return jnp.where(slot < 7, inner, outer)


def edge_kernel(*refs):
    sources, made, (send_a, send_b) = refs[:4], refs[4:6], refs[6:]
    lane, low = lane_of(), low_of()
    lat = lax.axis_index("lat")
    strips = {(i, g): strip_at(g, i // 2, i % 2, *sources) for i in range(3) for g in (0, 1, 6, 7)}
    order = [(q, i) for q in range(2) for i in range(3)]
    south = [strips[i, q] for q, i in order]
    north = [pltpu.roll(strips[i, 7 - q], 16, 1) for q, i in order]

    def store(source, ref, corners):
        packed = corners[0]
        for i in range(1, 6):
            packed = jnp.where(lane < 16 * i, packed, pltpu.roll(corners[i], 16 * i, 1))
        ref[7, :, :LANES] = jnp.where(low, source[7, :, :LANES], pltpu.roll(packed, 4, 0))
        ref[7, :, LANES:] = jnp.where(low, source[7, :, LANES:], packed)

    is_even = jnp.broadcast_to(lat % 2, (8, LANES)) == 0
    folds = jnp.broadcast_to(lat, (8, LANES)) == lax.axis_size("lat") - 1
    index = jnp.where(lane < 14, 13 - lane, lane)
    sign = jnp.where(low, 1.0, -1.0)
    signs = [1.0, sign, -sign]
    turned = [
        signs[i] * jnp.take_along_axis(x, index, axis=1, mode="promise_in_bounds") for (q, i), x in zip(order, north)
    ]
    store(made[0], send_a, [jnp.where(is_even, n, s) for n, s in zip(north, south)])
    store(made[1], send_b, [jnp.where(folds, t, jnp.where(is_even, s, n)) for n, s, t in zip(north, south, turned)])


def split_groups(groups):
    return {
        "c": groups["c"],
        "m": twice_low(groups["mu"]),
        "u": twice_high(groups["mu"]),
        "v": twice_low(groups["vw"]),
        "w": twice_high(groups["vw"]),
        "sx": twice_low(groups["sk"]),
        "k": twice_high(groups["sk"]),
    }


def third_tile(groups, bases):
    east = lane_of() < 64
    tile = lambda x, base: jnp.where(
        east, pltpu.roll(x, (2 * LANES - 4 - base) % LANES, 1), pltpu.roll(x, (2 * LANES - 10 - base) % LANES, 1)
    )
    return split_groups({n: tile(groups[n], bases[n]) for n in GROUPS})


def plus(tiles):
    last = lane_of() == LANES - 1
    turned = [pltpu.roll(t, LANES - 1, 1) for t in tiles]
    if len(tiles) == 1:
        return turned
    return [jnp.where(last, turned[(i + 1) % len(tiles)], turned[i]) for i in range(len(tiles))]


def minus(tiles, count=3, west=None):
    first = lane_of() == 0
    turned = [pltpu.roll(t, 1, 1) for t in tiles]
    if len(tiles) == 1:
        return turned
    before = [turned[-1] if west is None else west] + turned[:-1]
    return [jnp.where(first, before[i], turned[i]) for i in range(min(count, len(tiles)))]


def each(function, *lists):
    return [function(*values) for values in zip(*lists)]


def below(x):
    return pltpu.roll(x, 7, 0)


def above(x):
    return pltpu.roll(x, 1, 0)


def face_flux(here, there, speed, back, step, ahead):
    positive = speed >= 0.0
    upwind = jnp.where(positive, back, ahead)
    size = jnp.abs(speed)
    limited = jnp.minimum(jnp.maximum(upwind, jnp.minimum(step, 0.0)), jnp.maximum(step, 0.0))
    return speed * jnp.where(positive, here, there) + (size - size * size) * limited


def not_bottom():
    return lax.broadcasted_iota(jnp.int32, (8, LANES), 0) % 4 != 3


def open_below(marker):
    return jnp.where(not_bottom(), below(marker), 0.0)


def face_speed(one, two, half_open):
    return (one + two) * half_open


def advect_rows(get, first, count):
    c = {j: get("c", first + j) for j in range(-2, count + 2)}
    m = {j: get("m", first + j) for j in range(-2, count + 2)}
    v = {j: get("v", first + j) for j in range(-1, count + 1)}
    half = {j: each(lambda x: 0.5 * x, m[j]) for j in range(-2, count + 2)}
    opened = {j: each(jnp.multiply, half[j], m[j + 1]) for j in range(-2, count + 1)}
    step = {j: each(lambda a, b, o: (b - a) * o, c[j], c[j + 1], opened[j]) for j in range(-2, count + 1)}
    flux = {}
    for j in range(-1, count):
        speed = each(face_speed, v[j], v[j + 1], opened[j])
        flux[j] = each(face_flux, c[j], c[j + 1], speed, step[j - 1], step[j], step[j + 1])
    result = []
    for j in range(count):
        east = plus(c[j])
        opened_x = each(jnp.multiply, half[j], plus(m[j]))
        u = get("u", first + j)
        speed = each(face_speed, u, plus(u), opened_x)
        step_x = each(lambda a, b, o: (b - a) * o, c[j], east, opened_x)
        flux_x = each(face_flux, c[j], east, speed, minus(step_x), step_x, plus(step_x))
        total = each(lambda f, g, a, b: (f - g) + (a - b), flux_x, minus(flux_x), flux[j], flux[j - 1])
        w = get("w", first + j)

        def finish(value, marker, halved, down, across):
            opened_z = open_below(halved)
            under = below(value)
            step_z = (under - value) * opened_z
            speed_z = face_speed(down, below(down), opened_z)
            flux_z = face_flux(value, under, speed_z, above(step_z), step_z, below(step_z))
            return (value - across - (flux_z - above(flux_z))) * marker

        result.append(each(finish, c[j], m[j], half[j], w, total))
    return result


def slope_flux(k1, k2, opened, step, s1, s2, z1, z2):
    return (k1 + k2) * opened * (step + (s1 + s2) * (z1 + z2))


def eastward(a, m, k, sx, twice_z):
    opened = each(jnp.multiply, m, plus(m))
    step = each(lambda x, y, o: (y - x) * o, a, plus(a), opened)
    return step, each(slope_flux, k, plus(k), opened, step, sx, plus(sx), twice_z, plus(twice_z))


def diffuse_rows(get, first, count, beside=None):
    a = {j: get("a", first + j) for j in range(-1, count + 1)}
    m = {j: get("m", first + j) for j in range(-1, count + 1)}
    k = {j: get("k", first + j) for j in range(-1, count + 1)}
    sy = {j: get("sy", first + j) for j in range(-1, count + 1)}
    step_z, twice_z = {}, {}
    for j in range(-1, count + 1):
        wide = 3 if 0 <= j < count else 2
        step_z[j] = each(lambda x, o: (below(x) - x) * open_below(o), a[j][:wide], m[j])
        twice_z[j] = each(lambda x: above(x) + x, step_z[j])
    step_y, flux_y = {}, {}
    for j in range(-1, count):
        opened = each(jnp.multiply, m[j][:2], m[j + 1][:2])
        step_y[j] = each(lambda x, y, o: (y - x) * o, a[j][:2], a[j + 1][:2], opened)
        flux_y[j] = each(
            slope_flux, k[j], k[j + 1], opened, step_y[j], sy[j], sy[j + 1], twice_z[j], twice_z[j + 1]
        )
    result = []
    last = lane_of() == LANES - 1
    for j in range(count):
        sx = get("sx", first + j)
        step_x, flux_x = eastward(a[j], m[j], k[j], sx, twice_z[j])
        west = [None, None]
        if beside:
            east, west = beside(first + j)
            step_x = [step_x[0], jnp.where(last, east[0], step_x[1])]
            flux_x = [flux_x[0], jnp.where(last, east[1], flux_x[1])]
        twice_x = each(jnp.add, step_x, minus(step_x, 2, west[0]))
        twice_y = each(jnp.add, step_y[j - 1], step_y[j])
        total = each(lambda f, g, p, q: (f - g) + (p - q), flux_x, minus(flux_x, 2, west[1]), flux_y[j], flux_y[j - 1])

        def finish(value, marker, kappa, east, north, tx, ty, sz, across):
            face_east, face_north = east + below(east), north + below(north)
            flux_z = (kappa + below(kappa)) * open_below(marker) * (
                face_east * (tx + below(tx)) + face_north * (ty + below(ty))
                + (face_east * face_east + face_north * face_north) * (16.0 * sz)
            )
            return (value + across + (flux_z - above(flux_z))) * marker

        result.append(each(finish, a[j][:2], m[j], k[j], sx, sy[j], twice_x, twice_y, step_z[j], total))
    return result


def tiles_of(ref, row, count):
    return [ref[row, :, t * LANES : (t + 1) * LANES] for t in range(count)]


def interior_kernel(*refs):
    rows, advected, sources = refs[:5], refs[5], refs[6:10]
    out, kept, strips, narrow = refs[10:]
    lane = lane_of()
    near_east, near_west = lane >= LANES - 2, lane < 2

    full = []
    for g in range(8):
        groups = {n: strip_at(g, i // 2, i % 2, *sources) for i, n in enumerate(GROUPS)}
        full.append(split_groups(groups))
        for i, n in enumerate(GROUPS):
            strips[i, g] = groups[n]

    def get_strip(name, g):
        x = full[g % 8][name]
        return [x if 0 <= g < 8 else pltpu.roll(x, 16 if g < 0 else LANES - 16, 1)]

    for g, (a,) in enumerate(advect_rows(get_strip, 0, 8)):
        part = full[g]
        step_z = (below(a) - a) * open_below(part["m"])
        step, flux = eastward([a], [part["m"]], [part["k"]], [part["sx"]], [above(step_z) + step_z])
        narrow[0, g], narrow[1, g], narrow[2, g] = a, step[0], flux[0]

    def lanes_to(which, row, lane_from, lane_to):
        part = row // 8
        return pltpu.roll(narrow[which, row - 8 * part], lax.rem(2 * LANES + lane_to - lane_from - 16 * part, LANES), 1)

    def get(name, row):
        if name != "a":
            return field_tiles(rows, name, row)
        left, right = tiles_of(advected, row, 2)
        return [
            jnp.where(near_west, lanes_to(0, row, 10, 0), left),
            jnp.where(near_east, lanes_to(0, row, 3, LANES - 1), right),
        ]

    def beside(row):
        return [lanes_to(i, row, 3, LANES - 1) for i in (1, 2)], [lanes_to(i, row, 9, 0) for i in (1, 2)]

    for i, row in enumerate(KEPT):
        third = jnp.where(lane < 64, lanes_to(0, row, 4, 0), lanes_to(0, row, 9, LANES - 1))
        for t, tile in enumerate(get("a", row) + [third]):
            kept[i, :, t * LANES : (t + 1) * LANES] = tile

    def diffuse_block(block, carry):
        first = jnp.minimum(3 + 10 * block, ROWS - 3 - 10)
        for j, tiles in enumerate(diffuse_rows(get, first, 10, beside)):
            for t in range(2):
                out[first + j, :, t * LANES : (t + 1) * LANES] = tiles[t]
        return carry

    lax.fori_loop(0, 6, diffuse_block, 0)


def rim_kernel(*refs):
    got_a, got_b = refs[0], refs[1]
    fields = refs[2:7]
    strips, inner, kept, out, edges, sems = refs[7:]
    middle = pltpu.make_async_copy
    copies = [middle(inner.at[8:56, i], out.at[i, 8:56], sems.at[i]) for i in range(8)]
    for copy in copies:
        copy.start()
    low = low_of()
    lat = lax.axis_index("lat")
    even = jnp.broadcast_to(lat % 2, (8, LANES)) == 0
    floor = jnp.broadcast_to(lat, (8, LANES)) == 0

    def halo(is_north):
        def tile(i, h):
            a = got_a[i, :, h * LANES : (h + 1) * LANES]
            b = got_b[i, :, h * LANES : (h + 1) * LANES]
            if is_north:
                return jnp.where(even, a, b)
            return jnp.where(floor, 0.0, jnp.where(even, b, a))

        tiles = [[tile(i, h) for h in range(2)] for i in range(8)]
        high = lambda i: [twice_high(x) for x in tiles[i]]
        below_four = lambda i: [twice_low(x) for x in tiles[i]]
        corner = jnp.where(low, pltpu.roll(tiles[7][0], 4, 0), tiles[7][1])
        rows = []
        for q in range(3):
            bases = {n: 16 * (3 * min(q, 1) + min(i, 2)) for i, n in enumerate(GROUPS)}
            side = third_tile({n: corner for n in GROUPS}, bases)
            main = {"c": tiles[q], "m": below_four(3 + q)}
            if q < 2:
                main["v"] = high(3 + q)
            if q == 0:
                main.update(u=high(5), w=below_four(6), sy=high(6), k=below_four(7))
                main["sx"] = main["k"]
            rows.append({n: x + [side[n]] if n in side else x for n, x in main.items()})
        return rows

    for is_north in (False, True):
        rows = halo(is_north)
        start = ROWS - 2 if is_north else -1
        made, sides = {}, {}
        for row in range(*((ROWS - 4, ROWS) if is_north else (0, 4))):
            base = 16 * (row // 8)
            sides[row] = third_tile({n: strips[i, row % 8] for i, n in enumerate(GROUPS)}, dict.fromkeys(GROUPS, base))

        def get(name, row):
            if name == "a":
                return made[row] if row in made else tiles_of(kept, KEPT.index(row), 3)
            if row < 0:
                return rows[-row - 1][name]
            if row >= ROWS:
                return rows[row - ROWS][name]
            tiles = field_tiles(fields, name, row)
            return tiles if name == "sy" else tiles + [sides[row][name]]

        for j, tiles in enumerate(advect_rows(get, start, 3)):
            made[start + j] = tiles
        final = ROWS - 3 if is_north else 0
        base = ROWS - 8 if is_north else 0
        done = {final + j: x for j, x in enumerate(diffuse_rows(get, final, 3))}
        for h in range(2):
            stack = [done[j][h] if j in done else inner[j, :, h * LANES : (h + 1) * LANES] for j in range(base, base + 8)]
            edges[int(is_north), :, :, h * LANES : (h + 1) * LANES] = jnp.transpose(jnp.stack(stack), (1, 0, 2))
        copy = middle(edges.at[int(is_north)], out.at[:, base : base + 8], sems.at[8 + int(is_north)])
        copy.start()
        copies.append(copy)
    for copy in copies:
        copy.wait()


def call(kernel, shapes, *operands, **options):
    return pl.pallas_call(
        kernel,
        out_shape=[jax.ShapeDtypeStruct(s, F32) for s in shapes],
        in_specs=[VMEM] * len(operands),
        out_specs=[VMEM] * len(shapes),
        compiler_params=pltpu.CompilerParams(vmem_limit_bytes=LIMIT),
        **options,
    )(*operands)


def make(lons, lats):
    def spot(lon, lat):
        return (lon % lons) * lats + lat

    near = [(spot(i, j), spot(i ^ 1, j)) for i in range(lons) for j in range(lats)]
    far = [(spot(i, j), spot(i + 1 if i % 2 else i - 1, j)) for i in range(lons) for j in range(lats)]
    pair_a = [(spot(i, j), spot(i, j ^ 1)) for i in range(lons) for j in range(lats)]
    pair_b = []
    for i in range(lons):
        for j in range(lats):
            if j == 0:
                pair_b.append((spot(i, j), spot(i ^ 1, j)))
            elif j == lats - 1:
                pair_b.append((spot(i, j), spot(lons - 1 - i, j)))
            else:
                pair_b.append((spot(i, j), spot(i, j + 1 if j % 2 else j - 1)))

    def move(x, route):
        return lax.ppermute(x, ("lon", "lat"), route)

    def shards(tracers, velocity, slopes, diffusivity, sea_mask):
        plane = lambda x: x.reshape(-1, ROWS, 2 * LANES)
        arrays = [plane(tracers), plane(velocity), plane(slopes), diffusivity, sea_mask]
        arrays = [pltpu.with_memory_space_constraint(x, pltpu.HBM) for x in arrays]
        full, side = (ROWS, 8, 2 * LANES), (8, 8, LANES)
        *held, to_near, to_far, own, spare = pl.pallas_call(
            pack_kernel,
            out_shape=[jax.ShapeDtypeStruct(x.shape, x.dtype) for x in arrays]
            + [jax.ShapeDtypeStruct(shape, F32) for shape in [(4, 8, LANES)] * 2 + [side] * 2],
            in_specs=[pl.BlockSpec(memory_space=pltpu.HBM)] * 5,
            out_specs=[VMEM] * 9,
            scratch_shapes=[pltpu.SemaphoreType.DMA((CHUNKS, 5))],
            compiler_params=pltpu.CompilerParams(vmem_limit_bytes=LIMIT),
        )(*arrays)
        far_got, near_got = move(to_far, far), move(to_near, near)
        *rows, advected, made_a, made_b = call(
            advect_kernel, [full] * 6 + [(8, 8, 2 * LANES)] * 2, *held,
            cost_estimate=pl.CostEstimate(flops=10**7, bytes_accessed=6 * 10**6, transcendentals=0),
        )
        send_a, send_b = call(
            edge_kernel, [(8, 8, 2 * LANES)] * 2, far_got, near_got, own, spare, made_a, made_b,
            input_output_aliases={4: 0, 5: 1},
        )
        got_a, got_b = move(send_a, pair_a), move(send_b, pair_b)
        inner, kept, strips = call(
            interior_kernel, [full, (4, 8, 3 * LANES), (4,) + side], *rows, advected, far_got, near_got, own, spare,
            scratch_shapes=[pltpu.VMEM((3,) + side, F32)],
            cost_estimate=pl.CostEstimate(flops=2 * 10**7, bytes_accessed=10**7, transcendentals=0),
        )
        out = pl.pallas_call(
            rim_kernel,
            out_shape=jax.ShapeDtypeStruct((8, ROWS, 2 * LANES), F32),
            in_specs=[VMEM] * 10,
            out_specs=pl.BlockSpec(memory_space=pl.ANY),
            scratch_shapes=[pltpu.VMEM((2, 8, 8, 2 * LANES), F32), pltpu.SemaphoreType.DMA((10,))],
            compiler_params=pltpu.CompilerParams(vmem_limit_bytes=LIMIT),
        )(got_a, got_b, *rows, strips, inner, kept)
        return out.reshape(tracers.shape)

    return shards


def solution(mesh):
    return jax.shard_map(
        make(mesh.shape["lon"], mesh.shape["lat"]),
        mesh=mesh,
        in_specs=(
            P(None, None, "lat", "lon"),
            P(None, None, "lat", "lon"),
            P(None, None, "lat", "lon"),
            P(None, "lat", "lon"),
            P(None, "lat", "lon"),
        ),
        out_specs=P(None, None, "lat", "lon"),
        check_vma=False,
    )
```

```python
import jax
import jax.numpy as jnp
from jax import lax
from jax.experimental import pallas as pl
from jax.experimental.pallas import tpu as pltpu
from jax.sharding import PartitionSpec as P


ROWS = 64
LANES = 128
F32 = jnp.float32
VMEM = pl.BlockSpec(memory_space=pltpu.VMEM)
LIMIT = 16 * 1024 * 1024
CHUNKS = 2
GROUPS = ("c", "mu", "vw", "sk")
KEPT = (2, 3, ROWS - 4, ROWS - 3)


def lane_of():
    return lax.broadcasted_iota(jnp.int32, (8, LANES), 1)


def low_of():
    return lax.broadcasted_iota(jnp.int32, (8, LANES), 0) < 4


def twice_low(x):
    return jnp.where(low_of(), x, pltpu.roll(x, 4, 0))


def twice_high(x):
    return jnp.where(low_of(), pltpu.roll(x, 4, 0), x)


def field_half(rows, name, row, h):
    which, turn = {
        "u": (1, twice_low), "v": (1, twice_high), "w": (2, twice_high),
        "sx": (3, twice_low), "sy": (3, twice_high), "m": (4, twice_low), "k": (4, twice_high),
    }.get(name, (0, None))
    value = rows[which][row, :, h * LANES : (h + 1) * LANES]
    return turn(value) if turn else value


def field_tiles(rows, name, row):
    return [field_half(rows, name, row, h) for h in range(2)]


def row_planes(held, span, h):
    tracer, velocity, slope, kappa, mask = held
    wide = slice(h * LANES, (h + 1) * LANES)
    return [
        tracer[:, span, wide], velocity[0:8, span, wide], velocity[4:12, span, wide], slope[:, span, wide],
        jnp.concatenate([mask[:, span, wide].astype(F32), kappa[:, span, wide]], axis=0),
    ]


def scaled(groups):
    c, uv, vw, s, mk = groups
    return c, uv, vw, s * 0.125, mk * jnp.where(low_of(), 1.0, 0.5)


def pack_kernel(*refs):
    arrays, held, (to_near, to_far, own, spare), sems = refs[:5], refs[5:10], refs[10:14], refs[14]
    copies = []
    for chunk in range(CHUNKS):
        span = slice(chunk * ROWS // CHUNKS, (chunk + 1) * ROWS // CHUNKS)
        copies.append(
            [
                pltpu.make_async_copy(array.at[:, span], hold.at[:, span], sems.at[chunk, i])
                for i, (array, hold) in enumerate(zip(arrays, held))
            ]
        )
        for copy in copies[-1]:
            copy.start()
    lane, low = lane_of(), low_of()
    inside = lax.broadcasted_iota(jnp.int32, (8, 8, LANES), 2) < 64
    first, second = [None] * 8, [None] * 8
    for part in range(8):
        if part * CHUNKS % 8 == 0:
            for copy in copies[part * CHUNKS // 8]:
                copy.wait()
        span = slice(8 * part, 8 * part + 8)
        rims = []
        for left, right in zip(*[row_planes(held, span, h) for h in range(2)]):
            rims.append(jnp.transpose(jnp.where(inside, left, right), (1, 0, 2)))
        base = 16 * part
        before, half = lane < base, lane < base + 8
        for g in range(8):
            c, uv, vw, s, mk = scaled([x[g] for x in rims])
            mu = jnp.where(low, mk, pltpu.roll(uv, 4, 0))
            sk = jnp.where(low, s, mk)
            one = jnp.where(half, pltpu.roll(c, (base + 4) % LANES, 1), pltpu.roll(mu, (base + 12) % LANES, 1))
            two = jnp.where(half, pltpu.roll(vw, (base + 4) % LANES, 1), pltpu.roll(sk, (base + 12) % LANES, 1))
            first[g] = jnp.where(before, first[g], one) if part else one
            second[g] = jnp.where(before, second[g], two) if part else two
    for g in range(8):
        own[g] = first[g]
        spare[g] = second[g]
    slot = lane % 8
    to_east = jnp.broadcast_to(lax.axis_index("lon") % 2, (8, LANES)) == 0
    for pair in range(4):
        east, west = [], []
        for g in (2 * pair, 2 * pair + 1):
            east.append(jnp.where(slot == 0, pltpu.roll(second[g], LANES - 3, 1), first[g]))
            west.append(jnp.where(slot == 7, pltpu.roll(second[g], 3, 1), first[g]))
        eastern = jnp.where(slot < 4, east[0], pltpu.roll(east[1], 4, 1))
        western = jnp.where(slot < 4, pltpu.roll(west[0], LANES - 4, 1), west[1])
        to_near[pair] = jnp.where(to_east, eastern, western)
        to_far[pair] = jnp.where(to_east, western, eastern)


def advect_kernel(*refs):
    held, rows, advected, send_a, send_b = refs[:5], refs[5:10], refs[10], refs[11], refs[12]
    for part in range(8):
        for h in range(2):
            turned = [jnp.transpose(x, (1, 0, 2)) for x in row_planes(held, slice(8 * part, 8 * part + 8), h)]
            for g in range(8):
                for ref, value in zip(rows, scaled([x[g] for x in turned])):
                    ref[8 * part + g, :, h * LANES : (h + 1) * LANES] = value
    get = lambda name, row: field_tiles(rows, name, row)

    def advect_block(block, carry):
        first = 2 + 15 * block
        for j, tiles in enumerate(advect_rows(get, first, 15)[0]):
            for t in range(2):
                advected[first + j, :, t * LANES : (t + 1) * LANES] = tiles[t]
        return carry

    lax.fori_loop(0, 4, advect_block, 0)
    put_messages(rows, send_a, send_b)


def put_messages(rows, send_a, send_b):
    lane, low = lane_of(), low_of()
    lat = lax.axis_index("lat")

    first, last = lane < 2, lane >= LANES - 2

    def message(top):
        row = lambda q: jnp.where(top, ROWS - 1 - q, q)
        part = lambda name, q: field_tiles(rows, name, row(q))
        outward = jnp.where(jnp.broadcast_to(jnp.where(top, 1, 0), (8, LANES)) == 1, 1.0, -1.0)
        c, m, v = [part("c", q) for q in range(3)], [part("m", q) for q in range(3)], [part("v", q) for q in range(2)]
        half = each(lambda x: 0.5 * x, m[1])
        opened = each(jnp.multiply, half, m[0])
        step = each(lambda a, b, o: (a - b) * o, c[0], c[1], opened)
        inner = each(lambda a, b, x, y: (a - b) * (x * y), c[1], c[2], half, m[2])
        speed = each(lambda a, b, o: (a + b) * o * outward, v[0], v[1], opened)
        inflow = each(
            lambda a, b, s, x, y: s * jnp.where(s >= 0.0, a, b)
            + jnp.where(s >= 0.0, (jnp.abs(s) - s * s) * median(x, y), 0.0),
            c[1], c[0], speed, step, inner,
        )
        rest = each(lambda s: jnp.where(s >= 0.0, 0.0, jnp.abs(s) - s * s), speed)
        halved = each(lambda x: 0.5 * x, m[0])
        flux_x = zonal_flux(c[0], m[0], halved, part("u", 0))
        across = each(lambda f, g: f - g, flux_x, minus(flux_x))
        across = [jnp.where(first, 0.0, across[0]), jnp.where(last, 0.0, across[1])]
        down = each(vertical_divergence, c[0], halved, part("w", 0))
        cell = each(lambda a, x, z, f: a - x - z + f, c[0], across, down, inflow)
        pair = lambda a, b: each(lambda x, y: jnp.where(low, x, y), a, b)
        return [cell, step, c[0], pair(m[0], rest), pair(v[0], part("sy", 0)), part("k", 0)]

    def store(ref, tiles):
        for i, tile in enumerate(tiles):
            for h in range(2):
                ref[i, :, h * LANES : (h + 1) * LANES] = tile[h]

    even = lat % 2 == 0
    store(send_a, message(even))
    folds = lat == lax.axis_size("lat") - 1

    @pl.when(jnp.logical_not(folds))
    def _():
        store(send_b, message(jnp.logical_not(even)))

    @pl.when(folds)
    def _():
        backward = LANES - 1 - lane
        flip = lambda x: jnp.take_along_axis(x, backward, axis=1, mode="promise_in_bounds")
        turned = [[flip(tile[1]), flip(tile[0])] for tile in message(True)]
        turned[4] = [-x for x in turned[4]]
        store(send_b, turned)


def strip_at(g, which, late, from_far, from_near, own, spare):
    slot = lane_of() % 16
    far_is_west = jnp.broadcast_to(lax.axis_index("lon") % 2, (8, LANES)) == 0
    near, far, mine = from_near[g // 2], from_far[g // 2], (spare if which else own)[g]
    east, west = jnp.where(far_is_west, near, far), jnp.where(far_is_west, far, near)
    shift = lambda x, by: pltpu.roll(x, by % LANES, 1) if by else x
    odd = 4 * (g % 2)
    east = shift(east, (1 if which else 4) - odd - 8 * late)
    west = shift(west, (9 if which else 6) - odd - 8 * late)
    inner = jnp.where(slot < 4, shift(mine, -8 * late), east)
    outer = jnp.where(slot < 10, west, shift(mine, 6 - 8 * late))
    return jnp.where(slot < 7, inner, outer)


def edge_kernel(*refs):
    sources, made, (send_a, send_b) = refs[:4], refs[4:6], refs[6:]
    lane, low = lane_of(), low_of()
    lat = lax.axis_index("lat")
    strip = lambda i, g: strip_at(g, i // 2, i % 2, *sources)

    def beside(g, inner, turn):
        c, mu, vw = strip(0, g), strip(1, g), strip(2, g)
        m = twice_low(mu)
        flux_x = zonal_flux([c], [m], [0.5 * m], [twice_high(mu)])
        step = (c - strip(0, inner)) * (0.5 * m * twice_low(strip(1, inner)))
        values = [flux_x[0] - minus(flux_x)[0], c, step, jnp.where(low, mu, pltpu.roll(vw, 4, 0))]
        return [pltpu.roll(x, turn, 1) if turn else x for x in values]

    south, north = beside(0, 1, 0), beside(7, 6, 16)

    def store(source, ref, across, *corners):
        ref[0, :, :LANES] = source[0, :, :LANES] - jnp.where(lane < 2, pltpu.roll(across, LANES - 10, 1), 0.0)
        ref[0, :, LANES:] = source[0, :, LANES:] - jnp.where(lane >= LANES - 2, pltpu.roll(across, LANES - 4, 1), 0.0)
        packed = corners[0]
        for i in range(1, 3):
            packed = jnp.where(lane < 16 * i, packed, pltpu.roll(corners[i], 16 * i, 1))
        ref[5, :, :LANES] = jnp.where(low, source[5, :, :LANES], pltpu.roll(packed, 4, 0))
        ref[5, :, LANES:] = jnp.where(low, source[5, :, LANES:], packed)

    is_even = jnp.broadcast_to(lat % 2, (8, LANES)) == 0
    folds = jnp.broadcast_to(lat, (8, LANES)) == lax.axis_size("lat") - 1
    index = jnp.where(lane < 14, 13 - lane, lane)
    turned = [jnp.take_along_axis(x, index, axis=1, mode="promise_in_bounds") for x in north]
    turned[3] = jnp.where(low, turned[3], -turned[3])
    store(made[0], send_a, *[jnp.where(is_even, n, s) for n, s in zip(north, south)])
    store(made[1], send_b, *[jnp.where(folds, t, jnp.where(is_even, s, n)) for n, s, t in zip(north, south, turned)])


def split_groups(groups):
    return {
        "c": groups["c"],
        "m": twice_low(groups["mu"]),
        "u": twice_high(groups["mu"]),
        "v": twice_low(groups["vw"]),
        "w": twice_high(groups["vw"]),
        "sx": twice_low(groups["sk"]),
        "k": twice_high(groups["sk"]),
    }


def third_of(x, base):
    east, west = pltpu.roll(x, (2 * LANES - 4 - base) % LANES, 1), pltpu.roll(x, (2 * LANES - 10 - base) % LANES, 1)
    return jnp.where(lane_of() < 64, east, west)


def third_tile(groups, base):
    return split_groups({n: third_of(groups[n], base) for n in GROUPS})


def plus(tiles):
    last = lane_of() == LANES - 1
    turned = [pltpu.roll(t, LANES - 1, 1) for t in tiles]
    if len(tiles) == 1:
        return turned
    return [jnp.where(last, turned[(i + 1) % len(tiles)], turned[i]) for i in range(len(tiles))]


def minus(tiles, count=3, west=None):
    first = lane_of() == 0
    turned = [pltpu.roll(t, 1, 1) for t in tiles]
    if len(tiles) == 1:
        return turned
    before = [turned[-1] if west is None else west] + turned[:-1]
    return [jnp.where(first, before[i], turned[i]) for i in range(min(count, len(tiles)))]


def each(function, *lists):
    return [function(*values) for values in zip(*lists)]


def below(x):
    return pltpu.roll(x, 7, 0)


def above(x):
    return pltpu.roll(x, 1, 0)


def median(step, upwind):
    return jnp.minimum(jnp.maximum(upwind, jnp.minimum(step, 0.0)), jnp.maximum(step, 0.0))


def face_flux(here, there, speed, back, step, ahead):
    positive = speed >= 0.0
    upwind = jnp.where(positive, back, ahead)
    size = jnp.abs(speed)
    return speed * jnp.where(positive, here, there) + (size - size * size) * median(step, upwind)


def zonal_flux(c, m, half, u):
    east = plus(c)
    opened = each(jnp.multiply, half, plus(m))
    speed = each(face_speed, u, plus(u), opened)
    step = each(lambda a, b, o: (b - a) * o, c, east, opened)
    return each(face_flux, c, east, speed, minus(step), step, plus(step))


def vertical_divergence(value, half, down):
    opened = open_below(half)
    under = below(value)
    step = (under - value) * opened
    flux = face_flux(value, under, face_speed(down, below(down), opened), above(step), step, below(step))
    return flux - above(flux)


def not_bottom():
    return lax.broadcasted_iota(jnp.int32, (8, LANES), 0) % 4 != 3


def open_below(marker):
    return jnp.where(not_bottom(), below(marker), 0.0)


def face_speed(one, two, half_open):
    return (one + two) * half_open


def advect_rows(get, first, count, known=()):
    known = dict(known)
    low, high = (-1 if -2 in known else -2), (count + 1 if count in known else count + 2)
    c = {j: get("c", first + j) for j in range(low, high)}
    m = {j: get("m", first + j) for j in range(low, high)}
    v = {j: get("v", first + j) for j in range(-1, count + 1)}
    half = {j: each(lambda x: 0.5 * x, m[j]) for j in range(low, high)}
    opened = {j: each(jnp.multiply, half[j], m[j + 1]) for j in range(low, high - 1)}
    step = {j: each(lambda a, b, o: (b - a) * o, c[j], c[j + 1], opened[j]) for j in range(low, high - 1)}
    step.update(known)
    flux = {}
    for j in range(-1, count):
        speed = each(face_speed, v[j], v[j + 1], opened[j])
        flux[j] = each(face_flux, c[j], c[j + 1], speed, step[j - 1], step[j], step[j + 1])
    result = []
    for j in range(count):
        flux_x = zonal_flux(c[j], m[j], half[j], get("u", first + j))
        total = each(lambda f, g, a, b: (f - g) + (a - b), flux_x, minus(flux_x), flux[j], flux[j - 1])
        down = each(vertical_divergence, c[j], half[j], get("w", first + j))
        result.append(each(lambda a, x, z, o: (a - x - z) * o, c[j], total, down, m[j]))
    return result, flux, step


def slope_flux(k1, k2, opened, step, s1, s2, z1, z2):
    return (k1 + k2) * opened * (step + (s1 + s2) * (z1 + z2))


def eastward(a, m, k, sx, twice_z):
    opened = each(jnp.multiply, m, plus(m))
    step = each(lambda x, y, o: (y - x) * o, a, plus(a), opened)
    return step, each(slope_flux, k, plus(k), opened, step, sx, plus(sx), twice_z, plus(twice_z))


def diffuse_rows(get, first, count, beside=None):
    a = {j: get("a", first + j) for j in range(-1, count + 1)}
    m = {j: get("m", first + j) for j in range(-1, count + 1)}
    k = {j: get("k", first + j) for j in range(-1, count + 1)}
    sy = {j: get("sy", first + j) for j in range(-1, count + 1)}
    step_z, twice_z = {}, {}
    for j in range(-1, count + 1):
        wide = 3 if 0 <= j < count else 2
        step_z[j] = each(lambda x, o: (below(x) - x) * open_below(o), a[j][:wide], m[j])
        twice_z[j] = each(lambda x: above(x) + x, step_z[j])
    step_y, flux_y = {}, {}
    for j in range(-1, count):
        opened = each(jnp.multiply, m[j][:2], m[j + 1][:2])
        step_y[j] = each(lambda x, y, o: (y - x) * o, a[j][:2], a[j + 1][:2], opened)
        flux_y[j] = each(
            slope_flux, k[j], k[j + 1], opened, step_y[j], sy[j], sy[j + 1], twice_z[j], twice_z[j + 1]
        )
    result = []
    last = lane_of() == LANES - 1
    for j in range(count):
        sx = get("sx", first + j)
        step_x, flux_x = eastward(a[j], m[j], k[j], sx, twice_z[j])
        west = [None, None]
        if beside:
            east, west = beside(first + j)
            step_x = [step_x[0], jnp.where(last, east[0], step_x[1])]
            flux_x = [flux_x[0], jnp.where(last, east[1], flux_x[1])]
        twice_x = each(jnp.add, step_x, minus(step_x, 2, west[0]))
        twice_y = each(jnp.add, step_y[j - 1], step_y[j])
        total = each(lambda f, g, p, q: (f - g) + (p - q), flux_x, minus(flux_x, 2, west[1]), flux_y[j], flux_y[j - 1])

        def finish(value, marker, kappa, east, north, tx, ty, sz, across):
            face_east, face_north = east + below(east), north + below(north)
            flux_z = (kappa + below(kappa)) * open_below(marker) * (
                face_east * (tx + below(tx)) + face_north * (ty + below(ty))
                + (face_east * face_east + face_north * face_north) * (16.0 * sz)
            )
            return (value + across + (flux_z - above(flux_z))) * marker

        result.append(each(finish, a[j][:2], m[j], k[j], sx, sy[j], twice_x, twice_y, step_z[j], total))
    return result


def tiles_of(ref, row, count):
    return [ref[row, :, t * LANES : (t + 1) * LANES] for t in range(count)]


def interior_kernel(*refs):
    rows, advected, sources = refs[:5], refs[5], refs[6:10]
    out, kept, strips, narrow = refs[10:]
    lane = lane_of()
    near_east, near_west = lane >= LANES - 2, lane < 2

    full = []
    for g in range(8):
        groups = {n: strip_at(g, i // 2, i % 2, *sources) for i, n in enumerate(GROUPS)}
        full.append(split_groups(groups))
        for i, n in enumerate(GROUPS):
            strips[i, g] = groups[n]

    def get_strip(name, g):
        x = full[g % 8][name]
        return [x if 0 <= g < 8 else pltpu.roll(x, 16 if g < 0 else LANES - 16, 1)]

    for g, (a,) in enumerate(advect_rows(get_strip, 0, 8)[0]):
        part = full[g]
        step_z = (below(a) - a) * open_below(part["m"])
        step, flux = eastward([a], [part["m"]], [part["k"]], [part["sx"]], [above(step_z) + step_z])
        narrow[0, g], narrow[1, g], narrow[2, g] = a, step[0], flux[0]

    def lanes_to(which, row, lane_from, lane_to):
        part = row // 8
        return pltpu.roll(narrow[which, row - 8 * part], lax.rem(2 * LANES + lane_to - lane_from - 16 * part, LANES), 1)

    def get(name, row):
        if name != "a":
            return field_tiles(rows, name, row)
        left, right = tiles_of(advected, row, 2)
        return [
            jnp.where(near_west, lanes_to(0, row, 10, 0), left),
            jnp.where(near_east, lanes_to(0, row, 3, LANES - 1), right),
        ]

    def beside(row):
        return [lanes_to(i, row, 3, LANES - 1) for i in (1, 2)], [lanes_to(i, row, 9, 0) for i in (1, 2)]

    for i, row in enumerate(KEPT):
        third = jnp.where(lane < 64, lanes_to(0, row, 4, 0), lanes_to(0, row, 9, LANES - 1))
        for t, tile in enumerate(get("a", row) + [third]):
            kept[i, :, t * LANES : (t + 1) * LANES] = tile

    def diffuse_block(block, carry):
        first = jnp.minimum(3 + 10 * block, ROWS - 3 - 10)
        for j, tiles in enumerate(diffuse_rows(get, first, 10, beside)):
            for t in range(2):
                out[first + j, :, t * LANES : (t + 1) * LANES] = tiles[t]
        return carry

    lax.fori_loop(0, 6, diffuse_block, 0)


def rim_kernel(*refs):
    got_a, got_b = refs[0], refs[1]
    fields = refs[2:7]
    strips, inner, kept, out, edges, sems = refs[7:]
    middle = pltpu.make_async_copy
    copies = [middle(inner.at[8:56, i], out.at[i, 8:56], sems.at[i]) for i in range(8)]
    for copy in copies:
        copy.start()
    low = low_of()
    lat = lax.axis_index("lat")
    even = jnp.broadcast_to(lat % 2, (8, LANES)) == 0
    floor = jnp.broadcast_to(lat, (8, LANES)) == 0

    def halo(is_north):
        def tile(i, h):
            a = got_a[i, :, h * LANES : (h + 1) * LANES]
            b = got_b[i, :, h * LANES : (h + 1) * LANES]
            if is_north:
                return jnp.where(even, a, b)
            return jnp.where(floor, 0.0, jnp.where(even, b, a))

        tiles = [[tile(i, h) for h in range(2)] for i in range(6)]
        corner = jnp.where(low, pltpu.roll(tiles[5][0], 4, 0), tiles[5][1])
        c_side, step_side, mv = [third_of(corner, 16 * i) for i in range(3)]
        row = {
            "c": tiles[2] + [c_side],
            "m": each(twice_low, tiles[3]) + [twice_low(mv)],
            "v": each(twice_low, tiles[4]) + [twice_high(mv)],
            "sy": each(twice_high, tiles[4]),
            "k": each(twice_low, tiles[5]),
        }
        return row, tiles[0], tiles[1] + [step_side], each(twice_high, tiles[3])

    for is_north in (False, True):
        outer, cell, step_in, rest = halo(is_north)
        start, beyond = (ROWS - 2, ROWS) if is_north else (0, -1)
        made, sides = {}, {}
        for row in range(*((ROWS - 4, ROWS) if is_north else (0, 4))):
            base = 16 * (row // 8)
            sides[row] = third_tile({n: strips[i, row % 8] for i, n in enumerate(GROUPS)}, base)

        def get(name, row):
            if name == "a":
                return made[row] if row in made else tiles_of(kept, KEPT.index(row), 3)
            if row == beyond:
                return outer[name]
            tiles = field_tiles(fields, name, row)
            return tiles if name == "sy" else tiles + [sides[row][name]]

        known = {2: [-x for x in step_in]} if is_north else {-2: step_in}
        results, flux, step = advect_rows(get, start, 2, known)
        made.update(zip((start, start + 1), results))
        face, sign = (1, -1.0) if is_north else (-1, 1.0)
        made[beyond] = each(
            lambda q, g, s, t, f, o: (q + g * median(s, sign * t) - sign * f) * o,
            cell, rest, step_in, step[face], flux[face], outer["m"],
        )
        final = ROWS - 3 if is_north else 0
        base = ROWS - 8 if is_north else 0
        done = {final + j: x for j, x in enumerate(diffuse_rows(get, final, 3))}
        for h in range(2):
            stack = [done[j][h] if j in done else inner[j, :, h * LANES : (h + 1) * LANES] for j in range(base, base + 8)]
            edges[int(is_north), :, :, h * LANES : (h + 1) * LANES] = jnp.transpose(jnp.stack(stack), (1, 0, 2))
        copy = middle(edges.at[int(is_north)], out.at[:, base : base + 8], sems.at[8 + int(is_north)])
        copy.start()
        copies.append(copy)
    for copy in copies:
        copy.wait()


def call(kernel, shapes, *operands, **options):
    return pl.pallas_call(
        kernel,
        out_shape=[jax.ShapeDtypeStruct(s, F32) for s in shapes],
        in_specs=[VMEM] * len(operands),
        out_specs=[VMEM] * len(shapes),
        compiler_params=pltpu.CompilerParams(vmem_limit_bytes=LIMIT),
        **options,
    )(*operands)


def make(lons, lats):
    def spot(lon, lat):
        return (lon % lons) * lats + lat

    near = [(spot(i, j), spot(i ^ 1, j)) for i in range(lons) for j in range(lats)]
    far = [(spot(i, j), spot(i + 1 if i % 2 else i - 1, j)) for i in range(lons) for j in range(lats)]
    pair_a = [(spot(i, j), spot(i, j ^ 1)) for i in range(lons) for j in range(lats)]
    pair_b = []
    for i in range(lons):
        for j in range(lats):
            if j == 0:
                pair_b.append((spot(i, j), spot(i ^ 1, j)))
            elif j == lats - 1:
                pair_b.append((spot(i, j), spot(lons - 1 - i, j)))
            else:
                pair_b.append((spot(i, j), spot(i, j + 1 if j % 2 else j - 1)))

    def move(x, route):
        return lax.ppermute(x, ("lon", "lat"), route)

    def shards(tracers, velocity, slopes, diffusivity, sea_mask):
        plane = lambda x: x.reshape(-1, ROWS, 2 * LANES)
        arrays = [plane(tracers), plane(velocity), plane(slopes), diffusivity, sea_mask]
        arrays = [pltpu.with_memory_space_constraint(x, pltpu.HBM) for x in arrays]
        full, side = (ROWS, 8, 2 * LANES), (8, 8, LANES)
        *held, to_near, to_far, own, spare = pl.pallas_call(
            pack_kernel,
            out_shape=[jax.ShapeDtypeStruct(x.shape, x.dtype) for x in arrays]
            + [jax.ShapeDtypeStruct(shape, F32) for shape in [(4, 8, LANES)] * 2 + [side] * 2],
            in_specs=[pl.BlockSpec(memory_space=pltpu.HBM)] * 5,
            out_specs=[VMEM] * 9,
            scratch_shapes=[pltpu.SemaphoreType.DMA((CHUNKS, 5))],
            compiler_params=pltpu.CompilerParams(vmem_limit_bytes=LIMIT),
        )(*arrays)
        far_got, near_got = move(to_far, far), move(to_near, near)
        *rows, advected, made_a, made_b = call(
            advect_kernel, [full] * 6 + [(6, 8, 2 * LANES)] * 2, *held,
            cost_estimate=pl.CostEstimate(flops=10**7, bytes_accessed=6 * 10**6, transcendentals=0),
        )
        send_a, send_b = call(
            edge_kernel, [(6, 8, 2 * LANES)] * 2, far_got, near_got, own, spare, made_a, made_b,
            input_output_aliases={4: 0, 5: 1},
        )
        got_a, got_b = move(send_a, pair_a), move(send_b, pair_b)
        inner, kept, strips = call(
            interior_kernel, [full, (4, 8, 3 * LANES), (4,) + side], *rows, advected, far_got, near_got, own, spare,
            scratch_shapes=[pltpu.VMEM((3,) + side, F32)],
            cost_estimate=pl.CostEstimate(flops=2 * 10**7, bytes_accessed=10**7, transcendentals=0),
        )
        out = pl.pallas_call(
            rim_kernel,
            out_shape=jax.ShapeDtypeStruct((8, ROWS, 2 * LANES), F32),
            in_specs=[VMEM] * 10,
            out_specs=pl.BlockSpec(memory_space=pl.ANY),
            scratch_shapes=[pltpu.VMEM((2, 8, 8, 2 * LANES), F32), pltpu.SemaphoreType.DMA((10,))],
            compiler_params=pltpu.CompilerParams(vmem_limit_bytes=LIMIT),
        )(got_a, got_b, *rows, strips, inner, kept)
        return out.reshape(tracers.shape)

    return shards


def solution(mesh):
    return jax.shard_map(
        make(mesh.shape["lon"], mesh.shape["lat"]),
        mesh=mesh,
        in_specs=(
            P(None, None, "lat", "lon"),
            P(None, None, "lat", "lon"),
            P(None, None, "lat", "lon"),
            P(None, "lat", "lon"),
            P(None, "lat", "lon"),
        ),
        out_specs=P(None, None, "lat", "lon"),
        check_vma=False,
    )
```

```python
import jax
import jax.numpy as jnp
from jax import lax
from jax.experimental import pallas as pl
from jax.experimental.pallas import tpu as pltpu
from jax.sharding import PartitionSpec as P


ROWS = 64
LANES = 128
F32 = jnp.float32
VMEM = pl.BlockSpec(memory_space=pltpu.VMEM)
LIMIT = 16 * 1024 * 1024
CHUNKS = 2
GROUPS = ("c", "mu", "vw", "sk")
KEPT = (2, 3, ROWS - 4, ROWS - 3)


def lane_of():
    return lax.broadcasted_iota(jnp.int32, (8, LANES), 1)


def low_of():
    return lax.broadcasted_iota(jnp.int32, (8, LANES), 0) < 4


def twice_low(x):
    return jnp.where(low_of(), x, pltpu.roll(x, 4, 0))


def twice_high(x):
    return jnp.where(low_of(), pltpu.roll(x, 4, 0), x)


def field_half(rows, name, row, h):
    which, turn = {
        "u": (1, twice_low), "v": (1, twice_high), "w": (2, twice_high),
        "sx": (3, twice_low), "sy": (3, twice_high), "m": (4, twice_low), "k": (4, twice_high),
    }.get(name, (0, None))
    value = rows[which][row, :, h * LANES : (h + 1) * LANES]
    return turn(value) if turn else value


def field_tiles(rows, name, row):
    return [field_half(rows, name, row, h) for h in range(2)]


def row_planes(held, span, h):
    tracer, velocity, slope, kappa, mask = held
    wide = slice(h * LANES, (h + 1) * LANES)
    return [
        tracer[:, span, wide], velocity[0:8, span, wide], velocity[4:12, span, wide], slope[:, span, wide],
        jnp.concatenate([mask[:, span, wide].astype(F32), kappa[:, span, wide]], axis=0),
    ]


def scaled(groups):
    c, uv, vw, s, mk = groups
    return c, uv, vw, s * 0.125, mk * jnp.where(low_of(), 1.0, 0.5)


def pack_kernel(*refs):
    arrays, held, (to_near, to_far, own, spare), sems = refs[:5], refs[5:10], refs[10:14], refs[14]
    copies = []
    for chunk in range(CHUNKS):
        span = slice(chunk * ROWS // CHUNKS, (chunk + 1) * ROWS // CHUNKS)
        copies.append(
            [
                pltpu.make_async_copy(array.at[:, span], hold.at[:, span], sems.at[chunk, i])
                for i, (array, hold) in enumerate(zip(arrays, held))
            ]
        )
        for copy in copies[-1]:
            copy.start()
    lane, low = lane_of(), low_of()
    inside = lax.broadcasted_iota(jnp.int32, (8, 8, LANES), 2) < 64
    first, second = [None] * 8, [None] * 8
    for part in range(8):
        if part * CHUNKS % 8 == 0:
            for copy in copies[part * CHUNKS // 8]:
                copy.wait()
        span = slice(8 * part, 8 * part + 8)
        rims = []
        for left, right in zip(*[row_planes(held, span, h) for h in range(2)]):
            rims.append(jnp.transpose(jnp.where(inside, left, right), (1, 0, 2)))
        base = 16 * part
        before, half = lane < base, lane < base + 8
        for g in range(8):
            c, uv, vw, s, mk = scaled([x[g] for x in rims])
            mu = jnp.where(low, mk, pltpu.roll(uv, 4, 0))
            sk = jnp.where(low, s, mk)
            one = jnp.where(half, pltpu.roll(c, (base + 4) % LANES, 1), pltpu.roll(mu, (base + 12) % LANES, 1))
            two = jnp.where(half, pltpu.roll(vw, (base + 4) % LANES, 1), pltpu.roll(sk, (base + 12) % LANES, 1))
            first[g] = jnp.where(before, first[g], one) if part else one
            second[g] = jnp.where(before, second[g], two) if part else two
    for g in range(8):
        own[g] = first[g]
        spare[g] = second[g]
    slot = lane % 8
    to_east = jnp.broadcast_to(lax.axis_index("lon") % 2, (8, LANES)) == 0
    for pair in range(4):
        east, west = [], []
        for g in (2 * pair, 2 * pair + 1):
            east.append(jnp.where(slot == 0, pltpu.roll(second[g], LANES - 3, 1), first[g]))
            west.append(jnp.where(slot == 7, pltpu.roll(second[g], 3, 1), first[g]))
        eastern = jnp.where(slot < 4, east[0], pltpu.roll(east[1], 4, 1))
        western = jnp.where(slot < 4, pltpu.roll(west[0], LANES - 4, 1), west[1])
        to_near[pair] = jnp.where(to_east, eastern, western)
        to_far[pair] = jnp.where(to_east, western, eastern)


def advect_kernel(*refs):
    held, rows, advected, send_a, send_b = refs[:5], refs[5:10], refs[10], refs[11], refs[12]
    for part in range(8):
        for h in range(2):
            turned = [jnp.transpose(x, (1, 0, 2)) for x in row_planes(held, slice(8 * part, 8 * part + 8), h)]
            for g in range(8):
                for ref, value in zip(rows, scaled([x[g] for x in turned])):
                    ref[8 * part + g, :, h * LANES : (h + 1) * LANES] = value
    put_messages(rows, send_a, send_b)
    get = lambda name, row: field_tiles(rows, name, row)

    def advect_block(block, carry):
        first = 2 + 15 * block
        for j, tiles in enumerate(advect_rows(get, first, 15)[0]):
            for t in range(2):
                advected[first + j, :, t * LANES : (t + 1) * LANES] = tiles[t]
        return carry

    lax.fori_loop(0, 4, advect_block, 0)


def put_messages(rows, send_a, send_b):
    lane, low = lane_of(), low_of()
    lat = lax.axis_index("lat")

    first, last = lane < 2, lane >= LANES - 2

    def message(top):
        part = lambda name, q: field_tiles(rows, name, ROWS - 1 - q if top else q)
        outward = 1.0 if top else -1.0
        c, m, v = [part("c", q) for q in range(3)], [part("m", q) for q in range(3)], [part("v", q) for q in range(2)]
        half = each(lambda x: 0.5 * x, m[1])
        opened = each(jnp.multiply, half, m[0])
        step = each(lambda a, b, o: (a - b) * o, c[0], c[1], opened)
        inner = each(lambda a, b, x, y: (a - b) * (x * y), c[1], c[2], half, m[2])
        speed = each(lambda a, b, o: (a + b) * o * outward, v[0], v[1], opened)
        inflow = each(
            lambda a, b, s, x, y: s * jnp.where(s >= 0.0, a, b)
            + jnp.where(s >= 0.0, (jnp.abs(s) - s * s) * median(x, y), 0.0),
            c[1], c[0], speed, step, inner,
        )
        rest = each(lambda s: jnp.where(s >= 0.0, 0.0, jnp.abs(s) - s * s), speed)
        halved = each(lambda x: 0.5 * x, m[0])
        flux_x = zonal_flux(c[0], m[0], halved, part("u", 0))
        across = each(lambda f, g: f - g, flux_x, minus(flux_x))
        across = [jnp.where(first, 0.0, across[0]), jnp.where(last, 0.0, across[1])]
        down = each(vertical_divergence, c[0], halved, part("w", 0))
        cell = each(lambda a, x, z, f: a - x - z + f, c[0], across, down, inflow)
        pair = lambda a, b: each(lambda x, y: jnp.where(low, x, y), a, b)
        return [cell, step, c[0], pair(m[0], rest), pair(v[0], part("sy", 0)), part("k", 0)]

    backward = LANES - 1 - lane
    flip = lambda x: jnp.take_along_axis(x, backward, axis=1, mode="promise_in_bounds")
    is_even = jnp.broadcast_to(lat % 2, (8, LANES)) == 0
    folds = jnp.broadcast_to(lat, (8, LANES)) == lax.axis_size("lat") - 1
    north, south = message(True), message(False)
    for i, (top, bottom) in enumerate(zip(north, south)):
        for h in range(2):
            wide = slice(h * LANES, (h + 1) * LANES)
            turned = flip(top[1 - h])
            if i == 4:
                turned = -turned
            send_a[i, :, wide] = jnp.where(is_even, top[h], bottom[h])
            send_b[i, :, wide] = jnp.where(folds, turned, jnp.where(is_even, bottom[h], top[h]))


def strip_at(g, which, late, from_far, from_near, own, spare):
    slot = lane_of() % 16
    far_is_west = jnp.broadcast_to(lax.axis_index("lon") % 2, (8, LANES)) == 0
    near, far, mine = from_near[g // 2], from_far[g // 2], (spare if which else own)[g]
    east, west = jnp.where(far_is_west, near, far), jnp.where(far_is_west, far, near)
    shift = lambda x, by: pltpu.roll(x, by % LANES, 1) if by else x
    odd = 4 * (g % 2)
    east = shift(east, (1 if which else 4) - odd - 8 * late)
    west = shift(west, (9 if which else 6) - odd - 8 * late)
    inner = jnp.where(slot < 4, shift(mine, -8 * late), east)
    outer = jnp.where(slot < 10, west, shift(mine, 6 - 8 * late))
    return jnp.where(slot < 7, inner, outer)


def edge_kernel(*refs):
    sources, made, (send_a, send_b) = refs[:4], refs[4:6], refs[6:]
    lane, low = lane_of(), low_of()
    lat = lax.axis_index("lat")
    strip = lambda i, g: strip_at(g, i // 2, i % 2, *sources)

    def beside(g, inner, turn):
        c, mu, vw = strip(0, g), strip(1, g), strip(2, g)
        m = twice_low(mu)
        flux_x = zonal_flux([c], [m], [0.5 * m], [twice_high(mu)])
        step = (c - strip(0, inner)) * (0.5 * m * twice_low(strip(1, inner)))
        values = [flux_x[0] - minus(flux_x)[0], c, step, jnp.where(low, mu, pltpu.roll(vw, 4, 0))]
        return [pltpu.roll(x, turn, 1) if turn else x for x in values]

    south, north = beside(0, 1, 0), beside(7, 6, 16)

    def store(source, ref, across, *corners):
        ref[0, :, :LANES] = source[0, :, :LANES] - jnp.where(lane < 2, pltpu.roll(across, LANES - 10, 1), 0.0)
        ref[0, :, LANES:] = source[0, :, LANES:] - jnp.where(lane >= LANES - 2, pltpu.roll(across, LANES - 4, 1), 0.0)
        packed = corners[0]
        for i in range(1, 3):
            packed = jnp.where(lane < 16 * i, packed, pltpu.roll(corners[i], 16 * i, 1))
        ref[5, :, :LANES] = jnp.where(low, source[5, :, :LANES], pltpu.roll(packed, 4, 0))
        ref[5, :, LANES:] = jnp.where(low, source[5, :, LANES:], packed)

    is_even = jnp.broadcast_to(lat % 2, (8, LANES)) == 0
    folds = jnp.broadcast_to(lat, (8, LANES)) == lax.axis_size("lat") - 1
    index = jnp.where(lane < 14, 13 - lane, lane)
    turned = [jnp.take_along_axis(x, index, axis=1, mode="promise_in_bounds") for x in north]
    turned[3] = jnp.where(low, turned[3], -turned[3])
    store(made[0], send_a, *[jnp.where(is_even, n, s) for n, s in zip(north, south)])
    store(made[1], send_b, *[jnp.where(folds, t, jnp.where(is_even, s, n)) for n, s, t in zip(north, south, turned)])


def split_groups(groups):
    return {
        "c": groups["c"],
        "m": twice_low(groups["mu"]),
        "u": twice_high(groups["mu"]),
        "v": twice_low(groups["vw"]),
        "w": twice_high(groups["vw"]),
        "sx": twice_low(groups["sk"]),
        "k": twice_high(groups["sk"]),
    }


def third_of(x, base):
    east, west = pltpu.roll(x, (2 * LANES - 4 - base) % LANES, 1), pltpu.roll(x, (2 * LANES - 10 - base) % LANES, 1)
    return jnp.where(lane_of() < 64, east, west)


def third_tile(groups, base):
    return split_groups({n: third_of(groups[n], base) for n in GROUPS})


def plus(tiles):
    last = lane_of() == LANES - 1
    turned = [pltpu.roll(t, LANES - 1, 1) for t in tiles]
    if len(tiles) == 1:
        return turned
    return [jnp.where(last, turned[(i + 1) % len(tiles)], turned[i]) for i in range(len(tiles))]


def minus(tiles, count=3, west=None):
    first = lane_of() == 0
    turned = [pltpu.roll(t, 1, 1) for t in tiles]
    if len(tiles) == 1:
        return turned
    before = [turned[-1] if west is None else west] + turned[:-1]
    return [jnp.where(first, before[i], turned[i]) for i in range(min(count, len(tiles)))]


def each(function, *lists):
    return [function(*values) for values in zip(*lists)]


def below(x):
    return pltpu.roll(x, 7, 0)


def above(x):
    return pltpu.roll(x, 1, 0)


def median(step, upwind):
    return jnp.minimum(jnp.maximum(upwind, jnp.minimum(step, 0.0)), jnp.maximum(step, 0.0))


def face_flux(here, there, speed, back, step, ahead):
    positive = speed >= 0.0
    upwind = jnp.where(positive, back, ahead)
    size = jnp.abs(speed)
    return speed * jnp.where(positive, here, there) + (size - size * size) * median(step, upwind)


def zonal_flux(c, m, half, u):
    east = plus(c)
    opened = each(jnp.multiply, half, plus(m))
    speed = each(face_speed, u, plus(u), opened)
    step = each(lambda a, b, o: (b - a) * o, c, east, opened)
    return each(face_flux, c, east, speed, minus(step), step, plus(step))


def vertical_divergence(value, half, down):
    opened = open_below(half)
    under = below(value)
    step = (under - value) * opened
    flux = face_flux(value, under, face_speed(down, below(down), opened), above(step), step, below(step))
    return flux - above(flux)


def not_bottom():
    return lax.broadcasted_iota(jnp.int32, (8, LANES), 0) % 4 != 3


def open_below(marker):
    return jnp.where(not_bottom(), below(marker), 0.0)


def face_speed(one, two, half_open):
    return (one + two) * half_open


def advect_rows(get, first, count, known=()):
    known = dict(known)
    low, high = (-1 if -2 in known else -2), (count + 1 if count in known else count + 2)
    c = {j: get("c", first + j) for j in range(low, high)}
    m = {j: get("m", first + j) for j in range(low, high)}
    v = {j: get("v", first + j) for j in range(-1, count + 1)}
    half = {j: each(lambda x: 0.5 * x, m[j]) for j in range(low, high)}
    opened = {j: each(jnp.multiply, half[j], m[j + 1]) for j in range(low, high - 1)}
    step = {j: each(lambda a, b, o: (b - a) * o, c[j], c[j + 1], opened[j]) for j in range(low, high - 1)}
    step.update(known)
    flux = {}
    for j in range(-1, count):
        speed = each(face_speed, v[j], v[j + 1], opened[j])
        flux[j] = each(face_flux, c[j], c[j + 1], speed, step[j - 1], step[j], step[j + 1])
    result = []
    for j in range(count):
        flux_x = zonal_flux(c[j], m[j], half[j], get("u", first + j))
        total = each(lambda f, g, a, b: (f - g) + (a - b), flux_x, minus(flux_x), flux[j], flux[j - 1])
        down = each(vertical_divergence, c[j], half[j], get("w", first + j))
        result.append(each(lambda a, x, z, o: (a - x - z) * o, c[j], total, down, m[j]))
    return result, flux, step


def slope_flux(k1, k2, opened, step, s1, s2, z1, z2):
    return (k1 + k2) * opened * (step + (s1 + s2) * (z1 + z2))


def eastward(a, m, k, sx, twice_z):
    opened = each(jnp.multiply, m, plus(m))
    step = each(lambda x, y, o: (y - x) * o, a, plus(a), opened)
    return step, each(slope_flux, k, plus(k), opened, step, sx, plus(sx), twice_z, plus(twice_z))


def diffuse_rows(get, first, count, beside=None):
    a = {j: get("a", first + j) for j in range(-1, count + 1)}
    m = {j: get("m", first + j) for j in range(-1, count + 1)}
    k = {j: get("k", first + j) for j in range(-1, count + 1)}
    sy = {j: get("sy", first + j) for j in range(-1, count + 1)}
    step_z, twice_z = {}, {}
    for j in range(-1, count + 1):
        wide = 3 if 0 <= j < count else 2
        step_z[j] = each(lambda x, o: (below(x) - x) * open_below(o), a[j][:wide], m[j])
        twice_z[j] = each(lambda x: above(x) + x, step_z[j])
    step_y, flux_y = {}, {}
    for j in range(-1, count):
        opened = each(jnp.multiply, m[j][:2], m[j + 1][:2])
        step_y[j] = each(lambda x, y, o: (y - x) * o, a[j][:2], a[j + 1][:2], opened)
        flux_y[j] = each(
            slope_flux, k[j], k[j + 1], opened, step_y[j], sy[j], sy[j + 1], twice_z[j], twice_z[j + 1]
        )
    result = []
    last = lane_of() == LANES - 1
    for j in range(count):
        sx = get("sx", first + j)
        step_x, flux_x = eastward(a[j], m[j], k[j], sx, twice_z[j])
        west = [None, None]
        if beside:
            east, west = beside(first + j)
            step_x = [step_x[0], jnp.where(last, east[0], step_x[1])]
            flux_x = [flux_x[0], jnp.where(last, east[1], flux_x[1])]
        twice_x = each(jnp.add, step_x, minus(step_x, 2, west[0]))
        twice_y = each(jnp.add, step_y[j - 1], step_y[j])
        total = each(lambda f, g, p, q: (f - g) + (p - q), flux_x, minus(flux_x, 2, west[1]), flux_y[j], flux_y[j - 1])

        def finish(value, marker, kappa, east, north, tx, ty, sz, across):
            face_east, face_north = east + below(east), north + below(north)
            flux_z = (kappa + below(kappa)) * open_below(marker) * (
                face_east * (tx + below(tx)) + face_north * (ty + below(ty))
                + (face_east * face_east + face_north * face_north) * (16.0 * sz)
            )
            return (value + across + (flux_z - above(flux_z))) * marker

        result.append(each(finish, a[j][:2], m[j], k[j], sx, sy[j], twice_x, twice_y, step_z[j], total))
    return result


def tiles_of(ref, row, count):
    return [ref[row, :, t * LANES : (t + 1) * LANES] for t in range(count)]


def interior_kernel(*refs):
    rows, advected, sources = refs[:5], refs[5], refs[6:10]
    out, kept, strips, narrow = refs[10:]
    lane = lane_of()
    near_east, near_west = lane >= LANES - 2, lane < 2

    full = []
    for g in range(8):
        groups = {n: strip_at(g, i // 2, i % 2, *sources) for i, n in enumerate(GROUPS)}
        full.append(split_groups(groups))
        for i, n in enumerate(GROUPS):
            strips[i, g] = groups[n]

    def get_strip(name, g):
        x = full[g % 8][name]
        return [x if 0 <= g < 8 else pltpu.roll(x, 16 if g < 0 else LANES - 16, 1)]

    for g, (a,) in enumerate(advect_rows(get_strip, 0, 8)[0]):
        part = full[g]
        step_z = (below(a) - a) * open_below(part["m"])
        step, flux = eastward([a], [part["m"]], [part["k"]], [part["sx"]], [above(step_z) + step_z])
        narrow[0, g], narrow[1, g], narrow[2, g] = a, step[0], flux[0]

    def lanes_to(which, row, lane_from, lane_to):
        part = row // 8
        return pltpu.roll(narrow[which, row - 8 * part], lax.rem(2 * LANES + lane_to - lane_from - 16 * part, LANES), 1)

    def get(name, row):
        if name != "a":
            return field_tiles(rows, name, row)
        left, right = tiles_of(advected, row, 2)
        return [
            jnp.where(near_west, lanes_to(0, row, 10, 0), left),
            jnp.where(near_east, lanes_to(0, row, 3, LANES - 1), right),
        ]

    def beside(row):
        return [lanes_to(i, row, 3, LANES - 1) for i in (1, 2)], [lanes_to(i, row, 9, 0) for i in (1, 2)]

    for i, row in enumerate(KEPT):
        third = jnp.where(lane < 64, lanes_to(0, row, 4, 0), lanes_to(0, row, 9, LANES - 1))
        for t, tile in enumerate(get("a", row) + [third]):
            kept[i, :, t * LANES : (t + 1) * LANES] = tile

    def diffuse_block(block, carry):
        first = jnp.minimum(3 + 10 * block, ROWS - 3 - 10)
        for j, tiles in enumerate(diffuse_rows(get, first, 10, beside)):
            for t in range(2):
                out[first + j, :, t * LANES : (t + 1) * LANES] = tiles[t]
        return carry

    lax.fori_loop(0, 6, diffuse_block, 0)


def rim_kernel(*refs):
    got_a, got_b = refs[0], refs[1]
    fields = refs[2:7]
    strips, inner, kept, out, edges, sems = refs[7:]
    middle = pltpu.make_async_copy
    copies = [middle(inner.at[8:56, i], out.at[i, 8:56], sems.at[i]) for i in range(8)]
    for copy in copies:
        copy.start()
    low = low_of()
    lat = lax.axis_index("lat")
    even = jnp.broadcast_to(lat % 2, (8, LANES)) == 0
    floor = jnp.broadcast_to(lat, (8, LANES)) == 0

    def halo(is_north):
        def tile(i, h):
            a = got_a[i, :, h * LANES : (h + 1) * LANES]
            b = got_b[i, :, h * LANES : (h + 1) * LANES]
            if is_north:
                return jnp.where(even, a, b)
            return jnp.where(floor, 0.0, jnp.where(even, b, a))

        tiles = [[tile(i, h) for h in range(2)] for i in range(6)]
        corner = jnp.where(low, pltpu.roll(tiles[5][0], 4, 0), tiles[5][1])
        c_side, step_side, mv = [third_of(corner, 16 * i) for i in range(3)]
        row = {
            "c": tiles[2] + [c_side],
            "m": each(twice_low, tiles[3]) + [twice_low(mv)],
            "v": each(twice_low, tiles[4]) + [twice_high(mv)],
            "sy": each(twice_high, tiles[4]),
            "k": each(twice_low, tiles[5]),
        }
        return row, tiles[0], tiles[1] + [step_side], each(twice_high, tiles[3])

    for is_north in (False, True):
        outer, cell, step_in, rest = halo(is_north)
        start, beyond = (ROWS - 2, ROWS) if is_north else (0, -1)
        made, sides = {}, {}
        for row in range(*((ROWS - 4, ROWS) if is_north else (0, 4))):
            base = 16 * (row // 8)
            sides[row] = third_tile({n: strips[i, row % 8] for i, n in enumerate(GROUPS)}, base)

        def get(name, row):
            if name == "a":
                return made[row] if row in made else tiles_of(kept, KEPT.index(row), 3)
            if row == beyond:
                return outer[name]
            tiles = field_tiles(fields, name, row)
            return tiles if name == "sy" else tiles + [sides[row][name]]

        known = {2: [-x for x in step_in]} if is_north else {-2: step_in}
        results, flux, step = advect_rows(get, start, 2, known)
        made.update(zip((start, start + 1), results))
        face, sign = (1, -1.0) if is_north else (-1, 1.0)
        made[beyond] = each(
            lambda q, g, s, t, f, o: (q + g * median(s, sign * t) - sign * f) * o,
            cell, rest, step_in, step[face], flux[face], outer["m"],
        )
        final = ROWS - 3 if is_north else 0
        base = ROWS - 8 if is_north else 0
        done = {final + j: x for j, x in enumerate(diffuse_rows(get, final, 3))}
        for h in range(2):
            stack = [done[j][h] if j in done else inner[j, :, h * LANES : (h + 1) * LANES] for j in range(base, base + 8)]
            edges[int(is_north), :, :, h * LANES : (h + 1) * LANES] = jnp.transpose(jnp.stack(stack), (1, 0, 2))
        copy = middle(edges.at[int(is_north)], out.at[:, base : base + 8], sems.at[8 + int(is_north)])
        copy.start()
        copies.append(copy)
    for copy in copies:
        copy.wait()


def call(kernel, shapes, *operands, **options):
    return pl.pallas_call(
        kernel,
        out_shape=[jax.ShapeDtypeStruct(s, F32) for s in shapes],
        in_specs=[VMEM] * len(operands),
        out_specs=[VMEM] * len(shapes),
        compiler_params=pltpu.CompilerParams(vmem_limit_bytes=LIMIT),
        **options,
    )(*operands)


def make(lons, lats):
    def spot(lon, lat):
        return (lon % lons) * lats + lat

    near = [(spot(i, j), spot(i ^ 1, j)) for i in range(lons) for j in range(lats)]
    far = [(spot(i, j), spot(i + 1 if i % 2 else i - 1, j)) for i in range(lons) for j in range(lats)]
    pair_a = [(spot(i, j), spot(i, j ^ 1)) for i in range(lons) for j in range(lats)]
    pair_b = []
    for i in range(lons):
        for j in range(lats):
            if j == 0:
                pair_b.append((spot(i, j), spot(i ^ 1, j)))
            elif j == lats - 1:
                pair_b.append((spot(i, j), spot(lons - 1 - i, j)))
            else:
                pair_b.append((spot(i, j), spot(i, j + 1 if j % 2 else j - 1)))

    def move(x, route):
        return lax.ppermute(x, ("lon", "lat"), route)

    def shards(tracers, velocity, slopes, diffusivity, sea_mask):
        plane = lambda x: x.reshape(-1, ROWS, 2 * LANES)
        arrays = [plane(tracers), plane(velocity), plane(slopes), diffusivity, sea_mask]
        arrays = [pltpu.with_memory_space_constraint(x, pltpu.HBM) for x in arrays]
        full, side = (ROWS, 8, 2 * LANES), (8, 8, LANES)
        *held, to_near, to_far, own, spare = pl.pallas_call(
            pack_kernel,
            out_shape=[jax.ShapeDtypeStruct(x.shape, x.dtype) for x in arrays]
            + [jax.ShapeDtypeStruct(shape, F32) for shape in [(4, 8, LANES)] * 2 + [side] * 2],
            in_specs=[pl.BlockSpec(memory_space=pltpu.HBM)] * 5,
            out_specs=[VMEM] * 9,
            scratch_shapes=[pltpu.SemaphoreType.DMA((CHUNKS, 5))],
            compiler_params=pltpu.CompilerParams(vmem_limit_bytes=LIMIT),
        )(*arrays)
        far_got, near_got = move(to_far, far), move(to_near, near)
        *rows, advected, made_a, made_b = call(
            advect_kernel, [full] * 6 + [(6, 8, 2 * LANES)] * 2, *held,
            cost_estimate=pl.CostEstimate(flops=10**7, bytes_accessed=6 * 10**6, transcendentals=0),
        )
        send_a, send_b = call(
            edge_kernel, [(6, 8, 2 * LANES)] * 2, far_got, near_got, own, spare, made_a, made_b,
            input_output_aliases={4: 0, 5: 1},
        )
        got_a, got_b = move(send_a, pair_a), move(send_b, pair_b)
        inner, kept, strips = call(
            interior_kernel, [full, (4, 8, 3 * LANES), (4,) + side], *rows, advected, far_got, near_got, own, spare,
            scratch_shapes=[pltpu.VMEM((3,) + side, F32)],
            cost_estimate=pl.CostEstimate(flops=2 * 10**7, bytes_accessed=10**7, transcendentals=0),
        )
        out = pl.pallas_call(
            rim_kernel,
            out_shape=jax.ShapeDtypeStruct((8, ROWS, 2 * LANES), F32),
            in_specs=[VMEM] * 10,
            out_specs=pl.BlockSpec(memory_space=pl.ANY),
            scratch_shapes=[pltpu.VMEM((2, 8, 8, 2 * LANES), F32), pltpu.SemaphoreType.DMA((10,))],
            compiler_params=pltpu.CompilerParams(vmem_limit_bytes=LIMIT),
        )(got_a, got_b, *rows, strips, inner, kept)
        return out.reshape(tracers.shape)

    return shards


def solution(mesh):
    return jax.shard_map(
        make(mesh.shape["lon"], mesh.shape["lat"]),
        mesh=mesh,
        in_specs=(
            P(None, None, "lat", "lon"),
            P(None, None, "lat", "lon"),
            P(None, None, "lat", "lon"),
            P(None, "lat", "lon"),
            P(None, "lat", "lon"),
        ),
        out_specs=P(None, None, "lat", "lon"),
        check_vma=False,
    )
```

```python
import jax
import jax.numpy as jnp
from jax import lax
from jax.experimental import pallas as pl
from jax.experimental.pallas import tpu as pltpu
from jax.sharding import PartitionSpec as P


ROWS = 64
LANES = 128
F32 = jnp.float32
VMEM = pl.BlockSpec(memory_space=pltpu.VMEM)
LIMIT = 16 * 1024 * 1024
CHUNKS = 2
GROUPS = ("c", "mu", "vw", "sk")
KEPT = (2, 3, ROWS - 4, ROWS - 3)


def lane_of():
    return lax.broadcasted_iota(jnp.int32, (8, LANES), 1)


def low_of():
    return lax.broadcasted_iota(jnp.int32, (8, LANES), 0) < 4


def twice_low(x):
    return jnp.where(low_of(), x, pltpu.roll(x, 4, 0))


def twice_high(x):
    return jnp.where(low_of(), pltpu.roll(x, 4, 0), x)


def field_half(rows, name, row, h):
    which, turn = {
        "u": (1, twice_low), "v": (1, twice_high), "w": (2, twice_high),
        "sx": (3, twice_low), "sy": (3, twice_high), "m": (4, twice_low), "k": (4, twice_high),
    }.get(name, (0, None))
    value = rows[which][row, :, h * LANES : (h + 1) * LANES]
    return turn(value) if turn else value


def field_tiles(rows, name, row):
    return [field_half(rows, name, row, h) for h in range(2)]


def row_planes(held, span, h, both=True):
    tracer, velocity, slope, kappa, mask = held
    wide = slice(h * LANES, (h + 1) * LANES)
    return [
        tracer[:, span, wide], velocity[0:8, span, wide], velocity[4:12, span, wide],
        slope[:, span, wide] if both else jnp.concatenate([slope[0:4, span, wide]] * 2, axis=0),
        jnp.concatenate([mask[:, span, wide].astype(F32), kappa[:, span, wide]], axis=0),
    ]


def scaled(groups):
    c, uv, vw, s, mk = groups
    return c, uv, vw, s * 0.125, mk * jnp.where(low_of(), 1.0, 0.5)


def pack_kernel(*refs):
    arrays, held, (to_near, to_far, own, spare), sems = refs[:5], refs[5:10], refs[10:14], refs[14]
    copies = []
    for chunk in range(CHUNKS):
        span = slice(chunk * ROWS // CHUNKS, (chunk + 1) * ROWS // CHUNKS)
        ends = [array.shape[0] for array in arrays]
        ends[2] = 4
        copies.append(
            [
                pltpu.make_async_copy(array.at[:end, span], hold.at[:end, span], sems.at[chunk, i])
                for i, (array, hold, end) in enumerate(zip(arrays, held, ends))
            ]
        )
        for copy in copies[-1]:
            copy.start()
    northward = pltpu.make_async_copy(arrays[2].at[4:], held[2].at[4:], sems.at[0, 5])
    northward.start()
    lane, low = lane_of(), low_of()
    inside = lax.broadcasted_iota(jnp.int32, (8, 8, LANES), 2) < 64
    first, second = [None] * 8, [None] * 8
    for part in range(8):
        if part * CHUNKS % 8 == 0:
            for copy in copies[part * CHUNKS // 8]:
                copy.wait()
        span = slice(8 * part, 8 * part + 8)
        rims = []
        for left, right in zip(*[row_planes(held, span, h, False) for h in range(2)]):
            rims.append(jnp.transpose(jnp.where(inside, left, right), (1, 0, 2)))
        base = 16 * part
        before, half = lane < base, lane < base + 8
        for g in range(8):
            c, uv, vw, s, mk = scaled([x[g] for x in rims])
            mu = jnp.where(low, mk, pltpu.roll(uv, 4, 0))
            sk = jnp.where(low, s, mk)
            one = jnp.where(half, pltpu.roll(c, (base + 4) % LANES, 1), pltpu.roll(mu, (base + 12) % LANES, 1))
            two = jnp.where(half, pltpu.roll(vw, (base + 4) % LANES, 1), pltpu.roll(sk, (base + 12) % LANES, 1))
            first[g] = jnp.where(before, first[g], one) if part else one
            second[g] = jnp.where(before, second[g], two) if part else two
    for g in range(8):
        own[g] = first[g]
        spare[g] = second[g]
    slot = lane % 8
    to_east = jnp.broadcast_to(lax.axis_index("lon") % 2, (8, LANES)) == 0
    for pair in range(4):
        east, west = [], []
        for g in (2 * pair, 2 * pair + 1):
            east.append(jnp.where(slot == 0, pltpu.roll(second[g], LANES - 3, 1), first[g]))
            west.append(jnp.where(slot == 7, pltpu.roll(second[g], 3, 1), first[g]))
        eastern = jnp.where(slot < 4, east[0], pltpu.roll(east[1], 4, 1))
        western = jnp.where(slot < 4, pltpu.roll(west[0], LANES - 4, 1), west[1])
        to_near[pair] = jnp.where(to_east, eastern, western)
        to_far[pair] = jnp.where(to_east, western, eastern)
    northward.wait()


def advect_kernel(*refs):
    held, rows, advected, send_a, send_b = refs[:5], refs[5:10], refs[10], refs[11], refs[12]
    for part in range(8):
        for h in range(2):
            turned = [jnp.transpose(x, (1, 0, 2)) for x in row_planes(held, slice(8 * part, 8 * part + 8), h)]
            for g in range(8):
                for ref, value in zip(rows, scaled([x[g] for x in turned])):
                    ref[8 * part + g, :, h * LANES : (h + 1) * LANES] = value
    put_messages(rows, send_a, send_b)
    get = lambda name, row: field_tiles(rows, name, row)

    def advect_block(block, carry):
        first = 2 + 15 * block
        for j, tiles in enumerate(advect_rows(get, first, 15)[0]):
            for t in range(2):
                advected[first + j, :, t * LANES : (t + 1) * LANES] = tiles[t]
        return carry

    lax.fori_loop(0, 4, advect_block, 0)


def put_messages(rows, send_a, send_b):
    lane, low = lane_of(), low_of()
    lat = lax.axis_index("lat")

    first, last = lane < 2, lane >= LANES - 2

    def message(top):
        part = lambda name, q: field_tiles(rows, name, ROWS - 1 - q if top else q)
        outward = 1.0 if top else -1.0
        c, m, v = [part("c", q) for q in range(3)], [part("m", q) for q in range(3)], [part("v", q) for q in range(2)]
        half = each(lambda x: 0.5 * x, m[1])
        opened = each(jnp.multiply, half, m[0])
        step = each(lambda a, b, o: (a - b) * o, c[0], c[1], opened)
        inner = each(lambda a, b, x, y: (a - b) * (x * y), c[1], c[2], half, m[2])
        speed = each(lambda a, b, o: (a + b) * o * outward, v[0], v[1], opened)
        inflow = each(
            lambda a, b, s, x, y: s * jnp.where(s >= 0.0, a, b)
            + jnp.where(s >= 0.0, (jnp.abs(s) - s * s) * median(x, y), 0.0),
            c[1], c[0], speed, step, inner,
        )
        rest = each(lambda s: jnp.where(s >= 0.0, 0.0, jnp.abs(s) - s * s), speed)
        halved = each(lambda x: 0.5 * x, m[0])
        flux_x = zonal_flux(c[0], m[0], halved, part("u", 0))
        across = each(lambda f, g: f - g, flux_x, minus(flux_x))
        across = [jnp.where(first, 0.0, across[0]), jnp.where(last, 0.0, across[1])]
        down = each(vertical_divergence, c[0], halved, part("w", 0))
        cell = each(lambda a, x, z, f: a - x - z + f, c[0], across, down, inflow)
        pair = lambda a, b: each(lambda x, y: jnp.where(low, x, y), a, b)
        return [cell, step, c[0], pair(m[0], rest), pair(v[0], part("sy", 0)), part("k", 0)]

    backward = LANES - 1 - lane
    flip = lambda x: jnp.take_along_axis(x, backward, axis=1, mode="promise_in_bounds")
    is_even = jnp.broadcast_to(lat % 2, (8, LANES)) == 0
    folds = jnp.broadcast_to(lat, (8, LANES)) == lax.axis_size("lat") - 1
    north, south = message(True), message(False)
    for i, (top, bottom) in enumerate(zip(north, south)):
        for h in range(2):
            wide = slice(h * LANES, (h + 1) * LANES)
            turned = flip(top[1 - h])
            if i == 4:
                turned = -turned
            send_a[i, :, wide] = jnp.where(is_even, top[h], bottom[h])
            send_b[i, :, wide] = jnp.where(folds, turned, jnp.where(is_even, bottom[h], top[h]))


def strip_at(g, which, late, from_far, from_near, own, spare):
    slot = lane_of() % 16
    far_is_west = jnp.broadcast_to(lax.axis_index("lon") % 2, (8, LANES)) == 0
    near, far, mine = from_near[g // 2], from_far[g // 2], (spare if which else own)[g]
    east, west = jnp.where(far_is_west, near, far), jnp.where(far_is_west, far, near)
    shift = lambda x, by: pltpu.roll(x, by % LANES, 1) if by else x
    odd = 4 * (g % 2)
    east = shift(east, (1 if which else 4) - odd - 8 * late)
    west = shift(west, (9 if which else 6) - odd - 8 * late)
    inner = jnp.where(slot < 4, shift(mine, -8 * late), east)
    outer = jnp.where(slot < 10, west, shift(mine, 6 - 8 * late))
    return jnp.where(slot < 7, inner, outer)


def edge_kernel(*refs):
    sources, made, (send_a, send_b) = refs[:4], refs[4:6], refs[6:]
    lane, low = lane_of(), low_of()
    lat = lax.axis_index("lat")
    strip = lambda i, g: strip_at(g, i // 2, i % 2, *sources)

    def beside(g, inner):
        c, mu, vw = strip(0, g), strip(1, g), strip(2, g)
        shifts = (1, 0, LANES - 1, LANES - 2)
        moved = lambda x: [pltpu.roll(x, by, 1) if by else x for by in shifts]
        cells, pairs = moved(c), moved(mu)
        m = [twice_low(x) for x in pairs]
        half = [0.5 * x for x in m]
        steps = [(cells[n + 1] - cells[n]) * (half[n] * m[n + 1]) for n in range(3)]
        speed = face_speed(twice_high(pairs[1]), twice_high(pairs[2]), half[1] * m[2])
        flux = face_flux(cells[1], cells[2], speed, *steps)
        step = (c - strip(0, inner)) * (half[1] * twice_low(strip(1, inner)))
        return flux, c, step, jnp.where(low, mu, pltpu.roll(vw, 4, 0))

    def placed(values, base, backward):
        if backward:
            take = lambda x, at: jnp.take_along_axis(x, (base + at + LANES - lane) & (LANES - 1), axis=1, mode="promise_in_bounds")
            places = [(3, 2), (9, 8), 13, 29, 45]
        else:
            take = lambda x, at: pltpu.roll(x, (at - base) % LANES, 1) if (at - base) % LANES else x
            places = [(118, 119), (124, 125), 0, 16, 32]
        across = [take(values[0], at) - take(values[0], before) for at, before in places[:2]]
        c, step, mv = [take(x, at) for x, at in zip(values[1:], places[2:])]
        if backward:
            mv = jnp.where(low, mv, -mv)
        return across + [jnp.where(lane < 16, c, jnp.where(lane < 32, step, mv))]

    south, north = beside(0, 1), beside(7, 6)
    south, north, turned = placed(south, 0, False), placed(north, 112, False), placed(north, 112, True)

    def store(source, ref, left, right, packed):
        ref[0, :, :LANES] = source[0, :, :LANES] - jnp.where(lane < 2, left, 0.0)
        ref[0, :, LANES:] = source[0, :, LANES:] - jnp.where(lane >= LANES - 2, right, 0.0)
        ref[5, :, :LANES] = jnp.where(low, source[5, :, :LANES], pltpu.roll(packed, 4, 0))
        ref[5, :, LANES:] = jnp.where(low, source[5, :, LANES:], packed)

    is_even = jnp.broadcast_to(lat % 2, (8, LANES)) == 0
    folds = jnp.broadcast_to(lat, (8, LANES)) == lax.axis_size("lat") - 1
    store(made[0], send_a, *[jnp.where(is_even, n, s) for n, s in zip(north, south)])
    store(made[1], send_b, *[jnp.where(folds, t, jnp.where(is_even, s, n)) for n, s, t in zip(north, south, turned)])


def split_groups(groups):
    return {
        "c": groups["c"],
        "m": twice_low(groups["mu"]),
        "u": twice_high(groups["mu"]),
        "v": twice_low(groups["vw"]),
        "w": twice_high(groups["vw"]),
        "sx": twice_low(groups["sk"]),
        "k": twice_high(groups["sk"]),
    }


def third_of(x, base):
    east, west = pltpu.roll(x, (2 * LANES - 4 - base) % LANES, 1), pltpu.roll(x, (2 * LANES - 10 - base) % LANES, 1)
    return jnp.where(lane_of() < 64, east, west)


def third_tile(groups, base):
    return split_groups({n: third_of(groups[n], base) for n in GROUPS})


def plus(tiles):
    last = lane_of() == LANES - 1
    turned = [pltpu.roll(t, LANES - 1, 1) for t in tiles]
    if len(tiles) == 1:
        return turned
    return [jnp.where(last, turned[(i + 1) % len(tiles)], turned[i]) for i in range(len(tiles))]


def minus(tiles, count=3, west=None):
    first = lane_of() == 0
    turned = [pltpu.roll(t, 1, 1) for t in tiles]
    if len(tiles) == 1:
        return turned
    before = [turned[-1] if west is None else west] + turned[:-1]
    return [jnp.where(first, before[i], turned[i]) for i in range(min(count, len(tiles)))]


def each(function, *lists):
    return [function(*values) for values in zip(*lists)]


def below(x):
    return pltpu.roll(x, 7, 0)


def above(x):
    return pltpu.roll(x, 1, 0)


def median(step, upwind):
    return jnp.minimum(jnp.maximum(upwind, jnp.minimum(step, 0.0)), jnp.maximum(step, 0.0))


def face_flux(here, there, speed, back, step, ahead):
    positive = speed >= 0.0
    upwind = jnp.where(positive, back, ahead)
    size = jnp.abs(speed)
    return speed * jnp.where(positive, here, there) + (size - size * size) * median(step, upwind)


def zonal_flux(c, m, half, u):
    east = plus(c)
    opened = each(jnp.multiply, half, plus(m))
    speed = each(face_speed, u, plus(u), opened)
    step = each(lambda a, b, o: (b - a) * o, c, east, opened)
    return each(face_flux, c, east, speed, minus(step), step, plus(step))


def vertical_divergence(value, half, down):
    opened = open_below(half)
    under = below(value)
    step = (under - value) * opened
    flux = face_flux(value, under, face_speed(down, below(down), opened), above(step), step, below(step))
    return flux - above(flux)


def not_bottom():
    return lax.broadcasted_iota(jnp.int32, (8, LANES), 0) % 4 != 3


def open_below(marker):
    return jnp.where(not_bottom(), below(marker), 0.0)


def face_speed(one, two, half_open):
    return (one + two) * half_open


def advect_rows(get, first, count, known=()):
    known = dict(known)
    low, high = (-1 if -2 in known else -2), (count + 1 if count in known else count + 2)
    c = {j: get("c", first + j) for j in range(low, high)}
    m = {j: get("m", first + j) for j in range(low, high)}
    v = {j: get("v", first + j) for j in range(-1, count + 1)}
    half = {j: each(lambda x: 0.5 * x, m[j]) for j in range(low, high)}
    opened = {j: each(jnp.multiply, half[j], m[j + 1]) for j in range(low, high - 1)}
    step = {j: each(lambda a, b, o: (b - a) * o, c[j], c[j + 1], opened[j]) for j in range(low, high - 1)}
    step.update(known)
    flux = {}
    for j in range(-1, count):
        speed = each(face_speed, v[j], v[j + 1], opened[j])
        flux[j] = each(face_flux, c[j], c[j + 1], speed, step[j - 1], step[j], step[j + 1])
    result = []
    for j in range(count):
        flux_x = zonal_flux(c[j], m[j], half[j], get("u", first + j))
        total = each(lambda f, g, a, b: (f - g) + (a - b), flux_x, minus(flux_x), flux[j], flux[j - 1])
        down = each(vertical_divergence, c[j], half[j], get("w", first + j))
        result.append(each(lambda a, x, z, o: (a - x - z) * o, c[j], total, down, m[j]))
    return result, flux, step


def slope_flux(k1, k2, opened, step, s1, s2, z1, z2):
    return (k1 + k2) * opened * (step + (s1 + s2) * (z1 + z2))


def eastward(a, m, k, sx, twice_z):
    opened = each(jnp.multiply, m, plus(m))
    step = each(lambda x, y, o: (y - x) * o, a, plus(a), opened)
    return step, each(slope_flux, k, plus(k), opened, step, sx, plus(sx), twice_z, plus(twice_z))


def diffuse_rows(get, first, count, beside=None):
    a = {j: get("a", first + j) for j in range(-1, count + 1)}
    m = {j: get("m", first + j) for j in range(-1, count + 1)}
    k = {j: get("k", first + j) for j in range(-1, count + 1)}
    sy = {j: get("sy", first + j) for j in range(-1, count + 1)}
    step_z, twice_z = {}, {}
    for j in range(-1, count + 1):
        wide = 3 if 0 <= j < count else 2
        step_z[j] = each(lambda x, o: (below(x) - x) * open_below(o), a[j][:wide], m[j])
        twice_z[j] = each(lambda x: above(x) + x, step_z[j])
    step_y, flux_y = {}, {}
    for j in range(-1, count):
        opened = each(jnp.multiply, m[j][:2], m[j + 1][:2])
        step_y[j] = each(lambda x, y, o: (y - x) * o, a[j][:2], a[j + 1][:2], opened)
        flux_y[j] = each(
            slope_flux, k[j], k[j + 1], opened, step_y[j], sy[j], sy[j + 1], twice_z[j], twice_z[j + 1]
        )
    result = []
    last = lane_of() == LANES - 1
    for j in range(count):
        sx = get("sx", first + j)
        step_x, flux_x = eastward(a[j], m[j], k[j], sx, twice_z[j])
        west = [None, None]
        if beside:
            east, west = beside(first + j)
            step_x = [step_x[0], jnp.where(last, east[0], step_x[1])]
            flux_x = [flux_x[0], jnp.where(last, east[1], flux_x[1])]
        twice_x = each(jnp.add, step_x, minus(step_x, 2, west[0]))
        twice_y = each(jnp.add, step_y[j - 1], step_y[j])
        total = each(lambda f, g, p, q: (f - g) + (p - q), flux_x, minus(flux_x, 2, west[1]), flux_y[j], flux_y[j - 1])

        def finish(value, marker, kappa, east, north, tx, ty, sz, across):
            face_east, face_north = east + below(east), north + below(north)
            flux_z = (kappa + below(kappa)) * open_below(marker) * (
                face_east * (tx + below(tx)) + face_north * (ty + below(ty))
                + (face_east * face_east + face_north * face_north) * (16.0 * sz)
            )
            return (value + across + (flux_z - above(flux_z))) * marker

        result.append(each(finish, a[j][:2], m[j], k[j], sx, sy[j], twice_x, twice_y, step_z[j], total))
    return result


def tiles_of(ref, row, count):
    return [ref[row, :, t * LANES : (t + 1) * LANES] for t in range(count)]


def interior_kernel(*refs):
    rows, advected, sources = refs[:5], refs[5], refs[6:10]
    out, kept, strips, narrow = refs[10:]
    lane = lane_of()
    near_east, near_west = lane >= LANES - 2, lane < 2

    full = []
    for g in range(8):
        groups = {n: strip_at(g, i // 2, i % 2, *sources) for i, n in enumerate(GROUPS)}
        full.append(split_groups(groups))
        for i, n in enumerate(GROUPS):
            strips[i, g] = groups[n]

    def get_strip(name, g):
        x = full[g % 8][name]
        return [x if 0 <= g < 8 else pltpu.roll(x, 16 if g < 0 else LANES - 16, 1)]

    for g, (a,) in enumerate(advect_rows(get_strip, 0, 8)[0]):
        part = full[g]
        step_z = (below(a) - a) * open_below(part["m"])
        step, flux = eastward([a], [part["m"]], [part["k"]], [part["sx"]], [above(step_z) + step_z])
        narrow[0, g], narrow[1, g], narrow[2, g] = a, step[0], flux[0]

    def lanes_to(which, row, lane_from, lane_to):
        part = row // 8
        return pltpu.roll(narrow[which, row - 8 * part], lax.rem(2 * LANES + lane_to - lane_from - 16 * part, LANES), 1)

    def get(name, row):
        if name != "a":
            return field_tiles(rows, name, row)
        left, right = tiles_of(advected, row, 2)
        return [
            jnp.where(near_west, lanes_to(0, row, 10, 0), left),
            jnp.where(near_east, lanes_to(0, row, 3, LANES - 1), right),
        ]

    def beside(row):
        return [lanes_to(i, row, 3, LANES - 1) for i in (1, 2)], [lanes_to(i, row, 9, 0) for i in (1, 2)]

    for i, row in enumerate(KEPT):
        third = jnp.where(lane < 64, lanes_to(0, row, 4, 0), lanes_to(0, row, 9, LANES - 1))
        for t, tile in enumerate(get("a", row) + [third]):
            kept[i, :, t * LANES : (t + 1) * LANES] = tile

    def diffuse_block(block, carry):
        first = jnp.minimum(3 + 10 * block, ROWS - 3 - 10)
        for j, tiles in enumerate(diffuse_rows(get, first, 10, beside)):
            for t in range(2):
                out[first + j, :, t * LANES : (t + 1) * LANES] = tiles[t]
        return carry

    lax.fori_loop(0, 6, diffuse_block, 0)


def rim_kernel(*refs):
    got_a, got_b = refs[0], refs[1]
    fields = refs[2:7]
    strips, inner, kept, out, edges, sems = refs[7:]
    middle = pltpu.make_async_copy
    copies = [middle(inner.at[8:56, i], out.at[i, 8:56], sems.at[i]) for i in range(8)]
    for copy in copies:
        copy.start()
    low = low_of()
    lat = lax.axis_index("lat")
    even = jnp.broadcast_to(lat % 2, (8, LANES)) == 0
    floor = jnp.broadcast_to(lat, (8, LANES)) == 0

    def halo(is_north):
        def tile(i, h):
            a = got_a[i, :, h * LANES : (h + 1) * LANES]
            b = got_b[i, :, h * LANES : (h + 1) * LANES]
            if is_north:
                return jnp.where(even, a, b)
            return jnp.where(floor, 0.0, jnp.where(even, b, a))

        tiles = [[tile(i, h) for h in range(2)] for i in range(6)]
        corner = jnp.where(low, pltpu.roll(tiles[5][0], 4, 0), tiles[5][1])
        c_side, step_side, mv = [third_of(corner, 16 * i) for i in range(3)]
        row = {
            "c": tiles[2] + [c_side],
            "m": each(twice_low, tiles[3]) + [twice_low(mv)],
            "v": each(twice_low, tiles[4]) + [twice_high(mv)],
            "sy": each(twice_high, tiles[4]),
            "k": each(twice_low, tiles[5]),
        }
        return row, tiles[0], tiles[1] + [step_side], each(twice_high, tiles[3])

    for is_north in (False, True):
        outer, cell, step_in, rest = halo(is_north)
        start, beyond = (ROWS - 2, ROWS) if is_north else (0, -1)
        made, sides = {}, {}
        for row in range(*((ROWS - 4, ROWS) if is_north else (0, 4))):
            base = 16 * (row // 8)
            sides[row] = third_tile({n: strips[i, row % 8] for i, n in enumerate(GROUPS)}, base)

        def get(name, row):
            if name == "a":
                return made[row] if row in made else tiles_of(kept, KEPT.index(row), 3)
            if row == beyond:
                return outer[name]
            tiles = field_tiles(fields, name, row)
            return tiles if name == "sy" else tiles + [sides[row][name]]

        known = {2: [-x for x in step_in]} if is_north else {-2: step_in}
        results, flux, step = advect_rows(get, start, 2, known)
        made.update(zip((start, start + 1), results))
        face, sign = (1, -1.0) if is_north else (-1, 1.0)
        made[beyond] = each(
            lambda q, g, s, t, f, o: (q + g * median(s, sign * t) - sign * f) * o,
            cell, rest, step_in, step[face], flux[face], outer["m"],
        )
        final = ROWS - 3 if is_north else 0
        base = ROWS - 8 if is_north else 0
        done = {final + j: x for j, x in enumerate(diffuse_rows(get, final, 3))}
        for h in range(2):
            stack = [done[j][h] if j in done else inner[j, :, h * LANES : (h + 1) * LANES] for j in range(base, base + 8)]
            edges[int(is_north), :, :, h * LANES : (h + 1) * LANES] = jnp.transpose(jnp.stack(stack), (1, 0, 2))
        copy = middle(edges.at[int(is_north)], out.at[:, base : base + 8], sems.at[8 + int(is_north)])
        copy.start()
        copies.append(copy)
    for copy in copies:
        copy.wait()


def call(kernel, shapes, *operands, **options):
    return pl.pallas_call(
        kernel,
        out_shape=[jax.ShapeDtypeStruct(s, F32) for s in shapes],
        in_specs=[VMEM] * len(operands),
        out_specs=[VMEM] * len(shapes),
        compiler_params=pltpu.CompilerParams(vmem_limit_bytes=LIMIT),
        **options,
    )(*operands)


def make(lons, lats):
    def spot(lon, lat):
        return (lon % lons) * lats + lat

    near = [(spot(i, j), spot(i ^ 1, j)) for i in range(lons) for j in range(lats)]
    far = [(spot(i, j), spot(i + 1 if i % 2 else i - 1, j)) for i in range(lons) for j in range(lats)]
    pair_a = [(spot(i, j), spot(i, j ^ 1)) for i in range(lons) for j in range(lats)]
    pair_b = []
    for i in range(lons):
        for j in range(lats):
            if j == 0:
                pair_b.append((spot(i, j), spot(i ^ 1, j)))
            elif j == lats - 1:
                pair_b.append((spot(i, j), spot(lons - 1 - i, j)))
            else:
                pair_b.append((spot(i, j), spot(i, j + 1 if j % 2 else j - 1)))

    def move(x, route):
        return lax.ppermute(x, ("lon", "lat"), route)

    def shards(tracers, velocity, slopes, diffusivity, sea_mask):
        plane = lambda x: x.reshape(-1, ROWS, 2 * LANES)
        arrays = [plane(tracers), plane(velocity), plane(slopes), diffusivity, sea_mask]
        arrays = [pltpu.with_memory_space_constraint(x, pltpu.HBM) for x in arrays]
        full, side = (ROWS, 8, 2 * LANES), (8, 8, LANES)
        *held, to_near, to_far, own, spare = pl.pallas_call(
            pack_kernel,
            out_shape=[jax.ShapeDtypeStruct(x.shape, x.dtype) for x in arrays]
            + [jax.ShapeDtypeStruct(shape, F32) for shape in [(4, 8, LANES)] * 2 + [side] * 2],
            in_specs=[pl.BlockSpec(memory_space=pltpu.HBM)] * 5,
            out_specs=[VMEM] * 9,
            scratch_shapes=[pltpu.SemaphoreType.DMA((CHUNKS, 6))],
            compiler_params=pltpu.CompilerParams(vmem_limit_bytes=LIMIT),
        )(*arrays)
        far_got, near_got = move(to_far, far), move(to_near, near)
        *rows, advected, made_a, made_b = call(
            advect_kernel, [full] * 6 + [(6, 8, 2 * LANES)] * 2, *held,
            cost_estimate=pl.CostEstimate(flops=10**7, bytes_accessed=6 * 10**6, transcendentals=0),
        )
        send_a, send_b = call(
            edge_kernel, [(6, 8, 2 * LANES)] * 2, far_got, near_got, own, spare, made_a, made_b,
            input_output_aliases={4: 0, 5: 1},
        )
        got_a, got_b = move(send_a, pair_a), move(send_b, pair_b)
        inner, kept, strips = call(
            interior_kernel, [full, (4, 8, 3 * LANES), (4,) + side], *rows, advected, far_got, near_got, own, spare,
            scratch_shapes=[pltpu.VMEM((3,) + side, F32)],
            cost_estimate=pl.CostEstimate(flops=2 * 10**7, bytes_accessed=10**7, transcendentals=0),
        )
        out = pl.pallas_call(
            rim_kernel,
            out_shape=jax.ShapeDtypeStruct((8, ROWS, 2 * LANES), F32),
            in_specs=[VMEM] * 10,
            out_specs=pl.BlockSpec(memory_space=pl.ANY),
            scratch_shapes=[pltpu.VMEM((2, 8, 8, 2 * LANES), F32), pltpu.SemaphoreType.DMA((10,))],
            compiler_params=pltpu.CompilerParams(vmem_limit_bytes=LIMIT),
        )(got_a, got_b, *rows, strips, inner, kept)
        return out.reshape(tracers.shape)

    return shards


def solution(mesh):
    return jax.shard_map(
        make(mesh.shape["lon"], mesh.shape["lat"]),
        mesh=mesh,
        in_specs=(
            P(None, None, "lat", "lon"),
            P(None, None, "lat", "lon"),
            P(None, None, "lat", "lon"),
            P(None, "lat", "lon"),
            P(None, "lat", "lon"),
        ),
        out_specs=P(None, None, "lat", "lon"),
        check_vma=False,
    )
```

```python
import jax
import jax.numpy as jnp
from jax import lax
from jax.experimental import pallas as pl
from jax.experimental.pallas import tpu as pltpu
from jax.sharding import PartitionSpec as P


ROWS = 64
LANES = 128
F32 = jnp.float32
VMEM = pl.BlockSpec(memory_space=pltpu.VMEM)
LIMIT = 16 * 1024 * 1024
CHUNKS = 2
GROUPS = ("c", "mu", "vw", "sk")
KEPT = (2, 3, ROWS - 4, ROWS - 3)


def lane_of():
    return lax.broadcasted_iota(jnp.int32, (8, LANES), 1)


def low_of():
    return lax.broadcasted_iota(jnp.int32, (8, LANES), 0) < 4


def twice_low(x):
    return jnp.where(low_of(), x, pltpu.roll(x, 4, 0))


def twice_high(x):
    return jnp.where(low_of(), pltpu.roll(x, 4, 0), x)


def field_half(rows, name, row, h):
    which, turn = {
        "u": (1, twice_low), "v": (1, twice_high), "w": (2, twice_high),
        "sx": (3, twice_low), "sy": (3, twice_high), "m": (4, twice_low), "k": (4, twice_high),
    }.get(name, (0, None))
    value = rows[which][row, :, h * LANES : (h + 1) * LANES]
    return turn(value) if turn else value


def field_tiles(rows, name, row):
    return [field_half(rows, name, row, h) for h in range(2)]


def row_planes(held, span, h, both=True):
    tracer, velocity, slope, kappa, mask = held
    wide = slice(h * LANES, (h + 1) * LANES)
    return [
        tracer[:, span, wide], velocity[0:8, span, wide], velocity[4:12, span, wide],
        slope[:, span, wide] if both else jnp.concatenate([slope[0:4, span, wide]] * 2, axis=0),
        jnp.concatenate([mask[:, span, wide].astype(F32), kappa[:, span, wide]], axis=0),
    ]


def scaled(groups):
    c, uv, vw, s, mk = groups
    return c, uv, vw, s * 0.125, mk * jnp.where(low_of(), 1.0, 0.5)


def pack_kernel(*refs):
    arrays, held, (to_near, to_far, own, spare), sems = refs[:5], refs[5:10], refs[10:14], refs[14]
    copies = []
    for chunk in range(CHUNKS):
        span = slice(chunk * ROWS // CHUNKS, (chunk + 1) * ROWS // CHUNKS)
        ends = [array.shape[0] for array in arrays]
        ends[2] = 4
        copies.append(
            [
                pltpu.make_async_copy(array.at[:end, span], hold.at[:end, span], sems.at[chunk, i])
                for i, (array, hold, end) in enumerate(zip(arrays, held, ends))
            ]
        )
        for copy in copies[-1]:
            copy.start()
    northward = pltpu.make_async_copy(arrays[2].at[4:], held[2].at[4:], sems.at[0, 5])
    northward.start()
    lane, low = lane_of(), low_of()
    inside = lax.broadcasted_iota(jnp.int32, (8, 8, LANES), 2) < 64
    first, second = [None] * 8, [None] * 8
    for part in range(8):
        if part * CHUNKS % 8 == 0:
            for copy in copies[part * CHUNKS // 8]:
                copy.wait()
        span = slice(8 * part, 8 * part + 8)
        rims = []
        for left, right in zip(*[row_planes(held, span, h, False) for h in range(2)]):
            rims.append(jnp.transpose(jnp.where(inside, left, right), (1, 0, 2)))
        base = 16 * part
        before, half = lane < base, lane < base + 8
        for g in range(8):
            c, uv, vw, s, mk = scaled([x[g] for x in rims])
            mu = jnp.where(low, mk, pltpu.roll(uv, 4, 0))
            sk = jnp.where(low, s, mk)
            one = jnp.where(half, pltpu.roll(c, (base + 4) % LANES, 1), pltpu.roll(mu, (base + 12) % LANES, 1))
            two = jnp.where(half, pltpu.roll(vw, (base + 4) % LANES, 1), pltpu.roll(sk, (base + 12) % LANES, 1))
            first[g] = jnp.where(before, first[g], one) if part else one
            second[g] = jnp.where(before, second[g], two) if part else two
    for g in range(8):
        own[g] = first[g]
        spare[g] = second[g]
    slot = lane % 8
    to_east = jnp.broadcast_to(lax.axis_index("lon") % 2, (8, LANES)) == 0
    for pair in range(4):
        east, west = [], []
        for g in (2 * pair, 2 * pair + 1):
            east.append(jnp.where(slot == 0, pltpu.roll(second[g], LANES - 3, 1), first[g]))
            west.append(jnp.where(slot == 7, pltpu.roll(second[g], 3, 1), first[g]))
        eastern = jnp.where(slot < 4, east[0], pltpu.roll(east[1], 4, 1))
        western = jnp.where(slot < 4, pltpu.roll(west[0], LANES - 4, 1), west[1])
        to_near[pair] = jnp.where(to_east, eastern, western)
        to_far[pair] = jnp.where(to_east, western, eastern)
    northward.wait()


def advect_kernel(*refs):
    held, rows, advected, send_a, send_b = refs[:5], refs[5:10], refs[10], refs[11], refs[12]
    for part in range(8):
        for h in range(2):
            turned = [jnp.transpose(x, (1, 0, 2)) for x in row_planes(held, slice(8 * part, 8 * part + 8), h)]
            for g in range(8):
                for ref, value in zip(rows, scaled([x[g] for x in turned])):
                    ref[8 * part + g, :, h * LANES : (h + 1) * LANES] = value
    put_messages(rows, send_a, send_b)
    get = lambda name, row: field_tiles(rows, name, row)

    def advect_block(block, carry):
        first = 2 + 15 * block
        for j, tiles in enumerate(advect_rows(get, first, 15)[0]):
            for t in range(2):
                advected[first + j, :, t * LANES : (t + 1) * LANES] = tiles[t]
        return carry

    lax.fori_loop(0, 4, advect_block, 0)


def put_messages(rows, send_a, send_b):
    lane, low = lane_of(), low_of()
    lat = lax.axis_index("lat")

    first, last = lane < 2, lane >= LANES - 2

    def message(top):
        part = lambda name, q: field_tiles(rows, name, ROWS - 1 - q if top else q)
        outward = 1.0 if top else -1.0
        c, m, v = [part("c", q) for q in range(3)], [part("m", q) for q in range(3)], [part("v", q) for q in range(2)]
        half = each(lambda x: 0.5 * x, m[1])
        opened = each(jnp.multiply, half, m[0])
        step = each(lambda a, b, o: (a - b) * o, c[0], c[1], opened)
        inner = each(lambda a, b, x, y: (a - b) * (x * y), c[1], c[2], half, m[2])
        speed = each(lambda a, b, o: (a + b) * o * outward, v[0], v[1], opened)
        inflow = each(
            lambda a, b, s, x, y: s * jnp.where(s >= 0.0, a, b)
            + jnp.where(s >= 0.0, (jnp.abs(s) - s * s) * median(x, y), 0.0),
            c[1], c[0], speed, step, inner,
        )
        rest = each(lambda s: jnp.where(s >= 0.0, 0.0, jnp.abs(s) - s * s), speed)
        halved = each(lambda x: 0.5 * x, m[0])
        flux_x = zonal_flux(c[0], m[0], halved, part("u", 0))
        across = each(lambda f, g: f - g, flux_x, minus(flux_x))
        across = [jnp.where(first, 0.0, across[0]), jnp.where(last, 0.0, across[1])]
        down = each(vertical_divergence, c[0], halved, part("w", 0))
        cell = each(lambda a, x, z, f: a - x - z + f, c[0], across, down, inflow)
        pair = lambda a, b: each(lambda x, y: jnp.where(low, x, y), a, b)
        return [cell, step, c[0], pair(m[0], rest), pair(v[0], part("sy", 0)), part("k", 0)]

    backward = LANES - 1 - lane
    flip = lambda x: jnp.take_along_axis(x, backward, axis=1, mode="promise_in_bounds")
    is_even = jnp.broadcast_to(lat % 2, (8, LANES)) == 0
    folds = jnp.broadcast_to(lat, (8, LANES)) == lax.axis_size("lat") - 1
    north, south = message(True), message(False)
    for i, (top, bottom) in enumerate(zip(north, south)):
        for h in range(2):
            wide = slice(h * LANES, (h + 1) * LANES)
            turned = flip(top[1 - h])
            if i == 4:
                turned = -turned
            send_a[i, :, wide] = jnp.where(is_even, top[h], bottom[h])
            send_b[i, :, wide] = jnp.where(folds, turned, jnp.where(is_even, bottom[h], top[h]))


def strip_at(g, which, late, from_far, from_near, own, spare):
    slot = lane_of() % 16
    far_is_west = jnp.broadcast_to(lax.axis_index("lon") % 2, (8, LANES)) == 0
    near, far, mine = from_near[g // 2], from_far[g // 2], (spare if which else own)[g]
    east, west = jnp.where(far_is_west, near, far), jnp.where(far_is_west, far, near)
    shift = lambda x, by: pltpu.roll(x, by % LANES, 1) if by else x
    odd = 4 * (g % 2)
    east = shift(east, (1 if which else 4) - odd - 8 * late)
    west = shift(west, (9 if which else 6) - odd - 8 * late)
    inner = jnp.where(slot < 4, shift(mine, -8 * late), east)
    outer = jnp.where(slot < 10, west, shift(mine, 6 - 8 * late))
    return jnp.where(slot < 7, inner, outer)


def edge_kernel(*refs):
    sources, made, (send_a, send_b) = refs[:4], refs[4:6], refs[6:]
    lane, low = lane_of(), low_of()
    lat = lax.axis_index("lat")
    strip = lambda i, g: strip_at(g, i // 2, i % 2, *sources)

    def beside(g, inner):
        c, mu, vw = strip(0, g), strip(1, g), strip(2, g)
        shifts = (1, 0, LANES - 1, LANES - 2)
        moved = lambda x: [pltpu.roll(x, by, 1) if by else x for by in shifts]
        cells, pairs = moved(c), moved(mu)
        m = [twice_low(x) for x in pairs]
        half = [0.5 * x for x in m]
        steps = [(cells[n + 1] - cells[n]) * (half[n] * m[n + 1]) for n in range(3)]
        speed = face_speed(twice_high(pairs[1]), twice_high(pairs[2]), half[1] * m[2])
        flux = face_flux(cells[1], cells[2], speed, *steps)
        step = (c - strip(0, inner)) * (half[1] * twice_low(strip(1, inner)))
        return flux, c, step, jnp.where(low, mu, pltpu.roll(vw, 4, 0))

    def placed(values, base, backward):
        if backward:
            take = lambda x, at: jnp.take_along_axis(x, (base + at + LANES - lane) & (LANES - 1), axis=1, mode="promise_in_bounds")
            places = [(3, 2), (9, 8), 13, 29, 45]
        else:
            take = lambda x, at: pltpu.roll(x, (at - base) % LANES, 1) if (at - base) % LANES else x
            places = [(118, 119), (124, 125), 0, 16, 32]
        across = [take(values[0], at) - take(values[0], before) for at, before in places[:2]]
        c, step, mv = [take(x, at) for x, at in zip(values[1:], places[2:])]
        if backward:
            mv = jnp.where(low, mv, -mv)
        return across + [jnp.where(lane < 16, c, jnp.where(lane < 32, step, mv))]

    south, north = beside(0, 1), beside(7, 6)
    south, north, turned = placed(south, 0, False), placed(north, 112, False), placed(north, 112, True)

    def store(source, ref, left, right, packed):
        ref[0, :, :LANES] = source[0, :, :LANES] - jnp.where(lane < 2, left, 0.0)
        ref[0, :, LANES:] = source[0, :, LANES:] - jnp.where(lane >= LANES - 2, right, 0.0)
        ref[5, :, :LANES] = jnp.where(low, source[5, :, :LANES], pltpu.roll(packed, 4, 0))
        ref[5, :, LANES:] = jnp.where(low, source[5, :, LANES:], packed)

    is_even = jnp.broadcast_to(lat % 2, (8, LANES)) == 0
    folds = jnp.broadcast_to(lat, (8, LANES)) == lax.axis_size("lat") - 1
    store(made[0], send_a, *[jnp.where(is_even, n, s) for n, s in zip(north, south)])
    store(made[1], send_b, *[jnp.where(folds, t, jnp.where(is_even, s, n)) for n, s, t in zip(north, south, turned)])


def split_groups(groups):
    return {
        "c": groups["c"],
        "m": twice_low(groups["mu"]),
        "u": twice_high(groups["mu"]),
        "v": twice_low(groups["vw"]),
        "w": twice_high(groups["vw"]),
        "sx": twice_low(groups["sk"]),
        "k": twice_high(groups["sk"]),
    }


def third_of(x, base):
    east, west = pltpu.roll(x, (2 * LANES - 4 - base) % LANES, 1), pltpu.roll(x, (2 * LANES - 10 - base) % LANES, 1)
    return jnp.where(lane_of() < 64, east, west)


def third_tile(groups, base):
    return split_groups({n: third_of(groups[n], base) for n in GROUPS})


def plus(tiles):
    last = lane_of() == LANES - 1
    turned = [pltpu.roll(t, LANES - 1, 1) for t in tiles]
    if len(tiles) == 1:
        return turned
    return [jnp.where(last, turned[(i + 1) % len(tiles)], turned[i]) for i in range(len(tiles))]


def minus(tiles, count=3, west=None):
    first = lane_of() == 0
    turned = [pltpu.roll(t, 1, 1) for t in tiles]
    if len(tiles) == 1:
        return turned
    before = [turned[-1] if west is None else west] + turned[:-1]
    return [jnp.where(first, before[i], turned[i]) for i in range(min(count, len(tiles)))]


def each(function, *lists):
    return [function(*values) for values in zip(*lists)]


def below(x):
    return pltpu.roll(x, 7, 0)


def above(x):
    return pltpu.roll(x, 1, 0)


def median(step, upwind):
    return jnp.minimum(jnp.maximum(upwind, jnp.minimum(step, 0.0)), jnp.maximum(step, 0.0))


def face_flux(here, there, speed, back, step, ahead):
    positive = speed >= 0.0
    upwind = jnp.where(positive, back, ahead)
    size = jnp.abs(speed)
    return speed * jnp.where(positive, here, there) + (size - size * size) * median(step, upwind)


def zonal_flux(c, m, half, u):
    east = plus(c)
    opened = each(jnp.multiply, half, plus(m))
    speed = each(face_speed, u, plus(u), opened)
    step = each(lambda a, b, o: (b - a) * o, c, east, opened)
    return each(face_flux, c, east, speed, minus(step), step, plus(step))


def vertical_divergence(value, half, down):
    opened = open_below(half)
    under = below(value)
    step = (under - value) * opened
    flux = face_flux(value, under, face_speed(down, below(down), opened), above(step), step, below(step))
    return flux - above(flux)


def not_bottom():
    return lax.broadcasted_iota(jnp.int32, (8, LANES), 0) % 4 != 3


def open_below(marker):
    return jnp.where(not_bottom(), below(marker), 0.0)


def face_speed(one, two, half_open):
    return (one + two) * half_open


def advect_rows(get, first, count, known=()):
    known = dict(known)
    low, high = (-1 if -2 in known else -2), (count + 1 if count in known else count + 2)
    c = {j: get("c", first + j) for j in range(low, high)}
    m = {j: get("m", first + j) for j in range(low, high)}
    v = {j: get("v", first + j) for j in range(-1, count + 1)}
    half = {j: each(lambda x: 0.5 * x, m[j]) for j in range(low, high)}
    opened = {j: each(jnp.multiply, half[j], m[j + 1]) for j in range(low, high - 1)}
    step = {j: each(lambda a, b, o: (b - a) * o, c[j], c[j + 1], opened[j]) for j in range(low, high - 1)}
    step.update(known)
    flux = {}
    for j in range(-1, count):
        speed = each(face_speed, v[j], v[j + 1], opened[j])
        flux[j] = each(face_flux, c[j], c[j + 1], speed, step[j - 1], step[j], step[j + 1])
    result = []
    for j in range(count):
        flux_x = zonal_flux(c[j], m[j], half[j], get("u", first + j))
        total = each(lambda f, g, a, b: (f - g) + (a - b), flux_x, minus(flux_x), flux[j], flux[j - 1])
        down = each(vertical_divergence, c[j], half[j], get("w", first + j))
        result.append(each(lambda a, x, z, o: (a - x - z) * o, c[j], total, down, m[j]))
    return result, flux, step


def slope_flux(k1, k2, opened, step, s1, s2, z1, z2):
    return (k1 + k2) * opened * (step + (s1 + s2) * (z1 + z2))


def eastward(a, m, k, sx, twice_z):
    opened = each(jnp.multiply, m, plus(m))
    step = each(lambda x, y, o: (y - x) * o, a, plus(a), opened)
    return step, each(slope_flux, k, plus(k), opened, step, sx, plus(sx), twice_z, plus(twice_z))


def diffuse_rows(get, first, count, beside=None):
    a, m, k, sy, step_z, twice_z, step_y, flux_y = [{} for _ in range(8)]
    result = []
    last = lane_of() == LANES - 1

    def row_result(j):
        sx = get("sx", first + j)
        step_x, flux_x = eastward(a[j], m[j], k[j], sx, twice_z[j])
        west = [None, None]
        if beside:
            east, west = beside(first + j)
            step_x = [step_x[0], jnp.where(last, east[0], step_x[1])]
            flux_x = [flux_x[0], jnp.where(last, east[1], flux_x[1])]
        twice_x = each(jnp.add, step_x, minus(step_x, 2, west[0]))
        twice_y = each(jnp.add, step_y[j - 1], step_y[j])
        total = each(lambda f, g, p, q: (f - g) + (p - q), flux_x, minus(flux_x, 2, west[1]), flux_y[j], flux_y[j - 1])

        def finish(value, marker, kappa, east, north, tx, ty, sz, across):
            face_east, face_north = east + below(east), north + below(north)
            flux_z = (kappa + below(kappa)) * open_below(marker) * (
                face_east * (tx + below(tx)) + face_north * (ty + below(ty))
                + (face_east * face_east + face_north * face_north) * (16.0 * sz)
            )
            return (value + across + (flux_z - above(flux_z))) * marker

        result.append(each(finish, a[j][:2], m[j], k[j], sx, sy[j], twice_x, twice_y, step_z[j], total))

    for j in range(-1, count + 1):
        a[j], m[j], k[j], sy[j] = [get(name, first + j) for name in ("a", "m", "k", "sy")]
        wide = 3 if 0 <= j < count else 2
        step_z[j] = each(lambda x, o: (below(x) - x) * open_below(o), a[j][:wide], m[j])
        twice_z[j] = each(lambda x: above(x) + x, step_z[j])
        if j >= 0:
            opened = each(jnp.multiply, m[j - 1][:2], m[j][:2])
            step_y[j - 1] = each(lambda x, y, o: (y - x) * o, a[j - 1][:2], a[j][:2], opened)
            flux_y[j - 1] = each(
                slope_flux, k[j - 1], k[j], opened, step_y[j - 1], sy[j - 1], sy[j], twice_z[j - 1], twice_z[j]
            )
        if j >= 1:
            row_result(j - 1)
    return result


def tiles_of(ref, row, count):
    return [ref[row, :, t * LANES : (t + 1) * LANES] for t in range(count)]


def interior_kernel(*refs):
    rows, advected, sources = refs[:5], refs[5], refs[6:10]
    out, kept, strips, narrow = refs[10:]
    lane = lane_of()
    near_east, near_west = lane >= LANES - 2, lane < 2

    full = []
    for g in range(8):
        groups = {n: strip_at(g, i // 2, i % 2, *sources) for i, n in enumerate(GROUPS)}
        full.append(split_groups(groups))
        for i, n in enumerate(GROUPS):
            strips[i, g] = groups[n]

    def get_strip(name, g):
        x = full[g % 8][name]
        return [x if 0 <= g < 8 else pltpu.roll(x, 16 if g < 0 else LANES - 16, 1)]

    for g, (a,) in enumerate(advect_rows(get_strip, 0, 8)[0]):
        part = full[g]
        step_z = (below(a) - a) * open_below(part["m"])
        step, flux = eastward([a], [part["m"]], [part["k"]], [part["sx"]], [above(step_z) + step_z])
        narrow[0, g], narrow[1, g], narrow[2, g] = a, step[0], flux[0]

    def lanes_to(which, row, lane_from, lane_to):
        part = row // 8
        return pltpu.roll(narrow[which, row - 8 * part], lax.rem(2 * LANES + lane_to - lane_from - 16 * part, LANES), 1)

    def get(name, row):
        if name != "a":
            return field_tiles(rows, name, row)
        left, right = tiles_of(advected, row, 2)
        return [
            jnp.where(near_west, lanes_to(0, row, 10, 0), left),
            jnp.where(near_east, lanes_to(0, row, 3, LANES - 1), right),
        ]

    def beside(row):
        return [lanes_to(i, row, 3, LANES - 1) for i in (1, 2)], [lanes_to(i, row, 9, 0) for i in (1, 2)]

    for i, row in enumerate(KEPT):
        third = jnp.where(lane < 64, lanes_to(0, row, 4, 0), lanes_to(0, row, 9, LANES - 1))
        for t, tile in enumerate(get("a", row) + [third]):
            kept[i, :, t * LANES : (t + 1) * LANES] = tile

    def diffuse_block(block, carry):
        first = jnp.minimum(3 + 10 * block, ROWS - 3 - 10)
        for j, tiles in enumerate(diffuse_rows(get, first, 10, beside)):
            for t in range(2):
                out[first + j, :, t * LANES : (t + 1) * LANES] = tiles[t]
        return carry

    lax.fori_loop(0, 6, diffuse_block, 0)


def rim_kernel(*refs):
    got_a, got_b = refs[0], refs[1]
    fields = refs[2:7]
    strips, inner, kept, out, edges, sems = refs[7:]
    middle = pltpu.make_async_copy
    copies = [middle(inner.at[8:56, i], out.at[i, 8:56], sems.at[i]) for i in range(8)]
    for copy in copies:
        copy.start()
    low = low_of()
    lat = lax.axis_index("lat")
    even = jnp.broadcast_to(lat % 2, (8, LANES)) == 0
    floor = jnp.broadcast_to(lat, (8, LANES)) == 0

    def halo(is_north):
        def tile(i, h):
            a = got_a[i, :, h * LANES : (h + 1) * LANES]
            b = got_b[i, :, h * LANES : (h + 1) * LANES]
            if is_north:
                return jnp.where(even, a, b)
            return jnp.where(floor, 0.0, jnp.where(even, b, a))

        tiles = [[tile(i, h) for h in range(2)] for i in range(6)]
        corner = jnp.where(low, pltpu.roll(tiles[5][0], 4, 0), tiles[5][1])
        c_side, step_side, mv = [third_of(corner, 16 * i) for i in range(3)]
        row = {
            "c": tiles[2] + [c_side],
            "m": each(twice_low, tiles[3]) + [twice_low(mv)],
            "v": each(twice_low, tiles[4]) + [twice_high(mv)],
            "sy": each(twice_high, tiles[4]),
            "k": each(twice_low, tiles[5]),
        }
        return row, tiles[0], tiles[1] + [step_side], each(twice_high, tiles[3])

    for is_north in (False, True):
        outer, cell, step_in, rest = halo(is_north)
        start, beyond = (ROWS - 2, ROWS) if is_north else (0, -1)
        made, sides = {}, {}
        for row in range(*((ROWS - 4, ROWS) if is_north else (0, 4))):
            base = 16 * (row // 8)
            sides[row] = third_tile({n: strips[i, row % 8] for i, n in enumerate(GROUPS)}, base)

        def get(name, row):
            if name == "a":
                return made[row] if row in made else tiles_of(kept, KEPT.index(row), 3)
            if row == beyond:
                return outer[name]
            tiles = field_tiles(fields, name, row)
            return tiles if name == "sy" else tiles + [sides[row][name]]

        known = {2: [-x for x in step_in]} if is_north else {-2: step_in}
        results, flux, step = advect_rows(get, start, 2, known)
        made.update(zip((start, start + 1), results))
        face, sign = (1, -1.0) if is_north else (-1, 1.0)
        made[beyond] = each(
            lambda q, g, s, t, f, o: (q + g * median(s, sign * t) - sign * f) * o,
            cell, rest, step_in, step[face], flux[face], outer["m"],
        )
        final = ROWS - 3 if is_north else 0
        base = ROWS - 8 if is_north else 0
        done = {final + j: x for j, x in enumerate(diffuse_rows(get, final, 3))}
        for h in range(2):
            stack = [done[j][h] if j in done else inner[j, :, h * LANES : (h + 1) * LANES] for j in range(base, base + 8)]
            edges[int(is_north), :, :, h * LANES : (h + 1) * LANES] = jnp.transpose(jnp.stack(stack), (1, 0, 2))
        copy = middle(edges.at[int(is_north)], out.at[:, base : base + 8], sems.at[8 + int(is_north)])
        copy.start()
        copies.append(copy)
    for copy in copies:
        copy.wait()


def call(kernel, shapes, *operands, **options):
    return pl.pallas_call(
        kernel,
        out_shape=[jax.ShapeDtypeStruct(s, F32) for s in shapes],
        in_specs=[VMEM] * len(operands),
        out_specs=[VMEM] * len(shapes),
        compiler_params=pltpu.CompilerParams(vmem_limit_bytes=LIMIT),
        **options,
    )(*operands)


def make(lons, lats):
    def spot(lon, lat):
        return (lon % lons) * lats + lat

    near = [(spot(i, j), spot(i ^ 1, j)) for i in range(lons) for j in range(lats)]
    far = [(spot(i, j), spot(i + 1 if i % 2 else i - 1, j)) for i in range(lons) for j in range(lats)]
    pair_a = [(spot(i, j), spot(i, j ^ 1)) for i in range(lons) for j in range(lats)]
    pair_b = []
    for i in range(lons):
        for j in range(lats):
            if j == 0:
                pair_b.append((spot(i, j), spot(i ^ 1, j)))
            elif j == lats - 1:
                pair_b.append((spot(i, j), spot(lons - 1 - i, j)))
            else:
                pair_b.append((spot(i, j), spot(i, j + 1 if j % 2 else j - 1)))

    def move(x, route):
        return lax.ppermute(x, ("lon", "lat"), route)

    def shards(tracers, velocity, slopes, diffusivity, sea_mask):
        plane = lambda x: x.reshape(-1, ROWS, 2 * LANES)
        arrays = [plane(tracers), plane(velocity), plane(slopes), diffusivity, sea_mask]
        arrays = [pltpu.with_memory_space_constraint(x, pltpu.HBM) for x in arrays]
        full, side = (ROWS, 8, 2 * LANES), (8, 8, LANES)
        *held, to_near, to_far, own, spare = pl.pallas_call(
            pack_kernel,
            out_shape=[jax.ShapeDtypeStruct(x.shape, x.dtype) for x in arrays]
            + [jax.ShapeDtypeStruct(shape, F32) for shape in [(4, 8, LANES)] * 2 + [side] * 2],
            in_specs=[pl.BlockSpec(memory_space=pltpu.HBM)] * 5,
            out_specs=[VMEM] * 9,
            scratch_shapes=[pltpu.SemaphoreType.DMA((CHUNKS, 6))],
            compiler_params=pltpu.CompilerParams(vmem_limit_bytes=LIMIT),
        )(*arrays)
        far_got, near_got = move(to_far, far), move(to_near, near)
        *rows, advected, made_a, made_b = call(
            advect_kernel, [full] * 6 + [(6, 8, 2 * LANES)] * 2, *held,
            cost_estimate=pl.CostEstimate(flops=10**7, bytes_accessed=6 * 10**6, transcendentals=0),
        )
        send_a, send_b = call(
            edge_kernel, [(6, 8, 2 * LANES)] * 2, far_got, near_got, own, spare, made_a, made_b,
            input_output_aliases={4: 0, 5: 1},
        )
        got_a, got_b = move(send_a, pair_a), move(send_b, pair_b)
        inner, kept, strips = call(
            interior_kernel, [full, (4, 8, 3 * LANES), (4,) + side], *rows, advected, far_got, near_got, own, spare,
            scratch_shapes=[pltpu.VMEM((3,) + side, F32)],
            cost_estimate=pl.CostEstimate(flops=2 * 10**7, bytes_accessed=10**7, transcendentals=0),
        )
        out = pl.pallas_call(
            rim_kernel,
            out_shape=jax.ShapeDtypeStruct((8, ROWS, 2 * LANES), F32),
            in_specs=[VMEM] * 10,
            out_specs=pl.BlockSpec(memory_space=pl.ANY),
            scratch_shapes=[pltpu.VMEM((2, 8, 8, 2 * LANES), F32), pltpu.SemaphoreType.DMA((10,))],
            compiler_params=pltpu.CompilerParams(vmem_limit_bytes=LIMIT),
        )(got_a, got_b, *rows, strips, inner, kept)
        return out.reshape(tracers.shape)

    return shards


def solution(mesh):
    return jax.shard_map(
        make(mesh.shape["lon"], mesh.shape["lat"]),
        mesh=mesh,
        in_specs=(
            P(None, None, "lat", "lon"),
            P(None, None, "lat", "lon"),
            P(None, None, "lat", "lon"),
            P(None, "lat", "lon"),
            P(None, "lat", "lon"),
        ),
        out_specs=P(None, None, "lat", "lon"),
        check_vma=False,
    )
```

```python
import jax
import jax.numpy as jnp
from jax import lax
from jax.experimental import pallas as pl
from jax.experimental.pallas import tpu as pltpu
from jax.sharding import PartitionSpec as P


ROWS = 64
LANES = 128
F32 = jnp.float32
VMEM = pl.BlockSpec(memory_space=pltpu.VMEM)
LIMIT = 16 * 1024 * 1024
CHUNKS = 2
GROUPS = ("c", "mu", "vw", "sk")
KEPT = (2, 3, ROWS - 4, ROWS - 3)


def lane_of():
    return lax.broadcasted_iota(jnp.int32, (8, LANES), 1)


def low_of():
    return lax.broadcasted_iota(jnp.int32, (8, LANES), 0) < 4


def twice_low(x):
    return jnp.where(low_of(), x, pltpu.roll(x, 4, 0))


def twice_high(x):
    return jnp.where(low_of(), pltpu.roll(x, 4, 0), x)


def field_half(rows, name, row, h):
    which, turn = {
        "u": (1, twice_low), "v": (1, twice_high), "w": (2, twice_high),
        "sx": (3, twice_low), "sy": (3, twice_high), "m": (4, twice_low), "k": (4, twice_high),
    }.get(name, (0, None))
    value = rows[which][row, :, h * LANES : (h + 1) * LANES]
    return turn(value) if turn else value


def field_tiles(rows, name, row):
    return [field_half(rows, name, row, h) for h in range(2)]


def row_planes(held, span, h, both=True):
    tracer, velocity, slope, kappa, mask = held
    wide = slice(h * LANES, (h + 1) * LANES)
    return [
        tracer[:, span, wide], velocity[0:8, span, wide], velocity[4:12, span, wide],
        slope[:, span, wide] if both else jnp.concatenate([slope[0:4, span, wide]] * 2, axis=0),
        jnp.concatenate([mask[:, span, wide].astype(F32), kappa[:, span, wide]], axis=0),
    ]


def scaled(groups):
    c, uv, vw, s, mk = groups
    return c, uv, vw, s * 0.125, mk * jnp.where(low_of(), 1.0, 0.5)


def pack_kernel(*refs):
    arrays, held, (to_near, to_far, own, spare), sems = refs[:5], refs[5:10], refs[10:14], refs[14]
    copies = []
    for chunk in range(CHUNKS):
        span = slice(chunk * ROWS // CHUNKS, (chunk + 1) * ROWS // CHUNKS)
        ends = [array.shape[0] for array in arrays]
        ends[2] = 4
        copies.append(
            [
                pltpu.make_async_copy(array.at[:end, span], hold.at[:end, span], sems.at[chunk, i])
                for i, (array, hold, end) in enumerate(zip(arrays, held, ends))
            ]
        )
        for copy in copies[-1]:
            copy.start()
    northward = pltpu.make_async_copy(arrays[2].at[4:], held[2].at[4:], sems.at[0, 5])
    northward.start()
    lane, low = lane_of(), low_of()
    inside = lax.broadcasted_iota(jnp.int32, (8, 8, LANES), 2) < 64
    first, second = [None] * 8, [None] * 8
    for part in range(8):
        if part * CHUNKS % 8 == 0:
            for copy in copies[part * CHUNKS // 8]:
                copy.wait()
        span = slice(8 * part, 8 * part + 8)
        rims = []
        for left, right in zip(*[row_planes(held, span, h, False) for h in range(2)]):
            rims.append(jnp.transpose(jnp.where(inside, left, right), (1, 0, 2)))
        base = 16 * part
        before, half = lane < base, lane < base + 8
        for g in range(8):
            c, uv, vw, s, mk = scaled([x[g] for x in rims])
            mu = jnp.where(low, mk, pltpu.roll(uv, 4, 0))
            sk = jnp.where(low, s, mk)
            one = jnp.where(half, pltpu.roll(c, (base + 4) % LANES, 1), pltpu.roll(mu, (base + 12) % LANES, 1))
            two = jnp.where(half, pltpu.roll(vw, (base + 4) % LANES, 1), pltpu.roll(sk, (base + 12) % LANES, 1))
            first[g] = jnp.where(before, first[g], one) if part else one
            second[g] = jnp.where(before, second[g], two) if part else two
    for g in range(8):
        own[g] = first[g]
        spare[g] = second[g]
    slot = lane % 8
    to_east = jnp.broadcast_to(lax.axis_index("lon") % 2, (8, LANES)) == 0
    for pair in range(4):
        east, west = [], []
        for g in (2 * pair, 2 * pair + 1):
            east.append(jnp.where(slot == 0, pltpu.roll(second[g], LANES - 3, 1), first[g]))
            west.append(jnp.where(slot == 7, pltpu.roll(second[g], 3, 1), first[g]))
        eastern = jnp.where(slot < 4, east[0], pltpu.roll(east[1], 4, 1))
        western = jnp.where(slot < 4, pltpu.roll(west[0], LANES - 4, 1), west[1])
        to_near[pair] = jnp.where(to_east, eastern, western)
        to_far[pair] = jnp.where(to_east, western, eastern)
    northward.wait()


def advect_kernel(*refs):
    held, rows, advected, send_a, send_b = refs[:5], refs[5:10], refs[10], refs[11], refs[12]
    for part in range(8):
        for h in range(2):
            turned = [jnp.transpose(x, (1, 0, 2)) for x in row_planes(held, slice(8 * part, 8 * part + 8), h)]
            for g in range(8):
                for i, (ref, value) in enumerate(zip(rows, scaled([x[g] for x in turned]))):
                    if i != 3 or part in (0, 7):
                        ref[8 * part + g, :, h * LANES : (h + 1) * LANES] = value
    put_messages(rows, send_a, send_b)
    get = lambda name, row: field_tiles(rows, name, row)

    def advect_block(block, carry):
        first = 2 + 15 * block
        for j, tiles in enumerate(advect_rows(get, first, 15)[0]):
            for t in range(2):
                advected[first + j, :, t * LANES : (t + 1) * LANES] = tiles[t]
        return carry

    lax.fori_loop(0, 4, advect_block, 0)


def put_messages(rows, send_a, send_b):
    lane, low = lane_of(), low_of()
    lat = lax.axis_index("lat")

    first, last = lane < 2, lane >= LANES - 2

    def message(top):
        part = lambda name, q: field_tiles(rows, name, ROWS - 1 - q if top else q)
        outward = 1.0 if top else -1.0
        c, m, v = [part("c", q) for q in range(3)], [part("m", q) for q in range(3)], [part("v", q) for q in range(2)]
        half = each(lambda x: 0.5 * x, m[1])
        opened = each(jnp.multiply, half, m[0])
        step = each(lambda a, b, o: (a - b) * o, c[0], c[1], opened)
        inner = each(lambda a, b, x, y: (a - b) * (x * y), c[1], c[2], half, m[2])
        speed = each(lambda a, b, o: (a + b) * o * outward, v[0], v[1], opened)
        inflow = each(
            lambda a, b, s, x, y: s * jnp.where(s >= 0.0, a, b)
            + jnp.where(s >= 0.0, (jnp.abs(s) - s * s) * median(x, y), 0.0),
            c[1], c[0], speed, step, inner,
        )
        rest = each(lambda s: jnp.where(s >= 0.0, 0.0, jnp.abs(s) - s * s), speed)
        halved = each(lambda x: 0.5 * x, m[0])
        flux_x = zonal_flux(c[0], m[0], halved, part("u", 0))
        across = each(lambda f, g: f - g, flux_x, minus(flux_x))
        across = [jnp.where(first, 0.0, across[0]), jnp.where(last, 0.0, across[1])]
        down = each(vertical_divergence, c[0], halved, part("w", 0))
        cell = each(lambda a, x, z, f: a - x - z + f, c[0], across, down, inflow)
        pair = lambda a, b: each(lambda x, y: jnp.where(low, x, y), a, b)
        return [cell, step, c[0], pair(m[0], rest), pair(v[0], part("sy", 0)), part("k", 0)]

    backward = LANES - 1 - lane
    flip = lambda x: jnp.take_along_axis(x, backward, axis=1, mode="promise_in_bounds")
    is_even = jnp.broadcast_to(lat % 2, (8, LANES)) == 0
    folds = jnp.broadcast_to(lat, (8, LANES)) == lax.axis_size("lat") - 1
    north, south = message(True), message(False)
    for i, (top, bottom) in enumerate(zip(north, south)):
        for h in range(2):
            wide = slice(h * LANES, (h + 1) * LANES)
            turned = flip(top[1 - h])
            if i == 4:
                turned = -turned
            send_a[i, :, wide] = jnp.where(is_even, top[h], bottom[h])
            send_b[i, :, wide] = jnp.where(folds, turned, jnp.where(is_even, bottom[h], top[h]))


def strip_at(g, which, late, from_far, from_near, own, spare):
    slot = lane_of() % 16
    far_is_west = jnp.broadcast_to(lax.axis_index("lon") % 2, (8, LANES)) == 0
    near, far, mine = from_near[g // 2], from_far[g // 2], (spare if which else own)[g]
    east, west = jnp.where(far_is_west, near, far), jnp.where(far_is_west, far, near)
    shift = lambda x, by: pltpu.roll(x, by % LANES, 1) if by else x
    odd = 4 * (g % 2)
    east = shift(east, (1 if which else 4) - odd - 8 * late)
    west = shift(west, (9 if which else 6) - odd - 8 * late)
    inner = jnp.where(slot < 4, shift(mine, -8 * late), east)
    outer = jnp.where(slot < 10, west, shift(mine, 6 - 8 * late))
    return jnp.where(slot < 7, inner, outer)


def edge_kernel(*refs):
    sources, made, (send_a, send_b) = refs[:4], refs[4:6], refs[6:]
    lane, low = lane_of(), low_of()
    lat = lax.axis_index("lat")
    strip = lambda i, g: strip_at(g, i // 2, i % 2, *sources)

    def beside(g, inner):
        c, mu, vw = strip(0, g), strip(1, g), strip(2, g)
        shifts = (1, 0, LANES - 1, LANES - 2)
        moved = lambda x: [pltpu.roll(x, by, 1) if by else x for by in shifts]
        cells, pairs = moved(c), moved(mu)
        m = [twice_low(x) for x in pairs]
        half = [0.5 * x for x in m]
        steps = [(cells[n + 1] - cells[n]) * (half[n] * m[n + 1]) for n in range(3)]
        speed = face_speed(twice_high(pairs[1]), twice_high(pairs[2]), half[1] * m[2])
        flux = face_flux(cells[1], cells[2], speed, *steps)
        step = (c - strip(0, inner)) * (half[1] * twice_low(strip(1, inner)))
        return flux, c, step, jnp.where(low, mu, pltpu.roll(vw, 4, 0))

    def placed(values, base, backward):
        if backward:
            take = lambda x, at: jnp.take_along_axis(x, (base + at + LANES - lane) & (LANES - 1), axis=1, mode="promise_in_bounds")
            places = [(3, 2), (9, 8), 13, 29, 45]
        else:
            take = lambda x, at: pltpu.roll(x, (at - base) % LANES, 1) if (at - base) % LANES else x
            places = [(118, 119), (124, 125), 0, 16, 32]
        across = [take(values[0], at) - take(values[0], before) for at, before in places[:2]]
        c, step, mv = [take(x, at) for x, at in zip(values[1:], places[2:])]
        if backward:
            mv = jnp.where(low, mv, -mv)
        return across + [jnp.where(lane < 16, c, jnp.where(lane < 32, step, mv))]

    south, north = beside(0, 1), beside(7, 6)
    south, north, turned = placed(south, 0, False), placed(north, 112, False), placed(north, 112, True)

    def store(source, ref, left, right, packed):
        ref[0, :, :LANES] = source[0, :, :LANES] - jnp.where(lane < 2, left, 0.0)
        ref[0, :, LANES:] = source[0, :, LANES:] - jnp.where(lane >= LANES - 2, right, 0.0)
        ref[5, :, :LANES] = jnp.where(low, source[5, :, :LANES], pltpu.roll(packed, 4, 0))
        ref[5, :, LANES:] = jnp.where(low, source[5, :, LANES:], packed)

    is_even = jnp.broadcast_to(lat % 2, (8, LANES)) == 0
    folds = jnp.broadcast_to(lat, (8, LANES)) == lax.axis_size("lat") - 1
    store(made[0], send_a, *[jnp.where(is_even, n, s) for n, s in zip(north, south)])
    store(made[1], send_b, *[jnp.where(folds, t, jnp.where(is_even, s, n)) for n, s, t in zip(north, south, turned)])


def split_groups(groups):
    return {
        "c": groups["c"],
        "m": twice_low(groups["mu"]),
        "u": twice_high(groups["mu"]),
        "v": twice_low(groups["vw"]),
        "w": twice_high(groups["vw"]),
        "sx": twice_low(groups["sk"]),
        "k": twice_high(groups["sk"]),
    }


def third_of(x, base):
    east, west = pltpu.roll(x, (2 * LANES - 4 - base) % LANES, 1), pltpu.roll(x, (2 * LANES - 10 - base) % LANES, 1)
    return jnp.where(lane_of() < 64, east, west)


def third_tile(groups, base):
    return split_groups({n: third_of(groups[n], base) for n in GROUPS})


def plus(tiles):
    last = lane_of() == LANES - 1
    turned = [pltpu.roll(t, LANES - 1, 1) for t in tiles]
    if len(tiles) == 1:
        return turned
    return [jnp.where(last, turned[(i + 1) % len(tiles)], turned[i]) for i in range(len(tiles))]


def minus(tiles, count=3, west=None):
    first = lane_of() == 0
    turned = [pltpu.roll(t, 1, 1) for t in tiles]
    if len(tiles) == 1:
        return turned
    before = [turned[-1] if west is None else west] + turned[:-1]
    return [jnp.where(first, before[i], turned[i]) for i in range(min(count, len(tiles)))]


def each(function, *lists):
    return [function(*values) for values in zip(*lists)]


def below(x):
    return pltpu.roll(x, 7, 0)


def above(x):
    return pltpu.roll(x, 1, 0)


def median(step, upwind):
    return jnp.minimum(jnp.maximum(upwind, jnp.minimum(step, 0.0)), jnp.maximum(step, 0.0))


def face_flux(here, there, speed, back, step, ahead):
    positive = speed >= 0.0
    upwind = jnp.where(positive, back, ahead)
    size = jnp.abs(speed)
    return speed * jnp.where(positive, here, there) + (size - size * size) * median(step, upwind)


def zonal_flux(c, m, half, u):
    east = plus(c)
    opened = each(jnp.multiply, half, plus(m))
    speed = each(face_speed, u, plus(u), opened)
    step = each(lambda a, b, o: (b - a) * o, c, east, opened)
    return each(face_flux, c, east, speed, minus(step), step, plus(step))


def vertical_divergence(value, half, down):
    opened = open_below(half)
    under = below(value)
    step = (under - value) * opened
    flux = face_flux(value, under, face_speed(down, below(down), opened), above(step), step, below(step))
    return flux - above(flux)


def not_bottom():
    return lax.broadcasted_iota(jnp.int32, (8, LANES), 0) % 4 != 3


def open_below(marker):
    return jnp.where(not_bottom(), below(marker), 0.0)


def face_speed(one, two, half_open):
    return (one + two) * half_open


def advect_rows(get, first, count, known=()):
    known = dict(known)
    low, high = (-1 if -2 in known else -2), (count + 1 if count in known else count + 2)
    c = {j: get("c", first + j) for j in range(low, high)}
    m = {j: get("m", first + j) for j in range(low, high)}
    v = {j: get("v", first + j) for j in range(-1, count + 1)}
    half = {j: each(lambda x: 0.5 * x, m[j]) for j in range(low, high)}
    opened = {j: each(jnp.multiply, half[j], m[j + 1]) for j in range(low, high - 1)}
    step = {j: each(lambda a, b, o: (b - a) * o, c[j], c[j + 1], opened[j]) for j in range(low, high - 1)}
    step.update(known)
    flux = {}
    for j in range(-1, count):
        speed = each(face_speed, v[j], v[j + 1], opened[j])
        flux[j] = each(face_flux, c[j], c[j + 1], speed, step[j - 1], step[j], step[j + 1])
    result = []
    for j in range(count):
        flux_x = zonal_flux(c[j], m[j], half[j], get("u", first + j))
        total = each(lambda f, g, a, b: (f - g) + (a - b), flux_x, minus(flux_x), flux[j], flux[j - 1])
        down = each(vertical_divergence, c[j], half[j], get("w", first + j))
        result.append(each(lambda a, x, z, o: (a - x - z) * o, c[j], total, down, m[j]))
    return result, flux, step


def slope_flux(k1, k2, opened, step, s1, s2, z1, z2):
    return (k1 + k2) * opened * (step + (s1 + s2) * (z1 + z2))


def eastward(a, m, k, sx, twice_z):
    opened = each(jnp.multiply, m, plus(m))
    step = each(lambda x, y, o: (y - x) * o, a, plus(a), opened)
    return step, each(slope_flux, k, plus(k), opened, step, sx, plus(sx), twice_z, plus(twice_z))


def diffuse_rows(get, first, count, beside=None):
    a, m, k, sy, step_z, twice_z, step_y, flux_y = [{} for _ in range(8)]
    result = []
    last = lane_of() == LANES - 1

    def row_result(j):
        sx = get("sx", first + j)
        step_x, flux_x = eastward(a[j], m[j], k[j], sx, twice_z[j])
        west = [None, None]
        if beside:
            east, west = beside(first + j)
            step_x = [step_x[0], jnp.where(last, east[0], step_x[1])]
            flux_x = [flux_x[0], jnp.where(last, east[1], flux_x[1])]
        twice_x = each(jnp.add, step_x, minus(step_x, 2, west[0]))
        twice_y = each(jnp.add, step_y[j - 1], step_y[j])
        total = each(lambda f, g, p, q: (f - g) + (p - q), flux_x, minus(flux_x, 2, west[1]), flux_y[j], flux_y[j - 1])

        def finish(value, marker, kappa, east, north, tx, ty, sz, across):
            face_east, face_north = east + below(east), north + below(north)
            flux_z = (kappa + below(kappa)) * open_below(marker) * (
                face_east * (tx + below(tx)) + face_north * (ty + below(ty))
                + (face_east * face_east + face_north * face_north) * (16.0 * sz)
            )
            return (value + across + (flux_z - above(flux_z))) * marker

        result.append(each(finish, a[j][:2], m[j], k[j], sx, sy[j], twice_x, twice_y, step_z[j], total))

    for j in range(-1, count + 1):
        a[j], m[j], k[j], sy[j] = [get(name, first + j) for name in ("a", "m", "k", "sy")]
        wide = 3 if 0 <= j < count else 2
        step_z[j] = each(lambda x, o: (below(x) - x) * open_below(o), a[j][:wide], m[j])
        twice_z[j] = each(lambda x: above(x) + x, step_z[j])
        if j >= 0:
            opened = each(jnp.multiply, m[j - 1][:2], m[j][:2])
            step_y[j - 1] = each(lambda x, y, o: (y - x) * o, a[j - 1][:2], a[j][:2], opened)
            flux_y[j - 1] = each(
                slope_flux, k[j - 1], k[j], opened, step_y[j - 1], sy[j - 1], sy[j], twice_z[j - 1], twice_z[j]
            )
        if j >= 1:
            row_result(j - 1)
    return result


def tiles_of(ref, row, count):
    return [ref[row, :, t * LANES : (t + 1) * LANES] for t in range(count)]


def interior_kernel(*refs):
    rows, advected, sources, slope = refs[:5], refs[5], refs[6:10], refs[10]
    out, kept, strips, slope_rows, narrow = refs[11:]
    rows = rows[:3] + (slope_rows,) + rows[4:]
    for part in range(8):
        for h in range(2):
            wide = slice(h * LANES, (h + 1) * LANES)
            turned = jnp.transpose(slope[:, 8 * part : 8 * part + 8, wide], (1, 0, 2))
            slope_rows[8 * part : 8 * part + 8, :, wide] = turned * 0.125
    lane = lane_of()
    near_east, near_west = lane >= LANES - 2, lane < 2

    full = []
    for g in range(8):
        groups = {n: strip_at(g, i // 2, i % 2, *sources) for i, n in enumerate(GROUPS)}
        full.append(split_groups(groups))
        for i, n in enumerate(GROUPS):
            strips[i, g] = groups[n]

    def get_strip(name, g):
        x = full[g % 8][name]
        return [x if 0 <= g < 8 else pltpu.roll(x, 16 if g < 0 else LANES - 16, 1)]

    for g, (a,) in enumerate(advect_rows(get_strip, 0, 8)[0]):
        part = full[g]
        step_z = (below(a) - a) * open_below(part["m"])
        step, flux = eastward([a], [part["m"]], [part["k"]], [part["sx"]], [above(step_z) + step_z])
        narrow[0, g], narrow[1, g], narrow[2, g] = a, step[0], flux[0]

    def lanes_to(which, row, lane_from, lane_to):
        part = row // 8
        return pltpu.roll(narrow[which, row - 8 * part], lax.rem(2 * LANES + lane_to - lane_from - 16 * part, LANES), 1)

    def get(name, row):
        if name != "a":
            return field_tiles(rows, name, row)
        left, right = tiles_of(advected, row, 2)
        return [
            jnp.where(near_west, lanes_to(0, row, 10, 0), left),
            jnp.where(near_east, lanes_to(0, row, 3, LANES - 1), right),
        ]

    def beside(row):
        return [lanes_to(i, row, 3, LANES - 1) for i in (1, 2)], [lanes_to(i, row, 9, 0) for i in (1, 2)]

    for i, row in enumerate(KEPT):
        third = jnp.where(lane < 64, lanes_to(0, row, 4, 0), lanes_to(0, row, 9, LANES - 1))
        for t, tile in enumerate(get("a", row) + [third]):
            kept[i, :, t * LANES : (t + 1) * LANES] = tile

    def diffuse_block(block, carry):
        first = jnp.minimum(3 + 10 * block, ROWS - 3 - 10)
        for j, tiles in enumerate(diffuse_rows(get, first, 10, beside)):
            for t in range(2):
                out[first + j, :, t * LANES : (t + 1) * LANES] = tiles[t]
        return carry

    lax.fori_loop(0, 6, diffuse_block, 0)


def rim_kernel(*refs):
    got_a, got_b = refs[0], refs[1]
    fields = refs[2:7]
    strips, inner, kept, out, edges, sems = refs[7:]
    middle = pltpu.make_async_copy
    copies = [middle(inner.at[8:56, i], out.at[i, 8:56], sems.at[i]) for i in range(8)]
    for copy in copies:
        copy.start()
    low = low_of()
    lat = lax.axis_index("lat")
    even = jnp.broadcast_to(lat % 2, (8, LANES)) == 0
    floor = jnp.broadcast_to(lat, (8, LANES)) == 0

    def halo(is_north):
        def tile(i, h):
            a = got_a[i, :, h * LANES : (h + 1) * LANES]
            b = got_b[i, :, h * LANES : (h + 1) * LANES]
            if is_north:
                return jnp.where(even, a, b)
            return jnp.where(floor, 0.0, jnp.where(even, b, a))

        tiles = [[tile(i, h) for h in range(2)] for i in range(6)]
        corner = jnp.where(low, pltpu.roll(tiles[5][0], 4, 0), tiles[5][1])
        c_side, step_side, mv = [third_of(corner, 16 * i) for i in range(3)]
        row = {
            "c": tiles[2] + [c_side],
            "m": each(twice_low, tiles[3]) + [twice_low(mv)],
            "v": each(twice_low, tiles[4]) + [twice_high(mv)],
            "sy": each(twice_high, tiles[4]),
            "k": each(twice_low, tiles[5]),
        }
        return row, tiles[0], tiles[1] + [step_side], each(twice_high, tiles[3])

    for is_north in (False, True):
        outer, cell, step_in, rest = halo(is_north)
        start, beyond = (ROWS - 2, ROWS) if is_north else (0, -1)
        made, sides = {}, {}
        for row in range(*((ROWS - 4, ROWS) if is_north else (0, 4))):
            base = 16 * (row // 8)
            sides[row] = third_tile({n: strips[i, row % 8] for i, n in enumerate(GROUPS)}, base)

        def get(name, row):
            if name == "a":
                return made[row] if row in made else tiles_of(kept, KEPT.index(row), 3)
            if row == beyond:
                return outer[name]
            tiles = field_tiles(fields, name, row)
            return tiles if name == "sy" else tiles + [sides[row][name]]

        known = {2: [-x for x in step_in]} if is_north else {-2: step_in}
        results, flux, step = advect_rows(get, start, 2, known)
        made.update(zip((start, start + 1), results))
        face, sign = (1, -1.0) if is_north else (-1, 1.0)
        made[beyond] = each(
            lambda q, g, s, t, f, o: (q + g * median(s, sign * t) - sign * f) * o,
            cell, rest, step_in, step[face], flux[face], outer["m"],
        )
        final = ROWS - 3 if is_north else 0
        base = ROWS - 8 if is_north else 0
        done = {final + j: x for j, x in enumerate(diffuse_rows(get, final, 3))}
        for h in range(2):
            stack = [done[j][h] if j in done else inner[j, :, h * LANES : (h + 1) * LANES] for j in range(base, base + 8)]
            edges[int(is_north), :, :, h * LANES : (h + 1) * LANES] = jnp.transpose(jnp.stack(stack), (1, 0, 2))
        copy = middle(edges.at[int(is_north)], out.at[:, base : base + 8], sems.at[8 + int(is_north)])
        copy.start()
        copies.append(copy)
    for copy in copies:
        copy.wait()


def call(kernel, shapes, *operands, **options):
    return pl.pallas_call(
        kernel,
        out_shape=[jax.ShapeDtypeStruct(s, F32) for s in shapes],
        in_specs=[VMEM] * len(operands),
        out_specs=[VMEM] * len(shapes),
        compiler_params=pltpu.CompilerParams(vmem_limit_bytes=LIMIT),
        **options,
    )(*operands)


def make(lons, lats):
    def spot(lon, lat):
        return (lon % lons) * lats + lat

    near = [(spot(i, j), spot(i ^ 1, j)) for i in range(lons) for j in range(lats)]
    far = [(spot(i, j), spot(i + 1 if i % 2 else i - 1, j)) for i in range(lons) for j in range(lats)]
    pair_a = [(spot(i, j), spot(i, j ^ 1)) for i in range(lons) for j in range(lats)]
    pair_b = []
    for i in range(lons):
        for j in range(lats):
            if j == 0:
                pair_b.append((spot(i, j), spot(i ^ 1, j)))
            elif j == lats - 1:
                pair_b.append((spot(i, j), spot(lons - 1 - i, j)))
            else:
                pair_b.append((spot(i, j), spot(i, j + 1 if j % 2 else j - 1)))

    def move(x, route):
        return lax.ppermute(x, ("lon", "lat"), route)

    def shards(tracers, velocity, slopes, diffusivity, sea_mask):
        plane = lambda x: x.reshape(-1, ROWS, 2 * LANES)
        arrays = [plane(tracers), plane(velocity), plane(slopes), diffusivity, sea_mask]
        arrays = [pltpu.with_memory_space_constraint(x, pltpu.HBM) for x in arrays]
        full, side = (ROWS, 8, 2 * LANES), (8, 8, LANES)
        *held, to_near, to_far, own, spare = pl.pallas_call(
            pack_kernel,
            out_shape=[jax.ShapeDtypeStruct(x.shape, x.dtype) for x in arrays]
            + [jax.ShapeDtypeStruct(shape, F32) for shape in [(4, 8, LANES)] * 2 + [side] * 2],
            in_specs=[pl.BlockSpec(memory_space=pltpu.HBM)] * 5,
            out_specs=[VMEM] * 9,
            scratch_shapes=[pltpu.SemaphoreType.DMA((CHUNKS, 6))],
            compiler_params=pltpu.CompilerParams(vmem_limit_bytes=LIMIT),
        )(*arrays)
        far_got, near_got = move(to_far, far), move(to_near, near)
        *rows, advected, made_a, made_b = call(
            advect_kernel, [full] * 6 + [(6, 8, 2 * LANES)] * 2, *held,
            cost_estimate=pl.CostEstimate(flops=10**7, bytes_accessed=6 * 10**6, transcendentals=0),
        )
        send_a, send_b = call(
            edge_kernel, [(6, 8, 2 * LANES)] * 2, far_got, near_got, own, spare, made_a, made_b,
            input_output_aliases={4: 0, 5: 1},
        )
        got_a, got_b = move(send_a, pair_a), move(send_b, pair_b)
        inner, kept, strips, rows[3] = call(
            interior_kernel, [full, (4, 8, 3 * LANES), (4,) + side, full],
            *rows, advected, far_got, near_got, own, spare, held[2],
            scratch_shapes=[pltpu.VMEM((3,) + side, F32)],
            cost_estimate=pl.CostEstimate(flops=2 * 10**7, bytes_accessed=10**7, transcendentals=0),
        )
        out = pl.pallas_call(
            rim_kernel,
            out_shape=jax.ShapeDtypeStruct((8, ROWS, 2 * LANES), F32),
            in_specs=[VMEM] * 10,
            out_specs=pl.BlockSpec(memory_space=pl.ANY),
            scratch_shapes=[pltpu.VMEM((2, 8, 8, 2 * LANES), F32), pltpu.SemaphoreType.DMA((10,))],
            compiler_params=pltpu.CompilerParams(vmem_limit_bytes=LIMIT),
        )(got_a, got_b, *rows, strips, inner, kept)
        return out.reshape(tracers.shape)

    return shards


def solution(mesh):
    return jax.shard_map(
        make(mesh.shape["lon"], mesh.shape["lat"]),
        mesh=mesh,
        in_specs=(
            P(None, None, "lat", "lon"),
            P(None, None, "lat", "lon"),
            P(None, None, "lat", "lon"),
            P(None, "lat", "lon"),
            P(None, "lat", "lon"),
        ),
        out_specs=P(None, None, "lat", "lon"),
        check_vma=False,
    )
```

```python
import jax
import jax.numpy as jnp
from jax import lax
from jax.experimental import pallas as pl
from jax.experimental.pallas import tpu as pltpu
from jax.sharding import PartitionSpec as P


ROWS = 64
LANES = 128
F32 = jnp.float32
VMEM = pl.BlockSpec(memory_space=pltpu.VMEM)
LIMIT = 16 * 1024 * 1024
CHUNKS = 2
GROUPS = ("c", "mu", "vw", "sk")
KEPT = (2, 3, ROWS - 4, ROWS - 3)


def lane_of():
    return lax.broadcasted_iota(jnp.int32, (8, LANES), 1)


def low_of():
    return lax.broadcasted_iota(jnp.int32, (8, LANES), 0) < 4


def twice_low(x):
    return jnp.where(low_of(), x, pltpu.roll(x, 4, 0))


def twice_high(x):
    return jnp.where(low_of(), pltpu.roll(x, 4, 0), x)


def field_half(rows, name, row, h):
    which, turn = {
        "u": (1, twice_low), "v": (1, twice_high), "w": (2, twice_low),
        "sx": (3, twice_low), "sy": (3, twice_high), "m": (2, twice_high), "k": (4, None),
    }.get(name, (0, None))
    value = rows[which][row, :, h * LANES : (h + 1) * LANES]
    return turn(value) if turn else value


def field_tiles(rows, name, row):
    return [field_half(rows, name, row, h) for h in range(2)]


def row_planes(held, span, h, both=True):
    tracer, velocity, slope, kappa, mask = held
    wide = slice(h * LANES, (h + 1) * LANES)
    return [
        tracer[:, span, wide], velocity[0:8, span, wide], velocity[4:12, span, wide],
        slope[:, span, wide] if both else jnp.concatenate([slope[0:4, span, wide]] * 2, axis=0),
        jnp.concatenate([mask[:, span, wide].astype(F32), kappa[:, span, wide]], axis=0),
    ]


def scaled(groups):
    c, uv, vw, s, mk = groups
    return c, uv, vw, s * 0.125, mk * jnp.where(low_of(), 1.0, 0.5)


def pack_kernel(*refs):
    arrays, held, (to_near, to_far, own, spare), sems = refs[:5], refs[5:10], refs[10:14], refs[14]
    copies = []
    for chunk in range(CHUNKS):
        span = slice(chunk * ROWS // CHUNKS, (chunk + 1) * ROWS // CHUNKS)
        ends = [array.shape[0] for array in arrays]
        ends[2] = 4
        copies.append(
            [
                pltpu.make_async_copy(array.at[:end, span], hold.at[:end, span], sems.at[chunk, i])
                for i, (array, hold, end) in enumerate(zip(arrays, held, ends))
            ]
        )
        for copy in copies[-1]:
            copy.start()
    northward = pltpu.make_async_copy(arrays[2].at[4:], held[2].at[4:], sems.at[0, 5])
    northward.start()
    lane, low = lane_of(), low_of()
    inside = lax.broadcasted_iota(jnp.int32, (8, 8, LANES), 2) < 64
    first, second = [None] * 8, [None] * 8
    for part in range(8):
        if part * CHUNKS % 8 == 0:
            for copy in copies[part * CHUNKS // 8]:
                copy.wait()
        span = slice(8 * part, 8 * part + 8)
        rims = []
        for left, right in zip(*[row_planes(held, span, h, False) for h in range(2)]):
            rims.append(jnp.transpose(jnp.where(inside, left, right), (1, 0, 2)))
        base = 16 * part
        before, half = lane < base, lane < base + 8
        for g in range(8):
            c, uv, vw, s, mk = scaled([x[g] for x in rims])
            mu = jnp.where(low, mk, pltpu.roll(uv, 4, 0))
            sk = jnp.where(low, s, mk)
            one = jnp.where(half, pltpu.roll(c, (base + 4) % LANES, 1), pltpu.roll(mu, (base + 12) % LANES, 1))
            two = jnp.where(half, pltpu.roll(vw, (base + 4) % LANES, 1), pltpu.roll(sk, (base + 12) % LANES, 1))
            first[g] = jnp.where(before, first[g], one) if part else one
            second[g] = jnp.where(before, second[g], two) if part else two
    for g in range(8):
        own[g] = first[g]
        spare[g] = second[g]
    slot = lane % 8
    to_east = jnp.broadcast_to(lax.axis_index("lon") % 2, (8, LANES)) == 0
    for pair in range(4):
        east, west = [], []
        for g in (2 * pair, 2 * pair + 1):
            east.append(jnp.where(slot == 0, pltpu.roll(second[g], LANES - 3, 1), first[g]))
            west.append(jnp.where(slot == 7, pltpu.roll(second[g], 3, 1), first[g]))
        eastern = jnp.where(slot < 4, east[0], pltpu.roll(east[1], 4, 1))
        western = jnp.where(slot < 4, pltpu.roll(west[0], LANES - 4, 1), west[1])
        to_near[pair] = jnp.where(to_east, eastern, western)
        to_far[pair] = jnp.where(to_east, western, eastern)
    northward.wait()


def field_planes(held, span, h):
    tracer, velocity, slope, kappa, mask = held
    wide = slice(h * LANES, (h + 1) * LANES)
    return [
        tracer[:, span, wide], velocity[0:8, span, wide],
        jnp.concatenate([velocity[8:12, span, wide], mask[:, span, wide].astype(F32)], axis=0),
        slope[:, span, wide] * 0.125, jnp.concatenate([kappa[:, span, wide] * 0.5] * 2, axis=0),
    ]


def advect_kernel(*refs):
    held, rows, advected, send_a, send_b = refs[:5], refs[5:10], refs[10], refs[11], refs[12]
    for part in range(8):
        for h in range(2):
            span = slice(8 * part, 8 * part + 8)
            for i, x in enumerate(field_planes(held, span, h)):
                if i < 3 or part in (0, 7):
                    rows[i][span, :, h * LANES : (h + 1) * LANES] = jnp.transpose(x, (1, 0, 2))
    put_messages(rows, send_a, send_b)
    get = lambda name, row: field_tiles(rows, name, row)

    def advect_block(block, carry):
        first = 2 + 15 * block
        for j, tiles in enumerate(advect_rows(get, first, 15)[0]):
            for t in range(2):
                advected[first + j, :, t * LANES : (t + 1) * LANES] = tiles[t]
        return carry

    lax.fori_loop(0, 4, advect_block, 0)


def put_messages(rows, send_a, send_b):
    lane, low = lane_of(), low_of()
    lat = lax.axis_index("lat")

    first, last = lane < 2, lane >= LANES - 2

    def message(top):
        part = lambda name, q: field_tiles(rows, name, ROWS - 1 - q if top else q)
        outward = 1.0 if top else -1.0
        c, m, v = [part("c", q) for q in range(3)], [part("m", q) for q in range(3)], [part("v", q) for q in range(2)]
        half = each(lambda x: 0.5 * x, m[1])
        opened = each(jnp.multiply, half, m[0])
        step = each(lambda a, b, o: (a - b) * o, c[0], c[1], opened)
        inner = each(lambda a, b, x, y: (a - b) * (x * y), c[1], c[2], half, m[2])
        speed = each(lambda a, b, o: (a + b) * o * outward, v[0], v[1], opened)
        inflow = each(
            lambda a, b, s, x, y: s * jnp.where(s >= 0.0, a, b)
            + jnp.where(s >= 0.0, (jnp.abs(s) - s * s) * median(x, y), 0.0),
            c[1], c[0], speed, step, inner,
        )
        rest = each(lambda s: jnp.where(s >= 0.0, 0.0, jnp.abs(s) - s * s), speed)
        halved = each(lambda x: 0.5 * x, m[0])
        flux_x = zonal_flux(c[0], m[0], halved, part("u", 0))
        across = each(lambda f, g: f - g, flux_x, minus(flux_x))
        across = [jnp.where(first, 0.0, across[0]), jnp.where(last, 0.0, across[1])]
        down = each(vertical_divergence, c[0], halved, part("w", 0))
        cell = each(lambda a, x, z, f: a - x - z + f, c[0], across, down, inflow)
        pair = lambda a, b: each(lambda x, y: jnp.where(low, x, y), a, b)
        return [cell, step, c[0], pair(m[0], rest), pair(v[0], part("sy", 0)), part("k", 0)]

    backward = LANES - 1 - lane
    flip = lambda x: jnp.take_along_axis(x, backward, axis=1, mode="promise_in_bounds")
    is_even = jnp.broadcast_to(lat % 2, (8, LANES)) == 0
    folds = jnp.broadcast_to(lat, (8, LANES)) == lax.axis_size("lat") - 1
    north, south = message(True), message(False)
    for i, (top, bottom) in enumerate(zip(north, south)):
        for h in range(2):
            wide = slice(h * LANES, (h + 1) * LANES)
            turned = flip(top[1 - h])
            if i == 4:
                turned = -turned
            send_a[i, :, wide] = jnp.where(is_even, top[h], bottom[h])
            send_b[i, :, wide] = jnp.where(folds, turned, jnp.where(is_even, bottom[h], top[h]))


def strip_at(g, which, late, from_far, from_near, own, spare):
    slot = lane_of() % 16
    far_is_west = jnp.broadcast_to(lax.axis_index("lon") % 2, (8, LANES)) == 0
    near, far, mine = from_near[g // 2], from_far[g // 2], (spare if which else own)[g]
    east, west = jnp.where(far_is_west, near, far), jnp.where(far_is_west, far, near)
    shift = lambda x, by: pltpu.roll(x, by % LANES, 1) if by else x
    odd = 4 * (g % 2)
    east = shift(east, (1 if which else 4) - odd - 8 * late)
    west = shift(west, (9 if which else 6) - odd - 8 * late)
    inner = jnp.where(slot < 4, shift(mine, -8 * late), east)
    outer = jnp.where(slot < 10, west, shift(mine, 6 - 8 * late))
    return jnp.where(slot < 7, inner, outer)


def edge_kernel(*refs):
    sources, made, (send_a, send_b) = refs[:4], refs[4:6], refs[6:]
    lane, low = lane_of(), low_of()
    lat = lax.axis_index("lat")
    strip = lambda i, g: strip_at(g, i // 2, i % 2, *sources)

    def beside(g, inner):
        c, mu, vw = strip(0, g), strip(1, g), strip(2, g)
        shifts = (1, 0, LANES - 1, LANES - 2)
        moved = lambda x: [pltpu.roll(x, by, 1) if by else x for by in shifts]
        cells, pairs = moved(c), moved(mu)
        m = [twice_low(x) for x in pairs]
        half = [0.5 * x for x in m]
        steps = [(cells[n + 1] - cells[n]) * (half[n] * m[n + 1]) for n in range(3)]
        speed = face_speed(twice_high(pairs[1]), twice_high(pairs[2]), half[1] * m[2])
        flux = face_flux(cells[1], cells[2], speed, *steps)
        step = (c - strip(0, inner)) * (half[1] * twice_low(strip(1, inner)))
        return flux, c, step, jnp.where(low, mu, pltpu.roll(vw, 4, 0))

    def placed(values, base, backward):
        if backward:
            take = lambda x, at: jnp.take_along_axis(x, (base + at + LANES - lane) & (LANES - 1), axis=1, mode="promise_in_bounds")
            places = [(3, 2), (9, 8), 13, 29, 45]
        else:
            take = lambda x, at: pltpu.roll(x, (at - base) % LANES, 1) if (at - base) % LANES else x
            places = [(118, 119), (124, 125), 0, 16, 32]
        across = [take(values[0], at) - take(values[0], before) for at, before in places[:2]]
        c, step, mv = [take(x, at) for x, at in zip(values[1:], places[2:])]
        if backward:
            mv = jnp.where(low, mv, -mv)
        return across + [jnp.where(lane < 16, c, jnp.where(lane < 32, step, mv))]

    south, north = beside(0, 1), beside(7, 6)
    south, north, turned = placed(south, 0, False), placed(north, 112, False), placed(north, 112, True)

    def store(source, ref, left, right, packed):
        ref[0, :, :LANES] = source[0, :, :LANES] - jnp.where(lane < 2, left, 0.0)
        ref[0, :, LANES:] = source[0, :, LANES:] - jnp.where(lane >= LANES - 2, right, 0.0)
        ref[5, :, :LANES] = jnp.where(low, source[5, :, :LANES], pltpu.roll(packed, 4, 0))
        ref[5, :, LANES:] = jnp.where(low, source[5, :, LANES:], packed)

    is_even = jnp.broadcast_to(lat % 2, (8, LANES)) == 0
    folds = jnp.broadcast_to(lat, (8, LANES)) == lax.axis_size("lat") - 1
    store(made[0], send_a, *[jnp.where(is_even, n, s) for n, s in zip(north, south)])
    store(made[1], send_b, *[jnp.where(folds, t, jnp.where(is_even, s, n)) for n, s, t in zip(north, south, turned)])


def split_groups(groups):
    return {
        "c": groups["c"],
        "m": twice_low(groups["mu"]),
        "u": twice_high(groups["mu"]),
        "v": twice_low(groups["vw"]),
        "w": twice_high(groups["vw"]),
        "sx": twice_low(groups["sk"]),
        "k": twice_high(groups["sk"]),
    }


def third_of(x, base):
    east, west = pltpu.roll(x, (2 * LANES - 4 - base) % LANES, 1), pltpu.roll(x, (2 * LANES - 10 - base) % LANES, 1)
    return jnp.where(lane_of() < 64, east, west)


def third_tile(groups, base):
    return split_groups({n: third_of(groups[n], base) for n in GROUPS})


def plus(tiles):
    last = lane_of() == LANES - 1
    turned = [pltpu.roll(t, LANES - 1, 1) for t in tiles]
    if len(tiles) == 1:
        return turned
    return [jnp.where(last, turned[(i + 1) % len(tiles)], turned[i]) for i in range(len(tiles))]


def minus(tiles, count=3, west=None):
    first = lane_of() == 0
    turned = [pltpu.roll(t, 1, 1) for t in tiles]
    if len(tiles) == 1:
        return turned
    before = [turned[-1] if west is None else west] + turned[:-1]
    return [jnp.where(first, before[i], turned[i]) for i in range(min(count, len(tiles)))]


def each(function, *lists):
    return [function(*values) for values in zip(*lists)]


def below(x):
    return pltpu.roll(x, 7, 0)


def above(x):
    return pltpu.roll(x, 1, 0)


def median(step, upwind):
    return jnp.minimum(jnp.maximum(upwind, jnp.minimum(step, 0.0)), jnp.maximum(step, 0.0))


def face_flux(here, there, speed, back, step, ahead):
    positive = speed >= 0.0
    upwind = jnp.where(positive, back, ahead)
    size = jnp.abs(speed)
    return speed * jnp.where(positive, here, there) + (size - size * size) * median(step, upwind)


def zonal_flux(c, m, half, u):
    east = plus(c)
    opened = each(jnp.multiply, half, plus(m))
    speed = each(face_speed, u, plus(u), opened)
    step = each(lambda a, b, o: (b - a) * o, c, east, opened)
    return each(face_flux, c, east, speed, minus(step), step, plus(step))


def vertical_divergence(value, half, down):
    opened = open_below(half)
    under = below(value)
    step = (under - value) * opened
    flux = face_flux(value, under, face_speed(down, below(down), opened), above(step), step, below(step))
    return flux - above(flux)


def not_bottom():
    return lax.broadcasted_iota(jnp.int32, (8, LANES), 0) % 4 != 3


def open_below(marker):
    return jnp.where(not_bottom(), below(marker), 0.0)


def face_speed(one, two, half_open):
    return (one + two) * half_open


def advect_rows(get, first, count, known=()):
    known = dict(known)
    low, high = (-1 if -2 in known else -2), (count + 1 if count in known else count + 2)
    c = {j: get("c", first + j) for j in range(low, high)}
    m = {j: get("m", first + j) for j in range(low, high)}
    v = {j: get("v", first + j) for j in range(-1, count + 1)}
    half = {j: each(lambda x: 0.5 * x, m[j]) for j in range(low, high)}
    opened = {j: each(jnp.multiply, half[j], m[j + 1]) for j in range(low, high - 1)}
    step = {j: each(lambda a, b, o: (b - a) * o, c[j], c[j + 1], opened[j]) for j in range(low, high - 1)}
    step.update(known)
    flux = {}
    for j in range(-1, count):
        speed = each(face_speed, v[j], v[j + 1], opened[j])
        flux[j] = each(face_flux, c[j], c[j + 1], speed, step[j - 1], step[j], step[j + 1])
    result = []
    for j in range(count):
        flux_x = zonal_flux(c[j], m[j], half[j], get("u", first + j))
        total = each(lambda f, g, a, b: (f - g) + (a - b), flux_x, minus(flux_x), flux[j], flux[j - 1])
        down = each(vertical_divergence, c[j], half[j], get("w", first + j))
        result.append(each(lambda a, x, z, o: (a - x - z) * o, c[j], total, down, m[j]))
    return result, flux, step


def slope_flux(k1, k2, opened, step, s1, s2, z1, z2):
    return (k1 + k2) * opened * (step + (s1 + s2) * (z1 + z2))


def eastward(a, m, k, sx, twice_z):
    opened = each(jnp.multiply, m, plus(m))
    step = each(lambda x, y, o: (y - x) * o, a, plus(a), opened)
    return step, each(slope_flux, k, plus(k), opened, step, sx, plus(sx), twice_z, plus(twice_z))


def diffuse_rows(get, first, count, beside=None):
    a, m, k, sy, step_z, twice_z, step_y, flux_y = [{} for _ in range(8)]
    result = []
    last = lane_of() == LANES - 1

    def row_result(j):
        sx = get("sx", first + j)
        step_x, flux_x = eastward(a[j], m[j], k[j], sx, twice_z[j])
        west = [None, None]
        if beside:
            east, west = beside(first + j)
            step_x = [step_x[0], jnp.where(last, east[0], step_x[1])]
            flux_x = [flux_x[0], jnp.where(last, east[1], flux_x[1])]
        twice_x = each(jnp.add, step_x, minus(step_x, 2, west[0]))
        twice_y = each(jnp.add, step_y[j - 1], step_y[j])
        total = each(lambda f, g, p, q: (f - g) + (p - q), flux_x, minus(flux_x, 2, west[1]), flux_y[j], flux_y[j - 1])

        def finish(value, marker, kappa, east, north, tx, ty, sz, across):
            face_east, face_north = east + below(east), north + below(north)
            flux_z = (kappa + below(kappa)) * open_below(marker) * (
                face_east * (tx + below(tx)) + face_north * (ty + below(ty))
                + (face_east * face_east + face_north * face_north) * (16.0 * sz)
            )
            return (value + across + (flux_z - above(flux_z))) * marker

        result.append(each(finish, a[j][:2], m[j], k[j], sx, sy[j], twice_x, twice_y, step_z[j], total))

    for j in range(-1, count + 1):
        a[j], m[j], k[j], sy[j] = [get(name, first + j) for name in ("a", "m", "k", "sy")]
        wide = 3 if 0 <= j < count else 2
        step_z[j] = each(lambda x, o: (below(x) - x) * open_below(o), a[j][:wide], m[j])
        twice_z[j] = each(lambda x: above(x) + x, step_z[j])
        if j >= 0:
            opened = each(jnp.multiply, m[j - 1][:2], m[j][:2])
            step_y[j - 1] = each(lambda x, y, o: (y - x) * o, a[j - 1][:2], a[j][:2], opened)
            flux_y[j - 1] = each(
                slope_flux, k[j - 1], k[j], opened, step_y[j - 1], sy[j - 1], sy[j], twice_z[j - 1], twice_z[j]
            )
        if j >= 1:
            row_result(j - 1)
    return result


def tiles_of(ref, row, count):
    return [ref[row, :, t * LANES : (t + 1) * LANES] for t in range(count)]


def interior_kernel(*refs):
    rows, advected, sources, slope, kappa = refs[:5], refs[5], refs[6:10], refs[10], refs[11]
    out, kept, strips, slope_rows, kappa_rows, narrow = refs[12:]
    rows = rows[:3] + (slope_rows, kappa_rows)
    for part in range(8):
        for h in range(2):
            span, wide = slice(8 * part, 8 * part + 8), slice(h * LANES, (h + 1) * LANES)
            slope_rows[span, :, wide] = jnp.transpose(slope[:, span, wide] * 0.125, (1, 0, 2))
            twice = jnp.concatenate([kappa[:, span, wide] * 0.5] * 2, axis=0)
            kappa_rows[span, :, wide] = jnp.transpose(twice, (1, 0, 2))
    lane = lane_of()
    near_east, near_west = lane >= LANES - 2, lane < 2

    full = []
    for g in range(8):
        groups = {n: strip_at(g, i // 2, i % 2, *sources) for i, n in enumerate(GROUPS)}
        full.append(split_groups(groups))
        for i, n in enumerate(GROUPS):
            strips[i, g] = groups[n]

    def get_strip(name, g):
        x = full[g % 8][name]
        return [x if 0 <= g < 8 else pltpu.roll(x, 16 if g < 0 else LANES - 16, 1)]

    for g, (a,) in enumerate(advect_rows(get_strip, 0, 8)[0]):
        part = full[g]
        step_z = (below(a) - a) * open_below(part["m"])
        step, flux = eastward([a], [part["m"]], [part["k"]], [part["sx"]], [above(step_z) + step_z])
        narrow[0, g], narrow[1, g], narrow[2, g] = a, step[0], flux[0]

    def lanes_to(which, row, lane_from, lane_to):
        part = row // 8
        return pltpu.roll(narrow[which, row - 8 * part], lax.rem(2 * LANES + lane_to - lane_from - 16 * part, LANES), 1)

    def get(name, row):
        if name != "a":
            return field_tiles(rows, name, row)
        left, right = tiles_of(advected, row, 2)
        return [
            jnp.where(near_west, lanes_to(0, row, 10, 0), left),
            jnp.where(near_east, lanes_to(0, row, 3, LANES - 1), right),
        ]

    def beside(row):
        return [lanes_to(i, row, 3, LANES - 1) for i in (1, 2)], [lanes_to(i, row, 9, 0) for i in (1, 2)]

    for i, row in enumerate(KEPT):
        third = jnp.where(lane < 64, lanes_to(0, row, 4, 0), lanes_to(0, row, 9, LANES - 1))
        for t, tile in enumerate(get("a", row) + [third]):
            kept[i, :, t * LANES : (t + 1) * LANES] = tile

    def diffuse_block(block, carry):
        first = jnp.minimum(3 + 10 * block, ROWS - 3 - 10)
        for j, tiles in enumerate(diffuse_rows(get, first, 10, beside)):
            for t in range(2):
                out[first + j, :, t * LANES : (t + 1) * LANES] = tiles[t]
        return carry

    lax.fori_loop(0, 6, diffuse_block, 0)


def rim_kernel(*refs):
    got_a, got_b = refs[0], refs[1]
    fields = refs[2:7]
    strips, inner, kept, out, edges, sems = refs[7:]
    middle = pltpu.make_async_copy
    copies = [middle(inner.at[8:56, i], out.at[i, 8:56], sems.at[i]) for i in range(8)]
    for copy in copies:
        copy.start()
    low = low_of()
    lat = lax.axis_index("lat")
    even = jnp.broadcast_to(lat % 2, (8, LANES)) == 0
    floor = jnp.broadcast_to(lat, (8, LANES)) == 0

    def halo(is_north):
        def tile(i, h):
            a = got_a[i, :, h * LANES : (h + 1) * LANES]
            b = got_b[i, :, h * LANES : (h + 1) * LANES]
            if is_north:
                return jnp.where(even, a, b)
            return jnp.where(floor, 0.0, jnp.where(even, b, a))

        tiles = [[tile(i, h) for h in range(2)] for i in range(6)]
        corner = jnp.where(low, pltpu.roll(tiles[5][0], 4, 0), tiles[5][1])
        c_side, step_side, mv = [third_of(corner, 16 * i) for i in range(3)]
        row = {
            "c": tiles[2] + [c_side],
            "m": each(twice_low, tiles[3]) + [twice_low(mv)],
            "v": each(twice_low, tiles[4]) + [twice_high(mv)],
            "sy": each(twice_high, tiles[4]),
            "k": each(twice_low, tiles[5]),
        }
        return row, tiles[0], tiles[1] + [step_side], each(twice_high, tiles[3])

    for is_north in (False, True):
        outer, cell, step_in, rest = halo(is_north)
        start, beyond = (ROWS - 2, ROWS) if is_north else (0, -1)
        made, sides = {}, {}
        for row in range(*((ROWS - 4, ROWS) if is_north else (0, 4))):
            base = 16 * (row // 8)
            sides[row] = third_tile({n: strips[i, row % 8] for i, n in enumerate(GROUPS)}, base)

        def get(name, row):
            if name == "a":
                return made[row] if row in made else tiles_of(kept, KEPT.index(row), 3)
            if row == beyond:
                return outer[name]
            tiles = field_tiles(fields, name, row)
            return tiles if name == "sy" else tiles + [sides[row][name]]

        known = {2: [-x for x in step_in]} if is_north else {-2: step_in}
        results, flux, step = advect_rows(get, start, 2, known)
        made.update(zip((start, start + 1), results))
        face, sign = (1, -1.0) if is_north else (-1, 1.0)
        made[beyond] = each(
            lambda q, g, s, t, f, o: (q + g * median(s, sign * t) - sign * f) * o,
            cell, rest, step_in, step[face], flux[face], outer["m"],
        )
        final = ROWS - 3 if is_north else 0
        base = ROWS - 8 if is_north else 0
        done = {final + j: x for j, x in enumerate(diffuse_rows(get, final, 3))}
        for h in range(2):
            stack = [done[j][h] if j in done else inner[j, :, h * LANES : (h + 1) * LANES] for j in range(base, base + 8)]
            edges[int(is_north), :, :, h * LANES : (h + 1) * LANES] = jnp.transpose(jnp.stack(stack), (1, 0, 2))
        copy = middle(edges.at[int(is_north)], out.at[:, base : base + 8], sems.at[8 + int(is_north)])
        copy.start()
        copies.append(copy)
    for copy in copies:
        copy.wait()


def call(kernel, shapes, *operands, **options):
    return pl.pallas_call(
        kernel,
        out_shape=[jax.ShapeDtypeStruct(s, F32) for s in shapes],
        in_specs=[VMEM] * len(operands),
        out_specs=[VMEM] * len(shapes),
        compiler_params=pltpu.CompilerParams(vmem_limit_bytes=LIMIT),
        **options,
    )(*operands)


def make(lons, lats):
    def spot(lon, lat):
        return (lon % lons) * lats + lat

    near = [(spot(i, j), spot(i ^ 1, j)) for i in range(lons) for j in range(lats)]
    far = [(spot(i, j), spot(i + 1 if i % 2 else i - 1, j)) for i in range(lons) for j in range(lats)]
    pair_a = [(spot(i, j), spot(i, j ^ 1)) for i in range(lons) for j in range(lats)]
    pair_b = []
    for i in range(lons):
        for j in range(lats):
            if j == 0:
                pair_b.append((spot(i, j), spot(i ^ 1, j)))
            elif j == lats - 1:
                pair_b.append((spot(i, j), spot(lons - 1 - i, j)))
            else:
                pair_b.append((spot(i, j), spot(i, j + 1 if j % 2 else j - 1)))

    def move(x, route):
        return lax.ppermute(x, ("lon", "lat"), route)

    def shards(tracers, velocity, slopes, diffusivity, sea_mask):
        plane = lambda x: x.reshape(-1, ROWS, 2 * LANES)
        arrays = [plane(tracers), plane(velocity), plane(slopes), diffusivity, sea_mask]
        arrays = [pltpu.with_memory_space_constraint(x, pltpu.HBM) for x in arrays]
        full, side = (ROWS, 8, 2 * LANES), (8, 8, LANES)
        *held, to_near, to_far, own, spare = pl.pallas_call(
            pack_kernel,
            out_shape=[jax.ShapeDtypeStruct(x.shape, x.dtype) for x in arrays]
            + [jax.ShapeDtypeStruct(shape, F32) for shape in [(4, 8, LANES)] * 2 + [side] * 2],
            in_specs=[pl.BlockSpec(memory_space=pltpu.HBM)] * 5,
            out_specs=[VMEM] * 9,
            scratch_shapes=[pltpu.SemaphoreType.DMA((CHUNKS, 6))],
            compiler_params=pltpu.CompilerParams(vmem_limit_bytes=LIMIT),
        )(*arrays)
        far_got, near_got = move(to_far, far), move(to_near, near)
        *rows, advected, made_a, made_b = call(
            advect_kernel, [full] * 6 + [(6, 8, 2 * LANES)] * 2, *held,
            cost_estimate=pl.CostEstimate(flops=10**7, bytes_accessed=6 * 10**6, transcendentals=0),
        )
        send_a, send_b = call(
            edge_kernel, [(6, 8, 2 * LANES)] * 2, far_got, near_got, own, spare, made_a, made_b,
            input_output_aliases={4: 0, 5: 1},
        )
        got_a, got_b = move(send_a, pair_a), move(send_b, pair_b)
        inner, kept, strips, rows[3], rows[4] = call(
            interior_kernel, [full, (4, 8, 3 * LANES), (4,) + side, full, full],
            *rows, advected, far_got, near_got, own, spare, held[2], held[3],
            scratch_shapes=[pltpu.VMEM((3,) + side, F32)],
            cost_estimate=pl.CostEstimate(flops=2 * 10**7, bytes_accessed=10**7, transcendentals=0),
        )
        out = pl.pallas_call(
            rim_kernel,
            out_shape=jax.ShapeDtypeStruct((8, ROWS, 2 * LANES), F32),
            in_specs=[VMEM] * 10,
            out_specs=pl.BlockSpec(memory_space=pl.ANY),
            scratch_shapes=[pltpu.VMEM((2, 8, 8, 2 * LANES), F32), pltpu.SemaphoreType.DMA((10,))],
            compiler_params=pltpu.CompilerParams(vmem_limit_bytes=LIMIT),
        )(got_a, got_b, *rows, strips, inner, kept)
        return out.reshape(tracers.shape)

    return shards


def solution(mesh):
    return jax.shard_map(
        make(mesh.shape["lon"], mesh.shape["lat"]),
        mesh=mesh,
        in_specs=(
            P(None, None, "lat", "lon"),
            P(None, None, "lat", "lon"),
            P(None, None, "lat", "lon"),
            P(None, "lat", "lon"),
            P(None, "lat", "lon"),
        ),
        out_specs=P(None, None, "lat", "lon"),
        check_vma=False,
    )
```

```python
import jax
import jax.numpy as jnp
from jax import lax
from jax.experimental import pallas as pl
from jax.experimental.pallas import tpu as pltpu
from jax.sharding import PartitionSpec as P


ROWS = 64
LANES = 128
F32 = jnp.float32
VMEM = pl.BlockSpec(memory_space=pltpu.VMEM)
LIMIT = 16 * 1024 * 1024
CHUNKS = 1
GROUPS = ("c", "mu", "vw", "sk")
KEPT = (2, 3, ROWS - 4, ROWS - 3)


def lane_of():
    return lax.broadcasted_iota(jnp.int32, (8, LANES), 1)


def low_of():
    return lax.broadcasted_iota(jnp.int32, (8, LANES), 0) < 4


def twice_low(x):
    return jnp.where(low_of(), x, pltpu.roll(x, 4, 0))


def twice_high(x):
    return jnp.where(low_of(), pltpu.roll(x, 4, 0), x)


def field_half(rows, name, row, h):
    which, turn = {
        "u": (1, twice_low), "v": (1, twice_high), "w": (2, twice_high),
        "sx": (3, twice_low), "sy": (3, twice_high), "m": (4, twice_low), "k": (4, twice_high),
    }.get(name, (0, None))
    value = rows[which][row, :, h * LANES : (h + 1) * LANES]
    return turn(value) if turn else value


def field_tiles(rows, name, row):
    return [field_half(rows, name, row, h) for h in range(2)]


def row_planes(held, span, h, both=True):
    tracer, velocity, slope, kappa, mask = held
    wide = slice(h * LANES, (h + 1) * LANES)
    return [
        tracer[:, span, wide], velocity[0:8, span, wide], velocity[4:12, span, wide],
        slope[:, span, wide] if both else jnp.concatenate([slope[0:4, span, wide]] * 2, axis=0),
        jnp.concatenate([mask[:, span, wide].astype(F32), kappa[:, span, wide]], axis=0),
    ]


def scaled(groups):
    c, uv, vw, s, mk = groups
    return c, uv, vw, s * 0.125, mk * jnp.where(low_of(), 1.0, 0.5)


def pack_kernel(*refs):
    arrays, held, (to_near, to_far, own, spare), sems = refs[:5], refs[5:10], refs[10:14], refs[14]
    copies = []
    for chunk in range(CHUNKS):
        span = slice(chunk * ROWS // CHUNKS, (chunk + 1) * ROWS // CHUNKS)
        ends = [array.shape[0] for array in arrays]
        ends[2] = 4
        copies.append(
            [
                pltpu.make_async_copy(array.at[:end, span], hold.at[:end, span], sems.at[chunk, i])
                for i, (array, hold, end) in enumerate(zip(arrays, held, ends))
            ]
        )
        for copy in copies[-1]:
            copy.start()
    northward = pltpu.make_async_copy(arrays[2].at[4:], held[2].at[4:], sems.at[0, 5])
    northward.start()
    lane, low = lane_of(), low_of()
    inside = lax.broadcasted_iota(jnp.int32, (8, 8, LANES), 2) < 64
    first, second = [None] * 8, [None] * 8
    for part in range(8):
        if part * CHUNKS % 8 == 0:
            for copy in copies[part * CHUNKS // 8]:
                copy.wait()
        span = slice(8 * part, 8 * part + 8)
        rims = []
        for left, right in zip(*[row_planes(held, span, h, False) for h in range(2)]):
            rims.append(jnp.transpose(jnp.where(inside, left, right), (1, 0, 2)))
        base = 16 * part
        before, half = lane < base, lane < base + 8
        for g in range(8):
            c, uv, vw, s, mk = scaled([x[g] for x in rims])
            mu = jnp.where(low, mk, pltpu.roll(uv, 4, 0))
            sk = jnp.where(low, s, mk)
            one = jnp.where(half, pltpu.roll(c, (base + 4) % LANES, 1), pltpu.roll(mu, (base + 12) % LANES, 1))
            two = jnp.where(half, pltpu.roll(vw, (base + 4) % LANES, 1), pltpu.roll(sk, (base + 12) % LANES, 1))
            first[g] = jnp.where(before, first[g], one) if part else one
            second[g] = jnp.where(before, second[g], two) if part else two
    for g in range(8):
        own[g] = first[g]
        spare[g] = second[g]
    slot = lane % 8
    to_east = jnp.broadcast_to(lax.axis_index("lon") % 2, (8, LANES)) == 0
    for pair in range(4):
        east, west = [], []
        for g in (2 * pair, 2 * pair + 1):
            east.append(jnp.where(slot == 0, pltpu.roll(second[g], LANES - 3, 1), first[g]))
            west.append(jnp.where(slot == 7, pltpu.roll(second[g], 3, 1), first[g]))
        eastern = jnp.where(slot < 4, east[0], pltpu.roll(east[1], 4, 1))
        western = jnp.where(slot < 4, pltpu.roll(west[0], LANES - 4, 1), west[1])
        to_near[pair] = jnp.where(to_east, eastern, western)
        to_far[pair] = jnp.where(to_east, western, eastern)
    northward.wait()


def advect_kernel(*refs):
    held, rows, advected, send_a, send_b = refs[:5], refs[5:10], refs[10], refs[11], refs[12]
    for part in range(8):
        for h in range(2):
            turned = [jnp.transpose(x, (1, 0, 2)) for x in row_planes(held, slice(8 * part, 8 * part + 8), h)]
            for g in range(8):
                for i, (ref, value) in enumerate(zip(rows, scaled([x[g] for x in turned]))):
                    if i != 3 or part in (0, 7):
                        ref[8 * part + g, :, h * LANES : (h + 1) * LANES] = value
    put_messages(rows, send_a, send_b)
    get = lambda name, row: field_tiles(rows, name, row)

    def advect_block(block, carry):
        first = 2 + 15 * block
        for j, tiles in enumerate(advect_rows(get, first, 15)[0]):
            for t in range(2):
                advected[first + j, :, t * LANES : (t + 1) * LANES] = tiles[t]
        return carry

    lax.fori_loop(0, 4, advect_block, 0)


def put_messages(rows, send_a, send_b):
    lane, low = lane_of(), low_of()
    lat = lax.axis_index("lat")

    first, last = lane < 2, lane >= LANES - 2

    def message(top):
        part = lambda name, q: field_tiles(rows, name, ROWS - 1 - q if top else q)
        outward = 1.0 if top else -1.0
        c, m, v = [part("c", q) for q in range(3)], [part("m", q) for q in range(3)], [part("v", q) for q in range(2)]
        half = each(lambda x: 0.5 * x, m[1])
        opened = each(jnp.multiply, half, m[0])
        step = each(lambda a, b, o: (a - b) * o, c[0], c[1], opened)
        inner = each(lambda a, b, x, y: (a - b) * (x * y), c[1], c[2], half, m[2])
        speed = each(lambda a, b, o: (a + b) * o * outward, v[0], v[1], opened)
        inflow = each(
            lambda a, b, s, x, y: s * jnp.where(s >= 0.0, a, b)
            + jnp.where(s >= 0.0, (jnp.abs(s) - s * s) * median(x, y), 0.0),
            c[1], c[0], speed, step, inner,
        )
        rest = each(lambda s: jnp.where(s >= 0.0, 0.0, jnp.abs(s) - s * s), speed)
        halved = each(lambda x: 0.5 * x, m[0])
        flux_x = zonal_flux(c[0], m[0], halved, part("u", 0))
        across = each(lambda f, g: f - g, flux_x, minus(flux_x))
        across = [jnp.where(first, 0.0, across[0]), jnp.where(last, 0.0, across[1])]
        down = each(vertical_divergence, c[0], halved, part("w", 0))
        cell = each(lambda a, x, z, f: a - x - z + f, c[0], across, down, inflow)
        pair = lambda a, b: each(lambda x, y: jnp.where(low, x, y), a, b)
        return [cell, step, c[0], pair(m[0], rest), pair(v[0], part("sy", 0)), part("k", 0)]

    backward = LANES - 1 - lane
    flip = lambda x: jnp.take_along_axis(x, backward, axis=1, mode="promise_in_bounds")
    is_even = jnp.broadcast_to(lat % 2, (8, LANES)) == 0
    folds = jnp.broadcast_to(lat, (8, LANES)) == lax.axis_size("lat") - 1
    north, south = message(True), message(False)
    for i, (top, bottom) in enumerate(zip(north, south)):
        for h in range(2):
            wide = slice(h * LANES, (h + 1) * LANES)
            turned = flip(top[1 - h])
            if i == 4:
                turned = -turned
            send_a[i, :, wide] = jnp.where(is_even, top[h], bottom[h])
            send_b[i, :, wide] = jnp.where(folds, turned, jnp.where(is_even, bottom[h], top[h]))


def strip_at(g, which, late, from_far, from_near, own, spare):
    slot = lane_of() % 16
    far_is_west = jnp.broadcast_to(lax.axis_index("lon") % 2, (8, LANES)) == 0
    near, far, mine = from_near[g // 2], from_far[g // 2], (spare if which else own)[g]
    east, west = jnp.where(far_is_west, near, far), jnp.where(far_is_west, far, near)
    shift = lambda x, by: pltpu.roll(x, by % LANES, 1) if by else x
    odd = 4 * (g % 2)
    east = shift(east, (1 if which else 4) - odd - 8 * late)
    west = shift(west, (9 if which else 6) - odd - 8 * late)
    inner = jnp.where(slot < 4, shift(mine, -8 * late), east)
    outer = jnp.where(slot < 10, west, shift(mine, 6 - 8 * late))
    return jnp.where(slot < 7, inner, outer)


def edge_kernel(*refs):
    sources, made, (send_a, send_b) = refs[:4], refs[4:6], refs[6:]
    lane, low = lane_of(), low_of()
    lat = lax.axis_index("lat")
    strip = lambda i, g: strip_at(g, i // 2, i % 2, *sources)

    def beside(g, inner):
        c, mu, vw = strip(0, g), strip(1, g), strip(2, g)
        shifts = (1, 0, LANES - 1, LANES - 2)
        moved = lambda x: [pltpu.roll(x, by, 1) if by else x for by in shifts]
        cells, pairs = moved(c), moved(mu)
        m = [twice_low(x) for x in pairs]
        half = [0.5 * x for x in m]
        steps = [(cells[n + 1] - cells[n]) * (half[n] * m[n + 1]) for n in range(3)]
        speed = face_speed(twice_high(pairs[1]), twice_high(pairs[2]), half[1] * m[2])
        flux = face_flux(cells[1], cells[2], speed, *steps)
        step = (c - strip(0, inner)) * (half[1] * twice_low(strip(1, inner)))
        return flux, c, step, jnp.where(low, mu, pltpu.roll(vw, 4, 0))

    def placed(values, base, backward):
        if backward:
            take = lambda x, at: jnp.take_along_axis(x, (base + at + LANES - lane) & (LANES - 1), axis=1, mode="promise_in_bounds")
            places = [(3, 2), (9, 8), 13, 29, 45]
        else:
            take = lambda x, at: pltpu.roll(x, (at - base) % LANES, 1) if (at - base) % LANES else x
            places = [(118, 119), (124, 125), 0, 16, 32]
        across = [take(values[0], at) - take(values[0], before) for at, before in places[:2]]
        c, step, mv = [take(x, at) for x, at in zip(values[1:], places[2:])]
        if backward:
            mv = jnp.where(low, mv, -mv)
        return across + [jnp.where(lane < 16, c, jnp.where(lane < 32, step, mv))]

    south, north = beside(0, 1), beside(7, 6)
    south, north, turned = placed(south, 0, False), placed(north, 112, False), placed(north, 112, True)

    def store(source, ref, left, right, packed):
        ref[0, :, :LANES] = source[0, :, :LANES] - jnp.where(lane < 2, left, 0.0)
        ref[0, :, LANES:] = source[0, :, LANES:] - jnp.where(lane >= LANES - 2, right, 0.0)
        ref[5, :, :LANES] = jnp.where(low, source[5, :, :LANES], pltpu.roll(packed, 4, 0))
        ref[5, :, LANES:] = jnp.where(low, source[5, :, LANES:], packed)

    is_even = jnp.broadcast_to(lat % 2, (8, LANES)) == 0
    folds = jnp.broadcast_to(lat, (8, LANES)) == lax.axis_size("lat") - 1
    store(made[0], send_a, *[jnp.where(is_even, n, s) for n, s in zip(north, south)])
    store(made[1], send_b, *[jnp.where(folds, t, jnp.where(is_even, s, n)) for n, s, t in zip(north, south, turned)])


def split_groups(groups):
    return {
        "c": groups["c"],
        "m": twice_low(groups["mu"]),
        "u": twice_high(groups["mu"]),
        "v": twice_low(groups["vw"]),
        "w": twice_high(groups["vw"]),
        "sx": twice_low(groups["sk"]),
        "k": twice_high(groups["sk"]),
    }


def third_of(x, base):
    east, west = pltpu.roll(x, (2 * LANES - 4 - base) % LANES, 1), pltpu.roll(x, (2 * LANES - 10 - base) % LANES, 1)
    return jnp.where(lane_of() < 64, east, west)


def third_tile(groups, base):
    return split_groups({n: third_of(groups[n], base) for n in GROUPS})


def plus(tiles):
    last = lane_of() == LANES - 1
    turned = [pltpu.roll(t, LANES - 1, 1) for t in tiles]
    if len(tiles) == 1:
        return turned
    return [jnp.where(last, turned[(i + 1) % len(tiles)], turned[i]) for i in range(len(tiles))]


def minus(tiles, count=3, west=None):
    first = lane_of() == 0
    turned = [pltpu.roll(t, 1, 1) for t in tiles]
    if len(tiles) == 1:
        return turned
    before = [turned[-1] if west is None else west] + turned[:-1]
    return [jnp.where(first, before[i], turned[i]) for i in range(min(count, len(tiles)))]


def each(function, *lists):
    return [function(*values) for values in zip(*lists)]


def below(x):
    return pltpu.roll(x, 7, 0)


def above(x):
    return pltpu.roll(x, 1, 0)


def median(step, upwind):
    return jnp.minimum(jnp.maximum(upwind, jnp.minimum(step, 0.0)), jnp.maximum(step, 0.0))


def face_flux(here, there, speed, back, step, ahead):
    positive = speed >= 0.0
    upwind = jnp.where(positive, back, ahead)
    size = jnp.abs(speed)
    return speed * jnp.where(positive, here, there) + (size - size * size) * median(step, upwind)


def zonal_flux(c, m, half, u):
    east = plus(c)
    opened = each(jnp.multiply, half, plus(m))
    speed = each(face_speed, u, plus(u), opened)
    step = each(lambda a, b, o: (b - a) * o, c, east, opened)
    return each(face_flux, c, east, speed, minus(step), step, plus(step))


def vertical_divergence(value, half, down):
    opened = open_below(half)
    under = below(value)
    step = (under - value) * opened
    flux = face_flux(value, under, face_speed(down, below(down), opened), above(step), step, below(step))
    return flux - above(flux)


def not_bottom():
    return lax.broadcasted_iota(jnp.int32, (8, LANES), 0) % 4 != 3


def open_below(marker):
    return jnp.where(not_bottom(), below(marker), 0.0)


def face_speed(one, two, half_open):
    return (one + two) * half_open


def advect_rows(get, first, count, known=()):
    known = dict(known)
    low, high = (-1 if -2 in known else -2), (count + 1 if count in known else count + 2)
    c = {j: get("c", first + j) for j in range(low, high)}
    m = {j: get("m", first + j) for j in range(low, high)}
    v = {j: get("v", first + j) for j in range(-1, count + 1)}
    half = {j: each(lambda x: 0.5 * x, m[j]) for j in range(low, high)}
    opened = {j: each(jnp.multiply, half[j], m[j + 1]) for j in range(low, high - 1)}
    step = {j: each(lambda a, b, o: (b - a) * o, c[j], c[j + 1], opened[j]) for j in range(low, high - 1)}
    step.update(known)
    flux = {}
    for j in range(-1, count):
        speed = each(face_speed, v[j], v[j + 1], opened[j])
        flux[j] = each(face_flux, c[j], c[j + 1], speed, step[j - 1], step[j], step[j + 1])
    result = []
    for j in range(count):
        flux_x = zonal_flux(c[j], m[j], half[j], get("u", first + j))
        total = each(lambda f, g, a, b: (f - g) + (a - b), flux_x, minus(flux_x), flux[j], flux[j - 1])
        down = each(vertical_divergence, c[j], half[j], get("w", first + j))
        result.append(each(lambda a, x, z, o: (a - x - z) * o, c[j], total, down, m[j]))
    return result, flux, step


def slope_flux(k1, k2, opened, step, s1, s2, z1, z2):
    return (k1 + k2) * opened * (step + (s1 + s2) * (z1 + z2))


def eastward(a, m, k, sx, twice_z):
    opened = each(jnp.multiply, m, plus(m))
    step = each(lambda x, y, o: (y - x) * o, a, plus(a), opened)
    return step, each(slope_flux, k, plus(k), opened, step, sx, plus(sx), twice_z, plus(twice_z))


def diffuse_rows(get, first, count, beside=None):
    a, m, k, sy, step_z, twice_z, step_y, flux_y = [{} for _ in range(8)]
    last = lane_of() == LANES - 1

    def row_result(j):
        sx = get("sx", first + j)
        step_x, flux_x = eastward(a[j], m[j], k[j], sx, twice_z[j])
        west = [None, None]
        if beside:
            east, west = beside(first + j)
            step_x = [step_x[0], jnp.where(last, east[0], step_x[1])]
            flux_x = [flux_x[0], jnp.where(last, east[1], flux_x[1])]
        twice_x = each(jnp.add, step_x, minus(step_x, 2, west[0]))
        twice_y = each(jnp.add, step_y[j - 1], step_y[j])
        total = each(lambda f, g, p, q: (f - g) + (p - q), flux_x, minus(flux_x, 2, west[1]), flux_y[j], flux_y[j - 1])

        def finish(value, marker, kappa, east, north, tx, ty, sz, across):
            face_east, face_north = east + below(east), north + below(north)
            flux_z = (kappa + below(kappa)) * open_below(marker) * (
                face_east * (tx + below(tx)) + face_north * (ty + below(ty))
                + (face_east * face_east + face_north * face_north) * (16.0 * sz)
            )
            return (value + across + (flux_z - above(flux_z))) * marker

        return each(finish, a[j][:2], m[j], k[j], sx, sy[j], twice_x, twice_y, step_z[j], total)

    for j in range(-1, count + 1):
        a[j], m[j], k[j], sy[j] = [get(name, first + j) for name in ("a", "m", "k", "sy")]
        wide = 3 if 0 <= j < count else 2
        step_z[j] = each(lambda x, o: (below(x) - x) * open_below(o), a[j][:wide], m[j])
        twice_z[j] = each(lambda x: above(x) + x, step_z[j])
        if j >= 0:
            opened = each(jnp.multiply, m[j - 1][:2], m[j][:2])
            step_y[j - 1] = each(lambda x, y, o: (y - x) * o, a[j - 1][:2], a[j][:2], opened)
            flux_y[j - 1] = each(
                slope_flux, k[j - 1], k[j], opened, step_y[j - 1], sy[j - 1], sy[j], twice_z[j - 1], twice_z[j]
            )
        if j >= 1:
            yield row_result(j - 1)


def tiles_of(ref, row, count):
    return [ref[row, :, t * LANES : (t + 1) * LANES] for t in range(count)]


def interior_kernel(*refs):
    rows, advected, sources, slope = refs[:5], refs[5], refs[6:10], refs[10]
    out, kept, strips, slope_rows, narrow = refs[11:]
    rows = rows[:3] + (slope_rows,) + rows[4:]
    for part in range(8):
        for h in range(2):
            wide = slice(h * LANES, (h + 1) * LANES)
            turned = jnp.transpose(slope[:, 8 * part : 8 * part + 8, wide], (1, 0, 2))
            slope_rows[8 * part : 8 * part + 8, :, wide] = turned * 0.125
    lane = lane_of()
    near_east, near_west = lane >= LANES - 2, lane < 2

    full = []
    for g in range(8):
        groups = {n: strip_at(g, i // 2, i % 2, *sources) for i, n in enumerate(GROUPS)}
        full.append(split_groups(groups))
        for i, n in enumerate(GROUPS):
            strips[i, g] = groups[n]

    def get_strip(name, g):
        x = full[g % 8][name]
        return [x if 0 <= g < 8 else pltpu.roll(x, 16 if g < 0 else LANES - 16, 1)]

    for g, (a,) in enumerate(advect_rows(get_strip, 0, 8)[0]):
        part = full[g]
        step_z = (below(a) - a) * open_below(part["m"])
        step, flux = eastward([a], [part["m"]], [part["k"]], [part["sx"]], [above(step_z) + step_z])
        narrow[0, g], narrow[1, g], narrow[2, g] = a, step[0], flux[0]

    def lanes_to(which, row, lane_from, lane_to):
        part = row // 8
        return pltpu.roll(narrow[which, row - 8 * part], lax.rem(2 * LANES + lane_to - lane_from - 16 * part, LANES), 1)

    def get(name, row):
        if name != "a":
            return field_tiles(rows, name, row)
        left, right = tiles_of(advected, row, 2)
        return [
            jnp.where(near_west, lanes_to(0, row, 10, 0), left),
            jnp.where(near_east, lanes_to(0, row, 3, LANES - 1), right),
        ]

    def beside(row):
        return [lanes_to(i, row, 3, LANES - 1) for i in (1, 2)], [lanes_to(i, row, 9, 0) for i in (1, 2)]

    for i, row in enumerate(KEPT):
        third = jnp.where(lane < 64, lanes_to(0, row, 4, 0), lanes_to(0, row, 9, LANES - 1))
        for t, tile in enumerate(get("a", row) + [third]):
            kept[i, :, t * LANES : (t + 1) * LANES] = tile

    def diffuse_block(block, carry):
        first = jnp.minimum(3 + 12 * block, ROWS - 3 - 12)
        for j, tiles in enumerate(diffuse_rows(get, first, 12, beside)):
            for t in range(2):
                out[first + j, :, t * LANES : (t + 1) * LANES] = tiles[t]
        return carry

    lax.fori_loop(0, 5, diffuse_block, 0)


def rim_kernel(*refs):
    got_a, got_b = refs[0], refs[1]
    fields = refs[2:7]
    strips, inner, kept, out, edges, sems = refs[7:]
    middle = pltpu.make_async_copy
    copies = [middle(inner.at[8:56, i], out.at[i, 8:56], sems.at[i]) for i in range(8)]
    for copy in copies:
        copy.start()
    low = low_of()
    lat = lax.axis_index("lat")
    even = jnp.broadcast_to(lat % 2, (8, LANES)) == 0
    floor = jnp.broadcast_to(lat, (8, LANES)) == 0

    def halo(is_north):
        def tile(i, h):
            a = got_a[i, :, h * LANES : (h + 1) * LANES]
            b = got_b[i, :, h * LANES : (h + 1) * LANES]
            if is_north:
                return jnp.where(even, a, b)
            return jnp.where(floor, 0.0, jnp.where(even, b, a))

        tiles = [[tile(i, h) for h in range(2)] for i in range(6)]
        corner = jnp.where(low, pltpu.roll(tiles[5][0], 4, 0), tiles[5][1])
        c_side, step_side, mv = [third_of(corner, 16 * i) for i in range(3)]
        row = {
            "c": tiles[2] + [c_side],
            "m": each(twice_low, tiles[3]) + [twice_low(mv)],
            "v": each(twice_low, tiles[4]) + [twice_high(mv)],
            "sy": each(twice_high, tiles[4]),
            "k": each(twice_low, tiles[5]),
        }
        return row, tiles[0], tiles[1] + [step_side], each(twice_high, tiles[3])

    for is_north in (False, True):
        outer, cell, step_in, rest = halo(is_north)
        start, beyond = (ROWS - 2, ROWS) if is_north else (0, -1)
        made, sides = {}, {}
        for row in range(*((ROWS - 4, ROWS) if is_north else (0, 4))):
            base = 16 * (row // 8)
            sides[row] = third_tile({n: strips[i, row % 8] for i, n in enumerate(GROUPS)}, base)

        def get(name, row):
            if name == "a":
                return made[row] if row in made else tiles_of(kept, KEPT.index(row), 3)
            if row == beyond:
                return outer[name]
            tiles = field_tiles(fields, name, row)
            return tiles if name == "sy" else tiles + [sides[row][name]]

        known = {2: [-x for x in step_in]} if is_north else {-2: step_in}
        results, flux, step = advect_rows(get, start, 2, known)
        made.update(zip((start, start + 1), results))
        face, sign = (1, -1.0) if is_north else (-1, 1.0)
        made[beyond] = each(
            lambda q, g, s, t, f, o: (q + g * median(s, sign * t) - sign * f) * o,
            cell, rest, step_in, step[face], flux[face], outer["m"],
        )
        final = ROWS - 3 if is_north else 0
        base = ROWS - 8 if is_north else 0
        done = {final + j: x for j, x in enumerate(diffuse_rows(get, final, 3))}
        for h in range(2):
            stack = [done[j][h] if j in done else inner[j, :, h * LANES : (h + 1) * LANES] for j in range(base, base + 8)]
            edges[int(is_north), :, :, h * LANES : (h + 1) * LANES] = jnp.transpose(jnp.stack(stack), (1, 0, 2))
        copy = middle(edges.at[int(is_north)], out.at[:, base : base + 8], sems.at[8 + int(is_north)])
        copy.start()
        copies.append(copy)
    for copy in copies:
        copy.wait()


def call(kernel, shapes, *operands, **options):
    return pl.pallas_call(
        kernel,
        out_shape=[jax.ShapeDtypeStruct(s, F32) for s in shapes],
        in_specs=[VMEM] * len(operands),
        out_specs=[VMEM] * len(shapes),
        compiler_params=pltpu.CompilerParams(vmem_limit_bytes=LIMIT),
        **options,
    )(*operands)


def make(lons, lats):
    def spot(lon, lat):
        return (lon % lons) * lats + lat

    near = [(spot(i, j), spot(i ^ 1, j)) for i in range(lons) for j in range(lats)]
    far = [(spot(i, j), spot(i + 1 if i % 2 else i - 1, j)) for i in range(lons) for j in range(lats)]
    pair_a = [(spot(i, j), spot(i, j ^ 1)) for i in range(lons) for j in range(lats)]
    pair_b = []
    for i in range(lons):
        for j in range(lats):
            if j == 0:
                pair_b.append((spot(i, j), spot(i ^ 1, j)))
            elif j == lats - 1:
                pair_b.append((spot(i, j), spot(lons - 1 - i, j)))
            else:
                pair_b.append((spot(i, j), spot(i, j + 1 if j % 2 else j - 1)))

    def move(x, route):
        return lax.ppermute(x, ("lon", "lat"), route)

    def shards(tracers, velocity, slopes, diffusivity, sea_mask):
        plane = lambda x: x.reshape(-1, ROWS, 2 * LANES)
        arrays = [plane(tracers), plane(velocity), plane(slopes), diffusivity, sea_mask]
        arrays = [pltpu.with_memory_space_constraint(x, pltpu.HBM) for x in arrays]
        full, side = (ROWS, 8, 2 * LANES), (8, 8, LANES)
        *held, to_near, to_far, own, spare = pl.pallas_call(
            pack_kernel,
            out_shape=[jax.ShapeDtypeStruct(x.shape, x.dtype) for x in arrays]
            + [jax.ShapeDtypeStruct(shape, F32) for shape in [(4, 8, LANES)] * 2 + [side] * 2],
            in_specs=[pl.BlockSpec(memory_space=pltpu.HBM)] * 5,
            out_specs=[VMEM] * 9,
            scratch_shapes=[pltpu.SemaphoreType.DMA((CHUNKS, 6))],
            compiler_params=pltpu.CompilerParams(vmem_limit_bytes=LIMIT),
        )(*arrays)
        far_got, near_got = move(to_far, far), move(to_near, near)
        *rows, advected, made_a, made_b = call(
            advect_kernel, [full] * 6 + [(6, 8, 2 * LANES)] * 2, *held,
            cost_estimate=pl.CostEstimate(flops=10**7, bytes_accessed=6 * 10**6, transcendentals=0),
        )
        send_a, send_b = call(
            edge_kernel, [(6, 8, 2 * LANES)] * 2, far_got, near_got, own, spare, made_a, made_b,
            input_output_aliases={4: 0, 5: 1},
        )
        got_a, got_b = move(send_a, pair_a), move(send_b, pair_b)
        inner, kept, strips, rows[3] = call(
            interior_kernel, [full, (4, 8, 3 * LANES), (4,) + side, full],
            *rows, advected, far_got, near_got, own, spare, held[2],
            scratch_shapes=[pltpu.VMEM((3,) + side, F32)],
            cost_estimate=pl.CostEstimate(flops=2 * 10**7, bytes_accessed=10**7, transcendentals=0),
        )
        out = pl.pallas_call(
            rim_kernel,
            out_shape=jax.ShapeDtypeStruct((8, ROWS, 2 * LANES), F32),
            in_specs=[VMEM] * 10,
            out_specs=pl.BlockSpec(memory_space=pl.ANY),
            scratch_shapes=[pltpu.VMEM((2, 8, 8, 2 * LANES), F32), pltpu.SemaphoreType.DMA((10,))],
            compiler_params=pltpu.CompilerParams(vmem_limit_bytes=LIMIT),
        )(got_a, got_b, *rows, strips, inner, kept)
        return out.reshape(tracers.shape)

    return shards


def solution(mesh):
    return jax.shard_map(
        make(mesh.shape["lon"], mesh.shape["lat"]),
        mesh=mesh,
        in_specs=(
            P(None, None, "lat", "lon"),
            P(None, None, "lat", "lon"),
            P(None, None, "lat", "lon"),
            P(None, "lat", "lon"),
            P(None, "lat", "lon"),
        ),
        out_specs=P(None, None, "lat", "lon"),
        check_vma=False,
    )
```

```python
import jax
import jax.numpy as jnp
from jax import lax
from jax.experimental import pallas as pl
from jax.experimental.pallas import tpu as pltpu
from jax.sharding import PartitionSpec as P


ROWS = 64
LANES = 128
F32 = jnp.float32
VMEM = pl.BlockSpec(memory_space=pltpu.VMEM)
LIMIT = 16 * 1024 * 1024
CHUNKS = 2
GROUPS = ("c", "mu", "vw", "sk")
KEPT = (2, 3, ROWS - 4, ROWS - 3)


def lane_of():
    return lax.broadcasted_iota(jnp.int32, (8, LANES), 1)


def low_of():
    return lax.broadcasted_iota(jnp.int32, (8, LANES), 0) < 4


def twice_low(x):
    return jnp.where(low_of(), x, pltpu.roll(x, 4, 0))


def twice_high(x):
    return jnp.where(low_of(), pltpu.roll(x, 4, 0), x)


def field_half(rows, name, row, h):
    which, turn = {
        "u": (1, twice_low), "v": (1, twice_high), "w": (2, twice_high),
        "sx": (3, twice_low), "sy": (3, twice_high), "m": (4, twice_low), "k": (4, twice_high),
    }.get(name, (0, None))
    value = rows[which][row, :, h * LANES : (h + 1) * LANES]
    return turn(value) if turn else value


def field_tiles(rows, name, row):
    return [field_half(rows, name, row, h) for h in range(2)]


def row_planes(held, span, h, both=True):
    tracer, velocity, slope, kappa, mask = held
    wide = slice(h * LANES, (h + 1) * LANES)
    return [
        tracer[:, span, wide], velocity[0:8, span, wide], velocity[4:12, span, wide],
        slope[:, span, wide] if both else jnp.concatenate([slope[0:4, span, wide]] * 2, axis=0),
        jnp.concatenate([mask[:, span, wide].astype(F32), kappa[:, span, wide]], axis=0),
    ]


def scaled(groups):
    c, uv, vw, s, mk = groups
    return c, uv, vw, s * 0.125, mk * jnp.where(low_of(), 1.0, 0.5)


def pack_kernel(*refs):
    arrays, held, (to_near, to_far, own, spare), sems = refs[:5], refs[5:10], refs[10:14], refs[14]
    copies = []
    for chunk in range(CHUNKS):
        span = slice(chunk * ROWS // CHUNKS, (chunk + 1) * ROWS // CHUNKS)
        ends = [array.shape[0] for array in arrays]
        ends[2] = 4
        copies.append(
            [
                pltpu.make_async_copy(array.at[:end, span], hold.at[:end, span], sems.at[chunk, i])
                for i, (array, hold, end) in enumerate(zip(arrays, held, ends))
            ]
        )
        for copy in copies[-1]:
            copy.start()
    northward = pltpu.make_async_copy(arrays[2].at[4:], held[2].at[4:], sems.at[0, 5])
    northward.start()
    lane, low = lane_of(), low_of()
    inside = lax.broadcasted_iota(jnp.int32, (8, 8, LANES), 2) < 64
    first, second = [None] * 8, [None] * 8
    for part in range(8):
        if part * CHUNKS % 8 == 0:
            for copy in copies[part * CHUNKS // 8]:
                copy.wait()
        span = slice(8 * part, 8 * part + 8)
        rims = []
        for left, right in zip(*[row_planes(held, span, h, False) for h in range(2)]):
            rims.append(jnp.transpose(jnp.where(inside, left, right), (1, 0, 2)))
        base = 16 * part
        before, half = lane < base, lane < base + 8
        for g in range(8):
            c, uv, vw, s, mk = scaled([x[g] for x in rims])
            mu = jnp.where(low, mk, pltpu.roll(uv, 4, 0))
            sk = jnp.where(low, s, mk)
            one = jnp.where(half, pltpu.roll(c, (base + 4) % LANES, 1), pltpu.roll(mu, (base + 12) % LANES, 1))
            two = jnp.where(half, pltpu.roll(vw, (base + 4) % LANES, 1), pltpu.roll(sk, (base + 12) % LANES, 1))
            first[g] = jnp.where(before, first[g], one) if part else one
            second[g] = jnp.where(before, second[g], two) if part else two
    for g in range(8):
        own[g] = first[g]
        spare[g] = second[g]
    slot = lane % 8
    to_east = jnp.broadcast_to(lax.axis_index("lon") % 2, (8, LANES)) == 0
    for pair in range(4):
        east, west = [], []
        for g in (2 * pair, 2 * pair + 1):
            east.append(jnp.where(slot == 0, pltpu.roll(second[g], LANES - 3, 1), first[g]))
            west.append(jnp.where(slot == 7, pltpu.roll(second[g], 3, 1), first[g]))
        eastern = jnp.where(slot < 4, east[0], pltpu.roll(east[1], 4, 1))
        western = jnp.where(slot < 4, pltpu.roll(west[0], LANES - 4, 1), west[1])
        to_near[pair] = jnp.where(to_east, eastern, western)
        to_far[pair] = jnp.where(to_east, western, eastern)
    northward.wait()


def advect_kernel(*refs):
    held, rows, advected, send_a, send_b = refs[:5], refs[5:10], refs[10], refs[11], refs[12]
    for part in range(8):
        for h in range(2):
            turned = [jnp.transpose(x, (1, 0, 2)) for x in row_planes(held, slice(8 * part, 8 * part + 8), h)]
            for g in range(8):
                for i, (ref, value) in enumerate(zip(rows, scaled([x[g] for x in turned]))):
                    if i != 3 or part in (0, 7):
                        ref[8 * part + g, :, h * LANES : (h + 1) * LANES] = value
    put_messages(rows, send_a, send_b)
    get = lambda name, row: field_tiles(rows, name, row)

    def advect_block(block, carry):
        first = 2 + 15 * block
        for j, tiles in enumerate(advect_rows(get, first, 15)[0]):
            for t in range(2):
                advected[first + j, :, t * LANES : (t + 1) * LANES] = tiles[t]
        return carry

    lax.fori_loop(0, 4, advect_block, 0)


def put_messages(rows, send_a, send_b):
    lane, low = lane_of(), low_of()
    lat = lax.axis_index("lat")

    first, last = lane < 2, lane >= LANES - 2

    def message(top):
        part = lambda name, q: field_tiles(rows, name, ROWS - 1 - q if top else q)
        outward = 1.0 if top else -1.0
        c, m, v = [part("c", q) for q in range(3)], [part("m", q) for q in range(3)], [part("v", q) for q in range(2)]
        half = each(lambda x: 0.5 * x, m[1])
        opened = each(jnp.multiply, half, m[0])
        step = each(lambda a, b, o: (a - b) * o, c[0], c[1], opened)
        inner = each(lambda a, b, x, y: (a - b) * (x * y), c[1], c[2], half, m[2])
        speed = each(lambda a, b, o: (a + b) * o * outward, v[0], v[1], opened)
        inflow = each(
            lambda a, b, s, x, y: s * jnp.where(s >= 0.0, a, b)
            + jnp.where(s >= 0.0, (jnp.abs(s) - s * s) * median(x, y), 0.0),
            c[1], c[0], speed, step, inner,
        )
        rest = each(lambda s: jnp.where(s >= 0.0, 0.0, jnp.abs(s) - s * s), speed)
        halved = each(lambda x: 0.5 * x, m[0])
        flux_x = zonal_flux(c[0], m[0], halved, part("u", 0))
        across = each(lambda f, g: f - g, flux_x, minus(flux_x))
        across = [jnp.where(first, 0.0, across[0]), jnp.where(last, 0.0, across[1])]
        down = each(vertical_divergence, c[0], halved, part("w", 0))
        cell = each(lambda a, x, z, f: a - x - z + f, c[0], across, down, inflow)
        pair = lambda a, b: each(lambda x, y: jnp.where(low, x, y), a, b)
        return [cell, step, c[0], pair(m[0], rest), pair(v[0], part("sy", 0)), part("k", 0)]

    backward = LANES - 1 - lane
    flip = lambda x: jnp.take_along_axis(x, backward, axis=1, mode="promise_in_bounds")
    is_even = jnp.broadcast_to(lat % 2, (8, LANES)) == 0
    folds = jnp.broadcast_to(lat, (8, LANES)) == lax.axis_size("lat") - 1
    north, south = message(True), message(False)
    for i, (top, bottom) in enumerate(zip(north, south)):
        for h in range(2):
            wide = slice(h * LANES, (h + 1) * LANES)
            turned = flip(top[1 - h])
            if i == 4:
                turned = -turned
            send_a[i, :, wide] = jnp.where(is_even, top[h], bottom[h])
            send_b[i, :, wide] = jnp.where(folds, turned, jnp.where(is_even, bottom[h], top[h]))


def strip_at(g, which, late, from_far, from_near, own, spare):
    slot = lane_of() % 16
    far_is_west = jnp.broadcast_to(lax.axis_index("lon") % 2, (8, LANES)) == 0
    near, far, mine = from_near[g // 2], from_far[g // 2], (spare if which else own)[g]
    east, west = jnp.where(far_is_west, near, far), jnp.where(far_is_west, far, near)
    shift = lambda x, by: pltpu.roll(x, by % LANES, 1) if by else x
    odd = 4 * (g % 2)
    east = shift(east, (1 if which else 4) - odd - 8 * late)
    west = shift(west, (9 if which else 6) - odd - 8 * late)
    inner = jnp.where(slot < 4, shift(mine, -8 * late), east)
    outer = jnp.where(slot < 10, west, shift(mine, 6 - 8 * late))
    return jnp.where(slot < 7, inner, outer)


def edge_kernel(*refs):
    sources, made, (send_a, send_b) = refs[:4], refs[4:6], refs[6:]
    lane, low = lane_of(), low_of()
    lat = lax.axis_index("lat")
    strip = lambda i, g: strip_at(g, i // 2, i % 2, *sources)

    def beside(g, inner):
        c, mu, vw = strip(0, g), strip(1, g), strip(2, g)
        shifts = (1, 0, LANES - 1, LANES - 2)
        moved = lambda x: [pltpu.roll(x, by, 1) if by else x for by in shifts]
        cells, pairs = moved(c), moved(mu)
        m = [twice_low(x) for x in pairs]
        half = [0.5 * x for x in m]
        steps = [(cells[n + 1] - cells[n]) * (half[n] * m[n + 1]) for n in range(3)]
        speed = face_speed(twice_high(pairs[1]), twice_high(pairs[2]), half[1] * m[2])
        flux = face_flux(cells[1], cells[2], speed, *steps)
        step = (c - strip(0, inner)) * (half[1] * twice_low(strip(1, inner)))
        return flux, c, step, jnp.where(low, mu, pltpu.roll(vw, 4, 0))

    def placed(values, base, backward):
        if backward:
            take = lambda x, at: jnp.take_along_axis(x, (base + at + LANES - lane) & (LANES - 1), axis=1, mode="promise_in_bounds")
            places = [(3, 2), (9, 8), 13, 29, 45]
        else:
            take = lambda x, at: pltpu.roll(x, (at - base) % LANES, 1) if (at - base) % LANES else x
            places = [(118, 119), (124, 125), 0, 16, 32]
        across = [take(values[0], at) - take(values[0], before) for at, before in places[:2]]
        c, step, mv = [take(x, at) for x, at in zip(values[1:], places[2:])]
        if backward:
            mv = jnp.where(low, mv, -mv)
        return across + [jnp.where(lane < 16, c, jnp.where(lane < 32, step, mv))]

    south, north = beside(0, 1), beside(7, 6)
    south, north, turned = placed(south, 0, False), placed(north, 112, False), placed(north, 112, True)

    def store(source, ref, left, right, packed):
        ref[0, :, :LANES] = source[0, :, :LANES] - jnp.where(lane < 2, left, 0.0)
        ref[0, :, LANES:] = source[0, :, LANES:] - jnp.where(lane >= LANES - 2, right, 0.0)
        ref[5, :, :LANES] = jnp.where(low, source[5, :, :LANES], pltpu.roll(packed, 4, 0))
        ref[5, :, LANES:] = jnp.where(low, source[5, :, LANES:], packed)

    is_even = jnp.broadcast_to(lat % 2, (8, LANES)) == 0
    folds = jnp.broadcast_to(lat, (8, LANES)) == lax.axis_size("lat") - 1
    store(made[0], send_a, *[jnp.where(is_even, n, s) for n, s in zip(north, south)])
    store(made[1], send_b, *[jnp.where(folds, t, jnp.where(is_even, s, n)) for n, s, t in zip(north, south, turned)])


def split_groups(groups):
    return {
        "c": groups["c"],
        "m": twice_low(groups["mu"]),
        "u": twice_high(groups["mu"]),
        "v": twice_low(groups["vw"]),
        "w": twice_high(groups["vw"]),
        "sx": twice_low(groups["sk"]),
        "k": twice_high(groups["sk"]),
    }


def third_of(x, base):
    east, west = pltpu.roll(x, (2 * LANES - 4 - base) % LANES, 1), pltpu.roll(x, (2 * LANES - 10 - base) % LANES, 1)
    return jnp.where(lane_of() < 64, east, west)


def third_tile(groups, base):
    return split_groups({n: third_of(groups[n], base) for n in GROUPS})


def plus(tiles):
    last = lane_of() == LANES - 1
    turned = [pltpu.roll(t, LANES - 1, 1) for t in tiles]
    if len(tiles) == 1:
        return turned
    return [jnp.where(last, turned[(i + 1) % len(tiles)], turned[i]) for i in range(len(tiles))]


def minus(tiles, count=3, west=None):
    first = lane_of() == 0
    turned = [pltpu.roll(t, 1, 1) for t in tiles]
    if len(tiles) == 1:
        return turned
    before = [turned[-1] if west is None else west] + turned[:-1]
    return [jnp.where(first, before[i], turned[i]) for i in range(min(count, len(tiles)))]


def each(function, *lists):
    return [function(*values) for values in zip(*lists)]


def below(x):
    return pltpu.roll(x, 7, 0)


def above(x):
    return pltpu.roll(x, 1, 0)


def median(step, upwind):
    return jnp.minimum(jnp.maximum(upwind, jnp.minimum(step, 0.0)), jnp.maximum(step, 0.0))


def face_flux(here, there, speed, back, step, ahead):
    positive = speed >= 0.0
    upwind = jnp.where(positive, back, ahead)
    size = jnp.abs(speed)
    return speed * jnp.where(positive, here, there) + (size - size * size) * median(step, upwind)


def zonal_flux(c, m, half, u):
    east = plus(c)
    opened = each(jnp.multiply, half, plus(m))
    speed = each(face_speed, u, plus(u), opened)
    step = each(lambda a, b, o: (b - a) * o, c, east, opened)
    return each(face_flux, c, east, speed, minus(step), step, plus(step))


def vertical_divergence(value, half, down):
    opened = open_below(half)
    under = below(value)
    step = (under - value) * opened
    flux = face_flux(value, under, face_speed(down, below(down), opened), above(step), step, below(step))
    return flux - above(flux)


def not_bottom():
    return lax.broadcasted_iota(jnp.int32, (8, LANES), 0) % 4 != 3


def open_below(marker):
    return jnp.where(not_bottom(), below(marker), 0.0)


def face_speed(one, two, half_open):
    return (one + two) * half_open


def advect_rows(get, first, count, known=()):
    known = dict(known)
    low, high = (-1 if -2 in known else -2), (count + 1 if count in known else count + 2)
    c = {j: get("c", first + j) for j in range(low, high)}
    m = {j: get("m", first + j) for j in range(low, high)}
    v = {j: get("v", first + j) for j in range(-1, count + 1)}
    half = {j: each(lambda x: 0.5 * x, m[j]) for j in range(low, high)}
    opened = {j: each(jnp.multiply, half[j], m[j + 1]) for j in range(low, high - 1)}
    step = {j: each(lambda a, b, o: (b - a) * o, c[j], c[j + 1], opened[j]) for j in range(low, high - 1)}
    step.update(known)
    flux = {}
    for j in range(-1, count):
        speed = each(face_speed, v[j], v[j + 1], opened[j])
        flux[j] = each(face_flux, c[j], c[j + 1], speed, step[j - 1], step[j], step[j + 1])
    result = []
    for j in range(count):
        flux_x = zonal_flux(c[j], m[j], half[j], get("u", first + j))
        total = each(lambda f, g, a, b: (f - g) + (a - b), flux_x, minus(flux_x), flux[j], flux[j - 1])
        down = each(vertical_divergence, c[j], half[j], get("w", first + j))
        result.append(each(lambda a, x, z, o: (a - x - z) * o, c[j], total, down, m[j]))
    return result, flux, step


def slope_flux(k1, k2, opened, step, s1, s2, z1, z2):
    return (k1 + k2) * opened * (step + (s1 + s2) * (z1 + z2))


def eastward(a, m, k, sx, twice_z):
    opened = each(jnp.multiply, m, plus(m))
    step = each(lambda x, y, o: (y - x) * o, a, plus(a), opened)
    return step, each(slope_flux, k, plus(k), opened, step, sx, plus(sx), twice_z, plus(twice_z))


def diffuse_rows(get, first, count, beside=None):
    a, m, k, sy, step_z, twice_z, step_y, flux_y = [{} for _ in range(8)]
    result = []
    last = lane_of() == LANES - 1

    def row_result(j):
        sx = get("sx", first + j)
        step_x, flux_x = eastward(a[j], m[j], k[j], sx, twice_z[j])
        west = [None, None]
        if beside:
            east, west = beside(first + j)
            step_x = [step_x[0], jnp.where(last, east[0], step_x[1])]
            flux_x = [flux_x[0], jnp.where(last, east[1], flux_x[1])]
        twice_x = each(jnp.add, step_x, minus(step_x, 2, west[0]))
        twice_y = each(jnp.add, step_y[j - 1], step_y[j])
        total = each(lambda f, g, p, q: (f - g) + (p - q), flux_x, minus(flux_x, 2, west[1]), flux_y[j], flux_y[j - 1])

        def finish(value, marker, kappa, east, north, tx, ty, sz, across):
            face_east, face_north = east + below(east), north + below(north)
            flux_z = (kappa + below(kappa)) * open_below(marker) * (
                face_east * (tx + below(tx)) + face_north * (ty + below(ty))
                + (face_east * face_east + face_north * face_north) * (16.0 * sz)
            )
            return (value + across + (flux_z - above(flux_z))) * marker

        result.append(each(finish, a[j][:2], m[j], k[j], sx, sy[j], twice_x, twice_y, step_z[j], total))

    for j in range(-1, count + 1):
        a[j], m[j], k[j], sy[j] = [get(name, first + j) for name in ("a", "m", "k", "sy")]
        wide = 3 if 0 <= j < count else 2
        step_z[j] = each(lambda x, o: (below(x) - x) * open_below(o), a[j][:wide], m[j])
        twice_z[j] = each(lambda x: above(x) + x, step_z[j])
        if j >= 0:
            opened = each(jnp.multiply, m[j - 1][:2], m[j][:2])
            step_y[j - 1] = each(lambda x, y, o: (y - x) * o, a[j - 1][:2], a[j][:2], opened)
            flux_y[j - 1] = each(
                slope_flux, k[j - 1], k[j], opened, step_y[j - 1], sy[j - 1], sy[j], twice_z[j - 1], twice_z[j]
            )
        if j >= 1:
            row_result(j - 1)
    return result


def tiles_of(ref, row, count):
    return [ref[row, :, t * LANES : (t + 1) * LANES] for t in range(count)]


def interior_kernel(*refs):
    rows, advected, sources, slope = refs[:5], refs[5], refs[6:10], refs[10]
    out, kept, strips, slope_rows, narrow = refs[11:]
    rows = rows[:3] + (slope_rows,) + rows[4:]
    for part in range(8):
        for h in range(2):
            wide = slice(h * LANES, (h + 1) * LANES)
            turned = jnp.transpose(slope[:, 8 * part : 8 * part + 8, wide], (1, 0, 2))
            slope_rows[8 * part : 8 * part + 8, :, wide] = turned * 0.125
    lane = lane_of()
    near_east, near_west = lane >= LANES - 2, lane < 2

    full = []
    for g in range(8):
        groups = {n: strip_at(g, i // 2, i % 2, *sources) for i, n in enumerate(GROUPS)}
        full.append(split_groups(groups))
        for i, n in enumerate(GROUPS):
            strips[i, g] = groups[n]

    def get_strip(name, g):
        x = full[g % 8][name]
        return [x if 0 <= g < 8 else pltpu.roll(x, 16 if g < 0 else LANES - 16, 1)]

    for g, (a,) in enumerate(advect_rows(get_strip, 0, 8)[0]):
        part = full[g]
        step_z = (below(a) - a) * open_below(part["m"])
        step, flux = eastward([a], [part["m"]], [part["k"]], [part["sx"]], [above(step_z) + step_z])
        narrow[0, g], narrow[1, g], narrow[2, g] = a, step[0], flux[0]

    def lanes_to(which, row, lane_from, lane_to):
        part = row // 8
        return pltpu.roll(narrow[which, row - 8 * part], lax.rem(2 * LANES + lane_to - lane_from - 16 * part, LANES), 1)

    def get(name, row):
        if name != "a":
            return field_tiles(rows, name, row)
        left, right = tiles_of(advected, row, 2)
        return [
            jnp.where(near_west, lanes_to(0, row, 10, 0), left),
            jnp.where(near_east, lanes_to(0, row, 3, LANES - 1), right),
        ]

    def beside(row):
        return [lanes_to(i, row, 3, LANES - 1) for i in (1, 2)], [lanes_to(i, row, 9, 0) for i in (1, 2)]

    for i, row in enumerate(KEPT):
        third = jnp.where(lane < 64, lanes_to(0, row, 4, 0), lanes_to(0, row, 9, LANES - 1))
        for t, tile in enumerate(get("a", row) + [third]):
            kept[i, :, t * LANES : (t + 1) * LANES] = tile

    def diffuse_block(block, carry):
        first = jnp.minimum(3 + 10 * block, ROWS - 3 - 10)
        for j, tiles in enumerate(diffuse_rows(get, first, 10, beside)):
            for t in range(2):
                out[first + j, :, t * LANES : (t + 1) * LANES] = tiles[t]
        return carry

    lax.fori_loop(0, 6, diffuse_block, 0)


def rim_kernel(*refs):
    got_b, got_a = refs[0], refs[1]
    fields = refs[2:7]
    strips, inner, kept, out, edges, sems = refs[7:]
    middle = pltpu.make_async_copy
    copies = [middle(inner.at[8:56, i], out.at[i, 8:56], sems.at[i]) for i in range(8)]
    for copy in copies:
        copy.start()
    low = low_of()
    lat = lax.axis_index("lat")
    even = jnp.broadcast_to(lat % 2, (8, LANES)) == 0
    floor = jnp.broadcast_to(lat, (8, LANES)) == 0

    def halo(is_north):
        def tile(i, h):
            a = got_a[i, :, h * LANES : (h + 1) * LANES]
            b = got_b[i, :, h * LANES : (h + 1) * LANES]
            if is_north:
                return jnp.where(even, a, b)
            return jnp.where(floor, 0.0, jnp.where(even, b, a))

        tiles = [[tile(i, h) for h in range(2)] for i in range(6)]
        corner = jnp.where(low, pltpu.roll(tiles[5][0], 4, 0), tiles[5][1])
        c_side, step_side, mv = [third_of(corner, 16 * i) for i in range(3)]
        row = {
            "c": tiles[2] + [c_side],
            "m": each(twice_low, tiles[3]) + [twice_low(mv)],
            "v": each(twice_low, tiles[4]) + [twice_high(mv)],
            "sy": each(twice_high, tiles[4]),
            "k": each(twice_low, tiles[5]),
        }
        return row, tiles[0], tiles[1] + [step_side], each(twice_high, tiles[3])

    for is_north in (False, True):
        outer, cell, step_in, rest = halo(is_north)
        start, beyond = (ROWS - 2, ROWS) if is_north else (0, -1)
        made, sides = {}, {}
        for row in range(*((ROWS - 4, ROWS) if is_north else (0, 4))):
            base = 16 * (row // 8)
            sides[row] = third_tile({n: strips[i, row % 8] for i, n in enumerate(GROUPS)}, base)

        def get(name, row):
            if name == "a":
                return made[row] if row in made else tiles_of(kept, KEPT.index(row), 3)
            if row == beyond:
                return outer[name]
            tiles = field_tiles(fields, name, row)
            return tiles if name == "sy" else tiles + [sides[row][name]]

        known = {2: [-x for x in step_in]} if is_north else {-2: step_in}
        results, flux, step = advect_rows(get, start, 2, known)
        made.update(zip((start, start + 1), results))
        face, sign = (1, -1.0) if is_north else (-1, 1.0)
        made[beyond] = each(
            lambda q, g, s, t, f, o: (q + g * median(s, sign * t) - sign * f) * o,
            cell, rest, step_in, step[face], flux[face], outer["m"],
        )
        final = ROWS - 3 if is_north else 0
        base = ROWS - 8 if is_north else 0
        done = {final + j: x for j, x in enumerate(diffuse_rows(get, final, 3))}
        for h in range(2):
            stack = [done[j][h] if j in done else inner[j, :, h * LANES : (h + 1) * LANES] for j in range(base, base + 8)]
            edges[int(is_north), :, :, h * LANES : (h + 1) * LANES] = jnp.transpose(jnp.stack(stack), (1, 0, 2))
        copy = middle(edges.at[int(is_north)], out.at[:, base : base + 8], sems.at[8 + int(is_north)])
        copy.start()
        copies.append(copy)
    for copy in copies:
        copy.wait()


def call(kernel, shapes, *operands, **options):
    return pl.pallas_call(
        kernel,
        out_shape=[jax.ShapeDtypeStruct(s, F32) for s in shapes],
        in_specs=[VMEM] * len(operands),
        out_specs=[VMEM] * len(shapes),
        compiler_params=pltpu.CompilerParams(vmem_limit_bytes=LIMIT),
        **options,
    )(*operands)


def make(lons, lats):
    def spot(lon, lat):
        return (lon % lons) * lats + lat

    near = [(spot(i, j), spot(i ^ 1, j)) for i in range(lons) for j in range(lats)]
    far = [(spot(i, j), spot(i + 1 if i % 2 else i - 1, j)) for i in range(lons) for j in range(lats)]
    pair_a = [(spot(i, j), spot(i, j ^ 1)) for i in range(lons) for j in range(lats)]
    pair_b = []
    for i in range(lons):
        for j in range(lats):
            if j == 0:
                pair_b.append((spot(i, j), spot(i ^ 1, j)))
            elif j == lats - 1:
                pair_b.append((spot(i, j), spot(lons - 1 - i, j)))
            else:
                pair_b.append((spot(i, j), spot(i, j + 1 if j % 2 else j - 1)))

    def move(x, route):
        return lax.ppermute(x, ("lon", "lat"), route)

    def shards(tracers, velocity, slopes, diffusivity, sea_mask):
        plane = lambda x: x.reshape(-1, ROWS, 2 * LANES)
        arrays = [plane(tracers), plane(velocity), plane(slopes), diffusivity, sea_mask]
        arrays = [pltpu.with_memory_space_constraint(x, pltpu.HBM) for x in arrays]
        full, side = (ROWS, 8, 2 * LANES), (8, 8, LANES)
        *held, to_near, to_far, own, spare = pl.pallas_call(
            pack_kernel,
            out_shape=[jax.ShapeDtypeStruct(x.shape, x.dtype) for x in arrays]
            + [jax.ShapeDtypeStruct(shape, F32) for shape in [(4, 8, LANES)] * 2 + [side] * 2],
            in_specs=[pl.BlockSpec(memory_space=pltpu.HBM)] * 5,
            out_specs=[VMEM] * 9,
            scratch_shapes=[pltpu.SemaphoreType.DMA((CHUNKS, 6))],
            compiler_params=pltpu.CompilerParams(vmem_limit_bytes=LIMIT),
        )(*arrays)
        far_got, near_got = move(to_far, far), move(to_near, near)
        *rows, advected, made_a, made_b = call(
            advect_kernel, [full] * 6 + [(6, 8, 2 * LANES)] * 2, *held,
            cost_estimate=pl.CostEstimate(flops=10**7, bytes_accessed=6 * 10**6, transcendentals=0),
        )
        send_a, send_b = call(
            edge_kernel, [(6, 8, 2 * LANES)] * 2, far_got, near_got, own, spare, made_a, made_b,
            input_output_aliases={4: 0, 5: 1},
        )
        got_a, got_b = move(send_a, pair_a), move(send_b, pair_b)
        inner, kept, strips, rows[3] = call(
            interior_kernel, [full, (4, 8, 3 * LANES), (4,) + side, full],
            *rows, advected, far_got, near_got, own, spare, held[2],
            scratch_shapes=[pltpu.VMEM((3,) + side, F32)],
            cost_estimate=pl.CostEstimate(flops=2 * 10**7, bytes_accessed=10**7, transcendentals=0),
        )
        out = pl.pallas_call(
            rim_kernel,
            out_shape=jax.ShapeDtypeStruct((8, ROWS, 2 * LANES), F32),
            in_specs=[VMEM] * 10,
            out_specs=pl.BlockSpec(memory_space=pl.ANY),
            scratch_shapes=[pltpu.VMEM((2, 8, 8, 2 * LANES), F32), pltpu.SemaphoreType.DMA((10,))],
            compiler_params=pltpu.CompilerParams(vmem_limit_bytes=LIMIT),
        )(got_b, got_a, *rows, strips, inner, kept)
        return out.reshape(tracers.shape)

    return shards


def solution(mesh):
    return jax.shard_map(
        make(mesh.shape["lon"], mesh.shape["lat"]),
        mesh=mesh,
        in_specs=(
            P(None, None, "lat", "lon"),
            P(None, None, "lat", "lon"),
            P(None, None, "lat", "lon"),
            P(None, "lat", "lon"),
            P(None, "lat", "lon"),
        ),
        out_specs=P(None, None, "lat", "lon"),
        check_vma=False,
    )
```
